128 devices in a mesh: wide: 32 (over x, z, core), mp: 4 (over y).
Axes of the slice: x: 4, y: 4, z: 4, core: 2. Of those that a mesh axis runs over, the one named last changes fastest.
Arguments:
- points: bfloat16 [131072, 512], P('wide', 'mp'), may hold values from -16 to 16
- mask: int32 [131072], P('wide'), may hold values 0 or 1
- perm: int32 [131072], P('wide'), may hold values from 0 to 131071, as said below
- w_qkv: bfloat16 [3, 512, 512], P(None, None, 'mp'), may hold values from -8 to 8
- w_out: bfloat16 [512, 512], P('mp'), may hold values from -0.25 to 0.25
- w_gate_up: bfloat16 [2, 512, 2048], P(None, None, 'mp'), may hold values from -0.25 to 0.25
- w_down: bfloat16 [2048, 512], P('mp'), may hold values from -0.125 to 0.125
- w_coarse: bfloat16 [2, 3, 512, 512], P(None, None, None, 'mp'), may hold values from -8 to 8
- w_coarse_out: bfloat16 [2, 512, 512], P(None, 'mp'), may hold values from -1.5 to 1.5
Outputs:
- refreshed: float32 [131072, 512], P('wide', 'mp')
The draws below stay inside these ranges and needn't reach their ends.
Inputs may be any that keep to these rules, and one draw needn't show every extreme that they name: perm is a permutation of the 131072 rows; the 4096 rows of one index of wide send at most 256 rows to the block of any one index, and exactly 256 to some index in every draw.
All inputs are finite; a program needn't handle non-finite values. No bound on the sum of `mask` on one device may be relied on, other than what follows from the above.
Results may differ from the reference program's by a relative error of at most 0.039.
Values may be sent and summed in bfloat16 or wider, within the bound.
A program may use at most 128 MiB of HBM per device.

```python
import math
import jax
import jax.numpy as jnp
from jax import lax

D = 512
FF = 2048
BALL = 256
P_DEV = 4096
HEAD_DIM = 64
SHARDS = 32
GROUPS = 4
NPTS = 131072


def draw_perm(key, part):
    key = jax.random.fold_in(key, 7)
    subkeys = jax.random.split(key, 6)
    portion = P_DEV // SHARDS
    skewing = jax.random.randint(subkeys[0], (SHARDS // 2,), 0, portion + 1).at[0].set(portion)
    pattern = jnp.stack([portion + skewing, portion - skewing], 1).reshape(SHARDS)
    pattern = pattern[jax.random.permutation(subkeys[1], SHARDS)]
    row_labels = jax.random.permutation(subkeys[2], SHARDS)
    col_labels = jax.random.permutation(subkeys[3], SHARDS)
    counts = pattern[(col_labels[None, :] - row_labels[:, None]) % SHARDS]
    bucket_ends = jnp.cumsum(counts, 1)
    starts = bucket_ends - counts
    row_ids = jnp.arange(P_DEV, dtype=jnp.int32)
    target = jnp.sum((row_ids[None, :, None] >= bucket_ends[:, None, :]).astype(jnp.int32), 2)
    position = row_ids[None, :] - jnp.take_along_axis(starts, target, 1)
    offsets = jnp.cumsum(counts, 0) - counts
    landing = jnp.take_along_axis(offsets, target, 1) + position
    shuffles = jax.vmap(lambda seed_key: jax.random.permutation(seed_key, P_DEV))(jax.random.split(subkeys[4], SHARDS))
    placed = target * P_DEV + shuffles[target, landing]
    orders = jax.vmap(lambda seed_key: jax.random.permutation(seed_key, P_DEV))(jax.random.split(subkeys[5], SHARDS))
    spread_rows = jax.vmap(lambda order_row, placed_row: jnp.zeros((P_DEV,), jnp.int32).at[order_row].set(placed_row.astype(jnp.int32)))(orders, placed)
    return spread_rows.reshape(NPTS).astype(jnp.int32)


def draw_points(key, part):
    key = jax.random.fold_in(key, 11)
    subkeys = jax.random.split(key, 2)
    scale_cols = 0.15 * jnp.exp(jax.random.uniform(subkeys[0], (D,), jnp.float32, 0.0, math.log(10.0)))
    noise = jax.random.normal(subkeys[1], (NPTS, D), jnp.float32)
    values = noise * scale_cols[None, :]
    return jnp.clip(values, -16.0, 16.0).astype(jnp.bfloat16)


def draw_w_qkv(key, part):
    key = jax.random.fold_in(key, 13)
    matrix = jax.random.normal(key, (3, D, D), jnp.float32) * D ** (-0.5)
    matrix = matrix * jnp.array([1.5, 1.5, 1.0], jnp.float32)[:, None, None]
    return jnp.clip(matrix, -8.0, 8.0).astype(jnp.bfloat16)


def draw_w_coarse(key, part):
    key = jax.random.fold_in(key, 17)
    matrix = jax.random.normal(key, (2, 3, D, D), jnp.float32) * D ** (-0.5)
    matrix = matrix * jnp.array([1.5, 1.5, 1.0], jnp.float32)[None, :, None, None]
    return jnp.clip(matrix, -8.0, 8.0).astype(jnp.bfloat16)


def touch_ends(drawn, key, least, largest):
    longest = drawn.shape.index(max(drawn.shape))
    spots = []
    for shift in (0, 1):
        where = [jax.random.randint(jax.random.fold_in(key, axis), (), 0, length) for axis, length in enumerate(drawn.shape)]
        where[longest] = (where[longest] + shift) % drawn.shape[longest]
        spots.append(tuple(where))
    return drawn.at[spots[0]].set(least).at[spots[1]].set(largest)


def block_levels(rng, dims, cuts, low, high):
    def one(dim, blocks):
        draws = jax.random.uniform(jax.random.fold_in(jax.random.fold_in(rng, 6), dim), (blocks,), jnp.float32, low / len(cuts), high / len(cuts))
        return jnp.repeat(jnp.exp(draws), dims[dim] // blocks).reshape((-1,) + (1,) * (len(dims) - dim - 1))

    level = one(*cuts[0])
    for cut in cuts[1:]:
        level = level * one(*cut)
    return level


def bell_draw(rng, extent, deviation, bound, cuts=(), kind=jnp.bfloat16):
    gain = block_levels(rng, extent, cuts, -0.22, 0.18) if cuts else 1.0
    drawn = jax.random.normal(rng, extent, jnp.float32) * deviation * gain
    return jnp.minimum(jnp.maximum(drawn, -bound), bound).astype(kind)


def setup_inputs(seed: int = 0) -> dict:
    key_list = jax.random.split(jax.random.key(seed), 10)
    return {
        "points": draw_points(jax.random.fold_in(key_list[9], 71), 0),
        "mask": touch_ends((jax.random.randint(key_list[1], (NPTS,), 0, 4) < 3).astype(jnp.int32), jax.random.fold_in(key_list[1], 1), 0, 1),
        "perm": draw_perm(jax.random.fold_in(key_list[9], 71), 0),
        "w_qkv": draw_w_qkv(jax.random.fold_in(key_list[9], 71), 0),
        "w_out": bell_draw(key_list[4], (D, D), D ** -0.5, 0.25, ((0, 4),)),
        "w_gate_up": bell_draw(key_list[5], (2, D, FF), D ** -0.5, 0.25, ((2, 4),)),
        "w_down": bell_draw(key_list[6], (FF, D), FF ** -0.5, 0.125, ((0, 4),)),
        "w_coarse": draw_w_coarse(jax.random.fold_in(key_list[9], 71), 0),
        "w_coarse_out": bell_draw(key_list[8], (2, D, D), (D // 32) ** -0.5, 1.5, ((1, 4),)),
    }


def rms_norm(values):
    values = values.astype(jnp.float32)
    return values * lax.rsqrt(lax.optimization_barrier(jnp.mean(values * values, -1, keepdims=True)) + 1e-06)

def attend(queries, key_rows, value_rows, allowed):
    count_q = queries.shape[0]
    count_k = key_rows.shape[0]
    q_heads = queries.reshape(count_q, -1, HEAD_DIM).astype(jnp.float32)
    k_heads = key_rows.reshape(count_k, -1, HEAD_DIM).astype(jnp.float32)
    v_heads = value_rows.reshape(count_k, -1, HEAD_DIM).astype(jnp.float32)
    scores = jnp.einsum('qhe,khe->hqk', q_heads, k_heads) * HEAD_DIM ** (-0.5)
    scores = jnp.where(allowed[None], scores, -1e+30)
    scores = scores - lax.optimization_barrier(jnp.max(scores, -1, keepdims=True))
    expo = jnp.exp(scores)
    weights = (expo / lax.optimization_barrier(jnp.sum(expo, -1, keepdims=True))).astype(jnp.bfloat16)
    mixed_heads = jnp.einsum('hqk,khe->qhe', weights.astype(jnp.float32), v_heads)
    return mixed_heads.astype(jnp.bfloat16).reshape(count_q, -1)

def pool_rows(state_rows, row_mask, factor):
    count_rows = state_rows.shape[0] // factor
    weighted = state_rows.reshape(count_rows, factor, -1).astype(jnp.float32) * row_mask.reshape(count_rows, factor, 1).astype(jnp.float32)
    counted = lax.optimization_barrier(jnp.sum(row_mask.reshape(count_rows, factor), 1))
    pooled = lax.optimization_barrier(jnp.sum(weighted, 1)) / jnp.maximum(counted, 1).astype(jnp.float32)[:, None]
    return (rms_norm(pooled).astype(jnp.bfloat16), (counted > 0).astype(jnp.int32))

def rounded_sum(group_terms):
    rounded = group_terms.astype(jnp.bfloat16)
    rounded = lax.optimization_barrier(rounded)
    return lax.optimization_barrier(jnp.sum(rounded.astype(jnp.float32), 0))

def reference(points, mask, perm, w_qkv, w_out, w_gate_up, w_down, w_coarse, w_coarse_out):
    owned_rows = jnp.zeros_like(points).at[perm].set(points).reshape(SHARDS, P_DEV, D)
    owned_mask = jnp.zeros((NPTS,), jnp.int32).at[perm].set(mask).reshape(SHARDS, P_DEV)
    local = D // GROUPS
    hidden_local = FF // GROUPS
    ball_count = P_DEV // BALL
    ball_rows = jnp.arange(BALL, dtype=jnp.int32)
    diagonal = ball_rows[:, None] == ball_rows[None, :]

    def fine(pieces):
        block_rows, block_mask = pieces
        normed = rms_norm(block_rows).astype(jnp.bfloat16)
        projected = jnp.einsum('pd,tdc->tpc', normed.astype(jnp.float32), w_qkv.astype(jnp.float32)).astype(jnp.bfloat16)
        shaped = projected.reshape(3, ball_count, BALL, D)
        allowed = (block_mask.reshape(ball_count, 1, BALL) > 0) | diagonal[None]
        mixed_heads = jax.vmap(attend)(shaped[0], shaped[1], shaped[2], allowed).reshape(P_DEV, D)
        group_terms = jnp.einsum('pgc,gcd->gpd', mixed_heads.reshape(P_DEV, GROUPS, local).astype(jnp.float32), w_out.reshape(GROUPS, local, D).astype(jnp.float32))
        state_rows = block_rows.astype(jnp.float32) + rounded_sum(group_terms)
        level_one, keep_one = pool_rows(state_rows, block_mask, 4)
        level_two, keep_two = pool_rows(state_rows, block_mask, 8)
        return (state_rows, level_one, keep_one, level_two, keep_two)
    states, level_one, keep_one, level_two, keep_two = lax.map(fine, (owned_rows, owned_mask))
    qkv_one = jnp.einsum('spd,tdc->tspc', level_one.astype(jnp.float32), w_coarse[0].astype(jnp.float32)).astype(jnp.bfloat16)
    qkv_two = jnp.einsum('spd,tdc->tspc', level_two.astype(jnp.float32), w_coarse[1].astype(jnp.float32)).astype(jnp.bfloat16)
    rows_one = P_DEV // 4
    rows_two = P_DEV // 8

    def coarse(device_index):
        partner = jnp.bitwise_xor(device_index, 1)
        keys_one = jnp.concatenate([qkv_one[1, device_index], qkv_one[1, partner]], 0)
        values_one = jnp.concatenate([qkv_one[2, device_index], qkv_one[2, partner]], 0)
        flags_one = jnp.concatenate([keep_one[device_index], keep_one[partner]], 0)
        allowed_one = (flags_one > 0)[None, :] | (jnp.arange(2 * rows_one, dtype=jnp.int32)[None, :] == jnp.arange(rows_one, dtype=jnp.int32)[:, None])
        out_one = attend(qkv_one[0, device_index], keys_one, values_one, allowed_one)
        quartet = jnp.bitwise_xor(device_index, jnp.arange(4, dtype=jnp.int32))
        keys_two = qkv_two[1][quartet].reshape(4 * rows_two, D)
        values_two = qkv_two[2][quartet].reshape(4 * rows_two, D)
        flags_two = keep_two[quartet].reshape(4 * rows_two)
        allowed_two = (flags_two > 0)[None, :] | (jnp.arange(4 * rows_two, dtype=jnp.int32)[None, :] == jnp.arange(rows_two, dtype=jnp.int32)[:, None])
        out_two = attend(qkv_two[0, device_index], keys_two, values_two, allowed_two)
        lift_one = jnp.einsum('pgc,gcd->gpd', out_one.reshape(rows_one, GROUPS, local).astype(jnp.float32), w_coarse_out[0].reshape(GROUPS, local, D).astype(jnp.float32))
        lift_two = jnp.einsum('pgc,gcd->gpd', out_two.reshape(rows_two, GROUPS, local).astype(jnp.float32), w_coarse_out[1].reshape(GROUPS, local, D).astype(jnp.float32))
        state_rows = states[device_index]
        normed_state = rms_norm(state_rows).astype(jnp.bfloat16)
        gate_rows = jnp.dot(normed_state, w_gate_up[0], preferred_element_type=jnp.float32)
        up_rows = jnp.dot(normed_state, w_gate_up[1], preferred_element_type=jnp.float32)
        activated = (jax.nn.silu(gate_rows) * up_rows).astype(jnp.bfloat16)
        down_terms = jnp.einsum('pgf,gfd->gpd', activated.reshape(P_DEV, GROUPS, hidden_local).astype(jnp.float32), w_down.reshape(GROUPS, hidden_local, D).astype(jnp.float32))
        group_terms = down_terms + jnp.repeat(lift_one, 4, axis=1) + jnp.repeat(lift_two, 8, axis=1)
        return state_rows + rounded_sum(group_terms)
    updated = lax.map(coarse, jnp.arange(SHARDS, dtype=jnp.int32)).reshape(NPTS, D)
    return updated[perm]
```

```python
import functools

import jax
import jax.numpy as jnp
from jax import lax
from jax.experimental import pallas as pl
from jax.experimental.pallas import tpu as pltpu
from jax.sharding import PartitionSpec as P

BALL = 256
WIDE = 32
MP = 4
ROWS = 4096
CAP = 256
SLOTS = WIDE * CAP
QUARTER = ROWS // MP
WIDTH = 512
LOCAL = WIDTH // MP
HIDDEN = 2048
ONE = QUARTER // 4
TWO = QUARTER // 8
COARSE = ONE + TWO
F32 = jnp.float32
BF16 = jnp.bfloat16
I32 = jnp.int32
MESH = pl.DeviceIdType.MESH
ANY = pl.BlockSpec(memory_space=pl.ANY)
VMEM = pl.BlockSpec(memory_space=pltpu.VMEM)
SMEM = pl.BlockSpec(memory_space=pltpu.SMEM)
LIMIT = 56 * 1024 * 1024


def shape(dims, kind):
    return jax.ShapeDtypeStruct(dims, kind)


def params(collective=None):
    if collective is None:
        return pltpu.CompilerParams(vmem_limit_bytes=LIMIT)
    return pltpu.CompilerParams(
        vmem_limit_bytes=LIMIT, collective_id=collective, has_side_effects=True
    )


def dot(a, b):
    return jnp.dot(a, b, preferred_element_type=F32)


def dot_t(a, b):
    return lax.dot_general(a, b, (((1,), (1,)), ((), ())), preferred_element_type=F32)


def norm(values):
    return values * lax.rsqrt(jnp.mean(values * values, -1, keepdims=True) + 1e-06)


def rank_kernel(perm_ref, mask_ref, slot_ref, code_ref):
    perm = perm_ref[...]
    target = perm >> 12
    code_ref[...] = (perm & (ROWS - 1)) * 2 + mask_ref[...]
    rows = lax.broadcasted_iota(I32, (256, 256), 0)
    cols = lax.broadcasted_iota(I32, (256, 256), 1)
    upper = jnp.where(rows < cols, 1.0, 0.0).astype(BF16)
    which = lax.broadcasted_iota(I32, (WIDE, 256), 0)
    carry = jnp.zeros((WIDE, 1), F32)
    for c in range(ROWS // 256):
        hot = jnp.where(which == target[c : c + 1, :], 1.0, 0.0)
        before = dot(hot.astype(BF16), upper) + carry
        rank = jnp.sum(hot * before, 0, keepdims=True)
        slot_ref[c : c + 1, :] = target[c : c + 1, :] * CAP + rank.astype(I32)
        carry = carry + jnp.sum(hot, 1, keepdims=True)


def widen(src, dst, rows):
    @pl.loop(0, rows // 256)
    def _(i):
        at = pl.ds(pl.multiple_of(i * 256, 256), 256)
        dst[at, :] = src[at, :].astype(dst.dtype)


UNROLL = 16


def pack_kernel(slot_ref, code_ref, points_ref, none_ref, rows_ref, codes_ref, wide, packed):
    pltpu.sync_copy(none_ref, codes_ref)
    widen(points_ref, wide, ROWS)

    @pl.loop(0, SLOTS // 256)
    def _(i):
        packed[pl.ds(pl.multiple_of(i * 256, 256), 256), :] = jnp.zeros((256, LOCAL), F32)

    @pl.loop(0, ROWS // UNROLL)
    def _(i):
        base = i * UNROLL
        slots = [slot_ref[base + u] for u in range(UNROLL)]
        lines = [wide[pl.ds(base + u, 1), :] for u in range(UNROLL)]
        for u in range(UNROLL):
            packed[pl.ds(slots[u], 1), :] = lines[u]
        codes = [code_ref[base + u] for u in range(UNROLL)]
        for u in range(UNROLL):
            codes_ref[slots[u]] = codes[u]

    widen(packed, rows_ref, SLOTS)


def unpack_kernel(code_ref, got_ref, rows_ref, mask_ref, wide, owned):
    widen(got_ref, wide, SLOTS)

    @pl.loop(0, SLOTS // UNROLL)
    def _(i):
        base = i * UNROLL
        codes = [code_ref[base + u] for u in range(UNROLL)]
        lines = [wide[pl.ds(base + u, 1), :] for u in range(UNROLL)]
        for u in range(UNROLL):
            owned[pl.ds(codes[u] >> 1, 1), :] = lines[u]
        for u in range(UNROLL):
            mask_ref[codes[u] >> 1] = codes[u] & 1

    widen(owned, rows_ref, ROWS)


def repack_kernel(code_ref, rows_ref, out_ref, wide, packed):
    widen(rows_ref, wide, ROWS)

    @pl.loop(0, SLOTS // UNROLL)
    def _(i):
        base = i * UNROLL
        lines = [wide[pl.ds(code_ref[base + u] >> 1, 1), :] for u in range(UNROLL)]
        for u in range(UNROLL):
            packed[pl.ds(base + u, 1), :] = lines[u]

    widen(packed, out_ref, SLOTS)


def finish_kernel(slot_ref, got_ref, out_ref, wide):
    widen(got_ref, wide, SLOTS)

    @pl.loop(0, ROWS // UNROLL)
    def _(i):
        base = i * UNROLL
        lines = [wide[pl.ds(slot_ref[base + u], 1), :] for u in range(UNROLL)]
        for u in range(UNROLL):
            out_ref[pl.ds(base + u, 1), :] = lines[u]


def greet(axis, size):
    me = lax.axis_index(axis)
    barrier = pltpu.get_barrier_semaphore()

    @pl.loop(1, size)
    def _(k):
        pl.semaphore_signal(
            barrier, inc=1, device_id={axis: lax.rem(me + k, size)}, device_id_type=MESH
        )

    pl.semaphore_wait(barrier, size - 1)
    return me


def remote(src, dst, send, recv, device):
    return pltpu.make_async_remote_copy(
        src_ref=src, dst_ref=dst, send_sem=send, recv_sem=recv, device_id=device, device_id_type=MESH
    )


def shuffle_kernel(count, *refs):
    ins, outs = refs[:count], refs[count : 2 * count]
    send, recv, own = refs[2 * count :]
    me = greet("wide", WIDE)

    def copy(k, j):
        peer = lax.rem(me + k, WIDE)
        return remote(
            ins[j].at[peer], outs[j].at[me], send.at[k, j], recv.at[k, j], {"wide": peer}
        )

    @pl.loop(1, WIDE)
    def _(k):
        for j in range(count):
            copy(k, j).start()

    for j in range(count):
        mine = pltpu.make_async_copy(ins[j].at[me], outs[j].at[me], own.at[j])
        mine.start()
        mine.wait()

    @pl.loop(1, WIDE)
    def _(k):
        for j in range(count):
            copy(k, j).wait()


def shuffle(arrays, collective):
    count = len(arrays)
    return pl.pallas_call(
        functools.partial(shuffle_kernel, count),
        out_shape=[shape(a.shape, a.dtype) for a in arrays],
        in_specs=[ANY] * count,
        out_specs=[ANY] * count,
        scratch_shapes=[
            pltpu.SemaphoreType.DMA((WIDE, count)),
            pltpu.SemaphoreType.DMA((WIDE, count)),
            pltpu.SemaphoreType.DMA((count,)),
        ],
        compiler_params=params(collective),
    )(*arrays)


def swap_kernel(pick, place, src, dst, send, recv, own):
    me = greet("mp", MP)

    def copy(k):
        peer = lax.rem(me + k, MP)
        return remote(pick(src, peer), place(dst, me), send.at[k], recv.at[k], {"mp": peer})

    for k in (2, 1, 3):
        copy(k).start()
    mine = pltpu.make_async_copy(pick(src, me), place(dst, me), own)
    mine.start()
    mine.wait()
    for k in (1, 3, 2):
        copy(k).wait()


def swap(array, out, pick, place, collective):
    return pl.pallas_call(
        functools.partial(swap_kernel, pick, place),
        out_shape=out,
        in_specs=[ANY],
        out_specs=ANY,
        scratch_shapes=[
            pltpu.SemaphoreType.DMA((MP,)),
            pltpu.SemaphoreType.DMA((MP,)),
            pltpu.SemaphoreType.DMA,
        ],
        compiler_params=params(collective),
    )(array)


def columns(ref, which):
    return ref.at[:, pl.ds(pl.multiple_of(which * LOCAL, LOCAL), LOCAL)]


def block(ref, which):
    return ref.at[which]


def whole(ref, which):
    return ref


def attend_pair(queries, parts, low):
    mixed = []
    for head in range(2):
        mine = low if head == 0 else jnp.logical_not(low)
        q = jnp.where(mine, queries, jnp.zeros_like(queries))
        scores = [jnp.where(allowed, dot_t(q, keys), -1e30) for keys, _, allowed in parts]
        top = functools.reduce(jnp.maximum, [jnp.max(s, -1, keepdims=True) for s in scores])
        expo = [jnp.exp(s - top) for s in scores]
        total = sum(jnp.sum(e, -1, keepdims=True) for e in expo)
        out = sum(dot(e.astype(BF16), values) for e, (_, values, _) in zip(expo, parts))
        mixed.append(out / total)
    return jnp.where(low, mixed[0], mixed[1])


def fine_kernel(x_ref, mask_ref, qkv_ref, out_ref, state_ref, coarse_ref):
    x = x_ref[...].astype(F32)
    normed = norm(x).astype(BF16)
    q = (dot(normed, qkv_ref[0]) * 0.125).astype(BF16)
    k = dot(normed, qkv_ref[1]).astype(BF16)
    v = dot(normed, qkv_ref[2]).astype(BF16)
    rows = lax.broadcasted_iota(I32, (BALL, BALL), 0)
    cols = lax.broadcasted_iota(I32, (BALL, BALL), 1)
    real = mask_ref[0] > 0
    allowed = jnp.logical_or(real, rows == cols)
    low = lax.broadcasted_iota(I32, (BALL, 128), 1) < 64
    mixed = []
    for g in range(MP):
        at = slice(g * 128, (g + 1) * 128)
        mixed.append(attend_pair(q[:, at], [(k[:, at], v[:, at], allowed)], low).astype(BF16))
    state = x + dot(jnp.concatenate(mixed, 1), out_ref[...])
    state_ref[...] = state
    high = state.astype(BF16)
    rest = (state - high.astype(F32)).astype(BF16)
    for f, begin in ((4, 0), (8, BALL // 4)):
        count_rows = BALL // f
        r = lax.broadcasted_iota(I32, (count_rows, BALL), 0)
        c = lax.broadcasted_iota(I32, (count_rows, BALL), 1)
        hot = jnp.where(jnp.logical_and(r == c // f, real), 1.0, 0.0)
        counted = jnp.sum(hot, 1, keepdims=True)
        hot = hot.astype(BF16)
        pooled = (dot(hot, high) + dot(hot, rest)) / jnp.maximum(counted, 1.0)
        coarse_ref[0, begin : begin + count_rows, :] = norm(pooled).astype(BF16)


def fine(x, mask, w_qkv, w_out):
    balls = QUARTER // BALL
    return pl.pallas_call(
        fine_kernel,
        grid=(balls,),
        out_shape=[shape((QUARTER, WIDTH), F32), shape((balls, 96, WIDTH), BF16)],
        in_specs=[
            pl.BlockSpec((BALL, WIDTH), lambda i: (i, 0)),
            pl.BlockSpec((1, 1, BALL), lambda i: (i, 0, 0)),
            pl.BlockSpec((3, WIDTH, WIDTH), lambda i: (0, 0, 0)),
            pl.BlockSpec((WIDTH, WIDTH), lambda i: (0, 0)),
        ],
        out_specs=[
            pl.BlockSpec((BALL, WIDTH), lambda i: (i, 0)),
            pl.BlockSpec((1, 96, WIDTH), lambda i: (i, 0, 0)),
        ],
        compiler_params=params(),
    )(x, mask, w_qkv, w_out)


def forward_kernel(state_ref, gate_ref, up_ref, down_ref, out_ref):
    state = state_ref[...]
    normed = norm(state).astype(BF16)
    total = state
    for c in range(MP):
        gate = dot(normed, gate_ref[c])
        up = dot(normed, up_ref[c])
        activated = (gate / (1.0 + jnp.exp(-gate)) * up).astype(BF16)
        total = total + dot(activated, down_ref[c])
    out_ref[...] = total


def forward(state, gate_up, down):
    tiles = QUARTER // BALL
    return pl.pallas_call(
        forward_kernel,
        grid=(tiles,),
        out_shape=shape((QUARTER, WIDTH), F32),
        in_specs=[
            pl.BlockSpec((BALL, WIDTH), lambda i: (i, 0)),
            pl.BlockSpec((MP, None, WIDTH, WIDTH), lambda i: (0, 0, 0, 0)),
            pl.BlockSpec((MP, None, WIDTH, WIDTH), lambda i: (0, 1, 0, 0)),
            pl.BlockSpec((MP, WIDTH, WIDTH), lambda i: (0, 0, 0)),
        ],
        out_specs=pl.BlockSpec((BALL, WIDTH), lambda i: (i, 0)),
        compiler_params=params(),
    )(state, gate_up, gate_up, down)


def project_kernel(rows_ref, w_ref, one_ref, two_ref):
    for ball in range(QUARTER // BALL):
        rows = rows_ref[0, ball]
        for t in range(3):
            scale = 0.125 if t == 0 else 1.0
            one_ref[t, ball * 64 : (ball + 1) * 64, :] = (
                dot(rows[:64], w_ref[0, t]) * scale
            ).astype(BF16)
            two_ref[t, ball * 32 : (ball + 1) * 32, :] = (
                dot(rows[64:], w_ref[1, t]) * scale
            ).astype(BF16)


def project(rows, w_coarse):
    return pl.pallas_call(
        project_kernel,
        grid=(MP,),
        out_shape=[shape((3, 4 * ONE, LOCAL), BF16), shape((3, 4 * TWO, LOCAL), BF16)],
        in_specs=[
            pl.BlockSpec((1, 4, 96, WIDTH), lambda i: (i, 0, 0, 0)),
            pl.BlockSpec((2, 3, WIDTH, LOCAL), lambda i: (0, 0, 0, 0)),
        ],
        out_specs=[
            pl.BlockSpec((3, ONE, LOCAL), lambda i: (0, i, 0)),
            pl.BlockSpec((3, TWO, LOCAL), lambda i: (0, i, 0)),
        ],
        compiler_params=params(),
    )(rows, w_coarse)


def relatives(me):
    low = lax.rem(me, 2)
    high = lax.rem(me // 2, 2)
    first = me + 1 - 2 * low
    second = me + 2 - 4 * high
    third = first + 2 - 4 * high
    return (first, second, third)


def exchange_kernel(one, two, keep, mate_one, mate_two, mate_keep, send, recv):
    me = lax.axis_index("wide")
    others = relatives(me)
    barrier = pltpu.get_barrier_semaphore()
    for other in others:
        pl.semaphore_signal(barrier, inc=1, device_id={"wide": other}, device_id_type=MESH)
    pl.semaphore_wait(barrier, 3)
    copies = []
    for j in (1, 2, 0):
        to = {"wide": others[j]}
        copies.append(remote(two.at[1:], mate_two.at[j], send.at[j, 0], recv.at[j, 0], to))
        copies.append(remote(keep, mate_keep.at[j], send.at[j, 1], recv.at[j, 1], to))
    copies.append(
        remote(one.at[1:], mate_one, send.at[3, 0], recv.at[3, 0], {"wide": others[0]})
    )
    for copy in copies:
        copy.start()
    for copy in copies:
        copy.wait()


def exchange(one, two, keep, collective):
    return pl.pallas_call(
        exchange_kernel,
        out_shape=[
            shape((2, 4 * ONE, LOCAL), BF16),
            shape((3, 2, 4 * TWO, LOCAL), BF16),
            shape((3,) + keep.shape, I32),
        ],
        in_specs=[ANY] * 3,
        out_specs=[ANY] * 3,
        scratch_shapes=[pltpu.SemaphoreType.DMA((4, 2)), pltpu.SemaphoreType.DMA((4, 2))],
        compiler_params=params(collective),
    )(one, two, keep)


def coarse_kernel(one, two, mate_one, mate_two, keep, mate_keep, out):
    tile = 256
    low = lax.broadcasted_iota(I32, (tile, 128), 1) < 64
    flags = [keep[...]] + [mate_keep[j] for j in range(3)]

    def own(begin, real, length):
        rows = lax.broadcasted_iota(I32, (tile, length), 0) + begin
        cols = lax.broadcasted_iota(I32, (tile, length), 1)
        return jnp.logical_or(real, rows == cols)

    for t in range(4):
        begin = t * tile
        real = [flags[j][:, : 4 * ONE] > 0 for j in range(2)]
        parts = [
            (one[1], one[2], own(begin, real[0], 4 * ONE)),
            (mate_one[0], mate_one[1], real[1]),
        ]
        mixed = attend_pair(one[0, begin : begin + tile, :], parts, low)
        out[t, 0:256, :] = mixed.astype(BF16)
    for t in range(2):
        begin = t * tile
        real = [flags[j][:, 4 * ONE :] > 0 for j in range(4)]
        parts = [(two[1], two[2], own(begin, real[0], 4 * TWO))]
        for j in range(3):
            parts.append((mate_two[j, 0], mate_two[j, 1], real[j + 1]))
        mixed = attend_pair(two[0, begin : begin + tile, :], parts, low).astype(BF16)
        out[2 * t, 256:384, :] = mixed[:128]
        out[2 * t + 1, 256:384, :] = mixed[128:]


def coarse(one, two, mate_one, mate_two, keep, mate_keep):
    return pl.pallas_call(
        coarse_kernel,
        out_shape=shape((MP, COARSE, LOCAL), BF16),
        in_specs=[VMEM] * 6,
        out_specs=VMEM,
        compiler_params=params(),
    )(one, two, mate_one, mate_two, keep, mate_keep)


def lift_kernel(state_ref, mixed_ref, w_ref, out_ref):
    one = dot(mixed_ref[0:ONE, :], w_ref[0]).astype(BF16)
    two = dot(mixed_ref[ONE:COARSE, :], w_ref[1]).astype(BF16)
    for t in range(QUARTER // BALL):
        both = jnp.concatenate([one[t * 64 : (t + 1) * 64], two[t * 32 : (t + 1) * 32]], 0)
        r = lax.broadcasted_iota(I32, (BALL, 96), 0)
        c = lax.broadcasted_iota(I32, (BALL, 96), 1)
        hot = jnp.logical_or(
            jnp.logical_and(c < 64, r // 4 == c), jnp.logical_and(c >= 64, r // 8 == c - 64)
        )
        spread = dot(jnp.where(hot, 1.0, 0.0).astype(BF16), both)
        at = slice(t * BALL, (t + 1) * BALL)
        out_ref[at, :] = (state_ref[at, :] + spread).astype(BF16)


def lift(state, mixed, w_coarse_out):
    return pl.pallas_call(
        lift_kernel,
        out_shape=shape((QUARTER, WIDTH), BF16),
        in_specs=[VMEM] * 3,
        out_specs=VMEM,
        compiler_params=params(),
    )(state, mixed, w_coarse_out)


def on_device(points, mask, perm, w_qkv, w_out, w_gate_up, w_down, w_coarse, w_coarse_out):
    full_qkv = lax.all_gather(w_qkv, "mp", axis=2, tiled=True)
    full_out = lax.all_gather(w_out, "mp", axis=0, tiled=True)
    full_gate_up = lax.all_gather(w_gate_up, "mp", axis=0)
    full_down = lax.all_gather(w_down, "mp", axis=0)
    full_coarse_out = lax.all_gather(w_coarse_out, "mp", axis=1, tiled=True)

    slot, code = pl.pallas_call(
        rank_kernel,
        out_shape=[shape((16, 256), I32)] * 2,
        in_specs=[VMEM] * 2,
        out_specs=[VMEM] * 2,
        compiler_params=params(),
    )(perm.reshape(16, 256), mask.reshape(16, 256))
    slot = slot.reshape(ROWS)
    code = code.reshape(ROWS)
    rows, codes = pl.pallas_call(
        pack_kernel,
        out_shape=[shape((SLOTS, LOCAL), BF16), shape((SLOTS,), I32)],
        in_specs=[SMEM, SMEM, VMEM, ANY],
        out_specs=[VMEM, SMEM],
        scratch_shapes=[pltpu.VMEM((ROWS, LOCAL), F32), pltpu.VMEM((SLOTS, LOCAL), F32)],
        compiler_params=params(),
    )(slot, code, points, jnp.full((SLOTS,), 2 * ROWS, I32))
    got, got_code = shuffle(
        [rows.reshape(WIDE, CAP, LOCAL), codes.reshape(WIDE, 2, 128)], 1
    )
    got_code = got_code.reshape(SLOTS)
    owned, owned_mask = pl.pallas_call(
        unpack_kernel,
        out_shape=[shape((ROWS, LOCAL), BF16), shape((ROWS + 128,), I32)],
        in_specs=[SMEM, VMEM],
        out_specs=[VMEM, SMEM],
        scratch_shapes=[pltpu.VMEM((SLOTS, LOCAL), F32), pltpu.VMEM((ROWS + 8, LOCAL), F32)],
        compiler_params=params(),
    )(got_code, got.reshape(SLOTS, LOCAL))
    owned_mask = owned_mask[:ROWS]
    keep_one = (jnp.sum(owned_mask.reshape(ROWS // 4, 4), 1) > 0).astype(I32)
    keep_two = (jnp.sum(owned_mask.reshape(ROWS // 8, 8), 1) > 0).astype(I32)
    keep = jnp.concatenate([keep_one, keep_two]).reshape(1, 12 * 128)
    quarter_mask = lax.dynamic_slice_in_dim(
        owned_mask.reshape(MP, QUARTER), lax.axis_index("mp"), 1, 0
    ).reshape(QUARTER // BALL, 1, BALL)
    x = swap(
        owned.reshape(MP, QUARTER, LOCAL), shape((QUARTER, WIDTH), BF16), block, columns, 2
    )
    state, pooled = fine(x, quarter_mask, full_qkv, full_out)
    all_pooled = swap(pooled, shape((MP,) + pooled.shape, BF16), whole, block, 3)
    one, two = project(all_pooled, w_coarse)
    mate_one, mate_two, mate_keep = exchange(one, two, keep, 4)
    fed = forward(state, full_gate_up, full_down)
    mixed = coarse(one, two, mate_one, mate_two, keep, mate_keep)
    all_mixed = swap(mixed, shape((COARSE, WIDTH), BF16), block, columns, 5)
    result = lift(fed, all_mixed, full_coarse_out)
    updated = swap(result, shape((MP, QUARTER, LOCAL), BF16), columns, block, 6)
    back = pl.pallas_call(
        repack_kernel,
        out_shape=shape((SLOTS, LOCAL), BF16),
        in_specs=[SMEM, VMEM],
        out_specs=VMEM,
        scratch_shapes=[pltpu.VMEM((ROWS + 8, LOCAL), F32), pltpu.VMEM((SLOTS, LOCAL), F32)],
        compiler_params=params(),
    )(got_code, updated.reshape(ROWS, LOCAL))
    (returned,) = shuffle([back.reshape(WIDE, CAP, LOCAL)], 7)
    return pl.pallas_call(
        finish_kernel,
        out_shape=shape((ROWS, LOCAL), F32),
        in_specs=[SMEM, VMEM],
        out_specs=VMEM,
        scratch_shapes=[pltpu.VMEM((SLOTS, LOCAL), F32)],
        compiler_params=params(),
    )(slot, returned.reshape(SLOTS, LOCAL))


def solution(mesh):
    placed = (
        P("wide", "mp"),
        P("wide"),
        P("wide"),
        P(None, None, "mp"),
        P("mp", None),
        P(None, None, "mp"),
        P("mp", None),
        P(None, None, None, "mp"),
        P(None, "mp", None),
    )
    return jax.shard_map(
        on_device, mesh=mesh, in_specs=placed, out_specs=P("wide", "mp"), check_vma=False
    )
```

```python
import functools

import jax
import jax.numpy as jnp
from jax import lax
from jax.experimental import pallas as pl
from jax.experimental.pallas import tpu as pltpu
from jax.sharding import PartitionSpec as P

BALL = 256
WIDE = 32
MP = 4
ROWS = 4096
CAP = 256
SLOTS = WIDE * CAP
QUARTER = ROWS // MP
WIDTH = 512
LOCAL = WIDTH // MP
HIDDEN = 2048
ONE = QUARTER // 4
TWO = QUARTER // 8
COARSE = ONE + TWO
F32 = jnp.float32
BF16 = jnp.bfloat16
I32 = jnp.int32
MESH = pl.DeviceIdType.MESH
ANY = pl.BlockSpec(memory_space=pl.ANY)
VMEM = pl.BlockSpec(memory_space=pltpu.VMEM)
SMEM = pl.BlockSpec(memory_space=pltpu.SMEM)
LIMIT = 56 * 1024 * 1024


def shape(dims, kind):
    return jax.ShapeDtypeStruct(dims, kind)


def params(collective=None):
    if collective is None:
        return pltpu.CompilerParams(vmem_limit_bytes=LIMIT)
    return pltpu.CompilerParams(
        vmem_limit_bytes=LIMIT, collective_id=collective, has_side_effects=True
    )


def dot(a, b):
    return jnp.dot(a, b, preferred_element_type=F32)


def dot_t(a, b):
    return lax.dot_general(a, b, (((1,), (1,)), ((), ())), preferred_element_type=F32)


def norm(values):
    return values * lax.rsqrt(jnp.mean(values * values, -1, keepdims=True) + 1e-06)


UNROLL = 16
NONE = 2 * ROWS


def index_kernel(
    perm_ref, mask_ref, blank_ref, slot_ref, source_ref, codes_ref, slots, codes, slot_s, code_s, sems
):
    blanks = [
        pltpu.make_async_copy(blank_ref.at[0], source_ref, sems.at[0]),
        pltpu.make_async_copy(blank_ref.at[1], codes_ref, sems.at[1]),
    ]
    for copy in blanks:
        copy.start()
    perm = perm_ref[...]
    target = perm >> 12
    codes[...] = (perm & (ROWS - 1)) * 2 + mask_ref[...]
    rows = lax.broadcasted_iota(I32, (256, 256), 0)
    cols = lax.broadcasted_iota(I32, (256, 256), 1)
    upper = jnp.where(rows < cols, 1.0, 0.0).astype(BF16)
    which = lax.broadcasted_iota(I32, (WIDE, 256), 0)
    carry = jnp.zeros((WIDE, 1), F32)
    for c in range(ROWS // 256):
        hot = jnp.where(which == target[c : c + 1, :], 1.0, 0.0)
        before = dot(hot.astype(BF16), upper) + carry
        rank = jnp.sum(hot * before, 0, keepdims=True)
        slots[c : c + 1, :] = target[c : c + 1, :] * CAP + rank.astype(I32)
        carry = carry + jnp.sum(hot, 1, keepdims=True)
    slot_ref[...] = slots[...]
    moves = [
        pltpu.make_async_copy(slots, slot_s, sems.at[2]),
        pltpu.make_async_copy(codes, code_s, sems.at[3]),
    ]
    for copy in moves:
        copy.start()
    for copy in blanks + moves:
        copy.wait()
    for c in range(ROWS // 256):

        @pl.loop(0, 256 // UNROLL)
        def _(i):
            base = i * UNROLL
            at = [slot_s[c, base + u] for u in range(UNROLL)]
            code = [code_s[c, base + u] for u in range(UNROLL)]
            for u in range(UNROLL):
                source_ref[at[u]] = c * 256 + base + u
                codes_ref[at[u]] = code[u]


def index(perm, mask):
    blank = jnp.broadcast_to(jnp.array([[0], [NONE]], I32), (2, SLOTS))
    return pl.pallas_call(
        index_kernel,
        out_shape=[shape((16, 256), I32), shape((SLOTS,), I32), shape((SLOTS,), I32)],
        in_specs=[VMEM, VMEM, ANY],
        out_specs=[VMEM, SMEM, SMEM],
        scratch_shapes=[
            pltpu.VMEM((16, 256), I32),
            pltpu.VMEM((16, 256), I32),
            pltpu.SMEM((16, 256), I32),
            pltpu.SMEM((16, 256), I32),
            pltpu.SemaphoreType.DMA((4,)),
        ],
        compiler_params=params(),
    )(perm.reshape(16, 256), mask.reshape(16, 256), blank)


def widen(src, dst, rows):
    @pl.loop(0, rows // 256)
    def _(i):
        at = pl.ds(pl.multiple_of(i * 256, 256), 256)
        dst[at, :] = src[at, :].astype(dst.dtype)


def unpack_kernel(code_ref, got_ref, rows_ref, mask_ref, wide, owned):
    widen(got_ref, wide, SLOTS)

    @pl.loop(0, SLOTS // UNROLL)
    def _(i):
        base = i * UNROLL

        @pl.when(code_ref[base] < NONE)
        def _():
            codes = [code_ref[base + u] for u in range(UNROLL)]
            lines = [wide[pl.ds(base + u, 1), :] for u in range(UNROLL)]
            for u in range(UNROLL):
                owned[pl.ds(codes[u] >> 1, 1), :] = lines[u]
            for u in range(UNROLL):
                mask_ref[codes[u] >> 1] = codes[u] & 1

    widen(owned, rows_ref, ROWS)


def finish_kernel(slot_ref, got_ref, out_ref, wide):
    widen(got_ref, wide, SLOTS)

    @pl.loop(0, ROWS // UNROLL)
    def _(i):
        base = i * UNROLL
        lines = [wide[pl.ds(slot_ref[base + u], 1), :] for u in range(UNROLL)]
        for u in range(UNROLL):
            out_ref[pl.ds(base + u, 1), :] = lines[u]


def greet(axis, size):
    me = lax.axis_index(axis)
    barrier = pltpu.get_barrier_semaphore()

    @pl.loop(1, size)
    def _(k):
        pl.semaphore_signal(
            barrier, inc=1, device_id={axis: lax.rem(me + k, size)}, device_id_type=MESH
        )

    pl.semaphore_wait(barrier, size - 1)
    return me


def remote(src, dst, send, recv, device):
    return pltpu.make_async_remote_copy(
        src_ref=src, dst_ref=dst, send_sem=send, recv_sem=recv, device_id=device, device_id_type=MESH
    )


def gather_bucket(line, lookup, wide, staged, packed, peer):
    @pl.loop(0, CAP // UNROLL)
    def _(i):
        begin = i * UNROLL
        lines = [wide[pl.ds(lookup(peer * CAP + begin + u), 1), :] for u in range(UNROLL)]
        for u in range(UNROLL):
            staged[line, pl.ds(begin + u, 1), :] = lines[u]

    packed[peer] = staged[line].astype(BF16)


def send_kernel(
    source_ref, points_ref, codes_ref, qkv_ref, out_ref, gate_up_ref, down_ref, lift_ref,
    got_ref, got_codes_ref, all_qkv, all_out, all_gate_up, all_down, all_lift,
    wide, staged, packed, send, recv, own, w_send, w_recv, w_own,
):
    me = lax.axis_index("wide")
    mp = lax.axis_index("mp")
    core = lax.rem(me, 2)
    partner = me + 1 - 2 * core
    after, ahead = lax.rem(mp + 1, MP), lax.rem(mp + 2, MP)
    behind = lax.rem(mp + 3, MP)
    barrier = pltpu.get_barrier_semaphore()

    @pl.loop(1, WIDE)
    def _(k):
        pl.semaphore_signal(
            barrier, inc=1, device_id={"wide": lax.rem(me + k, WIDE)}, device_id_type=MESH
        )

    for other in (after, behind):
        pl.semaphore_signal(barrier, inc=1, device_id={"mp": other}, device_id_type=MESH)
    widen(points_ref, wide, ROWS)

    def part(first, count):
        def rows(ref, quarter):
            return pl.ds(pl.multiple_of(first * quarter, 16), count * quarter)

        def cut(j, ref, shard):
            if j == 0:
                return ref.at[rows(ref, 384), pl.ds(pl.multiple_of(shard * 128, 128), 128)]
            quarter = (0, 32, 256, 128, 64)[j]
            return ref.at[shard, rows(ref, quarter), :]

        def own_cut(j, ref):
            quarter = (384, 32, 256, 128, 64)[j]
            return ref.at[rows(ref, quarter), :]

        return cut, own_cut

    half, own_half = part(2 * core, 2)
    first, _ = part(2 * core, 1)
    second, _ = part(2 * core + 1, 1)
    every, own_every = part(0, 4)
    shards = [qkv_ref, out_ref, gate_up_ref, down_ref, lift_ref]
    full = [all_qkv, all_out, all_gate_up, all_down, all_lift]
    count = len(shards)

    def weight(j, kind, cut, src, shard, device):
        return remote(
            src, cut(j, full[j], shard), w_send.at[j, kind], w_recv.at[j, kind], device
        )

    def weight_copies(j):
        ref = full[j]
        mine = own_half(j, shards[j])
        return [
            weight(j, 0, half, mine, mp, {"mp": after}),
            weight(j, 1, half, mine, mp, {"mp": behind}),
            weight(j, 2, first, first(j, ref, behind), behind, {"mp": after}),
            weight(j, 3, second, second(j, ref, after), after, {"mp": behind}),
            weight(j, 4, half, half(j, ref, behind), behind, {"wide": partner}),
            weight(j, 5, half, half(j, ref, after), after, {"wide": partner}),
            weight(j, 6, first, first(j, ref, ahead), ahead, {"wide": partner}),
            weight(j, 7, second, second(j, ref, ahead), ahead, {"wide": partner}),
        ]

    weights = [weight_copies(j) for j in range(count)]

    def rows_copy(k):
        peer = lax.rem(me + k, WIDE)
        return remote(
            packed.at[peer], got_ref.at[me], send.at[k, 0], recv.at[k, 0], {"wide": peer}
        )

    def codes_copy(k):
        peer = lax.rem(me + k, WIDE)
        return remote(
            codes_ref.at[peer], got_codes_ref.at[me], send.at[k, 1], recv.at[k, 1], {"wide": peer}
        )

    pl.semaphore_wait(barrier, WIDE + 1)
    for j in range(count):
        weights[j][0].start()
        weights[j][1].start()

    @pl.loop(1, WIDE)
    def _(k):
        gather_bucket(0, lambda s: source_ref[s], wide, staged, packed, lax.rem(me + k, WIDE))
        rows_copy(k).start()
        codes_copy(k).start()

    gather_bucket(0, lambda s: source_ref[s], wide, staged, packed, me)
    mine = [
        pltpu.make_async_copy(packed.at[me], got_ref.at[me], own.at[0]),
        pltpu.make_async_copy(codes_ref.at[me], got_codes_ref.at[me], own.at[1]),
    ]
    for j in range(count):
        mine.append(
            pltpu.make_async_copy(own_every(j, shards[j]), every(j, full[j], mp), w_own.at[j])
        )
    for copy in mine:
        copy.start()
    for j in range(count):
        weights[j][0].wait_recv()
        weights[j][2].start()
        weights[j][4].start()
        weights[j][1].wait_recv()
        weights[j][3].start()
        weights[j][5].start()
    for j in range(count):
        weights[j][2].wait_recv()
        weights[j][6].start()
        weights[j][3].wait_recv()
        weights[j][7].start()
    for copy in mine:
        copy.wait()

    @pl.loop(1, WIDE)
    def _(k):
        rows_copy(k).wait()
        codes_copy(k).wait()

    for j in range(count):
        for kind in range(4):
            weights[j][kind].wait_send()
        for kind in range(4, 8):
            weights[j][kind].wait()


def send_rows(source, points, codes, weights, collective):
    return pl.pallas_call(
        send_kernel,
        out_shape=[
            shape((WIDE, CAP, LOCAL), BF16),
            shape((WIDE, 2, 128), I32),
            shape((3 * WIDTH, WIDTH), BF16),
            shape((MP, LOCAL, WIDTH), BF16),
            shape((MP, 2 * WIDTH, WIDTH), BF16),
            shape((MP, WIDTH, WIDTH), BF16),
            shape((MP, 2 * LOCAL, WIDTH), BF16),
        ],
        in_specs=[SMEM, VMEM] + [ANY] * 6,
        out_specs=[ANY] * 7,
        scratch_shapes=[
            pltpu.VMEM((ROWS, LOCAL), F32),
            pltpu.VMEM((1, CAP, LOCAL), F32),
            pltpu.VMEM((WIDE, CAP, LOCAL), BF16),
            pltpu.SemaphoreType.DMA((WIDE, 2)),
            pltpu.SemaphoreType.DMA((WIDE, 2)),
            pltpu.SemaphoreType.DMA((2,)),
            pltpu.SemaphoreType.DMA((5, 8)),
            pltpu.SemaphoreType.DMA((5, 8)),
            pltpu.SemaphoreType.DMA((5,)),
        ],
        compiler_params=params(collective),
    )(source, points, codes, *weights)


def return_kernel(
    code_ref, state_ref, mixed_ref, w_ref, got_ref,
    tiles, turned, wide, staged, packed, send, recv, own, m_send, m_recv, m_own,
):
    me = lax.axis_index("wide")
    mp = lax.axis_index("mp")
    barrier = pltpu.get_barrier_semaphore()

    @pl.loop(1, WIDE)
    def _(k):
        pl.semaphore_signal(
            barrier, inc=1, device_id={"wide": lax.rem(me + k, WIDE)}, device_id_type=MESH
        )

    for k in range(1, MP):
        pl.semaphore_signal(
            barrier, inc=1, device_id={"mp": lax.rem(mp + k, MP)}, device_id_type=MESH
        )

    lifted = []
    for level, rows in ((0, slice(0, ONE)), (1, slice(ONE, COARSE))):
        total = jnp.zeros((rows.stop - rows.start, WIDTH), F32)
        for g in range(MP):
            total = total + dot(
                mixed_ref[rows, g * LOCAL : (g + 1) * LOCAL],
                w_ref[g, level * LOCAL : (level + 1) * LOCAL, :],
            )
        lifted.append(total.astype(BF16))
    one, two = lifted
    r = lax.broadcasted_iota(I32, (BALL, 96), 0)
    c = lax.broadcasted_iota(I32, (BALL, 96), 1)
    hot = jnp.logical_or(
        jnp.logical_and(c < 64, r // 4 == c), jnp.logical_and(c >= 64, r // 8 == c - 64)
    )
    hot = jnp.where(hot, 1.0, 0.0).astype(BF16)

    def turn(k, t):
        peer = lax.rem(mp + k, MP)
        begin = pl.multiple_of(mp * QUARTER + t * BALL, BALL)
        return remote(
            tiles.at[pl.ds(t * BALL, BALL), pl.ds(pl.multiple_of(peer * LOCAL, LOCAL), LOCAL)],
            turned.at[pl.ds(begin, BALL), :],
            m_send.at[k, t],
            m_recv.at[k, t],
            {"mp": peer},
        )

    mine = []
    for t in range(QUARTER // BALL):
        both = jnp.concatenate([one[t * 64 : (t + 1) * 64], two[t * 32 : (t + 1) * 32]], 0)
        at = slice(t * BALL, (t + 1) * BALL)
        tiles[at, :] = (state_ref[at, :] + dot(hot, both)).astype(BF16)
        if t == 0:
            pl.semaphore_wait(barrier, WIDE - 1 + MP - 1)
        for k in (2, 1, 3):
            turn(k, t).start()
        mine.append(
            pltpu.make_async_copy(
                tiles.at[at, pl.ds(pl.multiple_of(mp * LOCAL, LOCAL), LOCAL)],
                turned.at[pl.ds(pl.multiple_of(mp * QUARTER + t * BALL, BALL), BALL), :],
                m_own.at[t],
            )
        )
        mine[-1].start()
    for t in range(QUARTER // BALL):
        mine[t].wait()
        for k in (1, 3, 2):
            turn(k, t).wait()
    widen(turned, wide, ROWS)
    wide[ROWS : ROWS + 8, :] = jnp.zeros((8, LOCAL), F32)

    def rows_copy(k):
        peer = lax.rem(me + k, WIDE)
        return remote(packed.at[peer], got_ref.at[me], send.at[k], recv.at[k], {"wide": peer})

    @pl.loop(1, WIDE)
    def _(k):
        gather_bucket(0, lambda s: code_ref[s] >> 1, wide, staged, packed, lax.rem(me + k, WIDE))
        rows_copy(k).start()

    gather_bucket(0, lambda s: code_ref[s] >> 1, wide, staged, packed, me)
    last = pltpu.make_async_copy(packed.at[me], got_ref.at[me], own)
    last.start()
    last.wait()

    @pl.loop(1, WIDE)
    def _(k):
        rows_copy(k).wait()


def return_rows(codes, state, mixed, w_lift, collective):
    return pl.pallas_call(
        return_kernel,
        out_shape=shape((WIDE, CAP, LOCAL), BF16),
        in_specs=[SMEM, VMEM, VMEM, VMEM],
        out_specs=ANY,
        scratch_shapes=[
            pltpu.VMEM((QUARTER, WIDTH), BF16),
            pltpu.VMEM((ROWS, LOCAL), BF16),
            pltpu.VMEM((ROWS + 8, LOCAL), F32),
            pltpu.VMEM((1, CAP, LOCAL), F32),
            pltpu.VMEM((WIDE, CAP, LOCAL), BF16),
            pltpu.SemaphoreType.DMA((WIDE,)),
            pltpu.SemaphoreType.DMA((WIDE,)),
            pltpu.SemaphoreType.DMA,
            pltpu.SemaphoreType.DMA((MP, 4)),
            pltpu.SemaphoreType.DMA((MP, 4)),
            pltpu.SemaphoreType.DMA((4,)),
        ],
        compiler_params=params(collective),
    )(codes, state, mixed, w_lift)


def swap_kernel(pick, place, src, dst, send, recv, own):
    me = greet("mp", MP)

    def copy(k):
        peer = lax.rem(me + k, MP)
        return remote(pick(src, peer), place(dst, me), send.at[k], recv.at[k], {"mp": peer})

    for k in (2, 1, 3):
        copy(k).start()
    mine = pltpu.make_async_copy(pick(src, me), place(dst, me), own)
    mine.start()
    mine.wait()
    for k in (1, 3, 2):
        copy(k).wait()


def swap(array, out, pick, place, collective):
    return pl.pallas_call(
        functools.partial(swap_kernel, pick, place),
        out_shape=out,
        in_specs=[ANY],
        out_specs=ANY,
        scratch_shapes=[
            pltpu.SemaphoreType.DMA((MP,)),
            pltpu.SemaphoreType.DMA((MP,)),
            pltpu.SemaphoreType.DMA,
        ],
        compiler_params=params(collective),
    )(array)


def columns(ref, which):
    return ref.at[:, pl.ds(pl.multiple_of(which * LOCAL, LOCAL), LOCAL)]


def block(ref, which):
    return ref.at[which]


def whole(ref, which):
    return ref


def attend_pair(queries, parts, low):
    mixed = []
    for head in range(2):
        mine = low if head == 0 else jnp.logical_not(low)
        q = jnp.where(mine, queries, jnp.zeros_like(queries))
        scores = [jnp.where(allowed, dot_t(q, keys), -1e30) for keys, _, allowed in parts]
        top = functools.reduce(jnp.maximum, [jnp.max(s, -1, keepdims=True) for s in scores])
        expo = [jnp.exp(s - top) for s in scores]
        total = sum(jnp.sum(e, -1, keepdims=True) for e in expo)
        out = sum(dot(e.astype(BF16), values) for e, (_, values, _) in zip(expo, parts))
        mixed.append(out / total)
    return jnp.where(low, mixed[0], mixed[1])


def fine_kernel(x_ref, mask_ref, qkv_ref, out_ref, state_ref, coarse_ref):
    x = x_ref[...].astype(F32)
    normed = norm(x).astype(BF16)
    q = (dot(normed, qkv_ref[0]) * 0.125).astype(BF16)
    k = dot(normed, qkv_ref[1]).astype(BF16)
    v = dot(normed, qkv_ref[2]).astype(BF16)
    rows = lax.broadcasted_iota(I32, (BALL, BALL), 0)
    cols = lax.broadcasted_iota(I32, (BALL, BALL), 1)
    real = mask_ref[0] > 0
    allowed = jnp.logical_or(real, rows == cols)
    low = lax.broadcasted_iota(I32, (BALL, 128), 1) < 64
    mixed = []
    for g in range(MP):
        at = slice(g * 128, (g + 1) * 128)
        mixed.append(attend_pair(q[:, at], [(k[:, at], v[:, at], allowed)], low).astype(BF16))
    state = x + dot(jnp.concatenate(mixed, 1), out_ref[...])
    state_ref[...] = state
    high = state.astype(BF16)
    rest = (state - high.astype(F32)).astype(BF16)
    for f, begin in ((4, 0), (8, BALL // 4)):
        count_rows = BALL // f
        r = lax.broadcasted_iota(I32, (count_rows, BALL), 0)
        c = lax.broadcasted_iota(I32, (count_rows, BALL), 1)
        hot = jnp.where(jnp.logical_and(r == c // f, real), 1.0, 0.0)
        counted = jnp.sum(hot, 1, keepdims=True)
        hot = hot.astype(BF16)
        pooled = (dot(hot, high) + dot(hot, rest)) / jnp.maximum(counted, 1.0)
        coarse_ref[0, begin : begin + count_rows, :] = norm(pooled).astype(BF16)


def fine(x, mask, w_qkv, w_out):
    balls = QUARTER // BALL
    return pl.pallas_call(
        fine_kernel,
        grid=(balls,),
        out_shape=[shape((QUARTER, WIDTH), F32), shape((balls, 96, WIDTH), BF16)],
        in_specs=[
            pl.BlockSpec((BALL, WIDTH), lambda i: (i, 0)),
            pl.BlockSpec((1, 1, BALL), lambda i: (i, 0, 0)),
            pl.BlockSpec((3, WIDTH, WIDTH), lambda i: (0, 0, 0)),
            pl.BlockSpec((WIDTH, WIDTH), lambda i: (0, 0)),
        ],
        out_specs=[
            pl.BlockSpec((BALL, WIDTH), lambda i: (i, 0)),
            pl.BlockSpec((1, 96, WIDTH), lambda i: (i, 0, 0)),
        ],
        compiler_params=params(),
    )(x, mask, w_qkv, w_out)


def forward_kernel(state_ref, gate_ref, up_ref, down_ref, out_ref):
    state = state_ref[...]
    normed = norm(state).astype(BF16)
    total = state
    for c in range(MP):
        gate = dot(normed, gate_ref[c])
        up = dot(normed, up_ref[c])
        activated = (gate / (1.0 + jnp.exp(-gate)) * up).astype(BF16)
        total = total + dot(activated, down_ref[c])
    out_ref[...] = total


def forward(state, gate_up, down):
    tiles = QUARTER // BALL
    return pl.pallas_call(
        forward_kernel,
        grid=(tiles,),
        out_shape=shape((QUARTER, WIDTH), F32),
        in_specs=[
            pl.BlockSpec((BALL, WIDTH), lambda i: (i, 0)),
            pl.BlockSpec((MP, None, WIDTH, WIDTH), lambda i: (0, 0, 0, 0)),
            pl.BlockSpec((MP, None, WIDTH, WIDTH), lambda i: (0, 1, 0, 0)),
            pl.BlockSpec((MP, WIDTH, WIDTH), lambda i: (0, 0, 0)),
        ],
        out_specs=pl.BlockSpec((BALL, WIDTH), lambda i: (i, 0)),
        compiler_params=params(),
    )(state, gate_up, gate_up, down)


def project_kernel(rows_ref, w_ref, one_ref, two_ref):
    for ball in range(QUARTER // BALL):
        rows = rows_ref[0, ball]
        for t in range(3):
            scale = 0.125 if t == 0 else 1.0
            one_ref[t, ball * 64 : (ball + 1) * 64, :] = (
                dot(rows[:64], w_ref[0, t]) * scale
            ).astype(BF16)
            two_ref[t, ball * 32 : (ball + 1) * 32, :] = (
                dot(rows[64:], w_ref[1, t]) * scale
            ).astype(BF16)


def project(rows, w_coarse):
    return pl.pallas_call(
        project_kernel,
        grid=(MP,),
        out_shape=[shape((3, 4 * ONE, LOCAL), BF16), shape((3, 4 * TWO, LOCAL), BF16)],
        in_specs=[
            pl.BlockSpec((1, 4, 96, WIDTH), lambda i: (i, 0, 0, 0)),
            pl.BlockSpec((2, 3, WIDTH, LOCAL), lambda i: (0, 0, 0, 0)),
        ],
        out_specs=[
            pl.BlockSpec((3, ONE, LOCAL), lambda i: (0, i, 0)),
            pl.BlockSpec((3, TWO, LOCAL), lambda i: (0, i, 0)),
        ],
        compiler_params=params(),
    )(rows, w_coarse)


def relatives(me):
    low = lax.rem(me, 2)
    high = lax.rem(me // 2, 2)
    first = me + 1 - 2 * low
    second = me + 2 - 4 * high
    third = first + 2 - 4 * high
    return (first, second, third)


def exchange_kernel(one, two, keep, mate_one, mate_two, mate_keep, send, recv):
    me = lax.axis_index("wide")
    others = relatives(me)
    barrier = pltpu.get_barrier_semaphore()
    for other in others:
        pl.semaphore_signal(barrier, inc=1, device_id={"wide": other}, device_id_type=MESH)
    pl.semaphore_wait(barrier, 3)
    copies = []
    for j in (1, 2, 0):
        to = {"wide": others[j]}
        copies.append(remote(two.at[1:], mate_two.at[j], send.at[j, 0], recv.at[j, 0], to))
        copies.append(remote(keep, mate_keep.at[j], send.at[j, 1], recv.at[j, 1], to))
    copies.append(
        remote(one.at[1:], mate_one, send.at[3, 0], recv.at[3, 0], {"wide": others[0]})
    )
    for copy in copies:
        copy.start()
    for copy in copies:
        copy.wait()


def exchange(one, two, keep, collective):
    return pl.pallas_call(
        exchange_kernel,
        out_shape=[
            shape((2, 4 * ONE, LOCAL), BF16),
            shape((3, 2, 4 * TWO, LOCAL), BF16),
            shape((3,) + keep.shape, I32),
        ],
        in_specs=[ANY] * 3,
        out_specs=[ANY] * 3,
        scratch_shapes=[pltpu.SemaphoreType.DMA((4, 2)), pltpu.SemaphoreType.DMA((4, 2))],
        compiler_params=params(collective),
    )(one, two, keep)


def coarse_kernel(one, two, mate_one, mate_two, keep, mate_keep, out):
    tile = 256
    low = lax.broadcasted_iota(I32, (tile, 128), 1) < 64
    flags = [keep[...]] + [mate_keep[j] for j in range(3)]

    def own(begin, real, length):
        rows = lax.broadcasted_iota(I32, (tile, length), 0) + begin
        cols = lax.broadcasted_iota(I32, (tile, length), 1)
        return jnp.logical_or(real, rows == cols)

    for t in range(4):
        begin = t * tile
        real = [flags[j][:, : 4 * ONE] > 0 for j in range(2)]
        parts = [
            (one[1], one[2], own(begin, real[0], 4 * ONE)),
            (mate_one[0], mate_one[1], real[1]),
        ]
        mixed = attend_pair(one[0, begin : begin + tile, :], parts, low)
        out[t, 0:256, :] = mixed.astype(BF16)
    for t in range(2):
        begin = t * tile
        real = [flags[j][:, 4 * ONE :] > 0 for j in range(4)]
        parts = [(two[1], two[2], own(begin, real[0], 4 * TWO))]
        for j in range(3):
            parts.append((mate_two[j, 0], mate_two[j, 1], real[j + 1]))
        mixed = attend_pair(two[0, begin : begin + tile, :], parts, low).astype(BF16)
        out[2 * t, 256:384, :] = mixed[:128]
        out[2 * t + 1, 256:384, :] = mixed[128:]


def coarse(one, two, mate_one, mate_two, keep, mate_keep):
    return pl.pallas_call(
        coarse_kernel,
        out_shape=shape((MP, COARSE, LOCAL), BF16),
        in_specs=[VMEM] * 6,
        out_specs=VMEM,
        compiler_params=params(),
    )(one, two, mate_one, mate_two, keep, mate_keep)


def on_device(points, mask, perm, w_qkv, w_out, w_gate_up, w_down, w_coarse, w_coarse_out):
    slot, source, codes = index(perm, mask)
    got, got_code, full_qkv, full_out, full_gate_up, full_down, full_lift = send_rows(
        source,
        points,
        codes.reshape(WIDE, 2, 128),
        [
            w_qkv.reshape(3 * WIDTH, LOCAL),
            w_out,
            w_gate_up.reshape(2 * WIDTH, WIDTH),
            w_down,
            w_coarse_out.reshape(2 * LOCAL, WIDTH),
        ],
        1,
    )
    full_qkv = full_qkv.reshape(3, WIDTH, WIDTH)
    full_out = full_out.reshape(WIDTH, WIDTH)
    full_gate_up = full_gate_up.reshape(MP, 2, WIDTH, WIDTH)
    got_code = got_code.reshape(SLOTS)
    owned, owned_mask = pl.pallas_call(
        unpack_kernel,
        out_shape=[shape((ROWS, LOCAL), BF16), shape((ROWS + 128,), I32)],
        in_specs=[SMEM, VMEM],
        out_specs=[VMEM, SMEM],
        scratch_shapes=[pltpu.VMEM((SLOTS, LOCAL), F32), pltpu.VMEM((ROWS + 8, LOCAL), F32)],
        compiler_params=params(),
    )(got_code, got.reshape(SLOTS, LOCAL))
    owned_mask = owned_mask[:ROWS]
    keep_one = (jnp.sum(owned_mask.reshape(ROWS // 4, 4), 1) > 0).astype(I32)
    keep_two = (jnp.sum(owned_mask.reshape(ROWS // 8, 8), 1) > 0).astype(I32)
    keep = jnp.concatenate([keep_one, keep_two]).reshape(1, 12 * 128)
    quarter_mask = lax.dynamic_slice_in_dim(
        owned_mask.reshape(MP, QUARTER), lax.axis_index("mp"), 1, 0
    ).reshape(QUARTER // BALL, 1, BALL)
    x = swap(
        owned.reshape(MP, QUARTER, LOCAL), shape((QUARTER, WIDTH), BF16), block, columns, 2
    )
    state, pooled = fine(x, quarter_mask, full_qkv, full_out)
    all_pooled = swap(pooled, shape((MP,) + pooled.shape, BF16), whole, block, 3)
    one, two = project(all_pooled, w_coarse)
    mate_one, mate_two, mate_keep = exchange(one, two, keep, 4)
    fed = forward(state, full_gate_up, full_down)
    mixed = coarse(one, two, mate_one, mate_two, keep, mate_keep)
    all_mixed = swap(mixed, shape((COARSE, WIDTH), BF16), block, columns, 5)
    returned = return_rows(got_code, fed, all_mixed, full_lift, 6)
    return pl.pallas_call(
        finish_kernel,
        out_shape=shape((ROWS, LOCAL), F32),
        in_specs=[SMEM, VMEM],
        out_specs=VMEM,
        scratch_shapes=[pltpu.VMEM((SLOTS, LOCAL), F32)],
        compiler_params=params(),
    )(slot.reshape(ROWS), returned.reshape(SLOTS, LOCAL))


def solution(mesh):
    placed = (
        P("wide", "mp"),
        P("wide"),
        P("wide"),
        P(None, None, "mp"),
        P("mp", None),
        P(None, None, "mp"),
        P("mp", None),
        P(None, None, None, "mp"),
        P(None, "mp", None),
    )
    return jax.shard_map(
        on_device, mesh=mesh, in_specs=placed, out_specs=P("wide", "mp"), check_vma=False
    )
```

```python
import functools

import jax
import jax.numpy as jnp
from jax import lax
from jax.experimental import pallas as pl
from jax.experimental.pallas import tpu as pltpu
from jax.sharding import PartitionSpec as P

BALL = 256
WIDE = 32
MP = 4
ROWS = 4096
CAP = 256
SLOTS = WIDE * CAP
QUARTER = ROWS // MP
WIDTH = 512
LOCAL = WIDTH // MP
HIDDEN = 2048
ONE = QUARTER // 4
TWO = QUARTER // 8
COARSE = ONE + TWO
F32 = jnp.float32
BF16 = jnp.bfloat16
I32 = jnp.int32
MESH = pl.DeviceIdType.MESH
ANY = pl.BlockSpec(memory_space=pl.ANY)
VMEM = pl.BlockSpec(memory_space=pltpu.VMEM)
SMEM = pl.BlockSpec(memory_space=pltpu.SMEM)
LIMIT = 56 * 1024 * 1024


def shape(dims, kind):
    return jax.ShapeDtypeStruct(dims, kind)


def params(collective=None):
    if collective is None:
        return pltpu.CompilerParams(vmem_limit_bytes=LIMIT)
    return pltpu.CompilerParams(
        vmem_limit_bytes=LIMIT, collective_id=collective, has_side_effects=True
    )


def dot(a, b):
    return jnp.dot(a, b, preferred_element_type=F32)


def dot_t(a, b):
    return lax.dot_general(a, b, (((1,), (1,)), ((), ())), preferred_element_type=F32)


def norm(values):
    return values * lax.rsqrt(jnp.mean(values * values, -1, keepdims=True) + 1e-06)


UNROLL = 16
NONE = 2 * ROWS


def index_kernel(perm_ref, mask_ref, slot_ref, source_ref, codes_ref):
    perm = perm_ref[...]
    target = perm >> 12
    code = (perm & (ROWS - 1)) * 2 + mask_ref[...]
    rows = lax.broadcasted_iota(I32, (256, 256), 0)
    cols = lax.broadcasted_iota(I32, (256, 256), 1)
    upper = jnp.where(rows < cols, 1.0, 0.0).astype(BF16)
    which = lax.broadcasted_iota(I32, (WIDE, 256), 0)
    lane = lax.broadcasted_iota(I32, (1, 256), 1).astype(F32)
    carry = jnp.zeros((WIDE, 1), F32)
    found = jnp.zeros((5 * WIDE, CAP), F32)
    for c in range(ROWS // 256):
        row = slice(c, c + 1)
        hot = jnp.where(which == target[row, :], 1.0, 0.0)
        before = dot(hot.astype(BF16), upper) + carry
        rank = jnp.sum(hot * before, 0, keepdims=True).astype(I32)
        slot_ref[row, :] = target[row, :] * CAP + rank
        carry = carry + jnp.sum(hot, 1, keepdims=True)
        placed = jnp.where(rows == rank, 1.0, 0.0).astype(BF16)
        high = (code[row, :] >> 6).astype(F32)
        low = (code[row, :] & 63).astype(F32)
        values = jnp.concatenate([hot * lane, hot * float(c), hot * high, hot * low, hot], 0)
        found = found + dot_t(values.astype(BF16), placed)
    source = found[:WIDE] + found[WIDE : 2 * WIDE] * 256.0
    source_ref[...] = source.astype(I32)
    codes = found[2 * WIDE : 3 * WIDE] * 64.0 + found[3 * WIDE : 4 * WIDE]
    codes_ref[...] = jnp.where(found[4 * WIDE :] > 0.5, codes.astype(I32), NONE)


def index(perm, mask):
    return pl.pallas_call(
        index_kernel,
        out_shape=[shape((16, 256), I32), shape((WIDE, CAP), I32), shape((WIDE, CAP), I32)],
        in_specs=[VMEM] * 2,
        out_specs=[VMEM] * 3,
        compiler_params=params(),
    )(perm.reshape(16, 256), mask.reshape(16, 256))


def inverse_kernel(codes_ref, slot_ref, mask_ref, keep_ref):
    balls = ROWS // BALL
    rows = lax.broadcasted_iota(I32, (256, 256), 0)
    which = lax.broadcasted_iota(I32, (balls, 256), 0)
    lane = lax.broadcasted_iota(I32, (1, 256), 1).astype(F32)
    found = jnp.zeros((3 * balls, 256), F32)
    for c in range(WIDE):
        code = codes_ref[c : c + 1, :]
        landing = code >> 1
        hot = jnp.where(which == (landing >> 8), 1.0, 0.0)
        placed = jnp.where(rows == (landing & 255), 1.0, 0.0).astype(BF16)
        real = (code & 1).astype(F32)
        values = jnp.concatenate([hot * lane, hot * float(c), hot * real], 0)
        found = found + dot_t(values.astype(BF16), placed)
    slot_ref[...] = (found[:balls] + found[balls : 2 * balls] * 256.0).astype(I32)
    mask = found[2 * balls :]
    mask_ref[...] = mask.astype(I32)
    r = lax.broadcasted_iota(I32, (256, 96), 0)
    c = lax.broadcasted_iota(I32, (256, 96), 1)
    hot = jnp.logical_or(
        jnp.logical_and(c < 64, r // 4 == c), jnp.logical_and(c >= 64, r // 8 == c - 64)
    )
    counts = dot(mask.astype(BF16), jnp.where(hot, 1.0, 0.0).astype(BF16))
    keep_ref[...] = jnp.where(counts > 0.5, 1, 0)


def inverse(codes):
    return pl.pallas_call(
        inverse_kernel,
        out_shape=[shape((16, 256), I32), shape((16, 256), I32), shape((16, 96), I32)],
        in_specs=[VMEM],
        out_specs=[VMEM] * 3,
        compiler_params=params(),
    )(codes)


def widen(src, dst, rows):
    @pl.loop(0, rows // 256)
    def _(i):
        at = pl.ds(pl.multiple_of(i * 256, 256), 256)
        dst[at, :] = src[at, :].astype(dst.dtype)


def finish_kernel(slot_ref, got_ref, out_ref, wide):
    widen(got_ref, wide, SLOTS)

    @pl.loop(0, ROWS // UNROLL)
    def _(i):
        base = i * UNROLL
        lines = [wide[pl.ds(slot_ref[base + u], 1), :] for u in range(UNROLL)]
        for u in range(UNROLL):
            out_ref[pl.ds(base + u, 1), :] = lines[u]


def greet(axis, size):
    me = lax.axis_index(axis)
    barrier = pltpu.get_barrier_semaphore()

    @pl.loop(1, size)
    def _(k):
        pl.semaphore_signal(
            barrier, inc=1, device_id={axis: lax.rem(me + k, size)}, device_id_type=MESH
        )

    pl.semaphore_wait(barrier, size - 1)
    return me


def remote(src, dst, send, recv, device):
    return pltpu.make_async_remote_copy(
        src_ref=src, dst_ref=dst, send_sem=send, recv_sem=recv, device_id=device, device_id_type=MESH
    )


def gather_bucket(line, lookup, wide, staged, packed, peer):
    @pl.loop(0, CAP // UNROLL)
    def _(i):
        begin = i * UNROLL
        lines = [wide[pl.ds(lookup(peer * CAP + begin + u), 1), :] for u in range(UNROLL)]
        for u in range(UNROLL):
            staged[line, pl.ds(begin + u, 1), :] = lines[u]

    packed[peer] = staged[line].astype(BF16)


def send_kernel(
    source_ref, points_ref, codes_ref, qkv_ref, out_ref, gate_up_ref, down_ref, lift_ref,
    got_ref, got_codes_ref, all_qkv, all_out, all_gate_up, all_down, all_lift,
    wide, staged, packed, send, recv, own, w_send, w_recv, w_own,
):
    me = lax.axis_index("wide")
    mp = lax.axis_index("mp")
    core = lax.rem(me, 2)
    partner = me + 1 - 2 * core
    after, ahead = lax.rem(mp + 1, MP), lax.rem(mp + 2, MP)
    behind = lax.rem(mp + 3, MP)
    barrier = pltpu.get_barrier_semaphore()

    @pl.loop(1, WIDE)
    def _(k):
        pl.semaphore_signal(
            barrier, inc=1, device_id={"wide": lax.rem(me + k, WIDE)}, device_id_type=MESH
        )

    for other in (after, behind):
        pl.semaphore_signal(barrier, inc=1, device_id={"mp": other}, device_id_type=MESH)
    widen(points_ref, wide, ROWS)

    def part(first, count):
        def rows(ref, quarter):
            return pl.ds(pl.multiple_of(first * quarter, 16), count * quarter)

        def cut(j, ref, shard):
            if j == 0:
                return ref.at[rows(ref, 384), pl.ds(pl.multiple_of(shard * 128, 128), 128)]
            quarter = (0, 32, 256, 128, 64)[j]
            return ref.at[shard, rows(ref, quarter), :]

        def own_cut(j, ref):
            quarter = (384, 32, 256, 128, 64)[j]
            return ref.at[rows(ref, quarter), :]

        return cut, own_cut

    half, own_half = part(2 * core, 2)
    first, _ = part(2 * core, 1)
    second, _ = part(2 * core + 1, 1)
    every, own_every = part(0, 4)
    shards = [qkv_ref, out_ref, gate_up_ref, down_ref, lift_ref]
    full = [all_qkv, all_out, all_gate_up, all_down, all_lift]
    count = len(shards)

    def weight(j, kind, cut, src, shard, device):
        return remote(
            src, cut(j, full[j], shard), w_send.at[j, kind], w_recv.at[j, kind], device
        )

    def weight_copies(j):
        ref = full[j]
        mine = own_half(j, shards[j])
        return [
            weight(j, 0, half, mine, mp, {"mp": after}),
            weight(j, 1, half, mine, mp, {"mp": behind}),
            weight(j, 2, first, first(j, ref, behind), behind, {"mp": after}),
            weight(j, 3, second, second(j, ref, after), after, {"mp": behind}),
            weight(j, 4, half, half(j, ref, behind), behind, {"wide": partner}),
            weight(j, 5, half, half(j, ref, after), after, {"wide": partner}),
            weight(j, 6, first, first(j, ref, ahead), ahead, {"wide": partner}),
            weight(j, 7, second, second(j, ref, ahead), ahead, {"wide": partner}),
        ]

    weights = [weight_copies(j) for j in range(count)]

    def rows_copy(k):
        peer = lax.rem(me + k, WIDE)
        return remote(
            packed.at[peer], got_ref.at[me], send.at[k, 0], recv.at[k, 0], {"wide": peer}
        )

    def codes_copy(k):
        peer = lax.rem(me + k, WIDE)
        return remote(
            codes_ref.at[peer], got_codes_ref.at[me], send.at[k, 1], recv.at[k, 1], {"wide": peer}
        )

    pl.semaphore_wait(barrier, WIDE + 1)
    for j in range(count):
        weights[j][0].start()
        weights[j][1].start()

    @pl.loop(1, WIDE)
    def _(k):
        gather_bucket(0, lambda s: source_ref[s], wide, staged, packed, lax.rem(me + k, WIDE))
        rows_copy(k).start()
        codes_copy(k).start()

    gather_bucket(0, lambda s: source_ref[s], wide, staged, packed, me)
    mine = [
        pltpu.make_async_copy(packed.at[me], got_ref.at[me], own.at[0]),
        pltpu.make_async_copy(codes_ref.at[me], got_codes_ref.at[me], own.at[1]),
    ]
    for j in range(count):
        mine.append(
            pltpu.make_async_copy(own_every(j, shards[j]), every(j, full[j], mp), w_own.at[j])
        )
    for copy in mine:
        copy.start()
    for j in range(count):
        weights[j][0].wait_recv()
        weights[j][2].start()
        weights[j][4].start()
        weights[j][1].wait_recv()
        weights[j][3].start()
        weights[j][5].start()
    for j in range(count):
        weights[j][2].wait_recv()
        weights[j][6].start()
        weights[j][3].wait_recv()
        weights[j][7].start()
    for copy in mine:
        copy.wait()

    @pl.loop(1, WIDE)
    def _(k):
        rows_copy(k).wait()
        codes_copy(k).wait()

    for j in range(count):
        for kind in range(4):
            weights[j][kind].wait_send()
        for kind in range(4, 8):
            weights[j][kind].wait()


def send_rows(source, points, codes, weights, collective):
    return pl.pallas_call(
        send_kernel,
        out_shape=[
            shape((WIDE, CAP, LOCAL), BF16),
            shape((WIDE, 2, 128), I32),
            shape((3 * WIDTH, WIDTH), BF16),
            shape((MP, LOCAL, WIDTH), BF16),
            shape((MP, 2 * WIDTH, WIDTH), BF16),
            shape((MP, WIDTH, WIDTH), BF16),
            shape((MP, 2 * LOCAL, WIDTH), BF16),
        ],
        in_specs=[SMEM, VMEM, ANY] + [VMEM] * 5,
        out_specs=[ANY] * 7,
        scratch_shapes=[
            pltpu.VMEM((ROWS, LOCAL), F32),
            pltpu.VMEM((1, CAP, LOCAL), F32),
            pltpu.VMEM((WIDE, CAP, LOCAL), BF16),
            pltpu.SemaphoreType.DMA((WIDE, 2)),
            pltpu.SemaphoreType.DMA((WIDE, 2)),
            pltpu.SemaphoreType.DMA((2,)),
            pltpu.SemaphoreType.DMA((5, 8)),
            pltpu.SemaphoreType.DMA((5, 8)),
            pltpu.SemaphoreType.DMA((5,)),
        ],
        compiler_params=params(collective),
    )(source, points, codes, *weights)


def return_kernel(
    code_ref, state_ref, mixed_ref, w_ref, got_ref,
    tiles, turned, wide, staged, packed, send, recv, own, m_send, m_recv, m_own,
):
    me = lax.axis_index("wide")
    mp = lax.axis_index("mp")
    barrier = pltpu.get_barrier_semaphore()

    @pl.loop(1, WIDE)
    def _(k):
        pl.semaphore_signal(
            barrier, inc=1, device_id={"wide": lax.rem(me + k, WIDE)}, device_id_type=MESH
        )

    for k in range(1, MP):
        pl.semaphore_signal(
            barrier, inc=1, device_id={"mp": lax.rem(mp + k, MP)}, device_id_type=MESH
        )

    lifted = []
    for level, rows in ((0, slice(0, ONE)), (1, slice(ONE, COARSE))):
        total = jnp.zeros((rows.stop - rows.start, WIDTH), F32)
        for g in range(MP):
            total = total + dot(
                mixed_ref[rows, g * LOCAL : (g + 1) * LOCAL],
                w_ref[g, level * LOCAL : (level + 1) * LOCAL, :],
            )
        lifted.append(total.astype(BF16))
    one, two = lifted
    r = lax.broadcasted_iota(I32, (BALL, 96), 0)
    c = lax.broadcasted_iota(I32, (BALL, 96), 1)
    hot = jnp.logical_or(
        jnp.logical_and(c < 64, r // 4 == c), jnp.logical_and(c >= 64, r // 8 == c - 64)
    )
    hot = jnp.where(hot, 1.0, 0.0).astype(BF16)

    def turn(k, t):
        peer = lax.rem(mp + k, MP)
        begin = pl.multiple_of(mp * QUARTER + t * BALL, BALL)
        return remote(
            tiles.at[pl.ds(t * BALL, BALL), pl.ds(pl.multiple_of(peer * LOCAL, LOCAL), LOCAL)],
            turned.at[pl.ds(begin, BALL), :],
            m_send.at[k, t],
            m_recv.at[k, t],
            {"mp": peer},
        )

    mine = []
    for t in range(QUARTER // BALL):
        both = jnp.concatenate([one[t * 64 : (t + 1) * 64], two[t * 32 : (t + 1) * 32]], 0)
        at = slice(t * BALL, (t + 1) * BALL)
        tiles[at, :] = (state_ref[at, :] + dot(hot, both)).astype(BF16)
        if t == 0:
            pl.semaphore_wait(barrier, WIDE - 1 + MP - 1)
        for k in (2, 1, 3):
            turn(k, t).start()
        mine.append(
            pltpu.make_async_copy(
                tiles.at[at, pl.ds(pl.multiple_of(mp * LOCAL, LOCAL), LOCAL)],
                turned.at[pl.ds(pl.multiple_of(mp * QUARTER + t * BALL, BALL), BALL), :],
                m_own.at[t],
            )
        )
        mine[-1].start()
    for t in range(QUARTER // BALL):
        mine[t].wait()
        for k in (1, 3, 2):
            turn(k, t).wait()
    widen(turned, wide, ROWS)
    wide[ROWS : ROWS + 8, :] = jnp.zeros((8, LOCAL), F32)

    def rows_copy(k):
        peer = lax.rem(me + k, WIDE)
        return remote(packed.at[peer], got_ref.at[me], send.at[k], recv.at[k], {"wide": peer})

    @pl.loop(1, WIDE)
    def _(k):
        gather_bucket(0, lambda s: code_ref[s] >> 1, wide, staged, packed, lax.rem(me + k, WIDE))
        rows_copy(k).start()

    gather_bucket(0, lambda s: code_ref[s] >> 1, wide, staged, packed, me)
    last = pltpu.make_async_copy(packed.at[me], got_ref.at[me], own)
    last.start()
    last.wait()

    @pl.loop(1, WIDE)
    def _(k):
        rows_copy(k).wait()


def return_rows(codes, state, mixed, w_lift, collective):
    return pl.pallas_call(
        return_kernel,
        out_shape=shape((WIDE, CAP, LOCAL), BF16),
        in_specs=[SMEM, VMEM, VMEM, VMEM],
        out_specs=ANY,
        scratch_shapes=[
            pltpu.VMEM((QUARTER, WIDTH), BF16),
            pltpu.VMEM((ROWS, LOCAL), BF16),
            pltpu.VMEM((ROWS + 8, LOCAL), F32),
            pltpu.VMEM((1, CAP, LOCAL), F32),
            pltpu.VMEM((WIDE, CAP, LOCAL), BF16),
            pltpu.SemaphoreType.DMA((WIDE,)),
            pltpu.SemaphoreType.DMA((WIDE,)),
            pltpu.SemaphoreType.DMA,
            pltpu.SemaphoreType.DMA((MP, 4)),
            pltpu.SemaphoreType.DMA((MP, 4)),
            pltpu.SemaphoreType.DMA((4,)),
        ],
        compiler_params=params(collective),
    )(codes, state, mixed, w_lift)


def swap_kernel(pick, place, src, dst, send, recv, own):
    me = greet("mp", MP)

    def copy(k):
        peer = lax.rem(me + k, MP)
        return remote(pick(src, peer), place(dst, me), send.at[k], recv.at[k], {"mp": peer})

    for k in (2, 1, 3):
        copy(k).start()
    mine = pltpu.make_async_copy(pick(src, me), place(dst, me), own)
    mine.start()
    mine.wait()
    for k in (1, 3, 2):
        copy(k).wait()


def swap(array, out, pick, place, collective):
    return pl.pallas_call(
        functools.partial(swap_kernel, pick, place),
        out_shape=out,
        in_specs=[ANY],
        out_specs=ANY,
        scratch_shapes=[
            pltpu.SemaphoreType.DMA((MP,)),
            pltpu.SemaphoreType.DMA((MP,)),
            pltpu.SemaphoreType.DMA,
        ],
        compiler_params=params(collective),
    )(array)


def columns(ref, which):
    return ref.at[:, pl.ds(pl.multiple_of(which * LOCAL, LOCAL), LOCAL)]


def block(ref, which):
    return ref.at[which]


def whole(ref, which):
    return ref


def attend_pair(queries, parts, low):
    mixed = []
    for head in range(2):
        mine = low if head == 0 else jnp.logical_not(low)
        q = jnp.where(mine, queries, jnp.zeros_like(queries))
        scores = [jnp.where(allowed, dot_t(q, keys), -1e30) for keys, _, allowed in parts]
        top = functools.reduce(jnp.maximum, [jnp.max(s, -1, keepdims=True) for s in scores])
        expo = [jnp.exp(s - top) for s in scores]
        total = sum(jnp.sum(e, -1, keepdims=True) for e in expo)
        out = sum(dot(e.astype(BF16), values) for e, (_, values, _) in zip(expo, parts))
        mixed.append(out / total)
    return jnp.where(low, mixed[0], mixed[1])


def fine_ball(x, real, qkv_ref, out_ref):
    x = x.astype(F32)
    normed = norm(x).astype(BF16)
    q = (dot(normed, qkv_ref[0]) * 0.125).astype(BF16)
    k = dot(normed, qkv_ref[1]).astype(BF16)
    v = dot(normed, qkv_ref[2]).astype(BF16)
    rows = lax.broadcasted_iota(I32, (BALL, BALL), 0)
    cols = lax.broadcasted_iota(I32, (BALL, BALL), 1)
    allowed = jnp.logical_or(real, rows == cols)
    low = lax.broadcasted_iota(I32, (BALL, 128), 1) < 64
    mixed = []
    for g in range(MP):
        at = slice(g * 128, (g + 1) * 128)
        mixed.append(attend_pair(q[:, at], [(k[:, at], v[:, at], allowed)], low).astype(BF16))
    state = x + dot(jnp.concatenate(mixed, 1), out_ref[...])
    high = state.astype(BF16)
    rest = (state - high.astype(F32)).astype(BF16)
    coarse = []
    for f in (4, 8):
        count_rows = BALL // f
        r = lax.broadcasted_iota(I32, (count_rows, BALL), 0)
        c = lax.broadcasted_iota(I32, (count_rows, BALL), 1)
        hot = jnp.where(jnp.logical_and(r == c // f, real), 1.0, 0.0)
        counted = jnp.sum(hot, 1, keepdims=True)
        hot = hot.astype(BF16)
        pooled = (dot(hot, high) + dot(hot, rest)) / jnp.maximum(counted, 1.0)
        coarse.append(norm(pooled).astype(BF16))
    return state, coarse


BALLS = QUARTER // BALL


def fine_kernel(
    slot_ref, got_ref, mask_ref, qkv_hbm, out_hbm, gate_up_hbm, down_hbm, fed_ref, coarse_ref,
    wide, staged, packed, x, state, pooled, qkv_ref, out_ref, gate_up_ref, down_ref,
    send, recv, own, c_send, c_recv, c_own, loads,
):
    mp = lax.axis_index("mp")
    barrier = pltpu.get_barrier_semaphore()
    for k in range(1, MP):
        pl.semaphore_signal(
            barrier, inc=1, device_id={"mp": lax.rem(mp + k, MP)}, device_id_type=MESH
        )
    load = [
        pltpu.make_async_copy(qkv_hbm, qkv_ref, loads.at[0]),
        pltpu.make_async_copy(out_hbm, out_ref, loads.at[1]),
        pltpu.make_async_copy(gate_up_hbm, gate_up_ref, loads.at[2]),
        pltpu.make_async_copy(down_hbm, down_ref, loads.at[3]),
    ]
    for copy in load:
        copy.start()
    widen(got_ref, wide, SLOTS)
    pl.semaphore_wait(barrier, MP - 1)

    def place(t):
        return x.at[
            pl.ds(pl.multiple_of(t * BALL, BALL), BALL),
            pl.ds(pl.multiple_of(mp * LOCAL, LOCAL), LOCAL),
        ]

    def turn(k, t):
        peer = lax.rem(mp + k, MP)
        return remote(
            packed.at[peer * BALLS + t], place(t), send.at[k, t], recv.at[k, t], {"mp": peer}
        )

    def keep(t):
        return pltpu.make_async_copy(packed.at[mp * BALLS + t], place(t), own.at[t])

    @pl.loop(0, BALLS)
    def _(t):
        for k in (2, 1, 3):
            peer = lax.rem(mp + k, MP)
            gather_bucket(0, lambda s: slot_ref[s], wide, staged, packed, peer * BALLS + t)
            turn(k, t).start()
        gather_bucket(0, lambda s: slot_ref[s], wide, staged, packed, mp * BALLS + t)
        keep(t).start()

    load[0].wait()
    load[1].wait()

    def share(k, t):
        peer = lax.rem(mp + k, MP)
        return remote(
            pooled.at[t], coarse_ref.at[mp, t], c_send.at[k, t], c_recv.at[k, t], {"mp": peer}
        )

    def hold(t):
        return pltpu.make_async_copy(pooled.at[t], coarse_ref.at[mp, t], c_own.at[t])

    @pl.loop(0, BALLS)
    def _(t):
        for k in (1, 3, 2):
            turn(k, t).wait_recv()
        keep(t).wait()
        at = pl.ds(pl.multiple_of(t * BALL, BALL), BALL)
        real = mask_ref[pl.ds(mp * BALLS + t, 1), :] > 0
        rows, coarse = fine_ball(x[at, :], real, qkv_ref, out_ref)
        state[at, :] = rows
        pooled[t, 0:64, :] = coarse[0]
        pooled[t, 64:96, :] = coarse[1]
        for k in (2, 1, 3):
            share(k, t).start()
        hold(t).start()

    load[2].wait()
    load[3].wait()

    @pl.loop(0, BALLS)
    def _(t):
        at = pl.ds(pl.multiple_of(t * BALL, BALL), BALL)
        fed_ref[at, :] = forward_tile(state[at, :], gate_up_ref, down_ref)

    @pl.loop(0, BALLS)
    def _(t):
        hold(t).wait()
        for k in (1, 3, 2):
            turn(k, t).wait_send()
            share(k, t).wait()


def fine(slots, got, mask, w_qkv, w_out, w_gate_up, w_down, collective):
    dma = pltpu.SemaphoreType.DMA
    return pl.pallas_call(
        fine_kernel,
        out_shape=[shape((QUARTER, WIDTH), F32), shape((MP, BALLS, 96, WIDTH), BF16)],
        in_specs=[SMEM, VMEM, VMEM] + [ANY] * 4,
        out_specs=[VMEM, ANY],
        scratch_shapes=[
            pltpu.VMEM((SLOTS, LOCAL), F32),
            pltpu.VMEM((1, CAP, LOCAL), F32),
            pltpu.VMEM((MP * BALLS, BALL, LOCAL), BF16),
            pltpu.VMEM((QUARTER, WIDTH), BF16),
            pltpu.VMEM((QUARTER, WIDTH), F32),
            pltpu.VMEM((BALLS, 96, WIDTH), BF16),
            pltpu.VMEM((3, WIDTH, WIDTH), BF16),
            pltpu.VMEM((WIDTH, WIDTH), BF16),
            pltpu.VMEM((MP, 2, WIDTH, WIDTH), BF16),
            pltpu.VMEM((MP, WIDTH, WIDTH), BF16),
            dma((MP, BALLS)), dma((MP, BALLS)), dma((BALLS,)),
            dma((MP, BALLS)), dma((MP, BALLS)), dma((BALLS,)), dma((4,)),
        ],
        compiler_params=params(collective),
    )(slots, got, mask, w_qkv, w_out, w_gate_up, w_down)


def forward_tile(state, gate_up_ref, down_ref):
    normed = norm(state).astype(BF16)
    total = state
    for c in range(MP):
        gate = dot(normed, gate_up_ref[c, 0])
        up = dot(normed, gate_up_ref[c, 1])
        activated = (gate / (1.0 + jnp.exp(-gate)) * up).astype(BF16)
        total = total + dot(activated, down_ref[c])
    return total


def project_kernel(rows_ref, w_ref, one_ref, two_ref):
    for ball in range(QUARTER // BALL):
        rows = rows_ref[0, ball]
        for t in range(3):
            scale = 0.125 if t == 0 else 1.0
            one_ref[t, ball * 64 : (ball + 1) * 64, :] = (
                dot(rows[:64], w_ref[0, t]) * scale
            ).astype(BF16)
            two_ref[t, ball * 32 : (ball + 1) * 32, :] = (
                dot(rows[64:], w_ref[1, t]) * scale
            ).astype(BF16)


def project(rows, w_coarse):
    return pl.pallas_call(
        project_kernel,
        grid=(MP,),
        out_shape=[shape((3, 4 * ONE, LOCAL), BF16), shape((3, 4 * TWO, LOCAL), BF16)],
        in_specs=[
            pl.BlockSpec((1, 4, 96, WIDTH), lambda i: (i, 0, 0, 0)),
            pl.BlockSpec((2, 3, WIDTH, LOCAL), lambda i: (0, 0, 0, 0)),
        ],
        out_specs=[
            pl.BlockSpec((3, ONE, LOCAL), lambda i: (0, i, 0)),
            pl.BlockSpec((3, TWO, LOCAL), lambda i: (0, i, 0)),
        ],
        compiler_params=params(),
    )(rows, w_coarse)


def relatives(me):
    low = lax.rem(me, 2)
    high = lax.rem(me // 2, 2)
    first = me + 1 - 2 * low
    second = me + 2 - 4 * high
    third = first + 2 - 4 * high
    return (first, second, third)


def exchange_kernel(one, two, keep, mate_one, mate_two, mate_keep, send, recv):
    me = lax.axis_index("wide")
    others = relatives(me)
    barrier = pltpu.get_barrier_semaphore()
    for other in others:
        pl.semaphore_signal(barrier, inc=1, device_id={"wide": other}, device_id_type=MESH)
    pl.semaphore_wait(barrier, 3)
    copies = []
    for j in (1, 2, 0):
        to = {"wide": others[j]}
        copies.append(remote(two.at[1:], mate_two.at[j], send.at[j, 0], recv.at[j, 0], to))
        copies.append(remote(keep, mate_keep.at[j], send.at[j, 1], recv.at[j, 1], to))
    copies.append(
        remote(one.at[1:], mate_one, send.at[3, 0], recv.at[3, 0], {"wide": others[0]})
    )
    for copy in copies:
        copy.start()
    for copy in copies:
        copy.wait()


def exchange(one, two, keep, collective):
    return pl.pallas_call(
        exchange_kernel,
        out_shape=[
            shape((2, 4 * ONE, LOCAL), BF16),
            shape((3, 2, 4 * TWO, LOCAL), BF16),
            shape((3,) + keep.shape, I32),
        ],
        in_specs=[ANY] * 3,
        out_specs=[ANY] * 3,
        scratch_shapes=[pltpu.SemaphoreType.DMA((4, 2)), pltpu.SemaphoreType.DMA((4, 2))],
        compiler_params=params(collective),
    )(one, two, keep)


def coarse_kernel(one, two, mate_one, mate_two, keep, mate_keep, out):
    tile = 256
    low = lax.broadcasted_iota(I32, (tile, 128), 1) < 64
    flags = [keep[...]] + [mate_keep[j] for j in range(3)]

    def own(begin, real, length):
        rows = lax.broadcasted_iota(I32, (tile, length), 0) + begin
        cols = lax.broadcasted_iota(I32, (tile, length), 1)
        return jnp.logical_or(real, rows == cols)

    for t in range(4):
        begin = t * tile
        real = [flags[j][:, : 4 * ONE] > 0 for j in range(2)]
        parts = [
            (one[1], one[2], own(begin, real[0], 4 * ONE)),
            (mate_one[0], mate_one[1], real[1]),
        ]
        mixed = attend_pair(one[0, begin : begin + tile, :], parts, low)
        out[t, 0:256, :] = mixed.astype(BF16)
    for t in range(2):
        begin = t * tile
        real = [flags[j][:, 4 * ONE :] > 0 for j in range(4)]
        parts = [(two[1], two[2], own(begin, real[0], 4 * TWO))]
        for j in range(3):
            parts.append((mate_two[j, 0], mate_two[j, 1], real[j + 1]))
        mixed = attend_pair(two[0, begin : begin + tile, :], parts, low).astype(BF16)
        out[2 * t, 256:384, :] = mixed[:128]
        out[2 * t + 1, 256:384, :] = mixed[128:]


def coarse(one, two, mate_one, mate_two, keep, mate_keep):
    return pl.pallas_call(
        coarse_kernel,
        out_shape=shape((MP, COARSE, LOCAL), BF16),
        in_specs=[VMEM] * 6,
        out_specs=VMEM,
        compiler_params=params(),
    )(one, two, mate_one, mate_two, keep, mate_keep)


def on_device(points, mask, perm, w_qkv, w_out, w_gate_up, w_down, w_coarse, w_coarse_out):
    slot, source, codes = index(perm, mask)
    got, got_code, full_qkv, full_out, full_gate_up, full_down, full_lift = send_rows(
        source.reshape(SLOTS),
        points,
        codes.reshape(WIDE, 2, 128),
        [
            w_qkv.reshape(3 * WIDTH, LOCAL),
            w_out,
            w_gate_up.reshape(2 * WIDTH, WIDTH),
            w_down,
            w_coarse_out.reshape(2 * LOCAL, WIDTH),
        ],
        1,
    )
    full_qkv = full_qkv.reshape(3, WIDTH, WIDTH)
    full_out = full_out.reshape(WIDTH, WIDTH)
    full_gate_up = full_gate_up.reshape(MP, 2, WIDTH, WIDTH)
    landed, owned_mask, kept = inverse(got_code.reshape(WIDE, CAP))
    got_code = got_code.reshape(SLOTS)
    keep = jnp.concatenate([kept[:, :64].reshape(1, 4 * ONE), kept[:, 64:].reshape(1, 4 * TWO)], 1)
    fed, all_pooled = fine(
        landed.reshape(ROWS), got.reshape(SLOTS, LOCAL), owned_mask,
        full_qkv, full_out, full_gate_up, full_down, 2,
    )
    one, two = project(all_pooled, w_coarse)
    mate_one, mate_two, mate_keep = exchange(one, two, keep, 4)
    mixed = coarse(one, two, mate_one, mate_two, keep, mate_keep)
    all_mixed = swap(mixed, shape((COARSE, WIDTH), BF16), block, columns, 5)
    returned = return_rows(got_code, fed, all_mixed, full_lift, 6)
    return pl.pallas_call(
        finish_kernel,
        out_shape=shape((ROWS, LOCAL), F32),
        in_specs=[SMEM, VMEM],
        out_specs=VMEM,
        scratch_shapes=[pltpu.VMEM((SLOTS, LOCAL), F32)],
        compiler_params=params(),
    )(slot.reshape(ROWS), returned.reshape(SLOTS, LOCAL))


def solution(mesh):
    placed = (
        P("wide", "mp"),
        P("wide"),
        P("wide"),
        P(None, None, "mp"),
        P("mp", None),
        P(None, None, "mp"),
        P("mp", None),
        P(None, None, None, "mp"),
        P(None, "mp", None),
    )
    return jax.shard_map(
        on_device, mesh=mesh, in_specs=placed, out_specs=P("wide", "mp"), check_vma=False
    )
```

```python
import functools

import jax
import jax.numpy as jnp
from jax import lax
from jax.experimental import pallas as pl
from jax.experimental.pallas import tpu as pltpu
from jax.sharding import PartitionSpec as P

BALL = 256
WIDE = 32
MP = 4
ROWS = 4096
CAP = 256
SLOTS = WIDE * CAP
QUARTER = ROWS // MP
WIDTH = 512
LOCAL = WIDTH // MP
HIDDEN = 2048
ONE = QUARTER // 4
TWO = QUARTER // 8
COARSE = ONE + TWO
F32 = jnp.float32
BF16 = jnp.bfloat16
I32 = jnp.int32
MESH = pl.DeviceIdType.MESH
ANY = pl.BlockSpec(memory_space=pl.ANY)
VMEM = pl.BlockSpec(memory_space=pltpu.VMEM)
SMEM = pl.BlockSpec(memory_space=pltpu.SMEM)
LIMIT = 56 * 1024 * 1024


def shape(dims, kind):
    return jax.ShapeDtypeStruct(dims, kind)


def params(collective=None):
    if collective is None:
        return pltpu.CompilerParams(vmem_limit_bytes=LIMIT)
    return pltpu.CompilerParams(
        vmem_limit_bytes=LIMIT, collective_id=collective, has_side_effects=True
    )


def dot(a, b):
    return jnp.dot(a, b, preferred_element_type=F32)


def dot_t(a, b):
    return lax.dot_general(a, b, (((1,), (1,)), ((), ())), preferred_element_type=F32)


def norm(values):
    return values * lax.rsqrt(jnp.mean(values * values, -1, keepdims=True) + 1e-06)


UNROLL = 16
NONE = 2 * ROWS


def index_kernel(perm_ref, mask_ref, slot_ref, source_ref, codes_ref):
    perm = perm_ref[...]
    target = perm >> 12
    code = (perm & (ROWS - 1)) * 2 + mask_ref[...]
    rows = lax.broadcasted_iota(I32, (CAP, 128), 0)
    upper = jnp.where(
        lax.broadcasted_iota(I32, (128, 128), 0) < lax.broadcasted_iota(I32, (128, 128), 1), 1.0, 0.0
    ).astype(BF16)
    which = lax.broadcasted_iota(I32, (WIDE, 128), 0)
    lane = lax.broadcasted_iota(I32, (1, 128), 1).astype(F32)
    carry = jnp.zeros((WIDE, 1), F32)
    found = jnp.zeros((5 * WIDE, CAP), F32)
    for c in range(ROWS // 128):
        row = slice(c, c + 1)
        hot = jnp.where(which == target[row, :], 1.0, 0.0)
        before = dot(hot.astype(BF16), upper) + carry
        rank = jnp.sum(hot * before, 0, keepdims=True).astype(I32)
        slot_ref[row, :] = target[row, :] * CAP + rank
        carry = carry + jnp.sum(hot, 1, keepdims=True)
        placed = jnp.where(rows == rank, 1.0, 0.0).astype(BF16)
        high = (code[row, :] >> 6).astype(F32)
        low = (code[row, :] & 63).astype(F32)
        values = jnp.concatenate([hot * lane, hot * float(c), hot * high, hot * low, hot], 0)
        found = found + dot_t(values.astype(BF16), placed)
    source = (found[:WIDE] + found[WIDE : 2 * WIDE] * 128.0).astype(I32)
    codes = (found[2 * WIDE : 3 * WIDE] * 64.0 + found[3 * WIDE : 4 * WIDE]).astype(I32)
    codes = jnp.where(found[4 * WIDE :] > 0.5, codes, NONE)
    for h in range(2):
        at = slice(h * 128, (h + 1) * 128)
        source_ref[:, h, :] = source[:, at]
        codes_ref[:, h, :] = codes[:, at]


def index(perm, mask):
    return pl.pallas_call(
        index_kernel,
        out_shape=[shape((32, 128), I32), shape((WIDE, 2, 128), I32), shape((WIDE, 2, 128), I32)],
        in_specs=[VMEM] * 2,
        out_specs=[VMEM] * 3,
        compiler_params=params(),
    )(perm.reshape(32, 128), mask.reshape(32, 128))


def run_matrix(r, c):
    hot = jnp.logical_or(
        jnp.logical_and(c < 64, r // 4 == c), jnp.logical_and(c >= 64, r // 8 == c - 64)
    )
    return jnp.where(hot, 1.0, 0.0).astype(BF16)


def inverse_kernel(codes_ref, slot_ref, mask_ref, keep_ref):
    balls = ROWS // BALL
    rows = lax.broadcasted_iota(I32, (256, 128), 0)
    which = lax.broadcasted_iota(I32, (balls, 128), 0)
    lane = lax.broadcasted_iota(I32, (1, 128), 1).astype(F32)
    found = jnp.zeros((3 * balls, 256), F32)
    for c in range(WIDE):
        for h in range(2):
            code = codes_ref[c, h : h + 1, :]
            landing = code >> 1
            hot = jnp.where(which == (landing >> 8), 1.0, 0.0)
            placed = jnp.where(rows == (landing & 255), 1.0, 0.0).astype(BF16)
            real = (code & 1).astype(F32)
            values = jnp.concatenate([hot * lane, hot * float(2 * c + h), hot * real], 0)
            found = found + dot_t(values.astype(BF16), placed)
    slots = (found[:balls] + found[balls : 2 * balls] * 128.0).astype(I32)
    for h in range(2):
        slot_ref[:, h, :] = slots[:, h * 128 : (h + 1) * 128]
    mask = found[2 * balls :]
    mask_ref[...] = mask.astype(I32)
    runs = run_matrix(
        lax.broadcasted_iota(I32, (256, 96), 0), lax.broadcasted_iota(I32, (256, 96), 1)
    )
    keep_ref[...] = jnp.where(dot(mask.astype(BF16), runs) > 0.5, 1, 0)


def inverse(codes):
    return pl.pallas_call(
        inverse_kernel,
        out_shape=[shape((16, 2, 128), I32), shape((16, 256), I32), shape((16, 96), I32)],
        in_specs=[VMEM],
        out_specs=[VMEM] * 3,
        compiler_params=params(),
    )(codes)


def widen(src, dst, rows):
    @pl.loop(0, rows // 256)
    def _(i):
        at = pl.ds(pl.multiple_of(i * 256, 256), 256)
        dst[at, :] = src[at, :].astype(dst.dtype)


def finish_kernel(slot_ref, got_ref, out_ref, wide):
    widen(got_ref, wide, SLOTS)

    @pl.loop(0, ROWS // UNROLL)
    def _(i):
        base = i * UNROLL
        lines = [wide[pl.ds(slot_ref[base + u], 1), :] for u in range(UNROLL)]
        for u in range(UNROLL):
            out_ref[pl.ds(base + u, 1), :] = lines[u]


def remote(src, dst, send, recv, device):
    return pltpu.make_async_remote_copy(
        src_ref=src, dst_ref=dst, send_sem=send, recv_sem=recv, device_id=device, device_id_type=MESH
    )


def gather_bucket(line, lookup, wide, staged, packed, peer):
    @pl.loop(0, CAP // UNROLL)
    def _(i):
        begin = i * UNROLL
        lines = [wide[pl.ds(lookup(peer * CAP + begin + u), 1), :] for u in range(UNROLL)]
        for u in range(UNROLL):
            staged[line, pl.ds(begin + u, 1), :] = lines[u]

    packed[peer] = staged[line].astype(BF16)


def send_kernel(
    source_ref, points_ref, codes_ref, qkv_ref, out_ref, gate_up_ref, down_ref, lift_ref,
    got_ref, got_codes_ref, all_qkv, all_out, all_gate_up, all_down, all_lift,
    wide, staged, packed, send, recv, own, w_send, w_recv, w_own,
):
    me = lax.axis_index("wide")
    mp = lax.axis_index("mp")
    core = lax.rem(me, 2)
    partner = me + 1 - 2 * core
    after, ahead = lax.rem(mp + 1, MP), lax.rem(mp + 2, MP)
    behind = lax.rem(mp + 3, MP)
    barrier = pltpu.get_barrier_semaphore()

    @pl.loop(1, WIDE)
    def _(k):
        pl.semaphore_signal(
            barrier, inc=1, device_id={"wide": lax.rem(me + k, WIDE)}, device_id_type=MESH
        )

    for other in (after, behind):
        pl.semaphore_signal(barrier, inc=1, device_id={"mp": other}, device_id_type=MESH)
    widen(points_ref, wide, ROWS)

    def part(first, count):
        def rows(ref, quarter):
            return pl.ds(pl.multiple_of(first * quarter, 16), count * quarter)

        def cut(j, ref, shard):
            if j == 0:
                return ref.at[rows(ref, 384), pl.ds(pl.multiple_of(shard * 128, 128), 128)]
            quarter = (0, 32, 256, 128, 64)[j]
            return ref.at[shard, rows(ref, quarter), :]

        def own_cut(j, ref):
            quarter = (384, 32, 256, 128, 64)[j]
            return ref.at[rows(ref, quarter), :]

        return cut, own_cut

    half, own_half = part(2 * core, 2)
    first, _ = part(2 * core, 1)
    second, _ = part(2 * core + 1, 1)
    every, own_every = part(0, 4)
    shards = [qkv_ref, out_ref, gate_up_ref, down_ref, lift_ref]
    full = [all_qkv, all_out, all_gate_up, all_down, all_lift]
    count = len(shards)

    def weight(j, kind, cut, src, shard, device):
        return remote(
            src, cut(j, full[j], shard), w_send.at[j, kind], w_recv.at[j, kind], device
        )

    def weight_copies(j):
        ref = full[j]
        mine = own_half(j, shards[j])
        return [
            weight(j, 0, half, mine, mp, {"mp": after}),
            weight(j, 1, half, mine, mp, {"mp": behind}),
            weight(j, 2, first, first(j, ref, behind), behind, {"mp": after}),
            weight(j, 3, second, second(j, ref, after), after, {"mp": behind}),
            weight(j, 4, half, half(j, ref, behind), behind, {"wide": partner}),
            weight(j, 5, half, half(j, ref, after), after, {"wide": partner}),
            weight(j, 6, first, first(j, ref, ahead), ahead, {"wide": partner}),
            weight(j, 7, second, second(j, ref, ahead), ahead, {"wide": partner}),
        ]

    weights = [weight_copies(j) for j in range(count)]

    def rows_copy(k):
        peer = lax.rem(me + k, WIDE)
        return remote(
            packed.at[peer], got_ref.at[me], send.at[k, 0], recv.at[k, 0], {"wide": peer}
        )

    def codes_copy(k):
        peer = lax.rem(me + k, WIDE)
        return remote(
            codes_ref.at[peer], got_codes_ref.at[me], send.at[k, 1], recv.at[k, 1], {"wide": peer}
        )

    pl.semaphore_wait(barrier, WIDE + 1)
    for j in range(count):
        weights[j][0].start()
        weights[j][1].start()

    @pl.loop(1, WIDE)
    def _(k):
        gather_bucket(0, lambda s: source_ref[s], wide, staged, packed, lax.rem(me + k, WIDE))
        rows_copy(k).start()
        codes_copy(k).start()

    gather_bucket(0, lambda s: source_ref[s], wide, staged, packed, me)
    mine = [
        pltpu.make_async_copy(packed.at[me], got_ref.at[me], own.at[0]),
        pltpu.make_async_copy(codes_ref.at[me], got_codes_ref.at[me], own.at[1]),
    ]
    for j in range(count):
        mine.append(
            pltpu.make_async_copy(own_every(j, shards[j]), every(j, full[j], mp), w_own.at[j])
        )
    for copy in mine:
        copy.start()
    for j in range(count):
        weights[j][0].wait_recv()
        weights[j][2].start()
        weights[j][4].start()
        weights[j][1].wait_recv()
        weights[j][3].start()
        weights[j][5].start()
    for j in range(count):
        weights[j][2].wait_recv()
        weights[j][6].start()
        weights[j][3].wait_recv()
        weights[j][7].start()
    for copy in mine:
        copy.wait()

    @pl.loop(1, WIDE)
    def _(k):
        rows_copy(k).wait()
        codes_copy(k).wait()

    for j in range(count):
        for kind in range(4):
            weights[j][kind].wait_send()
        for kind in range(4, 8):
            weights[j][kind].wait()


def send_rows(source, points, codes, weights, collective):
    return pl.pallas_call(
        send_kernel,
        out_shape=[
            shape((WIDE, CAP, LOCAL), BF16),
            shape((WIDE, 2, 128), I32),
            shape((3 * WIDTH, WIDTH), BF16),
            shape((MP, LOCAL, WIDTH), BF16),
            shape((MP, 2 * WIDTH, WIDTH), BF16),
            shape((MP, WIDTH, WIDTH), BF16),
            shape((MP, 2 * LOCAL, WIDTH), BF16),
        ],
        in_specs=[SMEM, VMEM, ANY] + [VMEM] * 5,
        out_specs=[ANY] * 7,
        scratch_shapes=[
            pltpu.VMEM((ROWS, LOCAL), F32),
            pltpu.VMEM((1, CAP, LOCAL), F32),
            pltpu.VMEM((WIDE, CAP, LOCAL), BF16),
            pltpu.SemaphoreType.DMA((WIDE, 2)),
            pltpu.SemaphoreType.DMA((WIDE, 2)),
            pltpu.SemaphoreType.DMA((2,)),
            pltpu.SemaphoreType.DMA((5, 8)),
            pltpu.SemaphoreType.DMA((5, 8)),
            pltpu.SemaphoreType.DMA((5,)),
        ],
        compiler_params=params(collective),
    )(source, points, codes, *weights)


def return_kernel(
    code_ref, turned_ref, lifted_ref, got_ref, wide, staged, packed, send, recv, own
):
    me = lax.axis_index("wide")
    barrier = pltpu.get_barrier_semaphore()

    @pl.loop(1, WIDE)
    def _(k):
        pl.semaphore_signal(
            barrier, inc=1, device_id={"wide": lax.rem(me + k, WIDE)}, device_id_type=MESH
        )

    runs = run_matrix(
        lax.broadcasted_iota(I32, (BALL, 96), 0), lax.broadcasted_iota(I32, (BALL, 96), 1)
    )

    @pl.loop(0, ROWS // BALL)
    def _(i):
        at = pl.ds(pl.multiple_of(i * BALL, BALL), BALL)
        wide[at, :] = turned_ref[at, :].astype(F32) + dot(runs, lifted_ref[i])

    wide[ROWS : ROWS + 8, :] = jnp.zeros((8, LOCAL), F32)
    pl.semaphore_wait(barrier, WIDE - 1)

    def rows_copy(k):
        peer = lax.rem(me + k, WIDE)
        return remote(packed.at[peer], got_ref.at[me], send.at[k], recv.at[k], {"wide": peer})

    @pl.loop(1, WIDE)
    def _(k):
        gather_bucket(0, lambda s: code_ref[s] >> 1, wide, staged, packed, lax.rem(me + k, WIDE))
        rows_copy(k).start()

    gather_bucket(0, lambda s: code_ref[s] >> 1, wide, staged, packed, me)
    last = pltpu.make_async_copy(packed.at[me], got_ref.at[me], own)
    last.start()
    last.wait()

    @pl.loop(1, WIDE)
    def _(k):
        rows_copy(k).wait()


def return_rows(codes, turned, lifted, collective):
    return pl.pallas_call(
        return_kernel,
        out_shape=shape((WIDE, CAP, LOCAL), BF16),
        in_specs=[SMEM, VMEM, VMEM],
        out_specs=ANY,
        scratch_shapes=[
            pltpu.VMEM((ROWS + 8, LOCAL), F32),
            pltpu.VMEM((1, CAP, LOCAL), F32),
            pltpu.VMEM((WIDE, CAP, LOCAL), BF16),
            pltpu.SemaphoreType.DMA((WIDE,)),
            pltpu.SemaphoreType.DMA((WIDE,)),
            pltpu.SemaphoreType.DMA,
        ],
        compiler_params=params(collective),
    )(codes, turned, lifted)


def attend_pair(queries, parts, low):
    mixed = []
    for head in range(2):
        mine = low if head == 0 else jnp.logical_not(low)
        q = jnp.where(mine, queries, jnp.zeros_like(queries))
        scores = [jnp.where(allowed, dot_t(q, keys), -1e30) for keys, _, allowed in parts]
        top = functools.reduce(jnp.maximum, [jnp.max(s, -1, keepdims=True) for s in scores])
        expo = [jnp.exp(s - top) for s in scores]
        total = sum(jnp.sum(e, -1, keepdims=True) for e in expo)
        out = sum(dot(e.astype(BF16), values) for e, (_, values, _) in zip(expo, parts))
        mixed.append(out / total)
    return jnp.where(low, mixed[0], mixed[1])


def fine_ball(x, real, qkv_ref, out_ref):
    x = x.astype(F32)
    normed = norm(x).astype(BF16)
    q = (dot(normed, qkv_ref[0]) * 0.125).astype(BF16)
    k = dot(normed, qkv_ref[1]).astype(BF16)
    v = dot(normed, qkv_ref[2]).astype(BF16)
    rows = lax.broadcasted_iota(I32, (BALL, BALL), 0)
    cols = lax.broadcasted_iota(I32, (BALL, BALL), 1)
    allowed = jnp.logical_or(real, rows == cols)
    low = lax.broadcasted_iota(I32, (BALL, 128), 1) < 64
    mixed = []
    for g in range(MP):
        at = slice(g * 128, (g + 1) * 128)
        mixed.append(attend_pair(q[:, at], [(k[:, at], v[:, at], allowed)], low).astype(BF16))
    state = x + dot(jnp.concatenate(mixed, 1), out_ref[...])
    high = state.astype(BF16)
    rest = (state - high.astype(F32)).astype(BF16)
    runs, counted = pooling(real, 4)
    pooled = (dot(runs, high) + dot(runs, rest)) / jnp.maximum(counted, 1.0)
    return state, pooled.astype(BF16)


def pooling(real, factor):
    count_rows = BALL // factor
    r = lax.broadcasted_iota(I32, (count_rows, BALL), 0)
    c = lax.broadcasted_iota(I32, (count_rows, BALL), 1)
    hot = jnp.where(jnp.logical_and(r == c // factor, real), 1.0, 0.0)
    return hot.astype(BF16), jnp.sum(hot, 1, keepdims=True)


BALLS = QUARTER // BALL


def forward_tile(state, gate_up_ref, down_ref):
    normed = norm(state).astype(BF16)
    total = state
    for c in range(MP):
        gate = dot(normed, gate_up_ref[c, 0])
        up = dot(normed, gate_up_ref[c, 1])
        activated = (gate / (1.0 + jnp.exp(-gate)) * up).astype(BF16)
        total = total + dot(activated, down_ref[c])
    return total


def relatives(me):
    low = lax.rem(me, 2)
    high = lax.rem(me // 2, 2)
    first = me + 1 - 2 * low
    second = me + 2 - 4 * high
    third = first + 2 - 4 * high
    return (first, second, third)


def middle_kernel(
    slot_ref, got_ref, mask_ref, keep_ref, qkv_hbm, out_hbm, gate_up_hbm, down_hbm, coarse_hbm,
    lift_hbm, turned_ref, lifted_ref,
    wide, staged, packed, x, state, pooled, tiles, one, two, mate_one, mate_two, mate_keep,
    mixed, all_mixed, lifted, qkv_ref, out_ref, gate_up_ref, down_ref, w_ref, lift_ref,
    x_sem, p_sem, e_sem, k_sem, m_sem, t_sem, l_sem, own, loads,
):
    me = lax.axis_index("wide")
    mp = lax.axis_index("mp")
    others = relatives(me)
    barrier = pltpu.get_barrier_semaphore()
    for k in range(1, MP):
        pl.semaphore_signal(
            barrier, inc=1, device_id={"mp": lax.rem(mp + k, MP)}, device_id_type=MESH
        )
    for other in others:
        pl.semaphore_signal(barrier, inc=1, device_id={"wide": other}, device_id_type=MESH)
    load = [
        pltpu.make_async_copy(src, dst, loads.at[j])
        for j, (src, dst) in enumerate([
            (qkv_hbm, qkv_ref),
            (out_hbm, out_ref),
            (gate_up_hbm, gate_up_ref),
            (down_hbm, down_ref),
            (coarse_hbm, w_ref),
            (lift_hbm, lift_ref),
        ])
    ]
    for copy in load:
        copy.start()
    widen(got_ref, wide, SLOTS)
    pl.semaphore_wait(barrier, MP + 2)

    def rows(t, size):
        return pl.ds(pl.multiple_of(t * size, size), size)

    def cols(g):
        return pl.ds(pl.multiple_of(g * LOCAL, LOCAL), LOCAL)

    def peer(k):
        return lax.rem(mp + k, MP)

    def to_mp(src, dst, sem, k, t):
        return remote(src, dst, sem.at[0, k, t], sem.at[1, k, t], {"mp": peer(k)})

    def turn(k, t):
        return to_mp(packed.at[peer(k) * BALLS + t], x.at[rows(t, BALL), cols(mp)], x_sem, k, t)

    def keep_turn(t):
        return pltpu.make_async_copy(
            packed.at[mp * BALLS + t], x.at[rows(t, BALL), cols(mp)], own.at[0, t]
        )

    @pl.loop(0, BALLS)
    def _(t):
        for k in (2, 1, 3):
            gather_bucket(0, lambda s: slot_ref[s], wide, staged, packed, peer(k) * BALLS + t)
            turn(k, t).start()
        gather_bucket(0, lambda s: slot_ref[s], wide, staged, packed, mp * BALLS + t)
        keep_turn(t).start()

    def flags(j):
        return remote(
            keep_ref, mate_keep.at[j], k_sem.at[0, j], k_sem.at[1, j], {"wide": others[j]}
        )

    for j in range(3):
        flags(j).start()
    load[0].wait()
    load[1].wait()

    def share(k, t):
        return to_mp(pooled.at[mp, t], pooled.at[mp, t], p_sem, k, t)

    @pl.loop(0, BALLS)
    def _(t):
        for k in (1, 3, 2):
            turn(k, t).wait_recv()
        keep_turn(t).wait()
        real = mask_ref[pl.ds(mp * BALLS + t, 1), :] > 0
        out, means = fine_ball(x[rows(t, BALL), :], real, qkv_ref, out_ref)
        state[rows(t, BALL), :] = out
        pooled[mp, t] = means
        for k in (2, 1, 3):
            share(k, t).start()

    load[2].wait()
    load[3].wait()

    def give(k, t):
        return to_mp(
            tiles.at[rows(t, BALL), cols(peer(k))],
            turned_ref.at[rows(mp * BALLS + t, BALL), :],
            t_sem,
            k,
            t,
        )

    def keep_give(t):
        return pltpu.make_async_copy(
            tiles.at[rows(t, BALL), cols(mp)],
            turned_ref.at[rows(mp * BALLS + t, BALL), :],
            own.at[1, t],
        )

    def feed(t):
        fed = forward_tile(state[rows(t, BALL), :], gate_up_ref, down_ref)
        tiles[rows(t, BALL), :] = fed.astype(BF16)
        for k in (2, 1, 3):
            give(k, t).start()
        keep_give(t).start()

    @pl.loop(0, FIRST)
    def _(t):
        feed(t)

    def pass_one(q):
        return remote(
            one.at[pl.ds(1, 2), rows(q, ONE), :],
            mate_one.at[:, rows(q, ONE), :],
            e_sem.at[0, 3, q],
            e_sem.at[1, 3, q],
            {"wide": others[0]},
        )

    def pass_two(j, q):
        return remote(
            two.at[pl.ds(1, 2), rows(q, TWO), :],
            mate_two.at[j, :, rows(q, TWO), :],
            e_sem.at[0, j, q],
            e_sem.at[1, j, q],
            {"wide": others[j]},
        )

    pair = lax.broadcasted_iota(I32, (32, 64), 0) == lax.broadcasted_iota(I32, (32, 64), 1) // 2
    pair = jnp.where(pair, 1.0, 0.0).astype(BF16)
    load[4].wait()

    def project(q):
        firsts, seconds = [], []
        for ball in range(BALLS):
            real = mask_ref[pl.ds(q * BALLS + ball, 1), :] > 0
            means = pooled[q, ball].astype(F32)
            firsts.append(norm(means).astype(BF16))
            sums = means * pooling(real, 4)[1]
            high = sums.astype(BF16)
            rest = (sums - high.astype(F32)).astype(BF16)
            counted = jnp.maximum(pooling(real, 8)[1], 1.0)
            seconds.append(norm((dot(pair, high) + dot(pair, rest)) / counted).astype(BF16))
        firsts = jnp.concatenate(firsts, 0)
        seconds = jnp.concatenate(seconds, 0)
        for t in (1, 2):
            two[t, rows(q, TWO), :] = dot(seconds, w_ref[1, t]).astype(BF16)
            one[t, rows(q, ONE), :] = dot(firsts, w_ref[0, t]).astype(BF16)
        for j in (1, 2, 0):
            pass_two(j, q).start()
        pass_one(q).start()
        two[0, rows(q, TWO), :] = (dot(seconds, w_ref[1, 0]) * 0.125).astype(BF16)
        one[0, rows(q, ONE), :] = (dot(firsts, w_ref[0, 0]) * 0.125).astype(BF16)

    project(mp)
    for k in (1, 3, 2):

        @pl.loop(0, BALLS)
        def _(t):
            share(MP - k, t).wait_recv()

        project(peer(k))

    @pl.loop(FIRST, SECOND)
    def _(t):
        feed(t)

    def hand(k, level):
        at = pl.ds(0, ONE) if level == 0 else pl.ds(ONE, TWO)
        return to_mp(mixed.at[peer(k), at, :], all_mixed.at[at, cols(mp)], m_sem, k, level)

    def keep_hand(level):
        at = pl.ds(0, ONE) if level == 0 else pl.ds(ONE, TWO)
        return pltpu.make_async_copy(
            mixed.at[mp, at, :], all_mixed.at[at, cols(mp)], own.at[2, level]
        )

    def own_keys(begin, real, count, length):
        r = lax.broadcasted_iota(I32, (count, length), 0) + begin
        c = lax.broadcasted_iota(I32, (count, length), 1)
        return jnp.logical_or(real, r == c)

    for j in range(3):
        flags(j).wait()

    @pl.loop(0, MP)
    def _(q):
        pass_one(q).wait()

    @pl.loop(1, MP + 1)
    def _(k):
        q = peer(k)
        low = lax.broadcasted_iota(I32, (ONE, 128), 1) < 64
        real = keep_ref[:, : 4 * ONE] > 0
        mate = mate_keep[0][:, : 4 * ONE] > 0
        parts = [
            (one[1], one[2], own_keys(q * ONE, real, ONE, 4 * ONE)),
            (mate_one[0], mate_one[1], mate),
        ]
        mixed[q, 0:ONE, :] = attend_pair(one[0, rows(q, ONE), :], parts, low).astype(BF16)

        @pl.when(k < MP)
        def _():
            hand(k, 0).start()

    keep_hand(0).start()

    @pl.loop(0, MP)
    def _(q):
        for j in range(3):
            pass_two(j, q).wait()

    @pl.loop(1, MP + 1)
    def _(k):
        q = peer(k)
        low = lax.broadcasted_iota(I32, (TWO, 128), 1) < 64
        real = keep_ref[:, 4 * ONE :] > 0
        parts = [(two[1], two[2], own_keys(q * TWO, real, TWO, 4 * TWO))]
        for j in range(3):
            parts.append((mate_two[j, 0], mate_two[j, 1], mate_keep[j][:, 4 * ONE :] > 0))
        mixed[q, ONE:COARSE, :] = attend_pair(two[0, rows(q, TWO), :], parts, low).astype(BF16)

        @pl.when(k < MP)
        def _():
            hand(k, 1).start()

    keep_hand(1).start()

    @pl.loop(SECOND, BALLS)
    def _(t):
        feed(t)

    load[5].wait()
    for level in range(2):
        keep_hand(level).wait()
        for k in (1, 3, 2):
            hand(k, level).wait()
    for level, begin, size in ((0, 0, 64), (1, ONE, 32)):
        span = slice(begin, begin + size * BALLS)
        total = jnp.zeros((size * BALLS, WIDTH), F32)
        for g in range(MP):
            total = total + dot(
                all_mixed[span, g * LOCAL : (g + 1) * LOCAL],
                lift_ref[g, level * LOCAL : (level + 1) * LOCAL, :],
            )
        total = total.astype(BF16)
        for ball in range(BALLS):
            at = slice(0, 64) if level == 0 else slice(64, 96)
            lifted[ball, at, :] = total[ball * size : (ball + 1) * size]

    def rise(k):
        return to_mp(lifted.at[:, :, cols(peer(k))], lifted_ref.at[mp], l_sem, k, 0)

    for k in (2, 1, 3):
        rise(k).start()
    keep_rise = pltpu.make_async_copy(lifted.at[:, :, cols(mp)], lifted_ref.at[mp], own.at[3, 0])
    keep_rise.start()

    @pl.loop(0, BALLS)
    def _(t):
        keep_give(t).wait()
        for k in (1, 3, 2):
            turn(k, t).wait_send()
            share(k, t).wait_send()
            give(k, t).wait()

    keep_rise.wait()
    for k in (1, 3, 2):
        rise(k).wait()


FIRST = 2
SECOND = 3


def middle(slots, got, mask, keep, weights, collective):
    dma = pltpu.SemaphoreType.DMA
    return pl.pallas_call(
        middle_kernel,
        out_shape=[shape((ROWS, LOCAL), BF16), shape((MP, BALLS, 96, LOCAL), BF16)],
        in_specs=[SMEM, VMEM, VMEM, VMEM] + [ANY] * 6,
        out_specs=[ANY, ANY],
        scratch_shapes=[
            pltpu.VMEM((SLOTS, LOCAL), F32),
            pltpu.VMEM((1, CAP, LOCAL), F32),
            pltpu.VMEM((MP * BALLS, BALL, LOCAL), BF16),
            pltpu.VMEM((QUARTER, WIDTH), BF16),
            pltpu.VMEM((QUARTER, WIDTH), F32),
            pltpu.VMEM((MP, BALLS, 64, WIDTH), BF16),
            pltpu.VMEM((QUARTER, WIDTH), BF16),
            pltpu.VMEM((3, 4 * ONE, LOCAL), BF16),
            pltpu.VMEM((3, 4 * TWO, LOCAL), BF16),
            pltpu.VMEM((2, 4 * ONE, LOCAL), BF16),
            pltpu.VMEM((3, 2, 4 * TWO, LOCAL), BF16),
            pltpu.VMEM((3, 1, 12 * 128), I32),
            pltpu.VMEM((MP, COARSE, LOCAL), BF16),
            pltpu.VMEM((COARSE, WIDTH), BF16),
            pltpu.VMEM((BALLS, 96, WIDTH), BF16),
            pltpu.VMEM((3, WIDTH, WIDTH), BF16),
            pltpu.VMEM((WIDTH, WIDTH), BF16),
            pltpu.VMEM((MP, 2, WIDTH, WIDTH), BF16),
            pltpu.VMEM((MP, WIDTH, WIDTH), BF16),
            pltpu.VMEM((2, 3, WIDTH, LOCAL), BF16),
            pltpu.VMEM((MP, 2 * LOCAL, WIDTH), BF16),
            dma((2, MP, BALLS)),
            dma((2, MP, BALLS)),
            dma((2, 4, MP)),
            dma((2, 3)),
            dma((2, MP, 2)),
            dma((2, MP, BALLS)),
            dma((2, MP, 1)),
            dma((4, BALLS)),
            dma((6,)),
        ],
        compiler_params=params(collective),
    )(slots, got, mask, keep, *weights)


def on_device(points, mask, perm, w_qkv, w_out, w_gate_up, w_down, w_coarse, w_coarse_out):
    slot, source, codes = index(perm, mask)
    got, got_code, full_qkv, full_out, full_gate_up, full_down, full_lift = send_rows(
        source.reshape(SLOTS),
        points,
        codes,
        [
            w_qkv.reshape(3 * WIDTH, LOCAL),
            w_out,
            w_gate_up.reshape(2 * WIDTH, WIDTH),
            w_down,
            w_coarse_out.reshape(2 * LOCAL, WIDTH),
        ],
        1,
    )
    full_qkv = full_qkv.reshape(3, WIDTH, WIDTH)
    full_out = full_out.reshape(WIDTH, WIDTH)
    full_gate_up = full_gate_up.reshape(MP, 2, WIDTH, WIDTH)
    landed, owned_mask, kept = inverse(got_code)
    keep = jnp.concatenate([kept[:, :64].reshape(1, 4 * ONE), kept[:, 64:].reshape(1, 4 * TWO)], 1)
    turned, lifted = middle(
        landed.reshape(ROWS), got.reshape(SLOTS, LOCAL), owned_mask, keep,
        [full_qkv, full_out, full_gate_up, full_down, w_coarse, full_lift], 2,
    )
    lifted = lifted.reshape(MP * BALLS, 96, LOCAL)
    returned = return_rows(got_code.reshape(SLOTS), turned, lifted, 3)
    return pl.pallas_call(
        finish_kernel,
        out_shape=shape((ROWS, LOCAL), F32),
        in_specs=[SMEM, VMEM],
        out_specs=VMEM,
        scratch_shapes=[pltpu.VMEM((SLOTS, LOCAL), F32)],
        compiler_params=params(),
    )(slot.reshape(ROWS), returned.reshape(SLOTS, LOCAL))


def solution(mesh):
    placed = (
        P("wide", "mp"),
        P("wide"),
        P("wide"),
        P(None, None, "mp"),
        P("mp", None),
        P(None, None, "mp"),
        P("mp", None),
        P(None, None, None, "mp"),
        P(None, "mp", None),
    )
    return jax.shard_map(
        on_device, mesh=mesh, in_specs=placed, out_specs=P("wide", "mp"), check_vma=False
    )
```

```python
import functools

import jax
import jax.numpy as jnp
from jax import lax
from jax.experimental import pallas as pl
from jax.experimental.pallas import tpu as pltpu
from jax.sharding import PartitionSpec as P

BALL = 256
WIDE = 32
MP = 4
ROWS = 4096
CAP = 256
SLOTS = WIDE * CAP
QUARTER = ROWS // MP
WIDTH = 512
LOCAL = WIDTH // MP
HIDDEN = 2048
ONE = QUARTER // 4
TWO = QUARTER // 8
COARSE = ONE + TWO
F32 = jnp.float32
BF16 = jnp.bfloat16
I32 = jnp.int32
MESH = pl.DeviceIdType.MESH
ANY = pl.BlockSpec(memory_space=pl.ANY)
VMEM = pl.BlockSpec(memory_space=pltpu.VMEM)
SMEM = pl.BlockSpec(memory_space=pltpu.SMEM)
LIMIT = 56 * 1024 * 1024


def shape(dims, kind):
    return jax.ShapeDtypeStruct(dims, kind)


def params(collective=None):
    if collective is None:
        return pltpu.CompilerParams(vmem_limit_bytes=LIMIT)
    return pltpu.CompilerParams(
        vmem_limit_bytes=LIMIT, collective_id=collective, has_side_effects=True
    )


def dot(a, b):
    return jnp.dot(a, b, preferred_element_type=F32)


def dot_t(a, b):
    return lax.dot_general(a, b, (((1,), (1,)), ((), ())), preferred_element_type=F32)


def norm(values):
    return values * lax.rsqrt(jnp.mean(values * values, -1, keepdims=True) + 1e-06)


UNROLL = 32
NONE = 2 * ROWS


def index_kernel(perm_ref, mask_ref, slot_ref, source_ref, codes_ref):
    perm = perm_ref[...]
    target = perm >> 12
    code = (perm & (ROWS - 1)) * 2 + mask_ref[...]
    rows = lax.broadcasted_iota(I32, (CAP, 128), 0)
    upper = jnp.where(
        lax.broadcasted_iota(I32, (128, 128), 0) < lax.broadcasted_iota(I32, (128, 128), 1), 1.0, 0.0
    ).astype(BF16)
    which = lax.broadcasted_iota(I32, (WIDE, 128), 0)
    lane = lax.broadcasted_iota(I32, (1, 128), 1).astype(F32)
    carry = jnp.zeros((WIDE, 1), F32)
    found = jnp.zeros((5 * WIDE, CAP), F32)
    for c in range(ROWS // 128):
        row = slice(c, c + 1)
        hot = jnp.where(which == target[row, :], 1.0, 0.0)
        before = dot(hot.astype(BF16), upper) + carry
        rank = jnp.sum(hot * before, 0, keepdims=True).astype(I32)
        slot_ref[row, :] = target[row, :] * CAP + rank
        carry = carry + jnp.sum(hot, 1, keepdims=True)
        placed = jnp.where(rows == rank, 1.0, 0.0).astype(BF16)
        high = (code[row, :] >> 6).astype(F32)
        low = (code[row, :] & 63).astype(F32)
        values = jnp.concatenate([hot * lane, hot * float(c), hot * high, hot * low, hot], 0)
        found = found + dot_t(values.astype(BF16), placed)
    source = (found[:WIDE] + found[WIDE : 2 * WIDE] * 128.0).astype(I32)
    codes = (found[2 * WIDE : 3 * WIDE] * 64.0 + found[3 * WIDE : 4 * WIDE]).astype(I32)
    codes = jnp.where(found[4 * WIDE :] > 0.5, codes, NONE)
    for h in range(2):
        at = slice(h * 128, (h + 1) * 128)
        source_ref[:, h, :] = source[:, at]
        codes_ref[:, h, :] = codes[:, at]


def index(perm, mask):
    return pl.pallas_call(
        index_kernel,
        out_shape=[shape((32, 128), I32), shape((WIDE, 2, 128), I32), shape((WIDE, 2, 128), I32)],
        in_specs=[VMEM] * 2,
        out_specs=[VMEM] * 3,
        compiler_params=params(),
    )(perm.reshape(32, 128), mask.reshape(32, 128))


def run_matrix(r, c):
    hot = jnp.logical_or(
        jnp.logical_and(c < 64, r // 4 == c), jnp.logical_and(c >= 64, r // 8 == c - 64)
    )
    return jnp.where(hot, 1.0, 0.0).astype(BF16)


def inverse_kernel(codes_ref, slot_ref, mask_ref, keep_ref):
    balls = ROWS // BALL
    rows = lax.broadcasted_iota(I32, (256, 128), 0)
    which = lax.broadcasted_iota(I32, (balls, 128), 0)
    lane = lax.broadcasted_iota(I32, (1, 128), 1).astype(F32)
    found = jnp.zeros((3 * balls, 256), F32)
    for c in range(WIDE):
        for h in range(2):
            code = codes_ref[c, h : h + 1, :]
            landing = code >> 1
            hot = jnp.where(which == (landing >> 8), 1.0, 0.0)
            placed = jnp.where(rows == (landing & 255), 1.0, 0.0).astype(BF16)
            real = (code & 1).astype(F32)
            values = jnp.concatenate([hot * lane, hot * float(2 * c + h), hot * real], 0)
            found = found + dot_t(values.astype(BF16), placed)
    slots = (found[:balls] + found[balls : 2 * balls] * 128.0).astype(I32)
    for h in range(2):
        slot_ref[:, h, :] = slots[:, h * 128 : (h + 1) * 128]
    mask = found[2 * balls :]
    mask_ref[...] = mask.astype(I32)
    runs = run_matrix(
        lax.broadcasted_iota(I32, (256, 96), 0), lax.broadcasted_iota(I32, (256, 96), 1)
    )
    keep_ref[...] = jnp.where(dot(mask.astype(BF16), runs) > 0.5, 1, 0)


def inverse(codes):
    return pl.pallas_call(
        inverse_kernel,
        out_shape=[shape((16, 2, 128), I32), shape((16, 256), I32), shape((16, 96), I32)],
        in_specs=[VMEM],
        out_specs=[VMEM] * 3,
        compiler_params=params(),
    )(codes)


def widen(src, dst, rows):
    @pl.loop(0, rows // 256)
    def _(i):
        at = pl.ds(pl.multiple_of(i * 256, 256), 256)
        dst[at, :] = src[at, :].astype(dst.dtype)


def finish_kernel(slot_ref, got_ref, out_ref, wide):
    widen(got_ref, wide, SLOTS)

    @pl.loop(0, ROWS // UNROLL)
    def _(i):
        base = i * UNROLL
        lines = [wide[pl.ds(slot_ref[base + u], 1), :] for u in range(UNROLL)]
        for u in range(UNROLL):
            out_ref[pl.ds(base + u, 1), :] = lines[u]


def remote(src, dst, send, recv, device):
    return pltpu.make_async_remote_copy(
        src_ref=src, dst_ref=dst, send_sem=send, recv_sem=recv, device_id=device, device_id_type=MESH
    )


def turn_of(me, k):
    return lax.rem(me + lax.rem(k * 7, WIDE), WIDE)


def gather_bucket(line, lookup, wide, staged, packed, peer):
    @pl.loop(0, CAP // UNROLL)
    def _(i):
        begin = i * UNROLL
        lines = [wide[pl.ds(lookup(peer * CAP + begin + u), 1), :] for u in range(UNROLL)]
        for u in range(UNROLL):
            staged[line, pl.ds(begin + u, 1), :] = lines[u]

    packed[peer] = staged[line].astype(BF16)


def send_kernel(
    source_ref, points_ref, codes_ref, qkv_ref, out_ref, gate_up_ref, down_ref, lift_ref,
    got_ref, got_codes_ref, all_qkv, all_out, all_gate_up, all_down, all_lift,
    wide, staged, packed, send, recv, own, w_send, w_recv, w_own,
):
    me = lax.axis_index("wide")
    mp = lax.axis_index("mp")
    core = lax.rem(me, 2)
    partner = me + 1 - 2 * core
    after, ahead = lax.rem(mp + 1, MP), lax.rem(mp + 2, MP)
    behind = lax.rem(mp + 3, MP)
    barrier = pltpu.get_barrier_semaphore()

    @pl.loop(1, WIDE)
    def _(k):
        pl.semaphore_signal(
            barrier, inc=1, device_id={"wide": lax.rem(me + k, WIDE)}, device_id_type=MESH
        )

    for other in (after, behind):
        pl.semaphore_signal(barrier, inc=1, device_id={"mp": other}, device_id_type=MESH)
    widen(points_ref, wide, ROWS)

    def part(first, count):
        def rows(ref, quarter):
            return pl.ds(pl.multiple_of(first * quarter, 16), count * quarter)

        def cut(j, ref, shard):
            if j == 0:
                return ref.at[rows(ref, 384), pl.ds(pl.multiple_of(shard * 128, 128), 128)]
            quarter = (0, 32, 256, 128, 64)[j]
            return ref.at[shard, rows(ref, quarter), :]

        def own_cut(j, ref):
            quarter = (384, 32, 256, 128, 64)[j]
            return ref.at[rows(ref, quarter), :]

        return cut, own_cut

    half, own_half = part(2 * core, 2)
    first, _ = part(2 * core, 1)
    second, _ = part(2 * core + 1, 1)
    every, own_every = part(0, 4)
    shards = [qkv_ref, out_ref, gate_up_ref, down_ref, lift_ref]
    full = [all_qkv, all_out, all_gate_up, all_down, all_lift]
    count = len(shards)

    def weight(j, kind, cut, src, shard, device):
        return remote(
            src, cut(j, full[j], shard), w_send.at[j, kind], w_recv.at[j, kind], device
        )

    def weight_copies(j):
        ref = full[j]
        mine = own_half(j, shards[j])
        return [
            weight(j, 0, half, mine, mp, {"mp": after}),
            weight(j, 1, half, mine, mp, {"mp": behind}),
            weight(j, 2, first, first(j, ref, behind), behind, {"mp": after}),
            weight(j, 3, second, second(j, ref, after), after, {"mp": behind}),
            weight(j, 4, half, half(j, ref, behind), behind, {"wide": partner}),
            weight(j, 5, half, half(j, ref, after), after, {"wide": partner}),
            weight(j, 6, first, first(j, ref, ahead), ahead, {"wide": partner}),
            weight(j, 7, second, second(j, ref, ahead), ahead, {"wide": partner}),
        ]

    weights = [weight_copies(j) for j in range(count)]

    def rows_copy(k):
        peer = turn_of(me, k)
        return remote(
            packed.at[peer], got_ref.at[me], send.at[k, 0], recv.at[k, 0], {"wide": peer}
        )

    def codes_copy(k):
        peer = turn_of(me, k)
        return remote(
            codes_ref.at[peer], got_codes_ref.at[me], send.at[k, 1], recv.at[k, 1], {"wide": peer}
        )

    pl.semaphore_wait(barrier, WIDE + 1)
    for j in range(count):
        weights[j][0].start()
        weights[j][1].start()

    @pl.loop(1, WIDE)
    def _(k):
        gather_bucket(0, lambda s: source_ref[s], wide, staged, packed, turn_of(me, k))
        rows_copy(k).start()
        codes_copy(k).start()

    gather_bucket(0, lambda s: source_ref[s], wide, staged, packed, me)
    mine = [
        pltpu.make_async_copy(packed.at[me], got_ref.at[me], own.at[0]),
        pltpu.make_async_copy(codes_ref.at[me], got_codes_ref.at[me], own.at[1]),
    ]
    for j in range(count):
        mine.append(
            pltpu.make_async_copy(own_every(j, shards[j]), every(j, full[j], mp), w_own.at[j])
        )
    for copy in mine:
        copy.start()
    for j in range(count):
        weights[j][0].wait_recv()
        weights[j][2].start()
        weights[j][4].start()
        weights[j][1].wait_recv()
        weights[j][3].start()
        weights[j][5].start()
    for j in range(count):
        weights[j][2].wait_recv()
        weights[j][6].start()
        weights[j][3].wait_recv()
        weights[j][7].start()
    for copy in mine:
        copy.wait()

    @pl.loop(1, WIDE)
    def _(k):
        rows_copy(k).wait()
        codes_copy(k).wait()

    for j in range(count):
        for kind in range(4):
            weights[j][kind].wait_send()
        for kind in range(4, 8):
            weights[j][kind].wait()


def send_rows(source, points, codes, weights, collective):
    return pl.pallas_call(
        send_kernel,
        out_shape=[
            shape((WIDE, CAP, LOCAL), BF16),
            shape((WIDE, 2, 128), I32),
            shape((3 * WIDTH, WIDTH), BF16),
            shape((MP, LOCAL, WIDTH), BF16),
            shape((MP, 2 * WIDTH, WIDTH), BF16),
            shape((MP, WIDTH, WIDTH), BF16),
            shape((MP, 2 * LOCAL, WIDTH), BF16),
        ],
        in_specs=[SMEM, VMEM, ANY] + [VMEM] * 5,
        out_specs=[ANY] * 7,
        scratch_shapes=[
            pltpu.VMEM((ROWS, LOCAL), F32),
            pltpu.VMEM((1, CAP, LOCAL), F32),
            pltpu.VMEM((WIDE, CAP, LOCAL), BF16),
            pltpu.SemaphoreType.DMA((WIDE, 2)),
            pltpu.SemaphoreType.DMA((WIDE, 2)),
            pltpu.SemaphoreType.DMA((2,)),
            pltpu.SemaphoreType.DMA((5, 8)),
            pltpu.SemaphoreType.DMA((5, 8)),
            pltpu.SemaphoreType.DMA((5,)),
        ],
        compiler_params=params(collective),
    )(source, points, codes, *weights)


def return_kernel(
    code_ref, turned_ref, lifted_ref, got_ref, wide, staged, packed, send, recv, own
):
    me = lax.axis_index("wide")
    barrier = pltpu.get_barrier_semaphore()

    @pl.loop(1, WIDE)
    def _(k):
        pl.semaphore_signal(
            barrier, inc=1, device_id={"wide": lax.rem(me + k, WIDE)}, device_id_type=MESH
        )

    runs = run_matrix(
        lax.broadcasted_iota(I32, (BALL, 96), 0), lax.broadcasted_iota(I32, (BALL, 96), 1)
    )

    @pl.loop(0, ROWS // BALL)
    def _(i):
        at = pl.ds(pl.multiple_of(i * BALL, BALL), BALL)
        wide[at, :] = turned_ref[at, :].astype(F32) + dot(runs, lifted_ref[i])

    wide[ROWS : ROWS + 8, :] = jnp.zeros((8, LOCAL), F32)
    pl.semaphore_wait(barrier, WIDE - 1)

    def rows_copy(k):
        peer = turn_of(me, k)
        return remote(packed.at[peer], got_ref.at[me], send.at[k], recv.at[k], {"wide": peer})

    @pl.loop(1, WIDE)
    def _(k):
        gather_bucket(0, lambda s: code_ref[s] >> 1, wide, staged, packed, turn_of(me, k))
        rows_copy(k).start()

    gather_bucket(0, lambda s: code_ref[s] >> 1, wide, staged, packed, me)
    last = pltpu.make_async_copy(packed.at[me], got_ref.at[me], own)
    last.start()
    last.wait()

    @pl.loop(1, WIDE)
    def _(k):
        rows_copy(k).wait()


def return_rows(codes, turned, lifted, collective):
    return pl.pallas_call(
        return_kernel,
        out_shape=shape((WIDE, CAP, LOCAL), BF16),
        in_specs=[SMEM, VMEM, VMEM],
        out_specs=ANY,
        scratch_shapes=[
            pltpu.VMEM((ROWS + 8, LOCAL), F32),
            pltpu.VMEM((1, CAP, LOCAL), F32),
            pltpu.VMEM((WIDE, CAP, LOCAL), BF16),
            pltpu.SemaphoreType.DMA((WIDE,)),
            pltpu.SemaphoreType.DMA((WIDE,)),
            pltpu.SemaphoreType.DMA,
        ],
        compiler_params=params(collective),
    )(codes, turned, lifted)


SCALE = 0.125 * 1.4426950408889634


def lanes(count):
    return lax.broadcasted_iota(I32, (count, 128), 1)


def columns_of(flags):
    size = 256
    eye = lax.broadcasted_iota(I32, (size, size), 0) == lax.broadcasted_iota(I32, (size, size), 1)
    eye = jnp.where(eye, 1.0, 0.0).astype(BF16)
    out = []
    for begin in range(0, flags.shape[1], size):
        row = jnp.where(flags[:, begin : begin + size], 1.0, 0.0)
        out.append(dot_t(eye, jnp.broadcast_to(row, (128, size)).astype(BF16)))
    return jnp.concatenate(out, 0)


def augment(keys, values, columns):
    lane = lanes(keys.shape[0])
    low = lane < 64
    bias = jnp.where(columns > 0.5, 0.0, -1e30)
    keys = keys.astype(F32)
    values = values.astype(F32)
    return (
        (
            jnp.where(low, keys, jnp.where(lane == 64, bias, 0.0)).astype(BF16),
            jnp.where(low, jnp.where(lane == 0, bias, 0.0), keys).astype(BF16),
        ),
        (jnp.where(low, values, 1.0).astype(BF16), jnp.where(low, 1.0, values).astype(BF16)),
    )


def attend_pair(queries, own_keys, own_values, masked, keys, values):
    count = queries.shape[0]
    lane = lanes(count)
    low = lane < 64
    queries = queries.astype(F32)
    own_keys = own_keys.astype(F32)
    own_values = own_values.astype(F32)
    out = []
    for head in range(2):
        mine = low if head == 0 else jnp.logical_not(low)
        spare = jnp.where(lane == (64 if head == 0 else 0), 1.0, 0.0)
        q = jnp.where(mine, queries, spare).astype(BF16)
        scores = dot_t(q, keys(head))
        alone = jnp.sum(jnp.where(mine, queries * own_keys, 0.0), -1, keepdims=True)
        top = jnp.maximum(jnp.max(scores, -1, keepdims=True), alone)
        weights = jnp.exp2(scores - top).astype(BF16)
        own = jnp.where(masked, jnp.exp2(alone - top), 0.0)
        total = dot(weights, values(head))
        out.append(total + own * jnp.where(mine, own_values, 1.0))
    sums = pltpu.roll(jnp.where(low, out[1], out[0]), 64, 1)
    return (jnp.where(low, out[0], out[1]) / sums).astype(BF16)


def fine_ball(x, real, qkv_ref, out_ref):
    x = x.astype(F32)
    normed = norm(x).astype(BF16)
    q = (dot(normed, qkv_ref[0]) * SCALE).astype(BF16)
    k = dot(normed, qkv_ref[1]).astype(BF16)
    v = dot(normed, qkv_ref[2]).astype(BF16)
    columns = columns_of(real)
    masked = columns[:, :1] < 0.5
    mixed = []
    for g in range(MP):
        at = slice(g * 128, (g + 1) * 128)
        keys, values = augment(k[:, at], v[:, at], columns)
        mixed.append(
            attend_pair(q[:, at], k[:, at], v[:, at], masked, keys.__getitem__, values.__getitem__)
        )
    state = x + dot(jnp.concatenate(mixed, 1), out_ref[...])
    high = state.astype(BF16)
    rest = (state - high.astype(F32)).astype(BF16)
    runs, counted = pooling(real, 4)
    pooled = (dot(runs, high) + dot(runs, rest)) / jnp.maximum(counted, 1.0)
    return state, pooled.astype(BF16)


def pooling(real, factor):
    count_rows = BALL // factor
    r = lax.broadcasted_iota(I32, (count_rows, BALL), 0)
    c = lax.broadcasted_iota(I32, (count_rows, BALL), 1)
    hot = jnp.where(jnp.logical_and(r == c // factor, real), 1.0, 0.0)
    return hot.astype(BF16), jnp.sum(hot, 1, keepdims=True)


BALLS = QUARTER // BALL


def forward_tile(state, gate_up_ref, down_ref):
    normed = norm(state).astype(BF16)
    total = state
    for c in range(MP):
        gate = dot(normed, gate_up_ref[c, 0])
        up = dot(normed, gate_up_ref[c, 1])
        half = gate * 0.5
        activated = ((half + half * jnp.tanh(half)) * up).astype(BF16)
        total = total + dot(activated, down_ref[c])
    return total


def relatives(me):
    low = lax.rem(me, 2)
    high = lax.rem(me // 2, 2)
    first = me + 1 - 2 * low
    second = me + 2 - 4 * high
    third = first + 2 - 4 * high
    return (first, second, third)


def middle_kernel(
    slot_ref, got_ref, mask_ref, keep_ref, qkv_hbm, out_hbm, gate_up_hbm, down_hbm, coarse_hbm,
    lift_hbm, turned_ref, lifted_ref,
    wide, staged, packed, x, state, pooled, tiles, one, two, mate_one, mate_two, mate_keep,
    mixed, all_mixed, lifted, keys_one, values_one, keys_two, values_two, qkv_ref, out_ref, gate_up_ref, down_ref, w_ref, lift_ref,
    x_sem, p_sem, e_sem, k_sem, m_sem, t_sem, l_sem, own, loads,
):
    me = lax.axis_index("wide")
    mp = lax.axis_index("mp")
    others = relatives(me)
    barrier = pltpu.get_barrier_semaphore()
    for k in range(1, MP):
        pl.semaphore_signal(
            barrier, inc=1, device_id={"mp": lax.rem(mp + k, MP)}, device_id_type=MESH
        )
    for other in others:
        pl.semaphore_signal(barrier, inc=1, device_id={"wide": other}, device_id_type=MESH)
    load = [
        pltpu.make_async_copy(src, dst, loads.at[j])
        for j, (src, dst) in enumerate([
            (qkv_hbm, qkv_ref),
            (out_hbm, out_ref),
            (gate_up_hbm, gate_up_ref),
            (down_hbm, down_ref),
            (coarse_hbm, w_ref),
            (lift_hbm, lift_ref),
        ])
    ]
    for copy in load:
        copy.start()
    widen(got_ref, wide, SLOTS)
    pl.semaphore_wait(barrier, MP + 2)

    def rows(t, size):
        return pl.ds(pl.multiple_of(t * size, size), size)

    def cols(g):
        return pl.ds(pl.multiple_of(g * LOCAL, LOCAL), LOCAL)

    def peer(k):
        return lax.rem(mp + k, MP)

    def to_mp(src, dst, sem, k, t):
        return remote(src, dst, sem.at[0, k, t], sem.at[1, k, t], {"mp": peer(k)})

    def turn(k, t):
        return to_mp(packed.at[peer(k) * BALLS + t], x.at[rows(t, BALL), cols(mp)], x_sem, k, t)

    def keep_turn(t):
        return pltpu.make_async_copy(
            packed.at[mp * BALLS + t], x.at[rows(t, BALL), cols(mp)], own.at[0, t]
        )

    @pl.loop(0, BALLS)
    def _(t):
        for k in (2, 1, 3):
            gather_bucket(0, lambda s: slot_ref[s], wide, staged, packed, peer(k) * BALLS + t)
            turn(k, t).start()
        gather_bucket(0, lambda s: slot_ref[s], wide, staged, packed, mp * BALLS + t)
        keep_turn(t).start()

    def flags(j):
        return remote(
            keep_ref, mate_keep.at[j], k_sem.at[0, j], k_sem.at[1, j], {"wide": others[j]}
        )

    for j in range(3):
        flags(j).start()
    load[0].wait()
    load[1].wait()

    def share(k, t):
        return to_mp(pooled.at[mp, t], pooled.at[mp, t], p_sem, k, t)

    @pl.loop(0, BALLS)
    def _(t):
        for k in (1, 3, 2):
            turn(k, t).wait_recv()
        keep_turn(t).wait()
        real = mask_ref[pl.ds(mp * BALLS + t, 1), :] > 0
        out, means = fine_ball(x[rows(t, BALL), :], real, qkv_ref, out_ref)
        state[rows(t, BALL), :] = out
        pooled[mp, t] = means
        for k in (2, 1, 3):
            share(k, t).start()

    load[2].wait()
    load[3].wait()

    def give(k, t):
        return to_mp(
            tiles.at[rows(t, BALL), cols(peer(k))],
            turned_ref.at[rows(mp * BALLS + t, BALL), :],
            t_sem,
            k,
            t,
        )

    def keep_give(t):
        return pltpu.make_async_copy(
            tiles.at[rows(t, BALL), cols(mp)],
            turned_ref.at[rows(mp * BALLS + t, BALL), :],
            own.at[1, t],
        )

    def feed(t, count):
        at = pl.ds(t * BALL, count * BALL)
        tiles[at, :] = forward_tile(state[at, :], gate_up_ref, down_ref).astype(BF16)
        for u in range(t, t + count):
            for k in (2, 1, 3):
                give(k, u).start()
            keep_give(u).start()

    feed(0, 2)

    def pass_one(q):
        return remote(
            one.at[pl.ds(1, 2), rows(q, ONE), :],
            mate_one.at[:, rows(q, ONE), :],
            e_sem.at[0, 3, q],
            e_sem.at[1, 3, q],
            {"wide": others[0]},
        )

    def pass_two(j, q):
        return remote(
            two.at[pl.ds(1, 2), rows(q, TWO), :],
            mate_two.at[j, :, rows(q, TWO), :],
            e_sem.at[0, j, q],
            e_sem.at[1, j, q],
            {"wide": others[j]},
        )

    pair = lax.broadcasted_iota(I32, (32, 64), 0) == lax.broadcasted_iota(I32, (32, 64), 1) // 2
    pair = jnp.where(pair, 1.0, 0.0).astype(BF16)
    load[4].wait()

    def project(q):
        firsts, seconds = [], []
        for ball in range(BALLS):
            real = mask_ref[pl.ds(q * BALLS + ball, 1), :] > 0
            means = pooled[q, ball].astype(F32)
            firsts.append(norm(means).astype(BF16))
            sums = means * pooling(real, 4)[1]
            high = sums.astype(BF16)
            rest = (sums - high.astype(F32)).astype(BF16)
            counted = jnp.maximum(pooling(real, 8)[1], 1.0)
            seconds.append(norm((dot(pair, high) + dot(pair, rest)) / counted).astype(BF16))
        firsts = jnp.concatenate(firsts, 0)
        seconds = jnp.concatenate(seconds, 0)
        for t in (1, 2):
            two[t, rows(q, TWO), :] = dot(seconds, w_ref[1, t]).astype(BF16)
            one[t, rows(q, ONE), :] = dot(firsts, w_ref[0, t]).astype(BF16)
        for j in (1, 2, 0):
            pass_two(j, q).start()
        pass_one(q).start()
        two[0, rows(q, TWO), :] = (dot(seconds, w_ref[1, 0]) * SCALE).astype(BF16)
        one[0, rows(q, ONE), :] = (dot(firsts, w_ref[0, 0]) * SCALE).astype(BF16)

    project(mp)
    for k in (1, 3, 2):

        @pl.loop(0, BALLS)
        def _(t):
            share(MP - k, t).wait_recv()

        project(peer(k))

    feed(2, 1)

    def hand_to(q, k, level):
        at = pl.ds(0, ONE) if level == 0 else pl.ds(ONE, TWO)
        return to_mp(mixed.at[q, at, :], all_mixed.at[at, cols(mp)], m_sem, k, level)

    def hand(k, level):
        return hand_to(peer(k), k, level)

    def keep_hand(level):
        at = pl.ds(0, ONE) if level == 0 else pl.ds(ONE, TWO)
        return pltpu.make_async_copy(
            mixed.at[mp, at, :], all_mixed.at[at, cols(mp)], own.at[2, level]
        )

    for j in range(3):
        flags(j).wait()

    def fill(keys_ref, values_ref, begin, src, first, flag):
        for c in range(src.shape[1] // 256):
            at = slice(c * 256, (c + 1) * 256)
            here = flag[:, first + c * 256 : first + (c + 1) * 256] > 0
            keys, values = augment(src[0, at, :], src[1, at, :], columns_of(here))
            to = slice(begin + c * 256, begin + (c + 1) * 256)
            for head in range(2):
                keys_ref[head, to, :] = keys[head]
                values_ref[head, to, :] = values[head]

    def masked_of(keys_ref, at):
        spare = keys_ref[0, at, :].astype(F32)
        return jnp.min(jnp.where(lanes(256) == 64, spare, 0.0), -1, keepdims=True) < 0.0

    mine = keep_ref[...]
    fill(keys_one, values_one, 0, one.at[1:], 0, mine)

    @pl.loop(0, MP)
    def _(q):
        pass_one(q).wait()

    fill(keys_one, values_one, 4 * ONE, mate_one, 0, mate_keep[0])

    @pl.loop(1, MP + 1)
    def _(k):
        q = peer(k)
        at = rows(q, ONE)
        mixed[q, 0:ONE, :] = attend_pair(
            one[0, at, :], one[1, at, :], one[2, at, :], masked_of(keys_one, at),
            lambda head: keys_one[head], lambda head: values_one[head],
        )

        @pl.when(k < MP)
        def _():
            hand(k, 0).start()

    keep_hand(0).start()

    fill(keys_two, values_two, 0, two.at[1:], 4 * ONE, mine)

    @pl.loop(0, MP)
    def _(q):
        for j in range(3):
            pass_two(j, q).wait()

    for j in range(3):
        fill(keys_two, values_two, (j + 1) * 4 * TWO, mate_two.at[j], 4 * ONE, mate_keep[j])

    @pl.loop(0, 2)
    def _(p):
        at = rows(p, 256)
        both = attend_pair(
            two[0, at, :], two[1, at, :], two[2, at, :], masked_of(keys_two, at),
            lambda head: keys_two[head], lambda head: values_two[head],
        )
        for h in range(2):
            q = p * 2 + h
            k = lax.rem(q + MP - mp, MP)
            mixed[q, ONE:COARSE, :] = both[h * TWO : (h + 1) * TWO]

            @pl.when(k > 0)
            def _():
                hand_to(q, k, 1).start()

    keep_hand(1).start()

    feed(3, 1)

    load[5].wait()
    for level in range(2):
        keep_hand(level).wait()
        for k in (1, 3, 2):
            hand(k, level).wait()
    for level, begin, size in ((0, 0, 64), (1, ONE, 32)):
        span = slice(begin, begin + size * BALLS)
        total = jnp.zeros((size * BALLS, WIDTH), F32)
        for g in range(MP):
            total = total + dot(
                all_mixed[span, g * LOCAL : (g + 1) * LOCAL],
                lift_ref[g, level * LOCAL : (level + 1) * LOCAL, :],
            )
        total = total.astype(BF16)
        for ball in range(BALLS):
            at = slice(0, 64) if level == 0 else slice(64, 96)
            lifted[ball, at, :] = total[ball * size : (ball + 1) * size]

    def rise(k):
        return to_mp(lifted.at[:, :, cols(peer(k))], lifted_ref.at[mp], l_sem, k, 0)

    for k in (2, 1, 3):
        rise(k).start()
    keep_rise = pltpu.make_async_copy(lifted.at[:, :, cols(mp)], lifted_ref.at[mp], own.at[3, 0])
    keep_rise.start()

    @pl.loop(0, BALLS)
    def _(t):
        keep_give(t).wait()
        for k in (1, 3, 2):
            turn(k, t).wait_send()
            share(k, t).wait_send()
            give(k, t).wait()

    keep_rise.wait()
    for k in (1, 3, 2):
        rise(k).wait()


def middle(slots, got, mask, keep, weights, collective):
    dma = pltpu.SemaphoreType.DMA
    return pl.pallas_call(
        middle_kernel,
        out_shape=[shape((ROWS, LOCAL), BF16), shape((MP, BALLS, 96, LOCAL), BF16)],
        in_specs=[SMEM, VMEM, VMEM, VMEM] + [ANY] * 6,
        out_specs=[ANY, ANY],
        scratch_shapes=[
            pltpu.VMEM((SLOTS, LOCAL), F32),
            pltpu.VMEM((1, CAP, LOCAL), F32),
            pltpu.VMEM((MP * BALLS, BALL, LOCAL), BF16),
            pltpu.VMEM((QUARTER, WIDTH), BF16),
            pltpu.VMEM((QUARTER, WIDTH), F32),
            pltpu.VMEM((MP, BALLS, 64, WIDTH), BF16),
            pltpu.VMEM((QUARTER, WIDTH), BF16),
            pltpu.VMEM((3, 4 * ONE, LOCAL), BF16),
            pltpu.VMEM((3, 4 * TWO, LOCAL), BF16),
            pltpu.VMEM((2, 4 * ONE, LOCAL), BF16),
            pltpu.VMEM((3, 2, 4 * TWO, LOCAL), BF16),
            pltpu.VMEM((3, 1, 12 * 128), I32),
            pltpu.VMEM((MP, COARSE, LOCAL), BF16),
            pltpu.VMEM((COARSE, WIDTH), BF16),
            pltpu.VMEM((BALLS, 96, WIDTH), BF16),
            pltpu.VMEM((2, 8 * ONE, LOCAL), BF16),
            pltpu.VMEM((2, 8 * ONE, LOCAL), BF16),
            pltpu.VMEM((2, 16 * TWO, LOCAL), BF16),
            pltpu.VMEM((2, 16 * TWO, LOCAL), BF16),
            pltpu.VMEM((3, WIDTH, WIDTH), BF16),
            pltpu.VMEM((WIDTH, WIDTH), BF16),
            pltpu.VMEM((MP, 2, WIDTH, WIDTH), BF16),
            pltpu.VMEM((MP, WIDTH, WIDTH), BF16),
            pltpu.VMEM((2, 3, WIDTH, LOCAL), BF16),
            pltpu.VMEM((MP, 2 * LOCAL, WIDTH), BF16),
            dma((2, MP, BALLS)),
            dma((2, MP, BALLS)),
            dma((2, 4, MP)),
            dma((2, 3)),
            dma((2, MP, 2)),
            dma((2, MP, BALLS)),
            dma((2, MP, 1)),
            dma((4, BALLS)),
            dma((6,)),
        ],
        compiler_params=params(collective),
    )(slots, got, mask, keep, *weights)


def on_device(points, mask, perm, w_qkv, w_out, w_gate_up, w_down, w_coarse, w_coarse_out):
    slot, source, codes = index(perm, mask)
    got, got_code, full_qkv, full_out, full_gate_up, full_down, full_lift = send_rows(
        source.reshape(SLOTS),
        points,
        codes,
        [
            w_qkv.reshape(3 * WIDTH, LOCAL),
            w_out,
            w_gate_up.reshape(2 * WIDTH, WIDTH),
            w_down,
            w_coarse_out.reshape(2 * LOCAL, WIDTH),
        ],
        1,
    )
    full_qkv = full_qkv.reshape(3, WIDTH, WIDTH)
    full_out = full_out.reshape(WIDTH, WIDTH)
    full_gate_up = full_gate_up.reshape(MP, 2, WIDTH, WIDTH)
    landed, owned_mask, kept = inverse(got_code)
    keep = jnp.concatenate([kept[:, :64].reshape(1, 4 * ONE), kept[:, 64:].reshape(1, 4 * TWO)], 1)
    turned, lifted = middle(
        landed.reshape(ROWS), got.reshape(SLOTS, LOCAL), owned_mask, keep,
        [full_qkv, full_out, full_gate_up, full_down, w_coarse, full_lift], 2,
    )
    lifted = lifted.reshape(MP * BALLS, 96, LOCAL)
    returned = return_rows(got_code.reshape(SLOTS), turned, lifted, 3)
    return pl.pallas_call(
        finish_kernel,
        out_shape=shape((ROWS, LOCAL), F32),
        in_specs=[SMEM, VMEM],
        out_specs=VMEM,
        scratch_shapes=[pltpu.VMEM((SLOTS, LOCAL), F32)],
        compiler_params=params(),
    )(slot.reshape(ROWS), returned.reshape(SLOTS, LOCAL))


def solution(mesh):
    placed = (
        P("wide", "mp"),
        P("wide"),
        P("wide"),
        P(None, None, "mp"),
        P("mp", None),
        P(None, None, "mp"),
        P("mp", None),
        P(None, None, None, "mp"),
        P(None, "mp", None),
    )
    return jax.shard_map(
        on_device, mesh=mesh, in_specs=placed, out_specs=P("wide", "mp"), check_vma=False
    )
```

```python
import functools

import jax
import jax.numpy as jnp
from jax import lax
from jax.experimental import pallas as pl
from jax.experimental.pallas import tpu as pltpu
from jax.sharding import PartitionSpec as P

BALL = 256
WIDE = 32
MP = 4
ROWS = 4096
CAP = 256
SLOTS = WIDE * CAP
QUARTER = ROWS // MP
WIDTH = 512
LOCAL = WIDTH // MP
HIDDEN = 2048
ONE = QUARTER // 4
TWO = QUARTER // 8
COARSE = ONE + TWO
F32 = jnp.float32
BF16 = jnp.bfloat16
I32 = jnp.int32
MESH = pl.DeviceIdType.MESH
ANY = pl.BlockSpec(memory_space=pl.ANY)
VMEM = pl.BlockSpec(memory_space=pltpu.VMEM)
SMEM = pl.BlockSpec(memory_space=pltpu.SMEM)
LIMIT = 56 * 1024 * 1024


def shape(dims, kind):
    return jax.ShapeDtypeStruct(dims, kind)


def params(collective=None):
    if collective is None:
        return pltpu.CompilerParams(vmem_limit_bytes=LIMIT)
    return pltpu.CompilerParams(
        vmem_limit_bytes=LIMIT, collective_id=collective, has_side_effects=True
    )


def dot(a, b):
    return jnp.dot(a, b, preferred_element_type=F32)


def dot_t(a, b):
    return lax.dot_general(a, b, (((1,), (1,)), ((), ())), preferred_element_type=F32)


def norm(values):
    return values * lax.rsqrt(jnp.mean(values * values, -1, keepdims=True) + 1e-06)


UNROLL = 32
NONE = 2 * ROWS


def index_kernel(perm_ref, mask_ref, slot_ref, source_ref, codes_ref):
    perm = perm_ref[...]
    target = perm >> 12
    code = (perm & (ROWS - 1)) * 2 + mask_ref[...]
    rows = lax.broadcasted_iota(I32, (CAP, 128), 0)
    upper = jnp.where(
        lax.broadcasted_iota(I32, (128, 128), 0) < lax.broadcasted_iota(I32, (128, 128), 1), 1.0, 0.0
    ).astype(BF16)
    which = lax.broadcasted_iota(I32, (WIDE, 128), 0)
    lane = lax.broadcasted_iota(I32, (1, 128), 1).astype(F32)
    carry = jnp.zeros((WIDE, 1), F32)
    found = jnp.zeros((5 * WIDE, CAP), F32)
    for c in range(ROWS // 128):
        row = slice(c, c + 1)
        hot = jnp.where(which == target[row, :], 1.0, 0.0)
        before = dot(hot.astype(BF16), upper) + carry
        rank = jnp.sum(hot * before, 0, keepdims=True).astype(I32)
        slot_ref[row, :] = target[row, :] * CAP + rank
        carry = carry + jnp.sum(hot, 1, keepdims=True)
        placed = jnp.where(rows == rank, 1.0, 0.0).astype(BF16)
        high = (code[row, :] >> 6).astype(F32)
        low = (code[row, :] & 63).astype(F32)
        values = jnp.concatenate([hot * lane, hot * float(c), hot * high, hot * low, hot], 0)
        found = found + dot_t(values.astype(BF16), placed)
    source = (found[:WIDE] + found[WIDE : 2 * WIDE] * 128.0).astype(I32)
    codes = (found[2 * WIDE : 3 * WIDE] * 64.0 + found[3 * WIDE : 4 * WIDE]).astype(I32)
    codes = jnp.where(found[4 * WIDE :] > 0.5, codes, NONE)
    for h in range(2):
        at = slice(h * 128, (h + 1) * 128)
        source_ref[:, h, :] = source[:, at]
        codes_ref[:, h, :] = codes[:, at]


def index(perm, mask):
    return pl.pallas_call(
        index_kernel,
        out_shape=[shape((32, 128), I32), shape((WIDE, 2, 128), I32), shape((WIDE, 2, 128), I32)],
        in_specs=[VMEM] * 2,
        out_specs=[VMEM] * 3,
        compiler_params=params(),
    )(perm.reshape(32, 128), mask.reshape(32, 128))


def invert(codes_ref, slot_ref, mask_ref, keep_ref):
    balls = ROWS // BALL
    rows = lax.broadcasted_iota(I32, (256, 128), 0)
    which = lax.broadcasted_iota(I32, (balls, 128), 0)
    lane = lax.broadcasted_iota(I32, (1, 128), 1).astype(F32)
    found = jnp.zeros((3 * balls, 256), F32)
    for c in range(WIDE):
        for h in range(2):
            code = codes_ref[c, h : h + 1, :]
            landing = code >> 1
            hot = jnp.where(which == (landing >> 8), 1.0, 0.0)
            placed = jnp.where(rows == (landing & 255), 1.0, 0.0).astype(BF16)
            real = (code & 1).astype(F32)
            values = jnp.concatenate([hot * lane, hot * float(2 * c + h), hot * real], 0)
            found = found + dot_t(values.astype(BF16), placed)
    slots = (found[:balls] + found[balls : 2 * balls] * 128.0).astype(I32)
    for h in range(2):
        slot_ref[:, h, :] = slots[:, h * 128 : (h + 1) * 128]
    mask = found[2 * balls :]
    mask_ref[...] = mask.astype(I32)
    mask = mask.astype(BF16)
    for f, first in ((4, 0), (8, 8)):
        side = f // 2
        count = balls // side
        total = jnp.zeros((count, 128), F32)
        for j in range(side):
            r = lax.broadcasted_iota(I32, (count, balls), 0)
            c = lax.broadcasted_iota(I32, (count, balls), 1)
            pick = jnp.where(c == r * side + j, 1.0, 0.0).astype(BF16)
            r = lax.broadcasted_iota(I32, (256, 128), 0)
            c = lax.broadcasted_iota(I32, (256, 128), 1)
            runs = jnp.where(c == r // f + j * (128 // side), 1.0, 0.0).astype(BF16)
            total = total + dot(dot(pick, mask).astype(BF16), runs)
        keep_ref[first : first + count, :] = jnp.where(total > 0.5, 1, 0)


def run_matrix(r, c):
    hot = jnp.logical_or(
        jnp.logical_and(c < 64, r // 4 == c), jnp.logical_and(c >= 64, r // 8 == c - 64)
    )
    return jnp.where(hot, 1.0, 0.0).astype(BF16)


def widen(src, dst, rows):
    @pl.loop(0, rows // 256)
    def _(i):
        at = pl.ds(pl.multiple_of(i * 256, 256), 256)
        dst[at, :] = src[at, :].astype(dst.dtype)


def finish_kernel(slot_ref, got_ref, out_ref, wide):
    widen(got_ref, wide, SLOTS)

    @pl.loop(0, ROWS // UNROLL)
    def _(i):
        base = i * UNROLL
        lines = [wide[pl.ds(slot_ref[base + u], 1), :] for u in range(UNROLL)]
        for u in range(UNROLL):
            out_ref[pl.ds(base + u, 1), :] = lines[u]


def remote(src, dst, send, recv, device):
    return pltpu.make_async_remote_copy(
        src_ref=src, dst_ref=dst, send_sem=send, recv_sem=recv, device_id=device, device_id_type=MESH
    )


def turn_of(me, k):
    return lax.rem(me + lax.rem(k * 7, WIDE), WIDE)


def gather_bucket(line, lookup, wide, staged, packed, peer):
    @pl.loop(0, CAP // UNROLL)
    def _(i):
        begin = i * UNROLL
        lines = [wide[pl.ds(lookup(peer * CAP + begin + u), 1), :] for u in range(UNROLL)]
        for u in range(UNROLL):
            staged[line, pl.ds(begin + u, 1), :] = lines[u]

    packed[peer] = staged[line].astype(BF16)


def send_kernel(
    source_ref, points_ref, codes_ref, qkv_ref, out_ref, gate_up_ref, down_ref,
    got_ref, got_codes_out, slot_ref, mask_ref, keep_ref, all_qkv, all_out, all_gate_up, all_down,
    got_codes_ref, wide, staged, packed, send, recv, own, w_send, w_recv, w_own,
):
    me = lax.axis_index("wide")
    mp = lax.axis_index("mp")
    core = lax.rem(me, 2)
    partner = me + 1 - 2 * core
    after, ahead = lax.rem(mp + 1, MP), lax.rem(mp + 2, MP)
    behind = lax.rem(mp + 3, MP)
    barrier = pltpu.get_barrier_semaphore()

    @pl.loop(1, WIDE)
    def _(k):
        pl.semaphore_signal(
            barrier, inc=1, device_id={"wide": lax.rem(me + k, WIDE)}, device_id_type=MESH
        )

    for other in (after, behind):
        pl.semaphore_signal(barrier, inc=1, device_id={"mp": other}, device_id_type=MESH)
    widen(points_ref, wide, ROWS)

    def part(first, count):
        def rows(ref, quarter):
            return pl.ds(pl.multiple_of(first * quarter, 16), count * quarter)

        def cut(j, ref, shard):
            if j == 0:
                return ref.at[rows(ref, 384), pl.ds(pl.multiple_of(shard * 128, 128), 128)]
            quarter = (0, 32, 256, 128)[j]
            return ref.at[shard, rows(ref, quarter), :]

        def own_cut(j, ref):
            quarter = (384, 32, 256, 128)[j]
            return ref.at[rows(ref, quarter), :]

        return cut, own_cut

    half, own_half = part(2 * core, 2)
    first, _ = part(2 * core, 1)
    second, _ = part(2 * core + 1, 1)
    every, own_every = part(0, 4)
    shards = [qkv_ref, out_ref, gate_up_ref, down_ref]
    full = [all_qkv, all_out, all_gate_up, all_down]
    count = len(shards)

    def weight(j, kind, cut, src, shard, device):
        return remote(
            src, cut(j, full[j], shard), w_send.at[j, kind], w_recv.at[j, kind], device
        )

    def weight_copies(j):
        ref = full[j]
        mine = own_half(j, shards[j])
        return [
            weight(j, 0, half, mine, mp, {"mp": after}),
            weight(j, 1, half, mine, mp, {"mp": behind}),
            weight(j, 2, first, first(j, ref, behind), behind, {"mp": after}),
            weight(j, 3, second, second(j, ref, after), after, {"mp": behind}),
            weight(j, 4, half, half(j, ref, behind), behind, {"wide": partner}),
            weight(j, 5, half, half(j, ref, after), after, {"wide": partner}),
            weight(j, 6, first, first(j, ref, ahead), ahead, {"wide": partner}),
            weight(j, 7, second, second(j, ref, ahead), ahead, {"wide": partner}),
        ]

    weights = [weight_copies(j) for j in range(count)]

    def rows_copy(k):
        peer = turn_of(me, k)
        return remote(
            packed.at[peer], got_ref.at[me], send.at[k, 0], recv.at[k, 0], {"wide": peer}
        )

    def codes_copy(k):
        peer = turn_of(me, k)
        return remote(
            codes_ref.at[peer], got_codes_ref.at[me], send.at[k, 1], recv.at[k, 1], {"wide": peer}
        )

    pl.semaphore_wait(barrier, WIDE + 1)
    for j in range(count):
        weights[j][0].start()
        weights[j][1].start()

    @pl.loop(1, WIDE)
    def _(k):
        codes_copy(k).start()

    @pl.loop(1, WIDE)
    def _(k):
        gather_bucket(0, lambda s: source_ref[s], wide, staged, packed, turn_of(me, k))
        rows_copy(k).start()

    gather_bucket(0, lambda s: source_ref[s], wide, staged, packed, me)
    mine = [
        pltpu.make_async_copy(packed.at[me], got_ref.at[me], own.at[0]),
        pltpu.make_async_copy(codes_ref.at[me], got_codes_ref.at[me], own.at[1]),
    ]
    for j in range(count):
        mine.append(
            pltpu.make_async_copy(own_every(j, shards[j]), every(j, full[j], mp), w_own.at[j])
        )
    for copy in mine:
        copy.start()

    def forward(j):
        weights[j][0].wait_recv()
        weights[j][2].start()
        weights[j][4].start()
        weights[j][1].wait_recv()
        weights[j][3].start()
        weights[j][5].start()

    def forward_last(j):
        weights[j][2].wait_recv()
        weights[j][6].start()
        weights[j][3].wait_recv()
        weights[j][7].start()

    forward(0)
    forward(1)
    for copy in mine:
        copy.wait()

    @pl.loop(1, WIDE)
    def _(k):
        codes_copy(k).wait()

    invert(got_codes_ref, slot_ref, mask_ref, keep_ref)
    got_codes_out[...] = got_codes_ref[...]
    for j in range(2, count):
        forward(j)
    for j in range(count):
        forward_last(j)

    @pl.loop(1, WIDE)
    def _(k):
        rows_copy(k).wait()

    for j in range(count):
        for kind in range(4):
            weights[j][kind].wait_send()
        for kind in range(4, 8):
            weights[j][kind].wait()


def send_rows(source, points, codes, weights, collective):
    return pl.pallas_call(
        send_kernel,
        out_shape=[
            shape((WIDE, CAP, LOCAL), BF16),
            shape((WIDE, 2, 128), I32),
            shape((16, 2, 128), I32),
            shape((16, 256), I32),
            shape((12, 128), I32),
            shape((3 * WIDTH, WIDTH), BF16),
            shape((MP, LOCAL, WIDTH), BF16),
            shape((MP, 2 * WIDTH, WIDTH), BF16),
            shape((MP, WIDTH, WIDTH), BF16),
        ],
        in_specs=[SMEM, VMEM, ANY] + [VMEM] * 4,
        out_specs=[ANY] + [VMEM] * 4 + [ANY] * 4,
        scratch_shapes=[
            pltpu.VMEM((WIDE, 2, 128), I32),
            pltpu.VMEM((ROWS, LOCAL), F32),
            pltpu.VMEM((1, CAP, LOCAL), F32),
            pltpu.VMEM((WIDE, CAP, LOCAL), BF16),
            pltpu.SemaphoreType.DMA((WIDE, 2)),
            pltpu.SemaphoreType.DMA((WIDE, 2)),
            pltpu.SemaphoreType.DMA((2,)),
            pltpu.SemaphoreType.DMA((4, 8)),
            pltpu.SemaphoreType.DMA((4, 8)),
            pltpu.SemaphoreType.DMA((4,)),
        ],
        compiler_params=params(collective),
    )(source, points, codes, *weights)


def return_kernel(
    code_ref, turned_ref, lifted_ref, got_ref, wide, staged, packed, send, recv, own
):
    me = lax.axis_index("wide")
    barrier = pltpu.get_barrier_semaphore()

    @pl.loop(1, WIDE)
    def _(k):
        pl.semaphore_signal(
            barrier, inc=1, device_id={"wide": lax.rem(me + k, WIDE)}, device_id_type=MESH
        )

    runs = run_matrix(
        lax.broadcasted_iota(I32, (BALL, 96), 0), lax.broadcasted_iota(I32, (BALL, 96), 1)
    )

    @pl.loop(0, ROWS // BALL)
    def _(i):
        at = pl.ds(pl.multiple_of(i * BALL, BALL), BALL)
        wide[at, :] = turned_ref[at, :].astype(F32) + dot(runs, lifted_ref[i])

    wide[ROWS : ROWS + 8, :] = jnp.zeros((8, LOCAL), F32)
    pl.semaphore_wait(barrier, WIDE - 1)

    def rows_copy(k):
        peer = turn_of(me, k)
        return remote(packed.at[peer], got_ref.at[me], send.at[k], recv.at[k], {"wide": peer})

    @pl.loop(1, WIDE)
    def _(k):
        gather_bucket(0, lambda s: code_ref[s] >> 1, wide, staged, packed, turn_of(me, k))
        rows_copy(k).start()

    gather_bucket(0, lambda s: code_ref[s] >> 1, wide, staged, packed, me)
    last = pltpu.make_async_copy(packed.at[me], got_ref.at[me], own)
    last.start()
    last.wait()

    @pl.loop(1, WIDE)
    def _(k):
        rows_copy(k).wait()


def return_rows(codes, turned, lifted, collective):
    return pl.pallas_call(
        return_kernel,
        out_shape=shape((WIDE, CAP, LOCAL), BF16),
        in_specs=[SMEM, VMEM, VMEM],
        out_specs=ANY,
        scratch_shapes=[
            pltpu.VMEM((ROWS + 8, LOCAL), F32),
            pltpu.VMEM((1, CAP, LOCAL), F32),
            pltpu.VMEM((WIDE, CAP, LOCAL), BF16),
            pltpu.SemaphoreType.DMA((WIDE,)),
            pltpu.SemaphoreType.DMA((WIDE,)),
            pltpu.SemaphoreType.DMA,
        ],
        compiler_params=params(collective),
    )(codes, turned, lifted)


SCALE = 0.125 * 1.4426950408889634


def lanes(count):
    return lax.broadcasted_iota(I32, (count, 128), 1)


def columns_of(flags):
    eye = lax.broadcasted_iota(I32, (128, 128), 0) == lax.broadcasted_iota(I32, (128, 128), 1)
    row = jnp.broadcast_to(jnp.where(flags, 1.0, 0.0), (128, 128)).astype(BF16)
    return dot_t(jnp.where(eye, 1.0, 0.0).astype(BF16), row)


def augment(keys, values, columns):
    lane = lanes(keys.shape[0])
    low = lane < 64
    bias = jnp.where(columns > 0.5, 0.0, -1e30)
    keys = keys.astype(F32)
    values = values.astype(F32)
    return (
        (
            jnp.where(low, keys, jnp.where(lane == 64, bias, 0.0)).astype(BF16),
            jnp.where(low, jnp.where(lane == 0, bias, 0.0), keys).astype(BF16),
        ),
        (jnp.where(low, values, 1.0).astype(BF16), jnp.where(low, 1.0, values).astype(BF16)),
    )


def attend_pair(queries, own_keys, own_values, masked, keys, values):
    count = queries.shape[0]
    lane = lanes(count)
    low = lane < 64
    queries = queries.astype(F32)
    own_keys = own_keys.astype(F32)
    own_values = own_values.astype(F32)
    out = []
    for head in range(2):
        mine = low if head == 0 else jnp.logical_not(low)
        spare = jnp.where(lane == (64 if head == 0 else 0), 1.0, 0.0)
        q = jnp.where(mine, queries, spare).astype(BF16)
        scores = dot_t(q, keys(head))
        alone = jnp.sum(jnp.where(mine, queries * own_keys, 0.0), -1, keepdims=True)
        top = jnp.maximum(jnp.max(scores, -1, keepdims=True), alone)
        weights = jnp.exp2(scores - top).astype(BF16)
        own = jnp.where(masked, jnp.exp2(alone - top), 0.0)
        total = dot(weights, values(head))
        out.append(total + own * jnp.where(mine, own_values, 1.0))
    sums = pltpu.roll(jnp.where(low, out[1], out[0]), 64, 1)
    return (jnp.where(low, out[0], out[1]) / sums).astype(BF16)


def attend_ball(queries, keys, values, allowed):
    low = lanes(BALL) < 64
    out = []
    for head in range(2):
        mine = low if head == 0 else jnp.logical_not(low)
        q = jnp.where(mine, queries, jnp.zeros_like(queries))
        scores = jnp.where(allowed, dot_t(q, keys), -1e30)
        weights = jnp.exp2(scores - jnp.max(scores, -1, keepdims=True))
        total = jnp.sum(weights, -1, keepdims=True)
        out.append(dot(weights.astype(BF16), values) / total)
    return jnp.where(low, out[0], out[1]).astype(BF16)


def fine_ball(x, real, qkv_ref, out_ref):
    x = x.astype(F32)
    normed = norm(x).astype(BF16)
    q = (dot(normed, qkv_ref[0]) * SCALE).astype(BF16)
    k = dot(normed, qkv_ref[1]).astype(BF16)
    v = dot(normed, qkv_ref[2]).astype(BF16)
    rows = lax.broadcasted_iota(I32, (BALL, BALL), 0)
    cols = lax.broadcasted_iota(I32, (BALL, BALL), 1)
    allowed = jnp.logical_or(real, rows == cols)
    mixed = []
    for g in range(MP):
        at = slice(g * 128, (g + 1) * 128)
        mixed.append(attend_ball(q[:, at], k[:, at], v[:, at], allowed))
    state = x + dot(jnp.concatenate(mixed, 1), out_ref[...])
    high = state.astype(BF16)
    rest = (state - high.astype(F32)).astype(BF16)
    runs, counted = pooling(real, 4)
    pooled = (dot(runs, high) + dot(runs, rest)) / jnp.maximum(counted, 1.0)
    return state, pooled.astype(BF16)


def pooling(real, factor):
    count_rows = BALL // factor
    r = lax.broadcasted_iota(I32, (count_rows, BALL), 0)
    c = lax.broadcasted_iota(I32, (count_rows, BALL), 1)
    hot = jnp.where(jnp.logical_and(r == c // factor, real), 1.0, 0.0)
    return hot.astype(BF16), jnp.sum(hot, 1, keepdims=True)


BALLS = QUARTER // BALL


def forward_tile(state, gate_up_ref, down_ref):
    normed = norm(state).astype(BF16)
    total = state
    for c in range(MP):
        gate = dot(normed, gate_up_ref[c, 0])
        up = dot(normed, gate_up_ref[c, 1])
        half = gate * 0.5
        activated = ((half + half * jnp.tanh(half)) * up).astype(BF16)
        total = total + dot(activated, down_ref[c])
    return total


def relatives(me):
    low = lax.rem(me, 2)
    high = lax.rem(me // 2, 2)
    first = me + 1 - 2 * low
    second = me + 2 - 4 * high
    third = first + 2 - 4 * high
    return (first, second, third)


def middle_kernel(
    slot_ref, got_ref, mask_ref, keep_ref, qkv_hbm, out_hbm, gate_up_hbm, down_hbm, coarse_hbm,
    lift_hbm, turned_ref, lifted_ref,
    wide, staged, packed, x, state, pooled, tiles, one, two, mate_one, mate_two, mate_keep,
    mixed, all_mixed, lifted, keys_one, values_one, keys_two, values_two, qkv_ref, out_ref, gate_up_ref, down_ref, w_ref, lift_ref,
    x_sem, p_sem, e_sem, k_sem, m_sem, t_sem, l_sem, w_sem, own, loads,
):
    me = lax.axis_index("wide")
    mp = lax.axis_index("mp")
    others = relatives(me)
    barrier = pltpu.get_barrier_semaphore()
    for k in range(1, MP):
        pl.semaphore_signal(
            barrier, inc=1, device_id={"mp": lax.rem(mp + k, MP)}, device_id_type=MESH
        )
    for other in others:
        pl.semaphore_signal(barrier, inc=1, device_id={"wide": other}, device_id_type=MESH)
    load = [
        pltpu.make_async_copy(src, dst, loads.at[j])
        for j, (src, dst) in enumerate([
            (qkv_hbm, qkv_ref),
            (out_hbm, out_ref),
            (gate_up_hbm, gate_up_ref),
            (down_hbm, down_ref),
            (coarse_hbm, w_ref),
            (lift_hbm, lift_ref.at[mp]),
        ])
    ]
    for copy in load:
        copy.start()
    widen(got_ref, wide, SLOTS)
    pl.semaphore_wait(barrier, MP + 2)

    def rows(t, size):
        return pl.ds(pl.multiple_of(t * size, size), size)

    def cols(g):
        return pl.ds(pl.multiple_of(g * LOCAL, LOCAL), LOCAL)

    def peer(k):
        return lax.rem(mp + k, MP)

    def to_mp(src, dst, sem, k, t):
        return remote(src, dst, sem.at[0, k, t], sem.at[1, k, t], {"mp": peer(k)})

    def turn(k, t):
        return to_mp(packed.at[peer(k) * BALLS + t], x.at[rows(t, BALL), cols(mp)], x_sem, k, t)

    def keep_turn(t):
        return pltpu.make_async_copy(
            packed.at[mp * BALLS + t], x.at[rows(t, BALL), cols(mp)], own.at[0, t]
        )

    @pl.loop(0, BALLS)
    def _(t):
        for k in (2, 1, 3):
            gather_bucket(0, lambda s: slot_ref[s], wide, staged, packed, peer(k) * BALLS + t)
            turn(k, t).start()
        gather_bucket(0, lambda s: slot_ref[s], wide, staged, packed, mp * BALLS + t)
        keep_turn(t).start()

    def flags(j):
        return remote(
            keep_ref, mate_keep.at[j], k_sem.at[0, j], k_sem.at[1, j], {"wide": others[j]}
        )

    for j in range(3):
        flags(j).start()
    load[0].wait()
    load[1].wait()

    def share(k, t):
        return to_mp(pooled.at[mp, t], pooled.at[mp, t], p_sem, k, t)

    @pl.loop(0, BALLS)
    def _(t):
        for k in (1, 3, 2):
            turn(k, t).wait_recv()
        keep_turn(t).wait()
        real = mask_ref[pl.ds(mp * BALLS + t, 1), :] > 0
        out, means = fine_ball(x[rows(t, BALL), :], real, qkv_ref, out_ref)
        state[rows(t, BALL), :] = out
        pooled[mp, t] = means
        for k in (2, 1, 3):
            share(k, t).start()

    core = lax.rem(me, 2)
    lift_half = pl.ds(pl.multiple_of(core * LOCAL, LOCAL), LOCAL)

    def weigh(k):
        part = lift_ref.at[mp, lift_half, :]
        return to_mp(part, part, w_sem, k, 0)

    def weigh_on(k):
        part = lift_ref.at[peer(MP - k), lift_half, :]
        return remote(part, part, w_sem.at[0, k, 1], w_sem.at[1, k, 1], {"wide": others[0]})

    load[5].wait()
    for k in (1, 3, 2):
        weigh(k).start()
    load[2].wait()
    load[3].wait()

    def give(k, t):
        return to_mp(
            tiles.at[rows(t, BALL), cols(peer(k))],
            turned_ref.at[rows(mp * BALLS + t, BALL), :],
            t_sem,
            k,
            t,
        )

    def keep_give(t):
        return pltpu.make_async_copy(
            tiles.at[rows(t, BALL), cols(mp)],
            turned_ref.at[rows(mp * BALLS + t, BALL), :],
            own.at[1, t],
        )

    def feed(t, count):
        at = pl.ds(t * BALL, count * BALL)
        tiles[at, :] = forward_tile(state[at, :], gate_up_ref, down_ref).astype(BF16)
        for u in range(t, t + count):
            for k in (2, 1, 3):
                give(k, u).start()
            keep_give(u).start()

    feed(0, 2)

    def pass_one(q):
        return remote(
            one.at[pl.ds(1, 2), rows(q, ONE), :],
            mate_one.at[:, rows(q, ONE), :],
            e_sem.at[0, 3, q],
            e_sem.at[1, 3, q],
            {"wide": others[0]},
        )

    def pass_two(j, q):
        return remote(
            two.at[pl.ds(1, 2), rows(q, TWO), :],
            mate_two.at[j, :, rows(q, TWO), :],
            e_sem.at[0, j, q],
            e_sem.at[1, j, q],
            {"wide": others[j]},
        )

    pair = lax.broadcasted_iota(I32, (32, 64), 0) == lax.broadcasted_iota(I32, (32, 64), 1) // 2
    pair = jnp.where(pair, 1.0, 0.0).astype(BF16)
    load[4].wait()

    def project(q):
        firsts, seconds = [], []
        for ball in range(BALLS):
            real = mask_ref[pl.ds(q * BALLS + ball, 1), :] > 0
            means = pooled[q, ball].astype(F32)
            firsts.append(norm(means).astype(BF16))
            sums = means * pooling(real, 4)[1]
            high = sums.astype(BF16)
            rest = (sums - high.astype(F32)).astype(BF16)
            counted = jnp.maximum(pooling(real, 8)[1], 1.0)
            seconds.append(norm((dot(pair, high) + dot(pair, rest)) / counted).astype(BF16))
        firsts = jnp.concatenate(firsts, 0)
        seconds = jnp.concatenate(seconds, 0)
        for t in (1, 2):
            two[t, rows(q, TWO), :] = dot(seconds, w_ref[1, t]).astype(BF16)
            one[t, rows(q, ONE), :] = dot(firsts, w_ref[0, t]).astype(BF16)
        for j in (1, 2, 0):
            pass_two(j, q).start()
        pass_one(q).start()
        two[0, rows(q, TWO), :] = (dot(seconds, w_ref[1, 0]) * SCALE).astype(BF16)
        one[0, rows(q, ONE), :] = (dot(firsts, w_ref[0, 0]) * SCALE).astype(BF16)

    project(mp)
    for k in (1, 3, 2):

        @pl.loop(0, BALLS)
        def _(t):
            share(MP - k, t).wait_recv()

        project(peer(k))

    feed(2, 1)
    for k in (1, 3, 2):
        weigh(k).wait_recv()
        weigh_on(k).start()

    def hand_to(q, k, level):
        at = pl.ds(0, ONE) if level == 0 else pl.ds(ONE, TWO)
        return to_mp(mixed.at[q, at, :], all_mixed.at[at, cols(mp)], m_sem, k, level)

    def hand(k, level):
        return hand_to(peer(k), k, level)

    def keep_hand(level):
        at = pl.ds(0, ONE) if level == 0 else pl.ds(ONE, TWO)
        return pltpu.make_async_copy(
            mixed.at[mp, at, :], all_mixed.at[at, cols(mp)], own.at[2, level]
        )

    for j in range(3):
        flags(j).wait()

    def fill(keys_ref, values_ref, begin, src, first, flag):
        for c in range(src.shape[1] // 128):
            at = slice(c * 128, (c + 1) * 128)
            here = flag[first + c : first + c + 1, :] > 0
            keys, values = augment(src[0, at, :], src[1, at, :], columns_of(here))
            to = slice(begin + c * 128, begin + (c + 1) * 128)
            for head in range(2):
                keys_ref[head, to, :] = keys[head]
                values_ref[head, to, :] = values[head]

    def masked_of(keys_ref, at):
        spare = keys_ref[0, at, :].astype(F32)
        return jnp.min(jnp.where(lanes(256) == 64, spare, 0.0), -1, keepdims=True) < 0.0

    mine = keep_ref[...]
    fill(keys_one, values_one, 0, one.at[1:], 0, mine)

    @pl.loop(0, MP)
    def _(q):
        pass_one(q).wait()

    fill(keys_one, values_one, 4 * ONE, mate_one, 0, mate_keep[0])

    @pl.loop(1, MP + 1)
    def _(k):
        q = peer(k)
        at = rows(q, ONE)
        mixed[q, 0:ONE, :] = attend_pair(
            one[0, at, :], one[1, at, :], one[2, at, :], masked_of(keys_one, at),
            lambda head: keys_one[head], lambda head: values_one[head],
        )

        @pl.when(k < MP)
        def _():
            hand(k, 0).start()

    keep_hand(0).start()

    fill(keys_two, values_two, 0, two.at[1:], 8, mine)

    @pl.loop(0, MP)
    def _(q):
        for j in range(3):
            pass_two(j, q).wait()

    for j in range(3):
        fill(keys_two, values_two, (j + 1) * 4 * TWO, mate_two.at[j], 8, mate_keep[j])

    @pl.loop(0, 2)
    def _(p):
        at = rows(p, 256)
        both = attend_pair(
            two[0, at, :], two[1, at, :], two[2, at, :], masked_of(keys_two, at),
            lambda head: keys_two[head], lambda head: values_two[head],
        )
        for h in range(2):
            q = p * 2 + h
            k = lax.rem(q + MP - mp, MP)
            mixed[q, ONE:COARSE, :] = both[h * TWO : (h + 1) * TWO]

            @pl.when(k > 0)
            def _():
                hand_to(q, k, 1).start()

    keep_hand(1).start()

    feed(3, 1)

    for k in (1, 3, 2):
        weigh(k).wait_send()
        weigh_on(k).wait()
    for level in range(2):
        keep_hand(level).wait()
        for k in (1, 3, 2):
            hand(k, level).wait()
    for level, begin, size in ((0, 0, 64), (1, ONE, 32)):
        span = slice(begin, begin + size * BALLS)
        total = jnp.zeros((size * BALLS, WIDTH), F32)
        for g in range(MP):
            total = total + dot(
                all_mixed[span, g * LOCAL : (g + 1) * LOCAL],
                lift_ref[g, level * LOCAL : (level + 1) * LOCAL, :],
            )
        total = total.astype(BF16)
        for ball in range(BALLS):
            at = slice(0, 64) if level == 0 else slice(64, 96)
            lifted[ball, at, :] = total[ball * size : (ball + 1) * size]

    def rise(k):
        return to_mp(lifted.at[:, :, cols(peer(k))], lifted_ref.at[mp], l_sem, k, 0)

    for k in (2, 1, 3):
        rise(k).start()
    keep_rise = pltpu.make_async_copy(lifted.at[:, :, cols(mp)], lifted_ref.at[mp], own.at[3, 0])
    keep_rise.start()

    @pl.loop(0, BALLS)
    def _(t):
        keep_give(t).wait()
        for k in (1, 3, 2):
            turn(k, t).wait_send()
            share(k, t).wait_send()
            give(k, t).wait()

    keep_rise.wait()
    for k in (1, 3, 2):
        rise(k).wait()


def middle(slots, got, mask, keep, weights, collective):
    dma = pltpu.SemaphoreType.DMA
    return pl.pallas_call(
        middle_kernel,
        out_shape=[shape((ROWS, LOCAL), BF16), shape((MP, BALLS, 96, LOCAL), BF16)],
        in_specs=[SMEM, VMEM, VMEM, VMEM] + [ANY] * 6,
        out_specs=[ANY, ANY],
        scratch_shapes=[
            pltpu.VMEM((SLOTS, LOCAL), F32),
            pltpu.VMEM((1, CAP, LOCAL), F32),
            pltpu.VMEM((MP * BALLS, BALL, LOCAL), BF16),
            pltpu.VMEM((QUARTER, WIDTH), BF16),
            pltpu.VMEM((QUARTER, WIDTH), F32),
            pltpu.VMEM((MP, BALLS, 64, WIDTH), BF16),
            pltpu.VMEM((QUARTER, WIDTH), BF16),
            pltpu.VMEM((3, 4 * ONE, LOCAL), BF16),
            pltpu.VMEM((3, 4 * TWO, LOCAL), BF16),
            pltpu.VMEM((2, 4 * ONE, LOCAL), BF16),
            pltpu.VMEM((3, 2, 4 * TWO, LOCAL), BF16),
            pltpu.VMEM((3, 12, 128), I32),
            pltpu.VMEM((MP, COARSE, LOCAL), BF16),
            pltpu.VMEM((COARSE, WIDTH), BF16),
            pltpu.VMEM((BALLS, 96, WIDTH), BF16),
            pltpu.VMEM((2, 8 * ONE, LOCAL), BF16),
            pltpu.VMEM((2, 8 * ONE, LOCAL), BF16),
            pltpu.VMEM((2, 16 * TWO, LOCAL), BF16),
            pltpu.VMEM((2, 16 * TWO, LOCAL), BF16),
            pltpu.VMEM((3, WIDTH, WIDTH), BF16),
            pltpu.VMEM((WIDTH, WIDTH), BF16),
            pltpu.VMEM((MP, 2, WIDTH, WIDTH), BF16),
            pltpu.VMEM((MP, WIDTH, WIDTH), BF16),
            pltpu.VMEM((2, 3, WIDTH, LOCAL), BF16),
            pltpu.VMEM((MP, 2 * LOCAL, WIDTH), BF16),
            dma((2, MP, BALLS)),
            dma((2, MP, BALLS)),
            dma((2, 4, MP)),
            dma((2, 3)),
            dma((2, MP, 2)),
            dma((2, MP, BALLS)),
            dma((2, MP, 1)),
            dma((2, MP, 2)),
            dma((4, BALLS)),
            dma((6,)),
        ],
        compiler_params=params(collective),
    )(slots, got, mask, keep, *weights)


def on_device(points, mask, perm, w_qkv, w_out, w_gate_up, w_down, w_coarse, w_coarse_out):
    slot, source, codes = index(perm, mask)
    got, got_code, landed, owned_mask, keep, full_qkv, full_out, full_gate_up, full_down = send_rows(
        source.reshape(SLOTS),
        points,
        codes,
        [
            w_qkv.reshape(3 * WIDTH, LOCAL),
            w_out,
            w_gate_up.reshape(2 * WIDTH, WIDTH),
            w_down,
        ],
        1,
    )
    full_qkv = full_qkv.reshape(3, WIDTH, WIDTH)
    full_out = full_out.reshape(WIDTH, WIDTH)
    full_gate_up = full_gate_up.reshape(MP, 2, WIDTH, WIDTH)
    own_lift = w_coarse_out.reshape(2 * LOCAL, WIDTH)
    turned, lifted = middle(
        landed.reshape(ROWS), got.reshape(SLOTS, LOCAL), owned_mask, keep,
        [full_qkv, full_out, full_gate_up, full_down, w_coarse, own_lift], 2,
    )
    lifted = lifted.reshape(MP * BALLS, 96, LOCAL)
    returned = return_rows(got_code.reshape(SLOTS), turned, lifted, 3)
    return pl.pallas_call(
        finish_kernel,
        out_shape=shape((ROWS, LOCAL), F32),
        in_specs=[SMEM, VMEM],
        out_specs=VMEM,
        scratch_shapes=[pltpu.VMEM((SLOTS, LOCAL), F32)],
        compiler_params=params(),
    )(slot.reshape(ROWS), returned.reshape(SLOTS, LOCAL))


def solution(mesh):
    placed = (
        P("wide", "mp"),
        P("wide"),
        P("wide"),
        P(None, None, "mp"),
        P("mp", None),
        P(None, None, "mp"),
        P("mp", None),
        P(None, None, None, "mp"),
        P(None, "mp", None),
    )
    return jax.shard_map(
        on_device, mesh=mesh, in_specs=placed, out_specs=P("wide", "mp"), check_vma=False
    )
```

```python
import functools

import jax
import jax.numpy as jnp
from jax import lax
from jax.experimental import pallas as pl
from jax.experimental.pallas import tpu as pltpu
from jax.sharding import PartitionSpec as P

BALL = 256
WIDE = 32
MP = 4
ROWS = 4096
CAP = 256
SLOTS = WIDE * CAP
QUARTER = ROWS // MP
WIDTH = 512
LOCAL = WIDTH // MP
HIDDEN = 2048
ONE = QUARTER // 4
TWO = QUARTER // 8
COARSE = ONE + TWO
F32 = jnp.float32
BF16 = jnp.bfloat16
I32 = jnp.int32
MESH = pl.DeviceIdType.MESH
ANY = pl.BlockSpec(memory_space=pl.ANY)
VMEM = pl.BlockSpec(memory_space=pltpu.VMEM)
SMEM = pl.BlockSpec(memory_space=pltpu.SMEM)
LIMIT = 56 * 1024 * 1024


def shape(dims, kind):
    return jax.ShapeDtypeStruct(dims, kind)


def params(collective=None):
    if collective is None:
        return pltpu.CompilerParams(vmem_limit_bytes=LIMIT)
    return pltpu.CompilerParams(
        vmem_limit_bytes=LIMIT, collective_id=collective, has_side_effects=True
    )


def dot(a, b):
    return jnp.dot(a, b, preferred_element_type=F32)


def dot_t(a, b):
    return lax.dot_general(a, b, (((1,), (1,)), ((), ())), preferred_element_type=F32)


def norm(values):
    return values * lax.rsqrt(jnp.mean(values * values, -1, keepdims=True) + 1e-06)


UNROLL = 32
NONE = 2 * ROWS


def index_kernel(perm_ref, mask_ref, slot_ref, source_ref, codes_ref):
    perm = perm_ref[...]
    target = perm >> 12
    code = (perm & (ROWS - 1)) * 2 + mask_ref[...]
    rows = lax.broadcasted_iota(I32, (CAP, 128), 0)
    upper = jnp.where(
        lax.broadcasted_iota(I32, (128, 128), 0) < lax.broadcasted_iota(I32, (128, 128), 1), 1.0, 0.0
    ).astype(BF16)
    which = lax.broadcasted_iota(I32, (WIDE, 128), 0)
    lane = lax.broadcasted_iota(I32, (1, 128), 1).astype(F32)
    carry = jnp.zeros((WIDE, 1), F32)
    found = jnp.zeros((5 * WIDE, CAP), F32)
    for c in range(ROWS // 128):
        row = slice(c, c + 1)
        hot = jnp.where(which == target[row, :], 1.0, 0.0)
        before = dot(hot.astype(BF16), upper) + carry
        rank = jnp.sum(hot * before, 0, keepdims=True).astype(I32)
        slot_ref[row, :] = target[row, :] * CAP + rank
        carry = carry + jnp.sum(hot, 1, keepdims=True)
        placed = jnp.where(rows == rank, 1.0, 0.0).astype(BF16)
        high = (code[row, :] >> 6).astype(F32)
        low = (code[row, :] & 63).astype(F32)
        values = jnp.concatenate([hot * lane, hot * float(c), hot * high, hot * low, hot], 0)
        found = found + dot_t(values.astype(BF16), placed)
    source = (found[:WIDE] + found[WIDE : 2 * WIDE] * 128.0).astype(I32)
    codes = (found[2 * WIDE : 3 * WIDE] * 64.0 + found[3 * WIDE : 4 * WIDE]).astype(I32)
    codes = jnp.where(found[4 * WIDE :] > 0.5, codes, NONE)
    for h in range(2):
        at = slice(h * 128, (h + 1) * 128)
        source_ref[:, h, :] = source[:, at]
        codes_ref[:, h, :] = codes[:, at]


def index(perm, mask):
    return pl.pallas_call(
        index_kernel,
        out_shape=[shape((32, 128), I32), shape((WIDE, 2, 128), I32), shape((WIDE, 2, 128), I32)],
        in_specs=[VMEM] * 2,
        out_specs=[VMEM] * 3,
        compiler_params=params(),
    )(perm.reshape(32, 128), mask.reshape(32, 128))


def invert(codes_ref, slot_ref, mask_ref, keep_ref):
    balls = ROWS // BALL
    rows = lax.broadcasted_iota(I32, (256, 128), 0)
    which = lax.broadcasted_iota(I32, (balls, 128), 0)
    lane = lax.broadcasted_iota(I32, (1, 128), 1).astype(F32)
    found = jnp.zeros((3 * balls, 256), F32)
    for c in range(WIDE):
        for h in range(2):
            code = codes_ref[c, h : h + 1, :]
            landing = code >> 1
            hot = jnp.where(which == (landing >> 8), 1.0, 0.0)
            placed = jnp.where(rows == (landing & 255), 1.0, 0.0).astype(BF16)
            real = (code & 1).astype(F32)
            values = jnp.concatenate([hot * lane, hot * float(2 * c + h), hot * real], 0)
            found = found + dot_t(values.astype(BF16), placed)
    slots = (found[:balls] + found[balls : 2 * balls] * 128.0).astype(I32)
    for h in range(2):
        slot_ref[:, h, :] = slots[:, h * 128 : (h + 1) * 128]
    mask = found[2 * balls :]
    mask_ref[...] = mask.astype(I32)
    mask = mask.astype(BF16)
    for f, first in ((4, 0), (8, 8)):
        side = f // 2
        count = balls // side
        total = jnp.zeros((count, 128), F32)
        for j in range(side):
            r = lax.broadcasted_iota(I32, (count, balls), 0)
            c = lax.broadcasted_iota(I32, (count, balls), 1)
            pick = jnp.where(c == r * side + j, 1.0, 0.0).astype(BF16)
            r = lax.broadcasted_iota(I32, (256, 128), 0)
            c = lax.broadcasted_iota(I32, (256, 128), 1)
            runs = jnp.where(c == r // f + j * (128 // side), 1.0, 0.0).astype(BF16)
            total = total + dot(dot(pick, mask).astype(BF16), runs)
        keep_ref[first : first + count, :] = jnp.where(total > 0.5, 1, 0)


def run_matrix(r, c):
    hot = jnp.logical_or(
        jnp.logical_and(c < 64, r // 4 == c), jnp.logical_and(c >= 64, r // 8 == c - 64)
    )
    return jnp.where(hot, 1.0, 0.0).astype(BF16)


def widen(src, dst, rows):
    @pl.loop(0, rows // 256)
    def _(i):
        at = pl.ds(pl.multiple_of(i * 256, 256), 256)
        dst[at, :] = src[at, :].astype(dst.dtype)


def finish_kernel(slot_ref, got_ref, out_ref, wide):
    widen(got_ref, wide, SLOTS)

    @pl.loop(0, ROWS // UNROLL)
    def _(i):
        base = i * UNROLL
        lines = [wide[pl.ds(slot_ref[base + u], 1), :] for u in range(UNROLL)]
        for u in range(UNROLL):
            out_ref[pl.ds(base + u, 1), :] = lines[u]


def remote(src, dst, send, recv, device):
    return pltpu.make_async_remote_copy(
        src_ref=src, dst_ref=dst, send_sem=send, recv_sem=recv, device_id=device, device_id_type=MESH
    )


def turn_of(me, k):
    return lax.rem(me + lax.rem(k * 7, WIDE), WIDE)


def gather_bucket(line, lookup, wide, staged, packed, peer):
    @pl.loop(0, CAP // UNROLL)
    def _(i):
        begin = i * UNROLL
        lines = [wide[pl.ds(lookup(peer * CAP + begin + u), 1), :] for u in range(UNROLL)]
        for u in range(UNROLL):
            staged[line, pl.ds(begin + u, 1), :] = lines[u]

    packed[peer] = staged[line].astype(BF16)


def send_kernel(
    source_ref, points_ref, codes_ref, qkv_ref, out_ref, lift_ref, down_ref,
    got_ref, got_codes_out, slot_ref, mask_ref, keep_ref, all_qkv, all_out, all_lift, all_down,
    got_codes_ref, wide, staged, packed, send, recv, own, w_send, w_recv, w_own,
):
    me = lax.axis_index("wide")
    mp = lax.axis_index("mp")
    core = lax.rem(me, 2)
    partner = me + 1 - 2 * core
    after, ahead = lax.rem(mp + 1, MP), lax.rem(mp + 2, MP)
    behind = lax.rem(mp + 3, MP)
    barrier = pltpu.get_barrier_semaphore()

    @pl.loop(1, WIDE)
    def _(k):
        pl.semaphore_signal(
            barrier, inc=1, device_id={"wide": lax.rem(me + k, WIDE)}, device_id_type=MESH
        )

    for other in (after, behind):
        pl.semaphore_signal(barrier, inc=1, device_id={"mp": other}, device_id_type=MESH)
    widen(points_ref, wide, ROWS)

    def part(first, count):
        def rows(ref, quarter):
            return pl.ds(pl.multiple_of(first * quarter, 16), count * quarter)

        def cut(j, ref, shard):
            if j == 0:
                return ref.at[rows(ref, 384), pl.ds(pl.multiple_of(shard * 128, 128), 128)]
            quarter = (0, 32, 64, 128)[j]
            return ref.at[shard, rows(ref, quarter), :]

        def own_cut(j, ref):
            quarter = (384, 32, 64, 128)[j]
            return ref.at[rows(ref, quarter), :]

        return cut, own_cut

    half, own_half = part(2 * core, 2)
    first, _ = part(2 * core, 1)
    second, _ = part(2 * core + 1, 1)
    every, own_every = part(0, 4)
    shards = [qkv_ref, out_ref, lift_ref, down_ref]
    full = [all_qkv, all_out, all_lift, all_down]
    count = len(shards)

    def weight(j, kind, cut, src, shard, device):
        return remote(
            src, cut(j, full[j], shard), w_send.at[j, kind], w_recv.at[j, kind], device
        )

    def weight_copies(j):
        ref = full[j]
        mine = own_half(j, shards[j])
        return [
            weight(j, 0, half, mine, mp, {"mp": after}),
            weight(j, 1, half, mine, mp, {"mp": behind}),
            weight(j, 2, first, first(j, ref, behind), behind, {"mp": after}),
            weight(j, 3, second, second(j, ref, after), after, {"mp": behind}),
            weight(j, 4, half, half(j, ref, behind), behind, {"wide": partner}),
            weight(j, 5, half, half(j, ref, after), after, {"wide": partner}),
            weight(j, 6, first, first(j, ref, ahead), ahead, {"wide": partner}),
            weight(j, 7, second, second(j, ref, ahead), ahead, {"wide": partner}),
        ]

    weights = [weight_copies(j) for j in range(count)]

    def rows_copy(k):
        peer = turn_of(me, k)
        return remote(
            packed.at[peer], got_ref.at[me], send.at[k, 0], recv.at[k, 0], {"wide": peer}
        )

    def codes_copy(k):
        peer = turn_of(me, k)
        return remote(
            codes_ref.at[peer], got_codes_ref.at[me], send.at[k, 1], recv.at[k, 1], {"wide": peer}
        )

    pl.semaphore_wait(barrier, WIDE + 1)
    for j in range(count):
        weights[j][0].start()
        weights[j][1].start()

    @pl.loop(1, WIDE)
    def _(k):
        codes_copy(k).start()

    @pl.loop(1, WIDE)
    def _(k):
        gather_bucket(0, lambda s: source_ref[s], wide, staged, packed, turn_of(me, k))
        rows_copy(k).start()

    gather_bucket(0, lambda s: source_ref[s], wide, staged, packed, me)
    mine = [
        pltpu.make_async_copy(packed.at[me], got_ref.at[me], own.at[0]),
        pltpu.make_async_copy(codes_ref.at[me], got_codes_ref.at[me], own.at[1]),
    ]
    for j in range(count):
        mine.append(
            pltpu.make_async_copy(own_every(j, shards[j]), every(j, full[j], mp), w_own.at[j])
        )
    for copy in mine:
        copy.start()

    def forward(j):
        weights[j][0].wait_recv()
        weights[j][2].start()
        weights[j][4].start()
        weights[j][1].wait_recv()
        weights[j][3].start()
        weights[j][5].start()

    def forward_last(j):
        weights[j][2].wait_recv()
        weights[j][6].start()
        weights[j][3].wait_recv()
        weights[j][7].start()

    forward(0)
    forward(1)
    for copy in mine:
        copy.wait()

    @pl.loop(1, WIDE)
    def _(k):
        codes_copy(k).wait()

    invert(got_codes_ref, slot_ref, mask_ref, keep_ref)
    got_codes_out[...] = got_codes_ref[...]
    for j in range(2, count):
        forward(j)
    for j in range(count):
        forward_last(j)

    @pl.loop(1, WIDE)
    def _(k):
        rows_copy(k).wait()

    for j in range(count):
        for kind in range(4):
            weights[j][kind].wait_send()
        for kind in range(4, 8):
            weights[j][kind].wait()


def send_rows(source, points, codes, weights, collective):
    return pl.pallas_call(
        send_kernel,
        out_shape=[
            shape((WIDE, CAP, LOCAL), BF16),
            shape((WIDE, 2, 128), I32),
            shape((16, 2, 128), I32),
            shape((16, 256), I32),
            shape((12, 128), I32),
            shape((3 * WIDTH, WIDTH), BF16),
            shape((MP, LOCAL, WIDTH), BF16),
            shape((MP, 2 * LOCAL, WIDTH), BF16),
            shape((MP, WIDTH, WIDTH), BF16),
        ],
        in_specs=[SMEM, VMEM, ANY] + [VMEM] * 4,
        out_specs=[ANY] + [VMEM] * 4 + [ANY] * 4,
        scratch_shapes=[
            pltpu.VMEM((WIDE, 2, 128), I32),
            pltpu.VMEM((ROWS, LOCAL), F32),
            pltpu.VMEM((1, CAP, LOCAL), F32),
            pltpu.VMEM((WIDE, CAP, LOCAL), BF16),
            pltpu.SemaphoreType.DMA((WIDE, 2)),
            pltpu.SemaphoreType.DMA((WIDE, 2)),
            pltpu.SemaphoreType.DMA((2,)),
            pltpu.SemaphoreType.DMA((4, 8)),
            pltpu.SemaphoreType.DMA((4, 8)),
            pltpu.SemaphoreType.DMA((4,)),
        ],
        compiler_params=params(collective),
    )(source, points, codes, *weights)


def return_kernel(
    code_ref, turned_ref, lifted_ref, got_ref, wide, staged, packed, send, recv, own
):
    me = lax.axis_index("wide")
    barrier = pltpu.get_barrier_semaphore()

    @pl.loop(1, WIDE)
    def _(k):
        pl.semaphore_signal(
            barrier, inc=1, device_id={"wide": lax.rem(me + k, WIDE)}, device_id_type=MESH
        )

    runs = run_matrix(
        lax.broadcasted_iota(I32, (BALL, 96), 0), lax.broadcasted_iota(I32, (BALL, 96), 1)
    )

    @pl.loop(0, ROWS // BALL)
    def _(i):
        at = pl.ds(pl.multiple_of(i * BALL, BALL), BALL)
        wide[at, :] = turned_ref[at, :].astype(F32) + dot(runs, lifted_ref[i])

    wide[ROWS : ROWS + 8, :] = jnp.zeros((8, LOCAL), F32)
    pl.semaphore_wait(barrier, WIDE - 1)

    def rows_copy(k):
        peer = turn_of(me, k)
        return remote(packed.at[peer], got_ref.at[me], send.at[k], recv.at[k], {"wide": peer})

    @pl.loop(1, WIDE)
    def _(k):
        gather_bucket(0, lambda s: code_ref[s] >> 1, wide, staged, packed, turn_of(me, k))
        rows_copy(k).start()

    gather_bucket(0, lambda s: code_ref[s] >> 1, wide, staged, packed, me)
    last = pltpu.make_async_copy(packed.at[me], got_ref.at[me], own)
    last.start()
    last.wait()

    @pl.loop(1, WIDE)
    def _(k):
        rows_copy(k).wait()


def return_rows(codes, turned, lifted, collective):
    return pl.pallas_call(
        return_kernel,
        out_shape=shape((WIDE, CAP, LOCAL), BF16),
        in_specs=[SMEM, VMEM, VMEM],
        out_specs=ANY,
        scratch_shapes=[
            pltpu.VMEM((ROWS + 8, LOCAL), F32),
            pltpu.VMEM((1, CAP, LOCAL), F32),
            pltpu.VMEM((WIDE, CAP, LOCAL), BF16),
            pltpu.SemaphoreType.DMA((WIDE,)),
            pltpu.SemaphoreType.DMA((WIDE,)),
            pltpu.SemaphoreType.DMA,
        ],
        compiler_params=params(collective),
    )(codes, turned, lifted)


SCALE = 0.125 * 1.4426950408889634


def lanes(count):
    return lax.broadcasted_iota(I32, (count, 128), 1)


def columns_of(flags):
    eye = lax.broadcasted_iota(I32, (128, 128), 0) == lax.broadcasted_iota(I32, (128, 128), 1)
    row = jnp.broadcast_to(jnp.where(flags, 1.0, 0.0), (128, 128)).astype(BF16)
    return dot_t(jnp.where(eye, 1.0, 0.0).astype(BF16), row)


def augment(keys, values, columns):
    lane = lanes(keys.shape[0])
    low = lane < 64
    bias = jnp.where(columns > 0.5, 0.0, -1e30)
    keys = keys.astype(F32)
    values = values.astype(F32)
    return (
        (
            jnp.where(low, keys, jnp.where(lane == 64, bias, 0.0)).astype(BF16),
            jnp.where(low, jnp.where(lane == 0, bias, 0.0), keys).astype(BF16),
        ),
        (jnp.where(low, values, 1.0).astype(BF16), jnp.where(low, 1.0, values).astype(BF16)),
    )


def attend_pair(queries, own_keys, own_values, masked, keys, values):
    count = queries.shape[0]
    lane = lanes(count)
    low = lane < 64
    queries = queries.astype(F32)
    own_keys = own_keys.astype(F32)
    own_values = own_values.astype(F32)
    out = []
    for head in range(2):
        mine = low if head == 0 else jnp.logical_not(low)
        spare = jnp.where(lane == (64 if head == 0 else 0), 1.0, 0.0)
        q = jnp.where(mine, queries, spare).astype(BF16)
        scores = dot_t(q, keys(head))
        alone = jnp.sum(jnp.where(mine, queries * own_keys, 0.0), -1, keepdims=True)
        top = jnp.maximum(jnp.max(scores, -1, keepdims=True), alone)
        weights = jnp.exp2(scores - top).astype(BF16)
        own = jnp.where(masked, jnp.exp2(alone - top), 0.0)
        total = dot(weights, values(head))
        out.append(total + own * jnp.where(mine, own_values, 1.0))
    sums = pltpu.roll(jnp.where(low, out[1], out[0]), 64, 1)
    return (jnp.where(low, out[0], out[1]) / sums).astype(BF16)


def attend_ball(queries, keys, values, allowed):
    low = lanes(BALL) < 64
    out = []
    for head in range(2):
        mine = low if head == 0 else jnp.logical_not(low)
        q = jnp.where(mine, queries, jnp.zeros_like(queries))
        scores = jnp.where(allowed, dot_t(q, keys), -1e30)
        weights = jnp.exp2(scores - jnp.max(scores, -1, keepdims=True))
        total = jnp.sum(weights, -1, keepdims=True)
        out.append(dot(weights.astype(BF16), values) / total)
    return jnp.where(low, out[0], out[1]).astype(BF16)


def fine_ball(x, real, qkv_ref, out_ref):
    x = x.astype(F32)
    normed = norm(x).astype(BF16)
    q = (dot(normed, qkv_ref[0]) * SCALE).astype(BF16)
    k = dot(normed, qkv_ref[1]).astype(BF16)
    v = dot(normed, qkv_ref[2]).astype(BF16)
    rows = lax.broadcasted_iota(I32, (BALL, BALL), 0)
    cols = lax.broadcasted_iota(I32, (BALL, BALL), 1)
    allowed = jnp.logical_or(real, rows == cols)
    mixed = []
    for g in range(MP):
        at = slice(g * 128, (g + 1) * 128)
        mixed.append(attend_ball(q[:, at], k[:, at], v[:, at], allowed))
    state = x + dot(jnp.concatenate(mixed, 1), out_ref[...])
    high = state.astype(BF16)
    rest = (state - high.astype(F32)).astype(BF16)
    runs, counted = pooling(real, 4)
    pooled = (dot(runs, high) + dot(runs, rest)) / jnp.maximum(counted, 1.0)
    return state, pooled.astype(BF16)


def pooling(real, factor):
    count_rows = BALL // factor
    r = lax.broadcasted_iota(I32, (count_rows, BALL), 0)
    c = lax.broadcasted_iota(I32, (count_rows, BALL), 1)
    hot = jnp.where(jnp.logical_and(r == c // factor, real), 1.0, 0.0)
    return hot.astype(BF16), jnp.sum(hot, 1, keepdims=True)


BALLS = QUARTER // BALL


def forward_tile(state, mp, gate_up_ref, down_ref):
    normed = norm(state).astype(BF16)
    total = state
    for c in range(MP):
        half = dot(normed, gate_up_ref[c, :WIDTH, :]) * 0.5
        up = dot(normed, gate_up_ref[c, WIDTH:, :])
        activated = ((half + half * jnp.tanh(half)) * up).astype(BF16)
        total = total + dot(activated, down_ref[lax.rem(mp + c, MP)])
    return total


def relatives(me):
    low = lax.rem(me, 2)
    high = lax.rem(me // 2, 2)
    first = me + 1 - 2 * low
    second = me + 2 - 4 * high
    third = first + 2 - 4 * high
    return (first, second, third)


def middle_kernel(
    slot_ref, got_ref, mask_ref, keep_ref, qkv_hbm, out_hbm, gate_up_hbm, down_hbm, coarse_hbm,
    lift_hbm, turned_ref, lifted_ref,
    wide, staged, packed, x, state, pooled, tiles, one, two, mate_one, mate_two, mate_keep,
    mixed, all_mixed, lifted, keys_one, values_one, keys_two, values_two, qkv_ref, out_ref, gate_up_ref, down_ref, w_ref, lift_ref,
    x_sem, p_sem, e_sem, k_sem, m_sem, t_sem, l_sem, g_sem, b_sem, f_sem, own, loads,
):
    me = lax.axis_index("wide")
    mp = lax.axis_index("mp")
    others = relatives(me)
    barrier = pltpu.get_barrier_semaphore()
    for k in range(1, MP):
        pl.semaphore_signal(
            barrier, inc=1, device_id={"mp": lax.rem(mp + k, MP)}, device_id_type=MESH
        )
    for other in (others[0], others[2]):
        pl.semaphore_signal(barrier, inc=1, device_id={"wide": other}, device_id_type=MESH)

    def chip(i):
        return 2 * lax.rem(i * 7, WIDE // 2)

    @pl.loop(1, WIDE // 2)
    def _(i):
        pl.semaphore_signal(
            barrier, inc=1, device_id={"wide": lax.rem(me + chip(i), WIDE)}, device_id_type=MESH
        )

    load = [
        pltpu.make_async_copy(src, dst, loads.at[j])
        for j, (src, dst) in enumerate([
            (qkv_hbm, qkv_ref),
            (out_hbm, out_ref),
            (gate_up_hbm, gate_up_ref.at[0]),
            (down_hbm, down_ref),
            (coarse_hbm, w_ref),
            (lift_hbm, lift_ref),
        ])
    ]
    for copy in load:
        copy.start()
    widen(got_ref, wide, SLOTS)
    pl.semaphore_wait(barrier, MP - 1 + 2 + WIDE // 2 - 1)

    def rows(t, size):
        return pl.ds(pl.multiple_of(t * size, size), size)

    def cols(g):
        return pl.ds(pl.multiple_of(g * LOCAL, LOCAL), LOCAL)

    def peer(k):
        return lax.rem(mp + k, MP)

    def to_mp(src, dst, sem, k, t):
        return remote(src, dst, sem.at[0, k, t], sem.at[1, k, t], {"mp": peer(k)})

    def piece(shards, owner):
        return gate_up_ref.at[shards, pl.ds(pl.multiple_of(owner * 32, 32), 32), :]

    def fetch(k):
        src = gate_up_hbm.at[pl.ds(pl.multiple_of(me * 32, 32), 32), :]
        return to_mp(src, piece(MP - k, me), g_sem, k, 0)

    def broadcast(i):
        part = piece(pl.ds(1, 3), me)
        to = {"wide": lax.rem(me + chip(i), WIDE)}
        return remote(part, part, b_sem.at[0, i], b_sem.at[1, i], to)

    def pass_on(i):
        part = piece(pl.ds(1, 3), lax.rem(me + WIDE - chip(i), WIDE))
        return remote(part, part, f_sem.at[0, i], f_sem.at[1, i], {"wide": others[0]})

    for k in (2, 1, 3):
        fetch(k).start()

    def turn(k, t):
        return to_mp(packed.at[peer(k) * BALLS + t], x.at[rows(t, BALL), cols(mp)], x_sem, k, t)

    def keep_turn(t):
        return pltpu.make_async_copy(
            packed.at[mp * BALLS + t], x.at[rows(t, BALL), cols(mp)], own.at[0, t]
        )

    @pl.loop(0, BALLS)
    def _(t):
        for k in (2, 1, 3):
            gather_bucket(0, lambda s: slot_ref[s], wide, staged, packed, peer(k) * BALLS + t)
            turn(k, t).start()
        gather_bucket(0, lambda s: slot_ref[s], wide, staged, packed, mp * BALLS + t)
        keep_turn(t).start()

    def flags(j):
        return remote(
            keep_ref, mate_keep.at[j], k_sem.at[0, j], k_sem.at[1, j], {"wide": others[j]}
        )

    for j in range(3):
        flags(j).start()
    for k in (1, 3, 2):
        fetch(k).wait_recv()

    @pl.loop(1, WIDE // 2)
    def _(i):
        broadcast(i).start()

    pass_on(0).start()
    load[0].wait()
    load[1].wait()

    def share(k, t):
        return to_mp(pooled.at[mp, t], pooled.at[mp, t], p_sem, k, t)

    @pl.loop(0, BALLS)
    def _(t):
        for k in (1, 3, 2):
            turn(k, t).wait_recv()
        keep_turn(t).wait()
        real = mask_ref[pl.ds(mp * BALLS + t, 1), :] > 0
        out, means = fine_ball(x[rows(t, BALL), :], real, qkv_ref, out_ref)
        state[rows(t, BALL), :] = out
        pooled[mp, t] = means
        for k in (2, 1, 3):
            share(k, t).start()

    load[2].wait()
    load[3].wait()

    def give(k, t):
        return to_mp(
            tiles.at[rows(t, BALL), cols(peer(k))],
            turned_ref.at[rows(mp * BALLS + t, BALL), :],
            t_sem,
            k,
            t,
        )

    def keep_give(t):
        return pltpu.make_async_copy(
            tiles.at[rows(t, BALL), cols(mp)],
            turned_ref.at[rows(mp * BALLS + t, BALL), :],
            own.at[1, t],
        )

    def feed(t, count):
        at = pl.ds(t * BALL, count * BALL)
        tiles[at, :] = forward_tile(state[at, :], mp, gate_up_ref, down_ref).astype(BF16)
        for u in range(t, t + count):
            for k in (2, 1, 3):
                give(k, u).start()
            keep_give(u).start()

    @pl.loop(1, WIDE // 2)
    def _(i):
        broadcast(i).wait_recv()
        pass_on(i).start()

    def pass_one(q):
        return remote(
            one.at[pl.ds(1, 2), rows(q, ONE), :],
            mate_one.at[:, rows(q, ONE), :],
            e_sem.at[0, 3, q],
            e_sem.at[1, 3, q],
            {"wide": others[0]},
        )

    def pass_two(j, q):
        return remote(
            two.at[pl.ds(1, 2), rows(q, TWO), :],
            mate_two.at[j, :, rows(q, TWO), :],
            e_sem.at[0, j, q],
            e_sem.at[1, j, q],
            {"wide": others[j]},
        )

    pair = lax.broadcasted_iota(I32, (32, 64), 0) == lax.broadcasted_iota(I32, (32, 64), 1) // 2
    pair = jnp.where(pair, 1.0, 0.0).astype(BF16)
    load[4].wait()

    def project(q):
        firsts, seconds = [], []
        for ball in range(BALLS):
            real = mask_ref[pl.ds(q * BALLS + ball, 1), :] > 0
            means = pooled[q, ball].astype(F32)
            firsts.append(norm(means).astype(BF16))
            sums = means * pooling(real, 4)[1]
            high = sums.astype(BF16)
            rest = (sums - high.astype(F32)).astype(BF16)
            counted = jnp.maximum(pooling(real, 8)[1], 1.0)
            seconds.append(norm((dot(pair, high) + dot(pair, rest)) / counted).astype(BF16))
        firsts = jnp.concatenate(firsts, 0)
        seconds = jnp.concatenate(seconds, 0)
        for t in (1, 2):
            two[t, rows(q, TWO), :] = dot(seconds, w_ref[1, t]).astype(BF16)
            one[t, rows(q, ONE), :] = dot(firsts, w_ref[0, t]).astype(BF16)
        for j in (1, 2, 0):
            pass_two(j, q).start()
        pass_one(q).start()
        two[0, rows(q, TWO), :] = (dot(seconds, w_ref[1, 0]) * SCALE).astype(BF16)
        one[0, rows(q, ONE), :] = (dot(firsts, w_ref[0, 0]) * SCALE).astype(BF16)

    project(mp)
    for k in (1, 3, 2):

        @pl.loop(0, BALLS)
        def _(t):
            share(MP - k, t).wait_recv()

        project(peer(k))

    @pl.loop(0, WIDE // 2)
    def _(i):
        pass_on(i).wait_recv()

    feed(0, 2)
    feed(2, 1)

    def hand_to(q, k, level):
        at = pl.ds(0, ONE) if level == 0 else pl.ds(ONE, TWO)
        return to_mp(mixed.at[q, at, :], all_mixed.at[at, cols(mp)], m_sem, k, level)

    def hand(k, level):
        return hand_to(peer(k), k, level)

    def keep_hand(level):
        at = pl.ds(0, ONE) if level == 0 else pl.ds(ONE, TWO)
        return pltpu.make_async_copy(
            mixed.at[mp, at, :], all_mixed.at[at, cols(mp)], own.at[2, level]
        )

    for j in range(3):
        flags(j).wait()

    def fill(keys_ref, values_ref, begin, src, first, flag):
        for c in range(src.shape[1] // 128):
            at = slice(c * 128, (c + 1) * 128)
            here = flag[first + c : first + c + 1, :] > 0
            keys, values = augment(src[0, at, :], src[1, at, :], columns_of(here))
            to = slice(begin + c * 128, begin + (c + 1) * 128)
            for head in range(2):
                keys_ref[head, to, :] = keys[head]
                values_ref[head, to, :] = values[head]

    def masked_of(keys_ref, at):
        spare = keys_ref[0, at, :].astype(F32)
        return jnp.min(jnp.where(lanes(256) == 64, spare, 0.0), -1, keepdims=True) < 0.0

    mine = keep_ref[...]
    fill(keys_one, values_one, 0, one.at[1:], 0, mine)

    @pl.loop(0, MP)
    def _(q):
        pass_one(q).wait()

    fill(keys_one, values_one, 4 * ONE, mate_one, 0, mate_keep[0])

    @pl.loop(1, MP + 1)
    def _(k):
        q = peer(k)
        at = rows(q, ONE)
        mixed[q, 0:ONE, :] = attend_pair(
            one[0, at, :], one[1, at, :], one[2, at, :], masked_of(keys_one, at),
            lambda head: keys_one[head], lambda head: values_one[head],
        )

        @pl.when(k < MP)
        def _():
            hand(k, 0).start()

    keep_hand(0).start()

    fill(keys_two, values_two, 0, two.at[1:], 8, mine)

    @pl.loop(0, MP)
    def _(q):
        for j in range(3):
            pass_two(j, q).wait()

    for j in range(3):
        fill(keys_two, values_two, (j + 1) * 4 * TWO, mate_two.at[j], 8, mate_keep[j])

    @pl.loop(0, 2)
    def _(p):
        at = rows(p, 256)
        both = attend_pair(
            two[0, at, :], two[1, at, :], two[2, at, :], masked_of(keys_two, at),
            lambda head: keys_two[head], lambda head: values_two[head],
        )
        for h in range(2):
            q = p * 2 + h
            k = lax.rem(q + MP - mp, MP)
            mixed[q, ONE:COARSE, :] = both[h * TWO : (h + 1) * TWO]

            @pl.when(k > 0)
            def _():
                hand_to(q, k, 1).start()

    keep_hand(1).start()

    feed(3, 1)

    load[5].wait()
    for level in range(2):
        keep_hand(level).wait()
        for k in (1, 3, 2):
            hand(k, level).wait()
    for level, begin, size in ((0, 0, 64), (1, ONE, 32)):
        span = slice(begin, begin + size * BALLS)
        total = jnp.zeros((size * BALLS, WIDTH), F32)
        for g in range(MP):
            total = total + dot(
                all_mixed[span, g * LOCAL : (g + 1) * LOCAL],
                lift_ref[g, level * LOCAL : (level + 1) * LOCAL, :],
            )
        total = total.astype(BF16)
        for ball in range(BALLS):
            at = slice(0, 64) if level == 0 else slice(64, 96)
            lifted[ball, at, :] = total[ball * size : (ball + 1) * size]

    def rise(k):
        return to_mp(lifted.at[:, :, cols(peer(k))], lifted_ref.at[mp], l_sem, k, 0)

    for k in (2, 1, 3):
        rise(k).start()
    keep_rise = pltpu.make_async_copy(lifted.at[:, :, cols(mp)], lifted_ref.at[mp], own.at[3, 0])
    keep_rise.start()

    @pl.loop(0, BALLS)
    def _(t):
        keep_give(t).wait()
        for k in (1, 3, 2):
            turn(k, t).wait_send()
            share(k, t).wait_send()
            give(k, t).wait()

    @pl.loop(1, WIDE // 2)
    def _(i):
        broadcast(i).wait_send()

    @pl.loop(0, WIDE // 2)
    def _(i):
        pass_on(i).wait_send()

    for k in (1, 3, 2):
        fetch(k).wait_send()
    keep_rise.wait()
    for k in (1, 3, 2):
        rise(k).wait()


def middle(slots, got, mask, keep, weights, collective):
    dma = pltpu.SemaphoreType.DMA
    return pl.pallas_call(
        middle_kernel,
        out_shape=[shape((ROWS, LOCAL), BF16), shape((MP, BALLS, 96, LOCAL), BF16)],
        in_specs=[SMEM, VMEM, VMEM, VMEM] + [ANY] * 6,
        out_specs=[ANY, ANY],
        scratch_shapes=[
            pltpu.VMEM((SLOTS, LOCAL), F32),
            pltpu.VMEM((1, CAP, LOCAL), F32),
            pltpu.VMEM((MP * BALLS, BALL, LOCAL), BF16),
            pltpu.VMEM((QUARTER, WIDTH), BF16),
            pltpu.VMEM((QUARTER, WIDTH), F32),
            pltpu.VMEM((MP, BALLS, 64, WIDTH), BF16),
            pltpu.VMEM((QUARTER, WIDTH), BF16),
            pltpu.VMEM((3, 4 * ONE, LOCAL), BF16),
            pltpu.VMEM((3, 4 * TWO, LOCAL), BF16),
            pltpu.VMEM((2, 4 * ONE, LOCAL), BF16),
            pltpu.VMEM((3, 2, 4 * TWO, LOCAL), BF16),
            pltpu.VMEM((3, 12, 128), I32),
            pltpu.VMEM((MP, COARSE, LOCAL), BF16),
            pltpu.VMEM((COARSE, WIDTH), BF16),
            pltpu.VMEM((BALLS, 96, WIDTH), BF16),
            pltpu.VMEM((2, 8 * ONE, LOCAL), BF16),
            pltpu.VMEM((2, 8 * ONE, LOCAL), BF16),
            pltpu.VMEM((2, 16 * TWO, LOCAL), BF16),
            pltpu.VMEM((2, 16 * TWO, LOCAL), BF16),
            pltpu.VMEM((3, WIDTH, WIDTH), BF16),
            pltpu.VMEM((WIDTH, WIDTH), BF16),
            pltpu.VMEM((MP, 2 * WIDTH, WIDTH), BF16),
            pltpu.VMEM((MP, WIDTH, WIDTH), BF16),
            pltpu.VMEM((2, 3, WIDTH, LOCAL), BF16),
            pltpu.VMEM((MP, 2 * LOCAL, WIDTH), BF16),
            dma((2, MP, BALLS)),
            dma((2, MP, BALLS)),
            dma((2, 4, MP)),
            dma((2, 3)),
            dma((2, MP, 2)),
            dma((2, MP, BALLS)),
            dma((2, MP, 1)),
            dma((2, MP, 1)),
            dma((2, WIDE // 2)),
            dma((2, WIDE // 2)),
            dma((4, BALLS)),
            dma((6,)),
        ],
        compiler_params=params(collective),
    )(slots, got, mask, keep, *weights)


def on_device(points, mask, perm, w_qkv, w_out, w_gate_up, w_down, w_coarse, w_coarse_out):
    slot, source, codes = index(perm, mask)
    got, got_code, landed, owned_mask, keep, full_qkv, full_out, full_lift, full_down = send_rows(
        source.reshape(SLOTS),
        points,
        codes,
        [
            w_qkv.reshape(3 * WIDTH, LOCAL),
            w_out,
            w_coarse_out.reshape(2 * LOCAL, WIDTH),
            w_down,
        ],
        1,
    )
    full_qkv = full_qkv.reshape(3, WIDTH, WIDTH)
    full_out = full_out.reshape(WIDTH, WIDTH)
    own_gate_up = w_gate_up.reshape(2 * WIDTH, WIDTH)
    turned, lifted = middle(
        landed.reshape(ROWS), got.reshape(SLOTS, LOCAL), owned_mask, keep,
        [full_qkv, full_out, own_gate_up, full_down, w_coarse, full_lift], 2,
    )
    lifted = lifted.reshape(MP * BALLS, 96, LOCAL)
    returned = return_rows(got_code.reshape(SLOTS), turned, lifted, 3)
    return pl.pallas_call(
        finish_kernel,
        out_shape=shape((ROWS, LOCAL), F32),
        in_specs=[SMEM, VMEM],
        out_specs=VMEM,
        scratch_shapes=[pltpu.VMEM((SLOTS, LOCAL), F32)],
        compiler_params=params(),
    )(slot.reshape(ROWS), returned.reshape(SLOTS, LOCAL))


def solution(mesh):
    placed = (
        P("wide", "mp"),
        P("wide"),
        P("wide"),
        P(None, None, "mp"),
        P("mp", None),
        P(None, None, "mp"),
        P("mp", None),
        P(None, None, None, "mp"),
        P(None, "mp", None),
    )
    return jax.shard_map(
        on_device, mesh=mesh, in_specs=placed, out_specs=P("wide", "mp"), check_vma=False
    )
```

```python
import functools

import jax
import jax.numpy as jnp
from jax import lax
from jax.experimental import pallas as pl
from jax.experimental.pallas import tpu as pltpu
from jax.sharding import PartitionSpec as P

BALL = 256
WIDE = 32
MP = 4
ROWS = 4096
CAP = 256
SLOTS = WIDE * CAP
QUARTER = ROWS // MP
WIDTH = 512
LOCAL = WIDTH // MP
HIDDEN = 2048
ONE = QUARTER // 4
TWO = QUARTER // 8
COARSE = ONE + TWO
F32 = jnp.float32
BF16 = jnp.bfloat16
I32 = jnp.int32
MESH = pl.DeviceIdType.MESH
ANY = pl.BlockSpec(memory_space=pl.ANY)
VMEM = pl.BlockSpec(memory_space=pltpu.VMEM)
SMEM = pl.BlockSpec(memory_space=pltpu.SMEM)
LIMIT = 56 * 1024 * 1024


def shape(dims, kind):
    return jax.ShapeDtypeStruct(dims, kind)


def params(collective=None):
    if collective is None:
        return pltpu.CompilerParams(vmem_limit_bytes=LIMIT)
    return pltpu.CompilerParams(
        vmem_limit_bytes=LIMIT, collective_id=collective, has_side_effects=True
    )


def dot(a, b):
    return jnp.dot(a, b, preferred_element_type=F32)


def dot_t(a, b):
    return lax.dot_general(a, b, (((1,), (1,)), ((), ())), preferred_element_type=F32)


def norm(values):
    return values * lax.rsqrt(jnp.mean(values * values, -1, keepdims=True) + 1e-06)


UNROLL = 32
NONE = 2 * ROWS


def index_kernel(perm_ref, mask_ref, slot_ref, source_ref, codes_ref):
    perm = perm_ref[...]
    target = perm >> 12
    code = (perm & (ROWS - 1)) * 2 + mask_ref[...]
    rows = lax.broadcasted_iota(I32, (CAP, 128), 0)
    upper = jnp.where(
        lax.broadcasted_iota(I32, (128, 128), 0) < lax.broadcasted_iota(I32, (128, 128), 1), 1.0, 0.0
    ).astype(BF16)
    which = lax.broadcasted_iota(I32, (WIDE, 128), 0)
    lane = lax.broadcasted_iota(I32, (1, 128), 1).astype(F32)
    carry = jnp.zeros((WIDE, 1), F32)
    found = jnp.zeros((5 * WIDE, CAP), F32)
    for c in range(ROWS // 128):
        row = slice(c, c + 1)
        hot = jnp.where(which == target[row, :], 1.0, 0.0)
        before = dot(hot.astype(BF16), upper) + carry
        rank = jnp.sum(hot * before, 0, keepdims=True).astype(I32)
        slot_ref[row, :] = target[row, :] * CAP + rank
        carry = carry + jnp.sum(hot, 1, keepdims=True)
        placed = jnp.where(rows == rank, 1.0, 0.0).astype(BF16)
        high = (code[row, :] >> 6).astype(F32)
        low = (code[row, :] & 63).astype(F32)
        values = jnp.concatenate([hot * lane, hot * float(c), hot * high, hot * low, hot], 0)
        found = found + dot_t(values.astype(BF16), placed)
    source = (found[:WIDE] + found[WIDE : 2 * WIDE] * 128.0).astype(I32)
    codes = (found[2 * WIDE : 3 * WIDE] * 64.0 + found[3 * WIDE : 4 * WIDE]).astype(I32)
    codes = jnp.where(found[4 * WIDE :] > 0.5, codes, NONE)
    for h in range(2):
        at = slice(h * 128, (h + 1) * 128)
        source_ref[:, h, :] = source[:, at]
        codes_ref[:, h, :] = codes[:, at]


def index(perm, mask):
    return pl.pallas_call(
        index_kernel,
        out_shape=[shape((32, 128), I32), shape((WIDE, 2, 128), I32), shape((WIDE, 2, 128), I32)],
        in_specs=[VMEM] * 2,
        out_specs=[VMEM] * 3,
        compiler_params=params(),
    )(perm.reshape(32, 128), mask.reshape(32, 128))


def invert(codes_ref, slot_ref, mask_ref, keep_ref):
    balls = ROWS // BALL
    rows = lax.broadcasted_iota(I32, (256, 128), 0)
    which = lax.broadcasted_iota(I32, (balls, 128), 0)
    lane = lax.broadcasted_iota(I32, (1, 128), 1).astype(F32)
    found = jnp.zeros((3 * balls, 256), F32)
    for c in range(WIDE):
        for h in range(2):
            code = codes_ref[c, h : h + 1, :]
            landing = code >> 1
            hot = jnp.where(which == (landing >> 8), 1.0, 0.0)
            placed = jnp.where(rows == (landing & 255), 1.0, 0.0).astype(BF16)
            real = (code & 1).astype(F32)
            values = jnp.concatenate([hot * lane, hot * float(2 * c + h), hot * real], 0)
            found = found + dot_t(values.astype(BF16), placed)
    slots = (found[:balls] + found[balls : 2 * balls] * 128.0).astype(I32)
    for h in range(2):
        slot_ref[:, h, :] = slots[:, h * 128 : (h + 1) * 128]
    mask = found[2 * balls :]
    mask_ref[...] = mask.astype(I32)
    mask = mask.astype(BF16)
    for f, first in ((4, 0), (8, 8)):
        side = f // 2
        count = balls // side
        total = jnp.zeros((count, 128), F32)
        for j in range(side):
            r = lax.broadcasted_iota(I32, (count, balls), 0)
            c = lax.broadcasted_iota(I32, (count, balls), 1)
            pick = jnp.where(c == r * side + j, 1.0, 0.0).astype(BF16)
            r = lax.broadcasted_iota(I32, (256, 128), 0)
            c = lax.broadcasted_iota(I32, (256, 128), 1)
            runs = jnp.where(c == r // f + j * (128 // side), 1.0, 0.0).astype(BF16)
            total = total + dot(dot(pick, mask).astype(BF16), runs)
        keep_ref[first : first + count, :] = jnp.where(total > 0.5, 1, 0)


def run_matrix(r, c):
    hot = jnp.logical_or(
        jnp.logical_and(c < 64, r // 4 == c), jnp.logical_and(c >= 64, r // 8 == c - 64)
    )
    return jnp.where(hot, 1.0, 0.0).astype(BF16)


def widen(src, dst, rows):
    @pl.loop(0, rows // 256)
    def _(i):
        at = pl.ds(pl.multiple_of(i * 256, 256), 256)
        dst[at, :] = src[at, :].astype(dst.dtype)


def finish_kernel(slot_ref, got_ref, out_ref, narrow, wide, done, in_sem, out_sem):
    def chunk(ref, i, size):
        return ref.at[pl.ds(pl.multiple_of(i * size, size), size), :]

    def load(i):
        return pltpu.make_async_copy(chunk(got_ref, i, 1024), chunk(narrow, i, 1024), in_sem.at[i])

    def store(i):
        return pltpu.make_async_copy(chunk(done, i, 512), chunk(out_ref, i, 512), out_sem.at[i])

    for i in range(SLOTS // 1024):
        load(i).start()
    for i in range(SLOTS // 1024):
        load(i).wait()
        widen(chunk(narrow, i, 1024), chunk(wide, i, 1024), 1024)

    @pl.loop(0, ROWS // 512)
    def _(i):
        @pl.loop(0, 512 // UNROLL)
        def _(j):
            base = i * 512 + j * UNROLL
            lines = [wide[pl.ds(slot_ref[base + u], 1), :] for u in range(UNROLL)]
            for u in range(UNROLL):
                done[pl.ds(base + u, 1), :] = lines[u]

        store(i).start()

    @pl.loop(0, ROWS // 512)
    def _(i):
        store(i).wait()


def remote(src, dst, send, recv, device):
    return pltpu.make_async_remote_copy(
        src_ref=src, dst_ref=dst, send_sem=send, recv_sem=recv, device_id=device, device_id_type=MESH
    )


def turn_of(me, k):
    return lax.rem(me + lax.rem(k * 7, WIDE), WIDE)


def gather_bucket(line, lookup, wide, staged, packed, peer):
    @pl.loop(0, CAP // UNROLL)
    def _(i):
        begin = i * UNROLL
        lines = [wide[pl.ds(lookup(peer * CAP + begin + u), 1), :] for u in range(UNROLL)]
        for u in range(UNROLL):
            staged[line, pl.ds(begin + u, 1), :] = lines[u]

    packed[peer] = staged[line].astype(BF16)


def send_kernel(
    source_ref, points_ref, codes_ref, qkv_ref, out_ref, lift_ref, down_ref,
    got_ref, got_codes_out, slot_ref, mask_ref, keep_ref, all_qkv, all_out, all_lift, all_down,
    got_codes_ref, wide, staged, packed, send, recv, own, w_send, w_recv, w_own,
):
    me = lax.axis_index("wide")
    mp = lax.axis_index("mp")
    core = lax.rem(me, 2)
    partner = me + 1 - 2 * core
    after, ahead = lax.rem(mp + 1, MP), lax.rem(mp + 2, MP)
    behind = lax.rem(mp + 3, MP)
    barrier = pltpu.get_barrier_semaphore()

    @pl.loop(1, WIDE)
    def _(k):
        pl.semaphore_signal(
            barrier, inc=1, device_id={"wide": lax.rem(me + k, WIDE)}, device_id_type=MESH
        )

    for other in (after, behind):
        pl.semaphore_signal(barrier, inc=1, device_id={"mp": other}, device_id_type=MESH)
    widen(points_ref, wide, ROWS)

    def part(first, count):
        def rows(ref, quarter):
            return pl.ds(pl.multiple_of(first * quarter, 16), count * quarter)

        def cut(j, ref, shard):
            if j == 0:
                return ref.at[rows(ref, 384), pl.ds(pl.multiple_of(shard * 128, 128), 128)]
            quarter = (0, 32, 64, 128)[j]
            return ref.at[shard, rows(ref, quarter), :]

        def own_cut(j, ref):
            quarter = (384, 32, 64, 128)[j]
            return ref.at[rows(ref, quarter), :]

        return cut, own_cut

    half, own_half = part(2 * core, 2)
    first, _ = part(2 * core, 1)
    second, _ = part(2 * core + 1, 1)
    every, own_every = part(0, 4)
    shards = [qkv_ref, out_ref, lift_ref, down_ref]
    full = [all_qkv, all_out, all_lift, all_down]
    count = len(shards)

    def weight(j, kind, cut, src, shard, device):
        return remote(
            src, cut(j, full[j], shard), w_send.at[j, kind], w_recv.at[j, kind], device
        )

    def weight_copies(j):
        ref = full[j]
        mine = own_half(j, shards[j])
        return [
            weight(j, 0, half, mine, mp, {"mp": after}),
            weight(j, 1, half, mine, mp, {"mp": behind}),
            weight(j, 2, first, first(j, ref, behind), behind, {"mp": after}),
            weight(j, 3, second, second(j, ref, after), after, {"mp": behind}),
            weight(j, 4, half, half(j, ref, behind), behind, {"wide": partner}),
            weight(j, 5, half, half(j, ref, after), after, {"wide": partner}),
            weight(j, 6, first, first(j, ref, ahead), ahead, {"wide": partner}),
            weight(j, 7, second, second(j, ref, ahead), ahead, {"wide": partner}),
        ]

    weights = [weight_copies(j) for j in range(count)]

    def rows_copy(k):
        peer = turn_of(me, k)
        return remote(
            packed.at[peer], got_ref.at[me], send.at[k, 0], recv.at[k, 0], {"wide": peer}
        )

    def codes_copy(k):
        peer = turn_of(me, k)
        return remote(
            codes_ref.at[peer], got_codes_ref.at[me], send.at[k, 1], recv.at[k, 1], {"wide": peer}
        )

    pl.semaphore_wait(barrier, WIDE + 1)
    for j in range(count):
        weights[j][0].start()
        weights[j][1].start()

    @pl.loop(1, WIDE)
    def _(k):
        codes_copy(k).start()

    @pl.loop(1, WIDE)
    def _(k):
        gather_bucket(0, lambda s: source_ref[s], wide, staged, packed, turn_of(me, k))
        rows_copy(k).start()

    gather_bucket(0, lambda s: source_ref[s], wide, staged, packed, me)
    mine = [
        pltpu.make_async_copy(packed.at[me], got_ref.at[me], own.at[0]),
        pltpu.make_async_copy(codes_ref.at[me], got_codes_ref.at[me], own.at[1]),
    ]
    for j in range(count):
        mine.append(
            pltpu.make_async_copy(own_every(j, shards[j]), every(j, full[j], mp), w_own.at[j])
        )
    for copy in mine:
        copy.start()

    def forward(j):
        weights[j][0].wait_recv()
        weights[j][2].start()
        weights[j][4].start()
        weights[j][1].wait_recv()
        weights[j][3].start()
        weights[j][5].start()

    def forward_last(j):
        weights[j][2].wait_recv()
        weights[j][6].start()
        weights[j][3].wait_recv()
        weights[j][7].start()

    forward(0)
    forward(1)
    for copy in mine:
        copy.wait()

    @pl.loop(1, WIDE)
    def _(k):
        codes_copy(k).wait()

    invert(got_codes_ref, slot_ref, mask_ref, keep_ref)
    got_codes_out[...] = got_codes_ref[...]
    for j in range(2, count):
        forward(j)
    for j in range(count):
        forward_last(j)

    @pl.loop(1, WIDE)
    def _(k):
        rows_copy(k).wait()

    for j in range(count):
        for kind in range(4):
            weights[j][kind].wait_send()
        for kind in range(4, 8):
            weights[j][kind].wait()


def send_rows(source, points, codes, weights, collective):
    return pl.pallas_call(
        send_kernel,
        out_shape=[
            shape((WIDE, CAP, LOCAL), BF16),
            shape((WIDE, 2, 128), I32),
            shape((16, 2, 128), I32),
            shape((16, 256), I32),
            shape((12, 128), I32),
            shape((3 * WIDTH, WIDTH), BF16),
            shape((MP, LOCAL, WIDTH), BF16),
            shape((MP, 2 * LOCAL, WIDTH), BF16),
            shape((MP, WIDTH, WIDTH), BF16),
        ],
        in_specs=[SMEM, VMEM, ANY] + [VMEM] * 4,
        out_specs=[ANY] + [VMEM] * 4 + [ANY] * 4,
        scratch_shapes=[
            pltpu.VMEM((WIDE, 2, 128), I32),
            pltpu.VMEM((ROWS, LOCAL), F32),
            pltpu.VMEM((1, CAP, LOCAL), F32),
            pltpu.VMEM((WIDE, CAP, LOCAL), BF16),
            pltpu.SemaphoreType.DMA((WIDE, 2)),
            pltpu.SemaphoreType.DMA((WIDE, 2)),
            pltpu.SemaphoreType.DMA((2,)),
            pltpu.SemaphoreType.DMA((4, 8)),
            pltpu.SemaphoreType.DMA((4, 8)),
            pltpu.SemaphoreType.DMA((4,)),
        ],
        compiler_params=params(collective),
    )(source, points, codes, *weights)


SCALE = 0.125 * 1.4426950408889634


def lanes(count):
    return lax.broadcasted_iota(I32, (count, 128), 1)


def columns_of(flags):
    eye = lax.broadcasted_iota(I32, (128, 128), 0) == lax.broadcasted_iota(I32, (128, 128), 1)
    row = jnp.broadcast_to(jnp.where(flags, 1.0, 0.0), (128, 128)).astype(BF16)
    return dot_t(jnp.where(eye, 1.0, 0.0).astype(BF16), row)


def augment(keys, values, columns):
    lane = lanes(keys.shape[0])
    low = lane < 64
    bias = jnp.where(columns > 0.5, 0.0, -1e30)
    keys = keys.astype(F32)
    values = values.astype(F32)
    return (
        (
            jnp.where(low, keys, jnp.where(lane == 64, bias, 0.0)).astype(BF16),
            jnp.where(low, jnp.where(lane == 0, bias, 0.0), keys).astype(BF16),
        ),
        (jnp.where(low, values, 1.0).astype(BF16), jnp.where(low, 1.0, values).astype(BF16)),
    )


def attend_pair(queries, own_keys, own_values, masked, keys, values):
    count = queries.shape[0]
    lane = lanes(count)
    low = lane < 64
    queries = queries.astype(F32)
    own_keys = own_keys.astype(F32)
    own_values = own_values.astype(F32)
    out = []
    for head in range(2):
        mine = low if head == 0 else jnp.logical_not(low)
        spare = jnp.where(lane == (64 if head == 0 else 0), 1.0, 0.0)
        q = jnp.where(mine, queries, spare).astype(BF16)
        scores = dot_t(q, keys(head))
        alone = jnp.sum(jnp.where(mine, queries * own_keys, 0.0), -1, keepdims=True)
        top = jnp.maximum(jnp.max(scores, -1, keepdims=True), alone)
        weights = jnp.exp2(scores - top).astype(BF16)
        own = jnp.where(masked, jnp.exp2(alone - top), 0.0)
        total = dot(weights, values(head))
        out.append(total + own * jnp.where(mine, own_values, 1.0))
    sums = pltpu.roll(jnp.where(low, out[1], out[0]), 64, 1)
    return (jnp.where(low, out[0], out[1]) / sums).astype(BF16)


def attend_ball(queries, keys, values, allowed):
    low = lanes(BALL) < 64
    out = []
    for head in range(2):
        mine = low if head == 0 else jnp.logical_not(low)
        q = jnp.where(mine, queries, jnp.zeros_like(queries))
        scores = jnp.where(allowed, dot_t(q, keys), -1e30)
        weights = jnp.exp2(scores - jnp.max(scores, -1, keepdims=True))
        total = jnp.sum(weights, -1, keepdims=True)
        out.append(dot(weights.astype(BF16), values) / total)
    return jnp.where(low, out[0], out[1]).astype(BF16)


def fine_ball(x, real, qkv_ref, out_ref):
    x = x.astype(F32)
    normed = norm(x).astype(BF16)
    q = (dot(normed, qkv_ref[0]) * SCALE).astype(BF16)
    k = dot(normed, qkv_ref[1]).astype(BF16)
    v = dot(normed, qkv_ref[2]).astype(BF16)
    rows = lax.broadcasted_iota(I32, (BALL, BALL), 0)
    cols = lax.broadcasted_iota(I32, (BALL, BALL), 1)
    allowed = jnp.logical_or(real, rows == cols)
    mixed = []
    for g in range(MP):
        at = slice(g * 128, (g + 1) * 128)
        mixed.append(attend_ball(q[:, at], k[:, at], v[:, at], allowed))
    state = x + dot(jnp.concatenate(mixed, 1), out_ref[...])
    high = state.astype(BF16)
    rest = (state - high.astype(F32)).astype(BF16)
    runs, counted = pooling(real, 4)
    pooled = (dot(runs, high) + dot(runs, rest)) / jnp.maximum(counted, 1.0)
    return state, pooled.astype(BF16)


def pooling(real, factor):
    count_rows = BALL // factor
    r = lax.broadcasted_iota(I32, (count_rows, BALL), 0)
    c = lax.broadcasted_iota(I32, (count_rows, BALL), 1)
    hot = jnp.where(jnp.logical_and(r == c // factor, real), 1.0, 0.0)
    return hot.astype(BF16), jnp.sum(hot, 1, keepdims=True)


BALLS = QUARTER // BALL


def forward_tile(state, mp, gate_up_ref, down_ref):
    normed = norm(state).astype(BF16)
    total = state
    for c in range(MP):
        half = dot(normed, gate_up_ref[c, :WIDTH, :]) * 0.5
        up = dot(normed, gate_up_ref[c, WIDTH:, :])
        activated = ((half + half * jnp.tanh(half)) * up).astype(BF16)
        total = total + dot(activated, down_ref[lax.rem(mp + c, MP)])
    return total


def relatives(me):
    low = lax.rem(me, 2)
    high = lax.rem(me // 2, 2)
    first = me + 1 - 2 * low
    second = me + 2 - 4 * high
    third = first + 2 - 4 * high
    return (first, second, third)


def middle_kernel(
    slot_ref, code_ref, got_ref, mask_ref, keep_ref, qkv_hbm, out_hbm, gate_up_hbm, down_hbm, coarse_hbm,
    lift_hbm, back_ref,
    turned_ref, lifted_ref, outgoing, r_sem,
    wide, staged, packed, x, state, pooled, tiles, one, two, mate_one, mate_two, mate_keep,
    mixed, all_mixed, lifted, keys_one, values_one, keys_two, values_two, qkv_ref, out_ref, gate_up_ref, down_ref, w_ref, lift_ref,
    x_sem, p_sem, e_sem, k_sem, m_sem, t_sem, l_sem, g_sem, b_sem, f_sem, own, loads,
):
    me = lax.axis_index("wide")
    mp = lax.axis_index("mp")
    others = relatives(me)
    barrier = pltpu.get_barrier_semaphore()
    for k in range(1, MP):
        pl.semaphore_signal(
            barrier, inc=1, device_id={"mp": lax.rem(mp + k, MP)}, device_id_type=MESH
        )

    @pl.loop(1, WIDE)
    def _(k):
        pl.semaphore_signal(
            barrier, inc=1, device_id={"wide": lax.rem(me + k, WIDE)}, device_id_type=MESH
        )

    def chip(i):
        return 2 * lax.rem(i * 7, WIDE // 2)

    load = [
        pltpu.make_async_copy(src, dst, loads.at[j])
        for j, (src, dst) in enumerate([
            (qkv_hbm, qkv_ref),
            (out_hbm, out_ref),
            (gate_up_hbm, gate_up_ref.at[0]),
            (down_hbm, down_ref),
            (coarse_hbm, w_ref),
            (lift_hbm, lift_ref),
        ])
    ]
    for copy in load:
        copy.start()
    widen(got_ref, wide, SLOTS)
    pl.semaphore_wait(barrier, MP - 1 + WIDE - 1)

    def rows(t, size):
        return pl.ds(pl.multiple_of(t * size, size), size)

    def cols(g):
        return pl.ds(pl.multiple_of(g * LOCAL, LOCAL), LOCAL)

    def peer(k):
        return lax.rem(mp + k, MP)

    def to_mp(src, dst, sem, k, t):
        return remote(src, dst, sem.at[0, k, t], sem.at[1, k, t], {"mp": peer(k)})

    def piece(shards, owner):
        return gate_up_ref.at[shards, pl.ds(pl.multiple_of(owner * 32, 32), 32), :]

    def fetch(k):
        src = gate_up_hbm.at[pl.ds(pl.multiple_of(me * 32, 32), 32), :]
        return to_mp(src, piece(MP - k, me), g_sem, k, 0)

    def broadcast(i):
        part = piece(pl.ds(1, 3), me)
        to = {"wide": lax.rem(me + chip(i), WIDE)}
        return remote(part, part, b_sem.at[0, i], b_sem.at[1, i], to)

    def pass_on(i):
        part = piece(pl.ds(1, 3), lax.rem(me + WIDE - chip(i), WIDE))
        return remote(part, part, f_sem.at[0, i], f_sem.at[1, i], {"wide": others[0]})

    for k in (2, 1, 3):
        fetch(k).start()

    def turn(k, t):
        return to_mp(packed.at[peer(k) * BALLS + t], x.at[rows(t, BALL), cols(mp)], x_sem, k, t)

    def keep_turn(t):
        return pltpu.make_async_copy(
            packed.at[mp * BALLS + t], x.at[rows(t, BALL), cols(mp)], own.at[0, t]
        )

    def send_ball(t):
        for k in (2, 1, 3):
            gather_bucket(0, lambda s: slot_ref[s], wide, staged, packed, peer(k) * BALLS + t)
            turn(k, t).start()
        gather_bucket(0, lambda s: slot_ref[s], wide, staged, packed, mp * BALLS + t)
        keep_turn(t).start()

    send_ball(0)
    for k in (1, 3, 2):
        fetch(k).wait_recv()

    @pl.loop(1, WIDE // 2)
    def _(i):
        broadcast(i).start()

    pass_on(0).start()

    @pl.loop(1, BALLS)
    def _(t):
        send_ball(t)

    def flags(j):
        return remote(
            keep_ref, mate_keep.at[j], k_sem.at[0, j], k_sem.at[1, j], {"wide": others[j]}
        )

    for j in range(3):
        flags(j).start()
    load[0].wait()
    load[1].wait()

    def share(k, t):
        return to_mp(pooled.at[mp, t], pooled.at[mp, t], p_sem, k, t)

    @pl.loop(0, BALLS)
    def _(t):
        for k in (1, 3, 2):
            turn(k, t).wait_recv()
        keep_turn(t).wait()
        real = mask_ref[pl.ds(mp * BALLS + t, 1), :] > 0
        out, means = fine_ball(x[rows(t, BALL), :], real, qkv_ref, out_ref)
        state[rows(t, BALL), :] = out
        pooled[mp, t] = means
        for k in (2, 1, 3):
            share(k, t).start()

    load[2].wait()
    load[3].wait()

    def give(k, t):
        return to_mp(
            tiles.at[rows(t, BALL), cols(peer(k))],
            turned_ref.at[rows(mp * BALLS + t, BALL), :],
            t_sem,
            k,
            t,
        )

    def keep_give(t):
        return pltpu.make_async_copy(
            tiles.at[rows(t, BALL), cols(mp)],
            turned_ref.at[rows(mp * BALLS + t, BALL), :],
            own.at[1, t],
        )

    def feed(t, count):
        at = pl.ds(t * BALL, count * BALL)
        tiles[at, :] = forward_tile(state[at, :], mp, gate_up_ref, down_ref).astype(BF16)
        for u in range(t, t + count):
            for k in (2, 1, 3):
                give(k, u).start()
            keep_give(u).start()

    @pl.loop(1, WIDE // 2)
    def _(i):
        broadcast(i).wait_recv()
        pass_on(i).start()

    def pass_one(q):
        return remote(
            one.at[pl.ds(1, 2), rows(q, ONE), :],
            mate_one.at[:, rows(q, ONE), :],
            e_sem.at[0, 3, q],
            e_sem.at[1, 3, q],
            {"wide": others[0]},
        )

    def pass_two(j, q):
        return remote(
            two.at[pl.ds(1, 2), rows(q, TWO), :],
            mate_two.at[j, :, rows(q, TWO), :],
            e_sem.at[0, j, q],
            e_sem.at[1, j, q],
            {"wide": others[j]},
        )

    pair = lax.broadcasted_iota(I32, (32, 64), 0) == lax.broadcasted_iota(I32, (32, 64), 1) // 2
    pair = jnp.where(pair, 1.0, 0.0).astype(BF16)
    load[4].wait()

    def project(q):
        firsts, seconds = [], []
        for ball in range(BALLS):
            real = mask_ref[pl.ds(q * BALLS + ball, 1), :] > 0
            means = pooled[q, ball].astype(F32)
            firsts.append(norm(means).astype(BF16))
            sums = means * pooling(real, 4)[1]
            high = sums.astype(BF16)
            rest = (sums - high.astype(F32)).astype(BF16)
            counted = jnp.maximum(pooling(real, 8)[1], 1.0)
            seconds.append(norm((dot(pair, high) + dot(pair, rest)) / counted).astype(BF16))
        firsts = jnp.concatenate(firsts, 0)
        seconds = jnp.concatenate(seconds, 0)
        for t in (1, 2):
            two[t, rows(q, TWO), :] = dot(seconds, w_ref[1, t]).astype(BF16)
            one[t, rows(q, ONE), :] = dot(firsts, w_ref[0, t]).astype(BF16)
        for j in (1, 2, 0):
            pass_two(j, q).start()
        pass_one(q).start()
        two[0, rows(q, TWO), :] = (dot(seconds, w_ref[1, 0]) * SCALE).astype(BF16)
        one[0, rows(q, ONE), :] = (dot(firsts, w_ref[0, 0]) * SCALE).astype(BF16)

    project(mp)
    for k in (1, 3, 2):

        @pl.loop(0, BALLS)
        def _(t):
            share(MP - k, t).wait_recv()

        project(peer(k))

    @pl.loop(0, WIDE // 2)
    def _(i):
        pass_on(i).wait_recv()

    feed(0, 2)
    feed(2, 1)

    def hand_to(q, k, level):
        at = pl.ds(0, ONE) if level == 0 else pl.ds(ONE, TWO)
        return to_mp(mixed.at[q, at, :], all_mixed.at[at, cols(mp)], m_sem, k, level)

    def hand(k, level):
        return hand_to(peer(k), k, level)

    def keep_hand(level):
        at = pl.ds(0, ONE) if level == 0 else pl.ds(ONE, TWO)
        return pltpu.make_async_copy(
            mixed.at[mp, at, :], all_mixed.at[at, cols(mp)], own.at[2, level]
        )

    for j in range(3):
        flags(j).wait()

    def fill(keys_ref, values_ref, begin, src, first, flag):
        for c in range(src.shape[1] // 128):
            at = slice(c * 128, (c + 1) * 128)
            here = flag[first + c : first + c + 1, :] > 0
            keys, values = augment(src[0, at, :], src[1, at, :], columns_of(here))
            to = slice(begin + c * 128, begin + (c + 1) * 128)
            for head in range(2):
                keys_ref[head, to, :] = keys[head]
                values_ref[head, to, :] = values[head]

    def masked_of(keys_ref, at):
        spare = keys_ref[0, at, :].astype(F32)
        return jnp.min(jnp.where(lanes(256) == 64, spare, 0.0), -1, keepdims=True) < 0.0

    mine = keep_ref[...]
    fill(keys_one, values_one, 0, one.at[1:], 0, mine)

    @pl.loop(0, MP)
    def _(q):
        pass_one(q).wait()

    fill(keys_one, values_one, 4 * ONE, mate_one, 0, mate_keep[0])

    @pl.loop(1, MP + 1)
    def _(k):
        q = peer(k)
        at = rows(q, ONE)
        mixed[q, 0:ONE, :] = attend_pair(
            one[0, at, :], one[1, at, :], one[2, at, :], masked_of(keys_one, at),
            lambda head: keys_one[head], lambda head: values_one[head],
        )

        @pl.when(k < MP)
        def _():
            hand(k, 0).start()

    keep_hand(0).start()

    fill(keys_two, values_two, 0, two.at[1:], 8, mine)

    @pl.loop(0, MP)
    def _(q):
        for j in range(3):
            pass_two(j, q).wait()

    for j in range(3):
        fill(keys_two, values_two, (j + 1) * 4 * TWO, mate_two.at[j], 8, mate_keep[j])

    @pl.loop(0, 2)
    def _(p):
        at = rows(p, 256)
        both = attend_pair(
            two[0, at, :], two[1, at, :], two[2, at, :], masked_of(keys_two, at),
            lambda head: keys_two[head], lambda head: values_two[head],
        )
        for h in range(2):
            q = p * 2 + h
            k = lax.rem(q + MP - mp, MP)
            mixed[q, ONE:COARSE, :] = both[h * TWO : (h + 1) * TWO]

            @pl.when(k > 0)
            def _():
                hand_to(q, k, 1).start()

    keep_hand(1).start()

    feed(3, 1)

    load[5].wait()
    for level in range(2):
        keep_hand(level).wait()
        for k in (1, 3, 2):
            hand(k, level).wait()
    for level, begin, size in ((0, 0, 64), (1, ONE, 32)):
        span = slice(begin, begin + size * BALLS)
        total = jnp.zeros((size * BALLS, WIDTH), F32)
        for g in range(MP):
            total = total + dot(
                all_mixed[span, g * LOCAL : (g + 1) * LOCAL],
                lift_ref[g, level * LOCAL : (level + 1) * LOCAL, :],
            )
        total = total.astype(BF16)
        for ball in range(BALLS):
            at = slice(0, 64) if level == 0 else slice(64, 96)
            lifted[ball, at, :] = total[ball * size : (ball + 1) * size]

    def rise(k):
        return to_mp(lifted.at[:, :, cols(peer(k))], lifted_ref.at[pl.ds(mp * BALLS, BALLS)], l_sem, k, 0)

    for k in (2, 1, 3):
        rise(k).start()
    keep_rise = pltpu.make_async_copy(
        lifted.at[:, :, cols(mp)], lifted_ref.at[pl.ds(mp * BALLS, BALLS)], own.at[3, 0]
    )
    keep_rise.start()

    @pl.loop(0, BALLS)
    def _(t):
        keep_give(t).wait()
        for k in (1, 3, 2):
            turn(k, t).wait_send()
            share(k, t).wait_send()
            give(k, t).wait()

    @pl.loop(1, WIDE // 2)
    def _(i):
        broadcast(i).wait_send()

    @pl.loop(0, WIDE // 2)
    def _(i):
        pass_on(i).wait_send()

    for k in (1, 3, 2):
        fetch(k).wait_send()
    keep_rise.wait()
    for k in (1, 3, 2):
        rise(k).wait()

    runs = run_matrix(
        lax.broadcasted_iota(I32, (BALL, 96), 0), lax.broadcasted_iota(I32, (BALL, 96), 1)
    )

    @pl.loop(0, ROWS // BALL)
    def _(i):
        at = rows(i, BALL)
        wide[at, :] = turned_ref[at, :].astype(F32) + dot(runs, lifted_ref[i])

    wide[ROWS : ROWS + 8, :] = jnp.zeros((8, LOCAL), F32)

    def rows_copy(k):
        to = turn_of(me, k)
        return remote(
            outgoing.at[to], back_ref.at[me], r_sem.at[0, k], r_sem.at[1, k], {"wide": to}
        )

    @pl.loop(1, WIDE)
    def _(k):
        gather_bucket(0, lambda s: code_ref[s] >> 1, wide, staged, outgoing, turn_of(me, k))
        rows_copy(k).start()

    gather_bucket(0, lambda s: code_ref[s] >> 1, wide, staged, outgoing, me)
    last = pltpu.make_async_copy(outgoing.at[me], back_ref.at[me], own.at[3, 1])
    last.start()
    last.wait()

    @pl.loop(1, WIDE)
    def _(k):
        rows_copy(k).wait()


def middle(slots, codes, got, mask, keep, weights, collective):
    dma = pltpu.SemaphoreType.DMA
    return pl.pallas_call(
        middle_kernel,
        out_shape=shape((WIDE, CAP, LOCAL), BF16),
        in_specs=[SMEM, SMEM, VMEM, VMEM, VMEM] + [ANY] * 6,
        out_specs=ANY,
        scratch_shapes=[
            pltpu.VMEM((ROWS, LOCAL), BF16),
            pltpu.VMEM((MP * BALLS, 96, LOCAL), BF16),
            pltpu.VMEM((WIDE, CAP, LOCAL), BF16),
            dma((2, WIDE)),
            pltpu.VMEM((SLOTS, LOCAL), F32),
            pltpu.VMEM((1, CAP, LOCAL), F32),
            pltpu.VMEM((MP * BALLS, BALL, LOCAL), BF16),
            pltpu.VMEM((QUARTER, WIDTH), BF16),
            pltpu.VMEM((QUARTER, WIDTH), F32),
            pltpu.VMEM((MP, BALLS, 64, WIDTH), BF16),
            pltpu.VMEM((QUARTER, WIDTH), BF16),
            pltpu.VMEM((3, 4 * ONE, LOCAL), BF16),
            pltpu.VMEM((3, 4 * TWO, LOCAL), BF16),
            pltpu.VMEM((2, 4 * ONE, LOCAL), BF16),
            pltpu.VMEM((3, 2, 4 * TWO, LOCAL), BF16),
            pltpu.VMEM((3, 12, 128), I32),
            pltpu.VMEM((MP, COARSE, LOCAL), BF16),
            pltpu.VMEM((COARSE, WIDTH), BF16),
            pltpu.VMEM((BALLS, 96, WIDTH), BF16),
            pltpu.VMEM((2, 8 * ONE, LOCAL), BF16),
            pltpu.VMEM((2, 8 * ONE, LOCAL), BF16),
            pltpu.VMEM((2, 16 * TWO, LOCAL), BF16),
            pltpu.VMEM((2, 16 * TWO, LOCAL), BF16),
            pltpu.VMEM((3, WIDTH, WIDTH), BF16),
            pltpu.VMEM((WIDTH, WIDTH), BF16),
            pltpu.VMEM((MP, 2 * WIDTH, WIDTH), BF16),
            pltpu.VMEM((MP, WIDTH, WIDTH), BF16),
            pltpu.VMEM((2, 3, WIDTH, LOCAL), BF16),
            pltpu.VMEM((MP, 2 * LOCAL, WIDTH), BF16),
            dma((2, MP, BALLS)),
            dma((2, MP, BALLS)),
            dma((2, 4, MP)),
            dma((2, 3)),
            dma((2, MP, 2)),
            dma((2, MP, BALLS)),
            dma((2, MP, 1)),
            dma((2, MP, 1)),
            dma((2, WIDE // 2)),
            dma((2, WIDE // 2)),
            dma((4, BALLS)),
            dma((6,)),
        ],
        compiler_params=params(collective),
    )(slots, codes, got, mask, keep, *weights)


def on_device(points, mask, perm, w_qkv, w_out, w_gate_up, w_down, w_coarse, w_coarse_out):
    slot, source, codes = index(perm, mask)
    got, got_code, landed, owned_mask, keep, full_qkv, full_out, full_lift, full_down = send_rows(
        source.reshape(SLOTS),
        points,
        codes,
        [
            w_qkv.reshape(3 * WIDTH, LOCAL),
            w_out,
            w_coarse_out.reshape(2 * LOCAL, WIDTH),
            w_down,
        ],
        1,
    )
    full_qkv = full_qkv.reshape(3, WIDTH, WIDTH)
    full_out = full_out.reshape(WIDTH, WIDTH)
    own_gate_up = w_gate_up.reshape(2 * WIDTH, WIDTH)
    returned = middle(
        landed.reshape(ROWS), got_code.reshape(SLOTS), got.reshape(SLOTS, LOCAL), owned_mask, keep,
        [full_qkv, full_out, own_gate_up, full_down, w_coarse, full_lift], 2,
    )
    return pl.pallas_call(
        finish_kernel,
        out_shape=shape((ROWS, LOCAL), F32),
        in_specs=[SMEM, ANY],
        out_specs=ANY,
        scratch_shapes=[
            pltpu.VMEM((SLOTS, LOCAL), BF16),
            pltpu.VMEM((SLOTS, LOCAL), F32),
            pltpu.VMEM((ROWS, LOCAL), F32),
            pltpu.SemaphoreType.DMA((SLOTS // 1024,)),
            pltpu.SemaphoreType.DMA((ROWS // 512,)),
        ],
        compiler_params=params(),
    )(slot.reshape(ROWS), returned.reshape(SLOTS, LOCAL))


def solution(mesh):
    placed = (
        P("wide", "mp"),
        P("wide"),
        P("wide"),
        P(None, None, "mp"),
        P("mp", None),
        P(None, None, "mp"),
        P("mp", None),
        P(None, None, None, "mp"),
        P(None, "mp", None),
    )
    return jax.shard_map(
        on_device, mesh=mesh, in_specs=placed, out_specs=P("wide", "mp"), check_vma=False
    )
```

```python
import functools

import jax
import jax.numpy as jnp
from jax import lax
from jax.experimental import pallas as pl
from jax.experimental.pallas import tpu as pltpu
from jax.sharding import PartitionSpec as P

BALL = 256
WIDE = 32
MP = 4
ROWS = 4096
CAP = 256
SLOTS = WIDE * CAP
QUARTER = ROWS // MP
WIDTH = 512
LOCAL = WIDTH // MP
HIDDEN = 2048
ONE = QUARTER // 4
TWO = QUARTER // 8
COARSE = ONE + TWO
F32 = jnp.float32
BF16 = jnp.bfloat16
I32 = jnp.int32
MESH = pl.DeviceIdType.MESH
ANY = pl.BlockSpec(memory_space=pl.ANY)
VMEM = pl.BlockSpec(memory_space=pltpu.VMEM)
SMEM = pl.BlockSpec(memory_space=pltpu.SMEM)
LIMIT = 56 * 1024 * 1024


def shape(dims, kind):
    return jax.ShapeDtypeStruct(dims, kind)


def params(collective=None):
    if collective is None:
        return pltpu.CompilerParams(vmem_limit_bytes=LIMIT)
    return pltpu.CompilerParams(
        vmem_limit_bytes=LIMIT, collective_id=collective, has_side_effects=True
    )


def dot(a, b):
    return jnp.dot(a, b, preferred_element_type=F32)


def dot_t(a, b):
    return lax.dot_general(a, b, (((1,), (1,)), ((), ())), preferred_element_type=F32)


def norm(values):
    return values * lax.rsqrt(jnp.mean(values * values, -1, keepdims=True) + 1e-06)


UNROLL = 32
NONE = 2 * ROWS


def index_kernel(perm_ref, mask_ref, slot_ref, source_ref, codes_ref):
    perm = perm_ref[...]
    target = perm >> 12
    code = (perm & (ROWS - 1)) * 2 + mask_ref[...]
    rows = lax.broadcasted_iota(I32, (CAP, 128), 0)
    upper = jnp.where(
        lax.broadcasted_iota(I32, (128, 128), 0) < lax.broadcasted_iota(I32, (128, 128), 1), 1.0, 0.0
    ).astype(BF16)
    which = lax.broadcasted_iota(I32, (WIDE, 128), 0)
    lane = lax.broadcasted_iota(I32, (1, 128), 1).astype(F32)
    carry = jnp.zeros((WIDE, 1), F32)
    found = jnp.zeros((5 * WIDE, CAP), F32)
    for c in range(ROWS // 128):
        row = slice(c, c + 1)
        hot = jnp.where(which == target[row, :], 1.0, 0.0)
        before = dot(hot.astype(BF16), upper) + carry
        rank = jnp.sum(hot * before, 0, keepdims=True).astype(I32)
        slot_ref[row, :] = target[row, :] * CAP + rank
        carry = carry + jnp.sum(hot, 1, keepdims=True)
        placed = jnp.where(rows == rank, 1.0, 0.0).astype(BF16)
        high = (code[row, :] >> 6).astype(F32)
        low = (code[row, :] & 63).astype(F32)
        values = jnp.concatenate([hot * lane, hot * float(c), hot * high, hot * low, hot], 0)
        found = found + dot_t(values.astype(BF16), placed)
    source = (found[:WIDE] + found[WIDE : 2 * WIDE] * 128.0).astype(I32)
    codes = (found[2 * WIDE : 3 * WIDE] * 64.0 + found[3 * WIDE : 4 * WIDE]).astype(I32)
    codes = jnp.where(found[4 * WIDE :] > 0.5, codes, NONE)
    for h in range(2):
        at = slice(h * 128, (h + 1) * 128)
        source_ref[:, h, :] = source[:, at]
        codes_ref[:, h, :] = codes[:, at]


def index(perm, mask):
    return pl.pallas_call(
        index_kernel,
        out_shape=[shape((32, 128), I32), shape((WIDE, 2, 128), I32), shape((WIDE, 2, 128), I32)],
        in_specs=[VMEM] * 2,
        out_specs=[VMEM] * 3,
        compiler_params=params(),
    )(perm.reshape(32, 128), mask.reshape(32, 128))


def invert(codes_ref, slot_ref, mask_ref, keep_ref):
    balls = ROWS // BALL
    rows = lax.broadcasted_iota(I32, (256, 128), 0)
    which = lax.broadcasted_iota(I32, (balls, 128), 0)
    lane = lax.broadcasted_iota(I32, (1, 128), 1).astype(F32)
    found = jnp.zeros((3 * balls, 256), F32)
    for c in range(WIDE):
        for h in range(2):
            code = codes_ref[c, h : h + 1, :]
            landing = code >> 1
            hot = jnp.where(which == (landing >> 8), 1.0, 0.0)
            placed = jnp.where(rows == (landing & 255), 1.0, 0.0).astype(BF16)
            real = (code & 1).astype(F32)
            values = jnp.concatenate([hot * lane, hot * float(2 * c + h), hot * real], 0)
            found = found + dot_t(values.astype(BF16), placed)
    slots = (found[:balls] + found[balls : 2 * balls] * 128.0).astype(I32)
    for h in range(2):
        slot_ref[:, h, :] = slots[:, h * 128 : (h + 1) * 128]
    mask = found[2 * balls :]
    mask_ref[...] = mask.astype(I32)
    mask = mask.astype(BF16)
    for f, first in ((4, 0), (8, 8)):
        side = f // 2
        count = balls // side
        total = jnp.zeros((count, 128), F32)
        for j in range(side):
            r = lax.broadcasted_iota(I32, (count, balls), 0)
            c = lax.broadcasted_iota(I32, (count, balls), 1)
            pick = jnp.where(c == r * side + j, 1.0, 0.0).astype(BF16)
            r = lax.broadcasted_iota(I32, (256, 128), 0)
            c = lax.broadcasted_iota(I32, (256, 128), 1)
            runs = jnp.where(c == r // f + j * (128 // side), 1.0, 0.0).astype(BF16)
            total = total + dot(dot(pick, mask).astype(BF16), runs)
        keep_ref[first : first + count, :] = jnp.where(total > 0.5, 1, 0)


def run_matrix(r, c):
    hot = jnp.logical_or(
        jnp.logical_and(c < 64, r // 4 == c), jnp.logical_and(c >= 64, r // 8 == c - 64)
    )
    return jnp.where(hot, 1.0, 0.0).astype(BF16)


def widen(src, dst, rows):
    @pl.loop(0, rows // 256)
    def _(i):
        at = pl.ds(pl.multiple_of(i * 256, 256), 256)
        dst[at, :] = src[at, :].astype(dst.dtype)


def finish_kernel(slot_ref, got_ref, out_ref, narrow, wide, done, in_sem, out_sem):
    def chunk(ref, i, size):
        return ref.at[pl.ds(pl.multiple_of(i * size, size), size), :]

    def load(i):
        return pltpu.make_async_copy(chunk(got_ref, i, 1024), chunk(narrow, i, 1024), in_sem.at[i])

    def store(i):
        return pltpu.make_async_copy(chunk(done, i, 512), chunk(out_ref, i, 512), out_sem.at[i])

    for i in range(SLOTS // 1024):
        load(i).start()
    for i in range(SLOTS // 1024):
        load(i).wait()
        widen(chunk(narrow, i, 1024), chunk(wide, i, 1024), 1024)

    @pl.loop(0, ROWS // 512)
    def _(i):
        @pl.loop(0, 512 // UNROLL)
        def _(j):
            base = i * 512 + j * UNROLL
            lines = [wide[pl.ds(slot_ref[base + u], 1), :] for u in range(UNROLL)]
            for u in range(UNROLL):
                done[pl.ds(base + u, 1), :] = lines[u]

        store(i).start()

    @pl.loop(0, ROWS // 512)
    def _(i):
        store(i).wait()


def remote(src, dst, send, recv, device):
    return pltpu.make_async_remote_copy(
        src_ref=src, dst_ref=dst, send_sem=send, recv_sem=recv, device_id=device, device_id_type=MESH
    )


def turn_of(me, k):
    return lax.rem(me + lax.rem(k * 7, WIDE), WIDE)


def gather_bucket(line, lookup, wide, staged, packed, peer):
    @pl.loop(0, CAP // UNROLL)
    def _(i):
        begin = i * UNROLL
        lines = [wide[pl.ds(lookup(peer * CAP + begin + u), 1), :] for u in range(UNROLL)]
        for u in range(UNROLL):
            staged[line, pl.ds(begin + u, 1), :] = lines[u]

    packed[peer] = staged[line].astype(BF16)


def send_kernel(
    source_ref, points_ref, codes_ref, qkv_ref, out_ref, lift_ref, down_ref, gate_ref,
    got_ref, got_codes_out, slot_ref, mask_ref, keep_ref, all_qkv, all_out, all_lift, all_down,
    all_gate,
    got_codes_ref, wide, staged, packed, send, recv, own, w_send, w_recv, w_own,
):
    me = lax.axis_index("wide")
    mp = lax.axis_index("mp")
    core = lax.rem(me, 2)
    partner = me + 1 - 2 * core
    after, ahead = lax.rem(mp + 1, MP), lax.rem(mp + 2, MP)
    behind = lax.rem(mp + 3, MP)
    barrier = pltpu.get_barrier_semaphore()

    @pl.loop(1, WIDE)
    def _(k):
        pl.semaphore_signal(
            barrier, inc=1, device_id={"wide": lax.rem(me + k, WIDE)}, device_id_type=MESH
        )

    for other in (after, behind):
        pl.semaphore_signal(barrier, inc=1, device_id={"mp": other}, device_id_type=MESH)
    widen(points_ref, wide, ROWS)

    def part(first, count):
        def rows(ref, quarter):
            return pl.ds(pl.multiple_of(first * quarter, 16), count * quarter)

        def cut(j, ref, shard):
            if j == 0:
                return ref.at[rows(ref, 384), pl.ds(pl.multiple_of(shard * 128, 128), 128)]
            quarter = (0, 32, 64, 128, 128)[j]
            return ref.at[shard, rows(ref, quarter), :]

        def own_cut(j, ref):
            quarter = (384, 32, 64, 128, 128)[j]
            return ref.at[rows(ref, quarter), :]

        return cut, own_cut

    half, own_half = part(2 * core, 2)
    first, _ = part(2 * core, 1)
    second, _ = part(2 * core + 1, 1)
    every, own_every = part(0, 4)
    shards = [qkv_ref, out_ref, lift_ref, down_ref, gate_ref]
    full = [all_qkv, all_out, all_lift, all_down, all_gate]
    count = len(shards)

    def weight(j, kind, cut, src, shard, device):
        return remote(
            src, cut(j, full[j], shard), w_send.at[j, kind], w_recv.at[j, kind], device
        )

    def weight_copies(j):
        ref = full[j]
        mine = own_half(j, shards[j])
        return [
            weight(j, 0, half, mine, mp, {"mp": after}),
            weight(j, 1, half, mine, mp, {"mp": behind}),
            weight(j, 2, first, first(j, ref, behind), behind, {"mp": after}),
            weight(j, 3, second, second(j, ref, after), after, {"mp": behind}),
            weight(j, 4, half, half(j, ref, behind), behind, {"wide": partner}),
            weight(j, 5, half, half(j, ref, after), after, {"wide": partner}),
            weight(j, 6, first, first(j, ref, ahead), ahead, {"wide": partner}),
            weight(j, 7, second, second(j, ref, ahead), ahead, {"wide": partner}),
        ]

    weights = [weight_copies(j) for j in range(count)]

    def rows_copy(k):
        peer = turn_of(me, k)
        return remote(
            packed.at[peer], got_ref.at[me], send.at[k, 0], recv.at[k, 0], {"wide": peer}
        )

    def codes_copy(k):
        peer = turn_of(me, k)
        return remote(
            codes_ref.at[peer], got_codes_ref.at[me], send.at[k, 1], recv.at[k, 1], {"wide": peer}
        )

    pl.semaphore_wait(barrier, WIDE + 1)
    for j in range(count):
        weights[j][0].start()
        weights[j][1].start()

    @pl.loop(1, WIDE)
    def _(k):
        codes_copy(k).start()

    @pl.loop(1, WIDE)
    def _(k):
        gather_bucket(0, lambda s: source_ref[s], wide, staged, packed, turn_of(me, k))
        rows_copy(k).start()

    gather_bucket(0, lambda s: source_ref[s], wide, staged, packed, me)
    mine = [
        pltpu.make_async_copy(packed.at[me], got_ref.at[me], own.at[0]),
        pltpu.make_async_copy(codes_ref.at[me], got_codes_ref.at[me], own.at[1]),
    ]
    for j in range(count):
        mine.append(
            pltpu.make_async_copy(own_every(j, shards[j]), every(j, full[j], mp), w_own.at[j])
        )
    for copy in mine:
        copy.start()

    def forward(j):
        weights[j][0].wait_recv()
        weights[j][2].start()
        weights[j][4].start()
        weights[j][1].wait_recv()
        weights[j][3].start()
        weights[j][5].start()

    def forward_last(j):
        weights[j][2].wait_recv()
        weights[j][6].start()
        weights[j][3].wait_recv()
        weights[j][7].start()

    forward(0)
    forward(1)
    for copy in mine:
        copy.wait()

    @pl.loop(1, WIDE)
    def _(k):
        codes_copy(k).wait()

    invert(got_codes_ref, slot_ref, mask_ref, keep_ref)
    got_codes_out[...] = got_codes_ref[...]
    for j in range(2, count):
        forward(j)
    for j in range(count):
        forward_last(j)

    @pl.loop(1, WIDE)
    def _(k):
        rows_copy(k).wait()

    for j in range(count):
        for kind in range(4):
            weights[j][kind].wait_send()
        for kind in range(4, 8):
            weights[j][kind].wait()


def send_rows(source, points, codes, weights, collective):
    return pl.pallas_call(
        send_kernel,
        out_shape=[
            shape((WIDE, CAP, LOCAL), BF16),
            shape((WIDE, 2, 128), I32),
            shape((16, 2, 128), I32),
            shape((16, 256), I32),
            shape((12, 128), I32),
            shape((3 * WIDTH, WIDTH), BF16),
            shape((MP, LOCAL, WIDTH), BF16),
            shape((MP, 2 * LOCAL, WIDTH), BF16),
            shape((MP, WIDTH, WIDTH), BF16),
            shape((MP, WIDTH, WIDTH), BF16),
        ],
        in_specs=[SMEM, VMEM, ANY] + [VMEM] * 5,
        out_specs=[ANY] + [VMEM] * 4 + [ANY] * 5,
        scratch_shapes=[
            pltpu.VMEM((WIDE, 2, 128), I32),
            pltpu.VMEM((ROWS, LOCAL), F32),
            pltpu.VMEM((1, CAP, LOCAL), F32),
            pltpu.VMEM((WIDE, CAP, LOCAL), BF16),
            pltpu.SemaphoreType.DMA((WIDE, 2)),
            pltpu.SemaphoreType.DMA((WIDE, 2)),
            pltpu.SemaphoreType.DMA((2,)),
            pltpu.SemaphoreType.DMA((5, 8)),
            pltpu.SemaphoreType.DMA((5, 8)),
            pltpu.SemaphoreType.DMA((5,)),
        ],
        compiler_params=params(collective),
    )(source, points, codes, *weights)


SCALE = 0.125 * 1.4426950408889634


def lanes(count):
    return lax.broadcasted_iota(I32, (count, 128), 1)


def columns_of(flags):
    eye = lax.broadcasted_iota(I32, (128, 128), 0) == lax.broadcasted_iota(I32, (128, 128), 1)
    row = jnp.broadcast_to(jnp.where(flags, 1.0, 0.0), (128, 128)).astype(BF16)
    return dot_t(jnp.where(eye, 1.0, 0.0).astype(BF16), row)


def augment(keys, values, columns):
    lane = lanes(keys.shape[0])
    low = lane < 64
    bias = jnp.where(columns > 0.5, 0.0, -1e30)
    keys = keys.astype(F32)
    values = values.astype(F32)
    return (
        (
            jnp.where(low, keys, jnp.where(lane == 64, bias, 0.0)).astype(BF16),
            jnp.where(low, jnp.where(lane == 0, bias, 0.0), keys).astype(BF16),
        ),
        (jnp.where(low, values, 1.0).astype(BF16), jnp.where(low, 1.0, values).astype(BF16)),
    )


def attend_pair(queries, own_keys, own_values, masked, keys, values):
    count = queries.shape[0]
    lane = lanes(count)
    low = lane < 64
    queries = queries.astype(F32)
    own_keys = own_keys.astype(F32)
    own_values = own_values.astype(F32)
    out = []
    for head in range(2):
        mine = low if head == 0 else jnp.logical_not(low)
        spare = jnp.where(lane == (64 if head == 0 else 0), 1.0, 0.0)
        q = jnp.where(mine, queries, spare).astype(BF16)
        scores = dot_t(q, keys(head))
        alone = jnp.sum(jnp.where(mine, queries * own_keys, 0.0), -1, keepdims=True)
        top = jnp.maximum(jnp.max(scores, -1, keepdims=True), alone)
        weights = jnp.exp2(scores - top).astype(BF16)
        own = jnp.where(masked, jnp.exp2(alone - top), 0.0)
        total = dot(weights, values(head))
        out.append(total + own * jnp.where(mine, own_values, 1.0))
    sums = pltpu.roll(jnp.where(low, out[1], out[0]), 64, 1)
    return (jnp.where(low, out[0], out[1]) / sums).astype(BF16)


def attend_ball(queries, keys, values, allowed):
    low = lanes(BALL) < 64
    out = []
    for head in range(2):
        mine = low if head == 0 else jnp.logical_not(low)
        q = jnp.where(mine, queries, jnp.zeros_like(queries))
        scores = jnp.where(allowed, dot_t(q, keys), -1e30)
        weights = jnp.exp2(scores - jnp.max(scores, -1, keepdims=True))
        total = jnp.sum(weights, -1, keepdims=True)
        out.append(dot(weights.astype(BF16), values) / total)
    return jnp.where(low, out[0], out[1]).astype(BF16)


def fine_ball(x, real, qkv_ref, out_ref):
    x = x.astype(F32)
    normed = norm(x).astype(BF16)
    q = (dot(normed, qkv_ref[0]) * SCALE).astype(BF16)
    k = dot(normed, qkv_ref[1]).astype(BF16)
    v = dot(normed, qkv_ref[2]).astype(BF16)
    rows = lax.broadcasted_iota(I32, (BALL, BALL), 0)
    cols = lax.broadcasted_iota(I32, (BALL, BALL), 1)
    allowed = jnp.logical_or(real, rows == cols)
    mixed = []
    for g in range(MP):
        at = slice(g * 128, (g + 1) * 128)
        mixed.append(attend_ball(q[:, at], k[:, at], v[:, at], allowed))
    state = x + dot(jnp.concatenate(mixed, 1), out_ref[...])
    high = state.astype(BF16)
    rest = (state - high.astype(F32)).astype(BF16)
    runs, counted = pooling(real, 4)
    pooled = (dot(runs, high) + dot(runs, rest)) / jnp.maximum(counted, 1.0)
    return state, pooled.astype(BF16)


def pooling(real, factor):
    count_rows = BALL // factor
    r = lax.broadcasted_iota(I32, (count_rows, BALL), 0)
    c = lax.broadcasted_iota(I32, (count_rows, BALL), 1)
    hot = jnp.where(jnp.logical_and(r == c // factor, real), 1.0, 0.0)
    return hot.astype(BF16), jnp.sum(hot, 1, keepdims=True)


BALLS = QUARTER // BALL


def forward_tile(state, mp, gate_ref, up_ref, down_ref):
    normed = norm(state).astype(BF16)
    total = state
    for c in range(MP):
        shard = lax.rem(mp + c, MP)
        half = dot(normed, gate_ref[shard]) * 0.5
        up = dot(normed, up_ref[c])
        activated = ((half + half * jnp.tanh(half)) * up).astype(BF16)
        total = total + dot(activated, down_ref[shard])
    return total


def relatives(me):
    low = lax.rem(me, 2)
    high = lax.rem(me // 2, 2)
    first = me + 1 - 2 * low
    second = me + 2 - 4 * high
    third = first + 2 - 4 * high
    return (first, second, third)


def middle_kernel(
    slot_ref, code_ref, got_ref, mask_ref, keep_ref, qkv_hbm, out_hbm, gate_up_hbm, gate_hbm, down_hbm, coarse_hbm,
    lift_hbm, back_ref,
    turned_ref, lifted_ref, outgoing, r_sem,
    wide, staged, packed, x, state, pooled, tiles, one, two, mate_one, mate_two, mate_keep,
    mixed, all_mixed, lifted, keys_one, values_one, keys_two, values_two, qkv_ref, out_ref, gate_ref, up_ref, down_ref, w_ref, lift_ref,
    x_sem, p_sem, e_sem, k_sem, m_sem, t_sem, l_sem, g_sem, b_sem, f_sem, own, loads,
):
    me = lax.axis_index("wide")
    mp = lax.axis_index("mp")
    others = relatives(me)
    barrier = pltpu.get_barrier_semaphore()
    for k in range(1, MP):
        pl.semaphore_signal(
            barrier, inc=1, device_id={"mp": lax.rem(mp + k, MP)}, device_id_type=MESH
        )

    @pl.loop(1, WIDE)
    def _(k):
        pl.semaphore_signal(
            barrier, inc=1, device_id={"wide": lax.rem(me + k, WIDE)}, device_id_type=MESH
        )

    def chip(i):
        return 2 * lax.rem(i * 7, WIDE // 2)

    load = [
        pltpu.make_async_copy(src, dst, loads.at[j])
        for j, (src, dst) in enumerate([
            (qkv_hbm, qkv_ref),
            (out_hbm, out_ref),
            (gate_up_hbm.at[pl.ds(WIDTH, WIDTH), :], up_ref.at[0]),
            (down_hbm, down_ref),
            (coarse_hbm, w_ref),
            (lift_hbm, lift_ref),
            (gate_hbm, gate_ref),
        ])
    ]
    for copy in load:
        copy.start()
    widen(got_ref, wide, SLOTS)
    pl.semaphore_wait(barrier, MP - 1 + WIDE - 1)

    def rows(t, size):
        return pl.ds(pl.multiple_of(t * size, size), size)

    def cols(g):
        return pl.ds(pl.multiple_of(g * LOCAL, LOCAL), LOCAL)

    def peer(k):
        return lax.rem(mp + k, MP)

    def to_mp(src, dst, sem, k, t):
        return remote(src, dst, sem.at[0, k, t], sem.at[1, k, t], {"mp": peer(k)})

    def piece(shards, owner):
        return up_ref.at[shards, pl.ds(pl.multiple_of(owner * 16, 16), 16), :]

    def fetch(k):
        src = gate_up_hbm.at[pl.ds(pl.multiple_of(WIDTH + me * 16, 16), 16), :]
        return to_mp(src, piece(MP - k, me), g_sem, k, 0)

    def broadcast(i):
        part = piece(pl.ds(1, 3), me)
        to = {"wide": lax.rem(me + chip(i), WIDE)}
        return remote(part, part, b_sem.at[0, i], b_sem.at[1, i], to)

    def pass_on(i):
        part = piece(pl.ds(1, 3), lax.rem(me + WIDE - chip(i), WIDE))
        return remote(part, part, f_sem.at[0, i], f_sem.at[1, i], {"wide": others[0]})

    for k in (2, 1, 3):
        fetch(k).start()

    def turn(k, t):
        return to_mp(packed.at[peer(k) * BALLS + t], x.at[rows(t, BALL), cols(mp)], x_sem, k, t)

    def keep_turn(t):
        return pltpu.make_async_copy(
            packed.at[mp * BALLS + t], x.at[rows(t, BALL), cols(mp)], own.at[0, t]
        )

    def send_ball(t):
        for k in (2, 1, 3):
            gather_bucket(0, lambda s: slot_ref[s], wide, staged, packed, peer(k) * BALLS + t)
            turn(k, t).start()
        gather_bucket(0, lambda s: slot_ref[s], wide, staged, packed, mp * BALLS + t)
        keep_turn(t).start()

    send_ball(0)
    for k in (1, 3, 2):
        fetch(k).wait_recv()

    @pl.loop(1, WIDE // 2)
    def _(i):
        broadcast(i).start()

    pass_on(0).start()

    @pl.loop(1, BALLS)
    def _(t):
        send_ball(t)

    def flags(j):
        return remote(
            keep_ref, mate_keep.at[j], k_sem.at[0, j], k_sem.at[1, j], {"wide": others[j]}
        )

    for j in range(3):
        flags(j).start()
    load[0].wait()
    load[1].wait()

    def share(k, t):
        return to_mp(pooled.at[mp, t], pooled.at[mp, t], p_sem, k, t)

    @pl.loop(0, BALLS)
    def _(t):
        for k in (1, 3, 2):
            turn(k, t).wait_recv()
        keep_turn(t).wait()
        real = mask_ref[pl.ds(mp * BALLS + t, 1), :] > 0
        out, means = fine_ball(x[rows(t, BALL), :], real, qkv_ref, out_ref)
        state[rows(t, BALL), :] = out
        pooled[mp, t] = means
        for k in (2, 1, 3):
            share(k, t).start()

    load[2].wait()
    load[3].wait()
    load[6].wait()

    def give(k, t):
        return to_mp(
            tiles.at[rows(t, BALL), cols(peer(k))],
            turned_ref.at[rows(mp * BALLS + t, BALL), :],
            t_sem,
            k,
            t,
        )

    def keep_give(t):
        return pltpu.make_async_copy(
            tiles.at[rows(t, BALL), cols(mp)],
            turned_ref.at[rows(mp * BALLS + t, BALL), :],
            own.at[1, t],
        )

    def feed(t, count):
        at = pl.ds(t * BALL, count * BALL)
        tiles[at, :] = forward_tile(state[at, :], mp, gate_ref, up_ref, down_ref).astype(BF16)
        for u in range(t, t + count):
            for k in (2, 1, 3):
                give(k, u).start()
            keep_give(u).start()

    @pl.loop(1, WIDE // 2)
    def _(i):
        broadcast(i).wait_recv()
        pass_on(i).start()

    @pl.loop(0, WIDE // 2)
    def _(i):
        pass_on(i).wait_recv()

    feed(0, 2)

    def pass_one(q):
        return remote(
            one.at[pl.ds(1, 2), rows(q, ONE), :],
            mate_one.at[:, rows(q, ONE), :],
            e_sem.at[0, 3, q],
            e_sem.at[1, 3, q],
            {"wide": others[0]},
        )

    def pass_two(j, q):
        return remote(
            two.at[pl.ds(1, 2), rows(q, TWO), :],
            mate_two.at[j, :, rows(q, TWO), :],
            e_sem.at[0, j, q],
            e_sem.at[1, j, q],
            {"wide": others[j]},
        )

    pair = lax.broadcasted_iota(I32, (32, 64), 0) == lax.broadcasted_iota(I32, (32, 64), 1) // 2
    pair = jnp.where(pair, 1.0, 0.0).astype(BF16)
    load[4].wait()

    def project(q):
        firsts, seconds = [], []
        for ball in range(BALLS):
            real = mask_ref[pl.ds(q * BALLS + ball, 1), :] > 0
            means = pooled[q, ball].astype(F32)
            firsts.append(norm(means).astype(BF16))
            sums = means * pooling(real, 4)[1]
            high = sums.astype(BF16)
            rest = (sums - high.astype(F32)).astype(BF16)
            counted = jnp.maximum(pooling(real, 8)[1], 1.0)
            seconds.append(norm((dot(pair, high) + dot(pair, rest)) / counted).astype(BF16))
        firsts = jnp.concatenate(firsts, 0)
        seconds = jnp.concatenate(seconds, 0)
        for t in (1, 2):
            two[t, rows(q, TWO), :] = dot(seconds, w_ref[1, t]).astype(BF16)
            one[t, rows(q, ONE), :] = dot(firsts, w_ref[0, t]).astype(BF16)
        for j in (1, 2, 0):
            pass_two(j, q).start()
        pass_one(q).start()
        two[0, rows(q, TWO), :] = (dot(seconds, w_ref[1, 0]) * SCALE).astype(BF16)
        one[0, rows(q, ONE), :] = (dot(firsts, w_ref[0, 0]) * SCALE).astype(BF16)

    project(mp)
    for k in (1, 3, 2):

        @pl.loop(0, BALLS)
        def _(t):
            share(MP - k, t).wait_recv()

        project(peer(k))

    feed(2, 1)

    def hand_to(q, k, level):
        at = pl.ds(0, ONE) if level == 0 else pl.ds(ONE, TWO)
        return to_mp(mixed.at[q, at, :], all_mixed.at[at, cols(mp)], m_sem, k, level)

    def hand(k, level):
        return hand_to(peer(k), k, level)

    def keep_hand(level):
        at = pl.ds(0, ONE) if level == 0 else pl.ds(ONE, TWO)
        return pltpu.make_async_copy(
            mixed.at[mp, at, :], all_mixed.at[at, cols(mp)], own.at[2, level]
        )

    for j in range(3):
        flags(j).wait()

    def fill(keys_ref, values_ref, begin, src, first, flag):
        for c in range(src.shape[1] // 128):
            at = slice(c * 128, (c + 1) * 128)
            here = flag[first + c : first + c + 1, :] > 0
            keys, values = augment(src[0, at, :], src[1, at, :], columns_of(here))
            to = slice(begin + c * 128, begin + (c + 1) * 128)
            for head in range(2):
                keys_ref[head, to, :] = keys[head]
                values_ref[head, to, :] = values[head]

    def masked_of(keys_ref, at):
        spare = keys_ref[0, at, :].astype(F32)
        return jnp.min(jnp.where(lanes(256) == 64, spare, 0.0), -1, keepdims=True) < 0.0

    mine = keep_ref[...]
    fill(keys_one, values_one, 0, one.at[1:], 0, mine)

    @pl.loop(0, MP)
    def _(q):
        pass_one(q).wait()

    fill(keys_one, values_one, 4 * ONE, mate_one, 0, mate_keep[0])

    @pl.loop(1, MP + 1)
    def _(k):
        q = peer(k)
        at = rows(q, ONE)
        mixed[q, 0:ONE, :] = attend_pair(
            one[0, at, :], one[1, at, :], one[2, at, :], masked_of(keys_one, at),
            lambda head: keys_one[head], lambda head: values_one[head],
        )

        @pl.when(k < MP)
        def _():
            hand(k, 0).start()

    keep_hand(0).start()

    fill(keys_two, values_two, 0, two.at[1:], 8, mine)

    @pl.loop(0, MP)
    def _(q):
        for j in range(3):
            pass_two(j, q).wait()

    for j in range(3):
        fill(keys_two, values_two, (j + 1) * 4 * TWO, mate_two.at[j], 8, mate_keep[j])

    @pl.loop(0, 2)
    def _(p):
        at = rows(p, 256)
        both = attend_pair(
            two[0, at, :], two[1, at, :], two[2, at, :], masked_of(keys_two, at),
            lambda head: keys_two[head], lambda head: values_two[head],
        )
        for h in range(2):
            q = p * 2 + h
            k = lax.rem(q + MP - mp, MP)
            mixed[q, ONE:COARSE, :] = both[h * TWO : (h + 1) * TWO]

            @pl.when(k > 0)
            def _():
                hand_to(q, k, 1).start()

    keep_hand(1).start()

    feed(3, 1)

    load[5].wait()
    for level in range(2):
        keep_hand(level).wait()
        for k in (1, 3, 2):
            hand(k, level).wait()
    for level, begin, size in ((0, 0, 64), (1, ONE, 32)):
        span = slice(begin, begin + size * BALLS)
        total = jnp.zeros((size * BALLS, WIDTH), F32)
        for g in range(MP):
            total = total + dot(
                all_mixed[span, g * LOCAL : (g + 1) * LOCAL],
                lift_ref[g, level * LOCAL : (level + 1) * LOCAL, :],
            )
        total = total.astype(BF16)
        for ball in range(BALLS):
            at = slice(0, 64) if level == 0 else slice(64, 96)
            lifted[ball, at, :] = total[ball * size : (ball + 1) * size]

    def rise(k):
        return to_mp(lifted.at[:, :, cols(peer(k))], lifted_ref.at[pl.ds(mp * BALLS, BALLS)], l_sem, k, 0)

    for k in (2, 1, 3):
        rise(k).start()
    keep_rise = pltpu.make_async_copy(
        lifted.at[:, :, cols(mp)], lifted_ref.at[pl.ds(mp * BALLS, BALLS)], own.at[3, 0]
    )
    keep_rise.start()

    @pl.loop(0, BALLS)
    def _(t):
        keep_give(t).wait()
        for k in (1, 3, 2):
            turn(k, t).wait_send()
            share(k, t).wait_send()
            give(k, t).wait()

    @pl.loop(1, WIDE // 2)
    def _(i):
        broadcast(i).wait_send()

    @pl.loop(0, WIDE // 2)
    def _(i):
        pass_on(i).wait_send()

    for k in (1, 3, 2):
        fetch(k).wait_send()
    keep_rise.wait()
    for k in (1, 3, 2):
        rise(k).wait()

    runs = run_matrix(
        lax.broadcasted_iota(I32, (BALL, 96), 0), lax.broadcasted_iota(I32, (BALL, 96), 1)
    )

    @pl.loop(0, ROWS // BALL)
    def _(i):
        at = rows(i, BALL)
        wide[at, :] = turned_ref[at, :].astype(F32) + dot(runs, lifted_ref[i])

    wide[ROWS : ROWS + 8, :] = jnp.zeros((8, LOCAL), F32)

    def rows_copy(k):
        to = turn_of(me, k)
        return remote(
            outgoing.at[to], back_ref.at[me], r_sem.at[0, k], r_sem.at[1, k], {"wide": to}
        )

    @pl.loop(1, WIDE)
    def _(k):
        gather_bucket(0, lambda s: code_ref[s] >> 1, wide, staged, outgoing, turn_of(me, k))
        rows_copy(k).start()

    gather_bucket(0, lambda s: code_ref[s] >> 1, wide, staged, outgoing, me)
    last = pltpu.make_async_copy(outgoing.at[me], back_ref.at[me], own.at[3, 1])
    last.start()
    last.wait()

    @pl.loop(1, WIDE)
    def _(k):
        rows_copy(k).wait()


def middle(slots, codes, got, mask, keep, weights, collective):
    dma = pltpu.SemaphoreType.DMA
    return pl.pallas_call(
        middle_kernel,
        out_shape=shape((WIDE, CAP, LOCAL), BF16),
        in_specs=[SMEM, SMEM, VMEM, VMEM, VMEM] + [ANY] * 7,
        out_specs=ANY,
        scratch_shapes=[
            pltpu.VMEM((ROWS, LOCAL), BF16),
            pltpu.VMEM((MP * BALLS, 96, LOCAL), BF16),
            pltpu.VMEM((WIDE, CAP, LOCAL), BF16),
            dma((2, WIDE)),
            pltpu.VMEM((SLOTS, LOCAL), F32),
            pltpu.VMEM((1, CAP, LOCAL), F32),
            pltpu.VMEM((MP * BALLS, BALL, LOCAL), BF16),
            pltpu.VMEM((QUARTER, WIDTH), BF16),
            pltpu.VMEM((QUARTER, WIDTH), F32),
            pltpu.VMEM((MP, BALLS, 64, WIDTH), BF16),
            pltpu.VMEM((QUARTER, WIDTH), BF16),
            pltpu.VMEM((3, 4 * ONE, LOCAL), BF16),
            pltpu.VMEM((3, 4 * TWO, LOCAL), BF16),
            pltpu.VMEM((2, 4 * ONE, LOCAL), BF16),
            pltpu.VMEM((3, 2, 4 * TWO, LOCAL), BF16),
            pltpu.VMEM((3, 12, 128), I32),
            pltpu.VMEM((MP, COARSE, LOCAL), BF16),
            pltpu.VMEM((COARSE, WIDTH), BF16),
            pltpu.VMEM((BALLS, 96, WIDTH), BF16),
            pltpu.VMEM((2, 8 * ONE, LOCAL), BF16),
            pltpu.VMEM((2, 8 * ONE, LOCAL), BF16),
            pltpu.VMEM((2, 16 * TWO, LOCAL), BF16),
            pltpu.VMEM((2, 16 * TWO, LOCAL), BF16),
            pltpu.VMEM((3, WIDTH, WIDTH), BF16),
            pltpu.VMEM((WIDTH, WIDTH), BF16),
            pltpu.VMEM((MP, WIDTH, WIDTH), BF16),
            pltpu.VMEM((MP, WIDTH, WIDTH), BF16),
            pltpu.VMEM((MP, WIDTH, WIDTH), BF16),
            pltpu.VMEM((2, 3, WIDTH, LOCAL), BF16),
            pltpu.VMEM((MP, 2 * LOCAL, WIDTH), BF16),
            dma((2, MP, BALLS)),
            dma((2, MP, BALLS)),
            dma((2, 4, MP)),
            dma((2, 3)),
            dma((2, MP, 2)),
            dma((2, MP, BALLS)),
            dma((2, MP, 1)),
            dma((2, MP, 1)),
            dma((2, WIDE // 2)),
            dma((2, WIDE // 2)),
            dma((4, BALLS)),
            dma((7,)),
        ],
        compiler_params=params(collective),
    )(slots, codes, got, mask, keep, *weights)


def on_device(points, mask, perm, w_qkv, w_out, w_gate_up, w_down, w_coarse, w_coarse_out):
    slot, source, codes = index(perm, mask)
    own_gate_up = w_gate_up.reshape(2 * WIDTH, WIDTH)
    got, got_code, landed, owned_mask, keep, full_qkv, full_out, full_lift, full_down, full_gate = (
        send_rows(
            source.reshape(SLOTS),
            points,
            codes,
            [
                w_qkv.reshape(3 * WIDTH, LOCAL),
                w_out,
                w_coarse_out.reshape(2 * LOCAL, WIDTH),
                w_down,
                own_gate_up,
            ],
            1,
        )
    )
    full_qkv = full_qkv.reshape(3, WIDTH, WIDTH)
    full_out = full_out.reshape(WIDTH, WIDTH)
    returned = middle(
        landed.reshape(ROWS), got_code.reshape(SLOTS), got.reshape(SLOTS, LOCAL), owned_mask, keep,
        [full_qkv, full_out, own_gate_up, full_gate, full_down, w_coarse, full_lift], 2,
    )
    return pl.pallas_call(
        finish_kernel,
        out_shape=shape((ROWS, LOCAL), F32),
        in_specs=[SMEM, ANY],
        out_specs=ANY,
        scratch_shapes=[
            pltpu.VMEM((SLOTS, LOCAL), BF16),
            pltpu.VMEM((SLOTS, LOCAL), F32),
            pltpu.VMEM((ROWS, LOCAL), F32),
            pltpu.SemaphoreType.DMA((SLOTS // 1024,)),
            pltpu.SemaphoreType.DMA((ROWS // 512,)),
        ],
        compiler_params=params(),
    )(slot.reshape(ROWS), returned.reshape(SLOTS, LOCAL))


def solution(mesh):
    placed = (
        P("wide", "mp"),
        P("wide"),
        P("wide"),
        P(None, None, "mp"),
        P("mp", None),
        P(None, None, "mp"),
        P("mp", None),
        P(None, None, None, "mp"),
        P(None, "mp", None),
    )
    return jax.shard_map(
        on_device, mesh=mesh, in_specs=placed, out_specs=P("wide", "mp"), check_vma=False
    )
```

```python
import functools

import jax
import jax.numpy as jnp
from jax import lax
from jax.experimental import pallas as pl
from jax.experimental.pallas import tpu as pltpu
from jax.sharding import PartitionSpec as P

BALL = 256
WIDE = 32
MP = 4
ROWS = 4096
CAP = 256
SLOTS = WIDE * CAP
QUARTER = ROWS // MP
WIDTH = 512
LOCAL = WIDTH // MP
HIDDEN = 2048
ONE = QUARTER // 4
TWO = QUARTER // 8
COARSE = ONE + TWO
F32 = jnp.float32
BF16 = jnp.bfloat16
I32 = jnp.int32
MESH = pl.DeviceIdType.MESH
ANY = pl.BlockSpec(memory_space=pl.ANY)
VMEM = pl.BlockSpec(memory_space=pltpu.VMEM)
SMEM = pl.BlockSpec(memory_space=pltpu.SMEM)
LIMIT = 56 * 1024 * 1024


def shape(dims, kind):
    return jax.ShapeDtypeStruct(dims, kind)


def params(collective=None):
    if collective is None:
        return pltpu.CompilerParams(vmem_limit_bytes=LIMIT)
    return pltpu.CompilerParams(
        vmem_limit_bytes=LIMIT, collective_id=collective, has_side_effects=True
    )


def dot(a, b):
    return jnp.dot(a, b, preferred_element_type=F32)


def dot_t(a, b):
    return lax.dot_general(a, b, (((1,), (1,)), ((), ())), preferred_element_type=F32)


def norm(values):
    return values * lax.rsqrt(jnp.mean(values * values, -1, keepdims=True) + 1e-06)


UNROLL = 32
NONE = 2 * ROWS


def index_kernel(perm_ref, mask_ref, slot_ref, source_ref, codes_ref):
    perm = perm_ref[...]
    target = perm >> 12
    code = (perm & (ROWS - 1)) * 2 + mask_ref[...]
    rows = lax.broadcasted_iota(I32, (CAP, 128), 0)
    upper = jnp.where(
        lax.broadcasted_iota(I32, (128, 128), 0) < lax.broadcasted_iota(I32, (128, 128), 1), 1.0, 0.0
    ).astype(BF16)
    which = lax.broadcasted_iota(I32, (WIDE, 128), 0)
    lane = lax.broadcasted_iota(I32, (1, 128), 1).astype(F32)
    carry = jnp.zeros((WIDE, 1), F32)
    found = jnp.zeros((5 * WIDE, CAP), F32)
    for c in range(ROWS // 128):
        row = slice(c, c + 1)
        hot = jnp.where(which == target[row, :], 1.0, 0.0)
        before = dot(hot.astype(BF16), upper) + carry
        rank = jnp.sum(hot * before, 0, keepdims=True).astype(I32)
        slot_ref[row, :] = target[row, :] * CAP + rank
        carry = carry + jnp.sum(hot, 1, keepdims=True)
        placed = jnp.where(rows == rank, 1.0, 0.0).astype(BF16)
        high = (code[row, :] >> 6).astype(F32)
        low = (code[row, :] & 63).astype(F32)
        values = jnp.concatenate([hot * lane, hot * float(c), hot * high, hot * low, hot], 0)
        found = found + dot_t(values.astype(BF16), placed)
    source = (found[:WIDE] + found[WIDE : 2 * WIDE] * 128.0).astype(I32)
    codes = (found[2 * WIDE : 3 * WIDE] * 64.0 + found[3 * WIDE : 4 * WIDE]).astype(I32)
    codes = jnp.where(found[4 * WIDE :] > 0.5, codes, NONE)
    for h in range(2):
        at = slice(h * 128, (h + 1) * 128)
        source_ref[:, h, :] = source[:, at]
        codes_ref[:, h, :] = codes[:, at]


def index(perm, mask):
    return pl.pallas_call(
        index_kernel,
        out_shape=[shape((32, 128), I32), shape((WIDE, 2, 128), I32), shape((WIDE, 2, 128), I32)],
        in_specs=[VMEM] * 2,
        out_specs=[VMEM] * 3,
        compiler_params=params(),
    )(perm.reshape(32, 128), mask.reshape(32, 128))


def invert(codes_ref, slot_ref, mask_ref, keep_ref):
    balls = ROWS // BALL
    rows = lax.broadcasted_iota(I32, (256, 128), 0)
    which = lax.broadcasted_iota(I32, (balls, 128), 0)
    lane = lax.broadcasted_iota(I32, (1, 128), 1).astype(F32)
    found = jnp.zeros((3 * balls, 256), F32)
    for c in range(WIDE):
        for h in range(2):
            code = codes_ref[c, h : h + 1, :]
            landing = code >> 1
            hot = jnp.where(which == (landing >> 8), 1.0, 0.0)
            placed = jnp.where(rows == (landing & 255), 1.0, 0.0).astype(BF16)
            real = (code & 1).astype(F32)
            values = jnp.concatenate([hot * lane, hot * float(2 * c + h), hot * real], 0)
            found = found + dot_t(values.astype(BF16), placed)
    slots = (found[:balls] + found[balls : 2 * balls] * 128.0).astype(I32)
    for h in range(2):
        slot_ref[:, h, :] = slots[:, h * 128 : (h + 1) * 128]
    mask = found[2 * balls :]
    mask_ref[...] = mask.astype(I32)
    mask = mask.astype(BF16)
    for f, first in ((4, 0), (8, 8)):
        side = f // 2
        count = balls // side
        total = jnp.zeros((count, 128), F32)
        for j in range(side):
            r = lax.broadcasted_iota(I32, (count, balls), 0)
            c = lax.broadcasted_iota(I32, (count, balls), 1)
            pick = jnp.where(c == r * side + j, 1.0, 0.0).astype(BF16)
            r = lax.broadcasted_iota(I32, (256, 128), 0)
            c = lax.broadcasted_iota(I32, (256, 128), 1)
            runs = jnp.where(c == r // f + j * (128 // side), 1.0, 0.0).astype(BF16)
            total = total + dot(dot(pick, mask).astype(BF16), runs)
        keep_ref[first : first + count, :] = jnp.where(total > 0.5, 1, 0)


def run_matrix(r, c):
    hot = jnp.logical_or(
        jnp.logical_and(c < 64, r // 4 == c), jnp.logical_and(c >= 64, r // 8 == c - 64)
    )
    return jnp.where(hot, 1.0, 0.0).astype(BF16)


def widen(src, dst, rows):
    @pl.loop(0, rows // 256)
    def _(i):
        at = pl.ds(pl.multiple_of(i * 256, 256), 256)
        dst[at, :] = src[at, :].astype(dst.dtype)


def finish_kernel(slot_ref, got_ref, out_ref, narrow, wide, done, in_sem, out_sem):
    def chunk(ref, i, size):
        return ref.at[pl.ds(pl.multiple_of(i * size, size), size), :]

    def load(i):
        return pltpu.make_async_copy(chunk(got_ref, i, 1024), chunk(narrow, i, 1024), in_sem.at[i])

    def store(i):
        return pltpu.make_async_copy(chunk(done, i, 512), chunk(out_ref, i, 512), out_sem.at[i])

    for i in range(SLOTS // 1024):
        load(i).start()
    for i in range(SLOTS // 1024):
        load(i).wait()
        widen(chunk(narrow, i, 1024), chunk(wide, i, 1024), 1024)

    @pl.loop(0, ROWS // 512)
    def _(i):
        @pl.loop(0, 512 // UNROLL)
        def _(j):
            base = i * 512 + j * UNROLL
            lines = [wide[pl.ds(slot_ref[base + u], 1), :] for u in range(UNROLL)]
            for u in range(UNROLL):
                done[pl.ds(base + u, 1), :] = lines[u]

        store(i).start()

    @pl.loop(0, ROWS // 512)
    def _(i):
        store(i).wait()


def remote(src, dst, send, recv, device):
    return pltpu.make_async_remote_copy(
        src_ref=src, dst_ref=dst, send_sem=send, recv_sem=recv, device_id=device, device_id_type=MESH
    )


def turn_of(me, k):
    return lax.rem(me + lax.rem(k * 7, WIDE), WIDE)


def gather_bucket(line, lookup, wide, staged, packed, peer):
    @pl.loop(0, CAP // UNROLL)
    def _(i):
        begin = i * UNROLL
        lines = [wide[pl.ds(lookup(peer * CAP + begin + u), 1), :] for u in range(UNROLL)]
        for u in range(UNROLL):
            staged[line, pl.ds(begin + u, 1), :] = lines[u]

    packed[peer] = staged[line].astype(BF16)


def send_kernel(
    source_ref, points_ref, codes_ref, qkv_ref, out_ref, down_ref, gate_ref,
    got_ref, got_codes_out, slot_ref, mask_ref, keep_ref, all_qkv, all_out, all_down, all_gate,
    got_codes_ref, wide, staged, packed, send, recv, own, w_send, w_recv, w_own,
):
    me = lax.axis_index("wide")
    mp = lax.axis_index("mp")
    core = lax.rem(me, 2)
    partner = me + 1 - 2 * core
    after, ahead = lax.rem(mp + 1, MP), lax.rem(mp + 2, MP)
    behind = lax.rem(mp + 3, MP)
    barrier = pltpu.get_barrier_semaphore()

    @pl.loop(1, WIDE)
    def _(k):
        pl.semaphore_signal(
            barrier, inc=1, device_id={"wide": lax.rem(me + k, WIDE)}, device_id_type=MESH
        )

    for other in (after, behind):
        pl.semaphore_signal(barrier, inc=1, device_id={"mp": other}, device_id_type=MESH)
    widen(points_ref, wide, ROWS)

    def part(first, count):
        def rows(ref, quarter):
            return pl.ds(pl.multiple_of(first * quarter, 16), count * quarter)

        def cut(j, ref, shard):
            if j == 0:
                return ref.at[rows(ref, 384), pl.ds(pl.multiple_of(shard * 128, 128), 128)]
            quarter = (0, 32, 128, 128)[j]
            return ref.at[shard, rows(ref, quarter), :]

        def own_cut(j, ref):
            quarter = (384, 32, 128, 128)[j]
            return ref.at[rows(ref, quarter), :]

        return cut, own_cut

    half, own_half = part(2 * core, 2)
    first, _ = part(2 * core, 1)
    second, _ = part(2 * core + 1, 1)
    every, own_every = part(0, 4)
    shards = [qkv_ref, out_ref, down_ref, gate_ref]
    full = [all_qkv, all_out, all_down, all_gate]
    count = len(shards)

    def weight(j, kind, cut, src, shard, device):
        return remote(
            src, cut(j, full[j], shard), w_send.at[j, kind], w_recv.at[j, kind], device
        )

    def weight_copies(j):
        ref = full[j]
        mine = own_half(j, shards[j])
        return [
            weight(j, 0, half, mine, mp, {"mp": after}),
            weight(j, 1, half, mine, mp, {"mp": behind}),
            weight(j, 2, first, first(j, ref, behind), behind, {"mp": after}),
            weight(j, 3, second, second(j, ref, after), after, {"mp": behind}),
            weight(j, 4, half, half(j, ref, behind), behind, {"wide": partner}),
            weight(j, 5, half, half(j, ref, after), after, {"wide": partner}),
            weight(j, 6, first, first(j, ref, ahead), ahead, {"wide": partner}),
            weight(j, 7, second, second(j, ref, ahead), ahead, {"wide": partner}),
        ]

    weights = [weight_copies(j) for j in range(count)]

    def rows_copy(k):
        peer = turn_of(me, k)
        return remote(
            packed.at[peer], got_ref.at[me], send.at[k, 0], recv.at[k, 0], {"wide": peer}
        )

    def codes_copy(k):
        peer = turn_of(me, k)
        return remote(
            codes_ref.at[peer], got_codes_ref.at[me], send.at[k, 1], recv.at[k, 1], {"wide": peer}
        )

    pl.semaphore_wait(barrier, WIDE + 1)
    for j in range(count):
        weights[j][0].start()
        weights[j][1].start()

    @pl.loop(1, WIDE)
    def _(k):
        codes_copy(k).start()

    @pl.loop(1, WIDE)
    def _(k):
        gather_bucket(0, lambda s: source_ref[s], wide, staged, packed, turn_of(me, k))
        rows_copy(k).start()

    gather_bucket(0, lambda s: source_ref[s], wide, staged, packed, me)
    mine = [
        pltpu.make_async_copy(packed.at[me], got_ref.at[me], own.at[0]),
        pltpu.make_async_copy(codes_ref.at[me], got_codes_ref.at[me], own.at[1]),
    ]
    for j in range(count):
        mine.append(
            pltpu.make_async_copy(own_every(j, shards[j]), every(j, full[j], mp), w_own.at[j])
        )
    for copy in mine:
        copy.start()

    def forward(j):
        weights[j][0].wait_recv()
        weights[j][2].start()
        weights[j][4].start()
        weights[j][1].wait_recv()
        weights[j][3].start()
        weights[j][5].start()

    def forward_last(j):
        weights[j][2].wait_recv()
        weights[j][6].start()
        weights[j][3].wait_recv()
        weights[j][7].start()

    for j in range(count):
        forward(j)
    for copy in mine:
        copy.wait()

    @pl.loop(1, WIDE)
    def _(k):
        codes_copy(k).wait()

    invert(got_codes_ref, slot_ref, mask_ref, keep_ref)
    got_codes_out[...] = got_codes_ref[...]
    for j in range(count):
        forward_last(j)

    @pl.loop(1, WIDE)
    def _(k):
        rows_copy(k).wait()

    for j in range(count):
        for kind in range(4):
            weights[j][kind].wait_send()
        for kind in range(4, 8):
            weights[j][kind].wait()


def send_rows(source, points, codes, weights, collective):
    return pl.pallas_call(
        send_kernel,
        out_shape=[
            shape((WIDE, CAP, LOCAL), BF16),
            shape((WIDE, 2, 128), I32),
            shape((16, 2, 128), I32),
            shape((16, 256), I32),
            shape((12, 128), I32),
            shape((3 * WIDTH, WIDTH), BF16),
            shape((MP, LOCAL, WIDTH), BF16),
            shape((MP, WIDTH, WIDTH), BF16),
            shape((MP, WIDTH, WIDTH), BF16),
        ],
        in_specs=[SMEM, VMEM, ANY] + [VMEM] * 4,
        out_specs=[ANY] + [VMEM] * 4 + [ANY] * 4,
        scratch_shapes=[
            pltpu.VMEM((WIDE, 2, 128), I32),
            pltpu.VMEM((ROWS, LOCAL), F32),
            pltpu.VMEM((1, CAP, LOCAL), F32),
            pltpu.VMEM((WIDE, CAP, LOCAL), BF16),
            pltpu.SemaphoreType.DMA((WIDE, 2)),
            pltpu.SemaphoreType.DMA((WIDE, 2)),
            pltpu.SemaphoreType.DMA((2,)),
            pltpu.SemaphoreType.DMA((4, 8)),
            pltpu.SemaphoreType.DMA((4, 8)),
            pltpu.SemaphoreType.DMA((4,)),
        ],
        compiler_params=params(collective),
    )(source, points, codes, *weights)


SCALE = 0.125 * 1.4426950408889634


def lanes(count):
    return lax.broadcasted_iota(I32, (count, 128), 1)


def columns_of(flags):
    eye = lax.broadcasted_iota(I32, (128, 128), 0) == lax.broadcasted_iota(I32, (128, 128), 1)
    row = jnp.broadcast_to(jnp.where(flags, 1.0, 0.0), (128, 128)).astype(BF16)
    return dot_t(jnp.where(eye, 1.0, 0.0).astype(BF16), row)


def augment(keys, values, columns):
    lane = lanes(keys.shape[0])
    low = lane < 64
    bias = jnp.where(columns > 0.5, 0.0, -1e30)
    keys = keys.astype(F32)
    values = values.astype(F32)
    return (
        (
            jnp.where(low, keys, jnp.where(lane == 64, bias, 0.0)).astype(BF16),
            jnp.where(low, jnp.where(lane == 0, bias, 0.0), keys).astype(BF16),
        ),
        (jnp.where(low, values, 1.0).astype(BF16), jnp.where(low, 1.0, values).astype(BF16)),
    )


def attend_pair(queries, own_keys, own_values, masked, keys, values):
    count = queries.shape[0]
    lane = lanes(count)
    low = lane < 64
    queries = queries.astype(F32)
    own_keys = own_keys.astype(F32)
    own_values = own_values.astype(F32)
    out = []
    for head in range(2):
        mine = low if head == 0 else jnp.logical_not(low)
        spare = jnp.where(lane == (64 if head == 0 else 0), 1.0, 0.0)
        q = jnp.where(mine, queries, spare).astype(BF16)
        scores = dot_t(q, keys(head))
        alone = jnp.sum(jnp.where(mine, queries * own_keys, 0.0), -1, keepdims=True)
        top = jnp.maximum(jnp.max(scores, -1, keepdims=True), alone)
        weights = jnp.exp2(scores - top).astype(BF16)
        own = jnp.where(masked, jnp.exp2(alone - top), 0.0)
        total = dot(weights, values(head))
        out.append(total + own * jnp.where(mine, own_values, 1.0))
    sums = pltpu.roll(jnp.where(low, out[1], out[0]), 64, 1)
    return (jnp.where(low, out[0], out[1]) / sums).astype(BF16)


def attend_ball(queries, keys, values, allowed):
    low = lanes(BALL) < 64
    out = []
    for head in range(2):
        mine = low if head == 0 else jnp.logical_not(low)
        q = jnp.where(mine, queries, jnp.zeros_like(queries))
        scores = jnp.where(allowed, dot_t(q, keys), -1e30)
        weights = jnp.exp2(scores - jnp.max(scores, -1, keepdims=True))
        total = jnp.sum(weights, -1, keepdims=True)
        out.append(dot(weights.astype(BF16), values) / total)
    return jnp.where(low, out[0], out[1]).astype(BF16)


def fine_ball(x, real, qkv_ref, out_ref):
    x = x.astype(F32)
    normed = norm(x).astype(BF16)
    q = (dot(normed, qkv_ref[0]) * SCALE).astype(BF16)
    k = dot(normed, qkv_ref[1]).astype(BF16)
    v = dot(normed, qkv_ref[2]).astype(BF16)
    rows = lax.broadcasted_iota(I32, (BALL, BALL), 0)
    cols = lax.broadcasted_iota(I32, (BALL, BALL), 1)
    allowed = jnp.logical_or(real, rows == cols)
    mixed = []
    for g in range(MP):
        at = slice(g * 128, (g + 1) * 128)
        mixed.append(attend_ball(q[:, at], k[:, at], v[:, at], allowed))
    state = x + dot(jnp.concatenate(mixed, 1), out_ref[...])
    high = state.astype(BF16)
    rest = (state - high.astype(F32)).astype(BF16)
    runs, counted = pooling(real, 4)
    pooled = (dot(runs, high) + dot(runs, rest)) / jnp.maximum(counted, 1.0)
    return state, pooled.astype(BF16)


def pooling(real, factor):
    count_rows = BALL // factor
    r = lax.broadcasted_iota(I32, (count_rows, BALL), 0)
    c = lax.broadcasted_iota(I32, (count_rows, BALL), 1)
    hot = jnp.where(jnp.logical_and(r == c // factor, real), 1.0, 0.0)
    return hot.astype(BF16), jnp.sum(hot, 1, keepdims=True)


BALLS = QUARTER // BALL


def forward_tile(state, mp, gate_ref, up_ref, down_ref):
    normed = norm(state).astype(BF16)
    total = state
    for c in range(MP):
        shard = lax.rem(mp + c, MP)
        half = dot(normed, gate_ref[shard]) * 0.5
        up = dot(normed, up_ref[c])
        activated = ((half + half * jnp.tanh(half)) * up).astype(BF16)
        total = total + dot(activated, down_ref[shard])
    return total


def relatives(me):
    low = lax.rem(me, 2)
    high = lax.rem(me // 2, 2)
    first = me + 1 - 2 * low
    second = me + 2 - 4 * high
    third = first + 2 - 4 * high
    return (first, second, third)


def middle_kernel(
    slot_ref, code_ref, got_ref, mask_ref, keep_ref, qkv_hbm, out_hbm, gate_up_hbm, gate_hbm, down_hbm, coarse_hbm,
    lift_hbm, back_ref,
    turned_ref, lifted_ref, outgoing, r_sem,
    wide, staged, packed, x, state, pooled, tiles, one, two, mate_one, mate_two, mate_keep,
    mixed, all_mixed, lifted, keys_one, values_one, keys_two, values_two, qkv_ref, out_ref, gate_ref, up_ref, down_ref, w_ref, lift_ref,
    x_sem, p_sem, e_sem, k_sem, m_sem, t_sem, l_sem, g_sem, b_sem, f_sem, own, loads,
):
    me = lax.axis_index("wide")
    mp = lax.axis_index("mp")
    others = relatives(me)
    barrier = pltpu.get_barrier_semaphore()
    for k in range(1, MP):
        pl.semaphore_signal(
            barrier, inc=1, device_id={"mp": lax.rem(mp + k, MP)}, device_id_type=MESH
        )

    @pl.loop(1, WIDE)
    def _(k):
        pl.semaphore_signal(
            barrier, inc=1, device_id={"wide": lax.rem(me + k, WIDE)}, device_id_type=MESH
        )

    def chip(i):
        return 2 * lax.rem(i * 7, WIDE // 2)

    load = [
        pltpu.make_async_copy(src, dst, loads.at[j])
        for j, (src, dst) in enumerate([
            (qkv_hbm, qkv_ref),
            (out_hbm, out_ref),
            (gate_up_hbm.at[pl.ds(WIDTH, WIDTH), :], up_ref.at[0]),
            (down_hbm, down_ref),
            (coarse_hbm, w_ref),
            (lift_hbm, lift_ref.at[0]),
            (gate_hbm, gate_ref),
        ])
    ]
    for copy in load:
        copy.start()
    widen(got_ref, wide, SLOTS)
    pl.semaphore_wait(barrier, MP - 1 + WIDE - 1)

    def rows(t, size):
        return pl.ds(pl.multiple_of(t * size, size), size)

    def cols(g):
        return pl.ds(pl.multiple_of(g * LOCAL, LOCAL), LOCAL)

    def peer(k):
        return lax.rem(mp + k, MP)

    def to_mp(src, dst, sem, k, t):
        return remote(src, dst, sem.at[0, k, t], sem.at[1, k, t], {"mp": peer(k)})

    def piece(shards, owner):
        return up_ref.at[shards, pl.ds(pl.multiple_of(owner * 16, 16), 16), :]

    def lift_rows(owner):
        return pl.ds(pl.multiple_of(owner // 2 * 16, 16), 16)

    def lift_cols(owner):
        return pl.ds(pl.multiple_of(lax.rem(owner, 2) * 256, 256), 256)

    def lift_piece(shards, owner):
        return lift_ref.at[shards, lift_rows(owner), lift_cols(owner)]

    def fetch(k):
        src = gate_up_hbm.at[pl.ds(pl.multiple_of(WIDTH + me * 16, 16), 16), :]
        return to_mp(src, piece(MP - k, me), g_sem, k, 0)

    def fetch_lift(k):
        src = lift_hbm.at[lift_rows(me), lift_cols(me)]
        return to_mp(src, lift_piece(MP - k, me), g_sem, k, 1)

    def spread_to(part, i, t):
        to = {"wide": lax.rem(me + chip(i), WIDE)}
        return remote(part, part, b_sem.at[0, i, t], b_sem.at[1, i, t], to)

    def broadcast(i):
        return spread_to(piece(pl.ds(1, 3), me), i, 0)

    def broadcast_lift(i):
        return spread_to(lift_piece(pl.ds(1, 3), me), i, 1)

    def hand_over(part, i, t):
        return remote(part, part, f_sem.at[0, i, t], f_sem.at[1, i, t], {"wide": others[0]})

    def pass_on(i):
        return hand_over(piece(pl.ds(1, 3), lax.rem(me + WIDE - chip(i), WIDE)), i, 0)

    def pass_on_lift(i):
        return hand_over(lift_piece(pl.ds(1, 3), lax.rem(me + WIDE - chip(i), WIDE)), i, 1)

    for k in (2, 1, 3):
        fetch(k).start()
        fetch_lift(k).start()

    def turn(k, t):
        return to_mp(packed.at[peer(k) * BALLS + t], x.at[rows(t, BALL), cols(mp)], x_sem, k, t)

    def keep_turn(t):
        return pltpu.make_async_copy(
            packed.at[mp * BALLS + t], x.at[rows(t, BALL), cols(mp)], own.at[0, t]
        )

    def send_ball(t):
        for k in (2, 1, 3):
            gather_bucket(0, lambda s: slot_ref[s], wide, staged, packed, peer(k) * BALLS + t)
            turn(k, t).start()
        gather_bucket(0, lambda s: slot_ref[s], wide, staged, packed, mp * BALLS + t)
        keep_turn(t).start()

    send_ball(0)
    for k in (1, 3, 2):
        fetch(k).wait_recv()
        fetch_lift(k).wait_recv()

    @pl.loop(1, WIDE // 2)
    def _(i):
        broadcast(i).start()

    pass_on(0).start()

    @pl.loop(1, BALLS)
    def _(t):
        send_ball(t)

    @pl.loop(1, WIDE // 2)
    def _(i):
        broadcast_lift(i).start()

    pass_on_lift(0).start()

    def flags(j):
        return remote(
            keep_ref, mate_keep.at[j], k_sem.at[0, j], k_sem.at[1, j], {"wide": others[j]}
        )

    for j in range(3):
        flags(j).start()
    load[0].wait()
    load[1].wait()

    def share(k, t):
        return to_mp(pooled.at[mp, t], pooled.at[mp, t], p_sem, k, t)

    @pl.loop(0, BALLS)
    def _(t):
        for k in (1, 3, 2):
            turn(k, t).wait_recv()
        keep_turn(t).wait()
        real = mask_ref[pl.ds(mp * BALLS + t, 1), :] > 0
        out, means = fine_ball(x[rows(t, BALL), :], real, qkv_ref, out_ref)
        state[rows(t, BALL), :] = out
        pooled[mp, t] = means
        for k in (2, 1, 3):
            share(k, t).start()

    load[2].wait()
    load[3].wait()
    load[6].wait()

    def give(k, t):
        return to_mp(
            tiles.at[rows(t, BALL), cols(peer(k))],
            turned_ref.at[rows(mp * BALLS + t, BALL), :],
            t_sem,
            k,
            t,
        )

    def keep_give(t):
        return pltpu.make_async_copy(
            tiles.at[rows(t, BALL), cols(mp)],
            turned_ref.at[rows(mp * BALLS + t, BALL), :],
            own.at[1, t],
        )

    def feed(t, count):
        at = pl.ds(t * BALL, count * BALL)
        tiles[at, :] = forward_tile(state[at, :], mp, gate_ref, up_ref, down_ref).astype(BF16)
        for u in range(t, t + count):
            for k in (2, 1, 3):
                give(k, u).start()
            keep_give(u).start()

    @pl.loop(1, WIDE // 2)
    def _(i):
        broadcast(i).wait_recv()
        pass_on(i).start()

    @pl.loop(0, WIDE // 2)
    def _(i):
        pass_on(i).wait_recv()

    feed(0, 2)

    def pass_one(q):
        return remote(
            one.at[pl.ds(1, 2), rows(q, ONE), :],
            mate_one.at[:, rows(q, ONE), :],
            e_sem.at[0, 3, q],
            e_sem.at[1, 3, q],
            {"wide": others[0]},
        )

    def pass_two(j, q):
        return remote(
            two.at[pl.ds(1, 2), rows(q, TWO), :],
            mate_two.at[j, :, rows(q, TWO), :],
            e_sem.at[0, j, q],
            e_sem.at[1, j, q],
            {"wide": others[j]},
        )

    pair = lax.broadcasted_iota(I32, (32, 64), 0) == lax.broadcasted_iota(I32, (32, 64), 1) // 2
    pair = jnp.where(pair, 1.0, 0.0).astype(BF16)
    load[4].wait()

    def project(q):
        firsts, seconds = [], []
        for ball in range(BALLS):
            real = mask_ref[pl.ds(q * BALLS + ball, 1), :] > 0
            means = pooled[q, ball].astype(F32)
            firsts.append(norm(means).astype(BF16))
            sums = means * pooling(real, 4)[1]
            high = sums.astype(BF16)
            rest = (sums - high.astype(F32)).astype(BF16)
            counted = jnp.maximum(pooling(real, 8)[1], 1.0)
            seconds.append(norm((dot(pair, high) + dot(pair, rest)) / counted).astype(BF16))
        firsts = jnp.concatenate(firsts, 0)
        seconds = jnp.concatenate(seconds, 0)
        for t in (1, 2):
            two[t, rows(q, TWO), :] = dot(seconds, w_ref[1, t]).astype(BF16)
            one[t, rows(q, ONE), :] = dot(firsts, w_ref[0, t]).astype(BF16)
        for j in (1, 2, 0):
            pass_two(j, q).start()
        pass_one(q).start()
        two[0, rows(q, TWO), :] = (dot(seconds, w_ref[1, 0]) * SCALE).astype(BF16)
        one[0, rows(q, ONE), :] = (dot(firsts, w_ref[0, 0]) * SCALE).astype(BF16)

    project(mp)
    for k in (1, 3, 2):

        @pl.loop(0, BALLS)
        def _(t):
            share(MP - k, t).wait_recv()

        project(peer(k))

    feed(2, 1)

    @pl.loop(1, WIDE // 2)
    def _(i):
        broadcast_lift(i).wait_recv()
        pass_on_lift(i).start()


    def hand_to(q, k, level):
        at = pl.ds(0, ONE) if level == 0 else pl.ds(ONE, TWO)
        return to_mp(mixed.at[q, at, :], all_mixed.at[at, cols(mp)], m_sem, k, level)

    def hand(k, level):
        return hand_to(peer(k), k, level)

    def keep_hand(level):
        at = pl.ds(0, ONE) if level == 0 else pl.ds(ONE, TWO)
        return pltpu.make_async_copy(
            mixed.at[mp, at, :], all_mixed.at[at, cols(mp)], own.at[2, level]
        )

    for j in range(3):
        flags(j).wait()

    def fill(keys_ref, values_ref, begin, src, first, flag):
        for c in range(src.shape[1] // 128):
            at = slice(c * 128, (c + 1) * 128)
            here = flag[first + c : first + c + 1, :] > 0
            keys, values = augment(src[0, at, :], src[1, at, :], columns_of(here))
            to = slice(begin + c * 128, begin + (c + 1) * 128)
            for head in range(2):
                keys_ref[head, to, :] = keys[head]
                values_ref[head, to, :] = values[head]

    def masked_of(keys_ref, at):
        spare = keys_ref[0, at, :].astype(F32)
        return jnp.min(jnp.where(lanes(256) == 64, spare, 0.0), -1, keepdims=True) < 0.0

    mine = keep_ref[...]
    fill(keys_one, values_one, 0, one.at[1:], 0, mine)

    @pl.loop(0, MP)
    def _(q):
        pass_one(q).wait()

    fill(keys_one, values_one, 4 * ONE, mate_one, 0, mate_keep[0])

    @pl.loop(1, MP + 1)
    def _(k):
        q = peer(k)
        at = rows(q, ONE)
        mixed[q, 0:ONE, :] = attend_pair(
            one[0, at, :], one[1, at, :], one[2, at, :], masked_of(keys_one, at),
            lambda head: keys_one[head], lambda head: values_one[head],
        )

        @pl.when(k < MP)
        def _():
            hand(k, 0).start()

    keep_hand(0).start()

    fill(keys_two, values_two, 0, two.at[1:], 8, mine)

    @pl.loop(0, MP)
    def _(q):
        for j in range(3):
            pass_two(j, q).wait()

    for j in range(3):
        fill(keys_two, values_two, (j + 1) * 4 * TWO, mate_two.at[j], 8, mate_keep[j])

    @pl.loop(0, 2)
    def _(p):
        at = rows(p, 256)
        both = attend_pair(
            two[0, at, :], two[1, at, :], two[2, at, :], masked_of(keys_two, at),
            lambda head: keys_two[head], lambda head: values_two[head],
        )
        for h in range(2):
            q = p * 2 + h
            k = lax.rem(q + MP - mp, MP)
            mixed[q, ONE:COARSE, :] = both[h * TWO : (h + 1) * TWO]

            @pl.when(k > 0)
            def _():
                hand_to(q, k, 1).start()

    keep_hand(1).start()

    feed(3, 1)

    load[5].wait()

    @pl.loop(0, WIDE // 2)
    def _(i):
        pass_on_lift(i).wait_recv()

    for level in range(2):
        keep_hand(level).wait()
        for k in (1, 3, 2):
            hand(k, level).wait()
    for level, begin, size in ((0, 0, 64), (1, ONE, 32)):
        span = slice(begin, begin + size * BALLS)
        total = jnp.zeros((size * BALLS, WIDTH), F32)
        for g in range(MP):
            total = total + dot(
                all_mixed[span, cols(peer(g))],
                lift_ref[g, level * LOCAL : (level + 1) * LOCAL, :],
            )
        total = total.astype(BF16)
        for ball in range(BALLS):
            at = slice(0, 64) if level == 0 else slice(64, 96)
            lifted[ball, at, :] = total[ball * size : (ball + 1) * size]

    def rise(k):
        return to_mp(lifted.at[:, :, cols(peer(k))], lifted_ref.at[pl.ds(mp * BALLS, BALLS)], l_sem, k, 0)

    for k in (2, 1, 3):
        rise(k).start()
    keep_rise = pltpu.make_async_copy(
        lifted.at[:, :, cols(mp)], lifted_ref.at[pl.ds(mp * BALLS, BALLS)], own.at[3, 0]
    )
    keep_rise.start()

    @pl.loop(0, BALLS)
    def _(t):
        keep_give(t).wait()
        for k in (1, 3, 2):
            turn(k, t).wait_send()
            share(k, t).wait_send()
            give(k, t).wait()

    @pl.loop(1, WIDE // 2)
    def _(i):
        broadcast(i).wait_send()
        broadcast_lift(i).wait_send()

    @pl.loop(0, WIDE // 2)
    def _(i):
        pass_on(i).wait_send()
        pass_on_lift(i).wait_send()

    for k in (1, 3, 2):
        fetch(k).wait_send()
        fetch_lift(k).wait_send()
    keep_rise.wait()
    for k in (1, 3, 2):
        rise(k).wait()

    runs = run_matrix(
        lax.broadcasted_iota(I32, (BALL, 96), 0), lax.broadcasted_iota(I32, (BALL, 96), 1)
    )

    @pl.loop(0, ROWS // BALL)
    def _(i):
        at = rows(i, BALL)
        wide[at, :] = turned_ref[at, :].astype(F32) + dot(runs, lifted_ref[i])

    wide[ROWS : ROWS + 8, :] = jnp.zeros((8, LOCAL), F32)

    def rows_copy(k):
        to = turn_of(me, k)
        return remote(
            outgoing.at[to], back_ref.at[me], r_sem.at[0, k], r_sem.at[1, k], {"wide": to}
        )

    @pl.loop(1, WIDE)
    def _(k):
        gather_bucket(0, lambda s: code_ref[s] >> 1, wide, staged, outgoing, turn_of(me, k))
        rows_copy(k).start()

    gather_bucket(0, lambda s: code_ref[s] >> 1, wide, staged, outgoing, me)
    last = pltpu.make_async_copy(outgoing.at[me], back_ref.at[me], own.at[3, 1])
    last.start()
    last.wait()

    @pl.loop(1, WIDE)
    def _(k):
        rows_copy(k).wait()


def middle(slots, codes, got, mask, keep, weights, collective):
    dma = pltpu.SemaphoreType.DMA
    return pl.pallas_call(
        middle_kernel,
        out_shape=shape((WIDE, CAP, LOCAL), BF16),
        in_specs=[SMEM, SMEM, VMEM, VMEM, VMEM] + [ANY] * 7,
        out_specs=ANY,
        scratch_shapes=[
            pltpu.VMEM((ROWS, LOCAL), BF16),
            pltpu.VMEM((MP * BALLS, 96, LOCAL), BF16),
            pltpu.VMEM((WIDE, CAP, LOCAL), BF16),
            dma((2, WIDE)),
            pltpu.VMEM((SLOTS, LOCAL), F32),
            pltpu.VMEM((1, CAP, LOCAL), F32),
            pltpu.VMEM((MP * BALLS, BALL, LOCAL), BF16),
            pltpu.VMEM((QUARTER, WIDTH), BF16),
            pltpu.VMEM((QUARTER, WIDTH), F32),
            pltpu.VMEM((MP, BALLS, 64, WIDTH), BF16),
            pltpu.VMEM((QUARTER, WIDTH), BF16),
            pltpu.VMEM((3, 4 * ONE, LOCAL), BF16),
            pltpu.VMEM((3, 4 * TWO, LOCAL), BF16),
            pltpu.VMEM((2, 4 * ONE, LOCAL), BF16),
            pltpu.VMEM((3, 2, 4 * TWO, LOCAL), BF16),
            pltpu.VMEM((3, 12, 128), I32),
            pltpu.VMEM((MP, COARSE, LOCAL), BF16),
            pltpu.VMEM((COARSE, WIDTH), BF16),
            pltpu.VMEM((BALLS, 96, WIDTH), BF16),
            pltpu.VMEM((2, 8 * ONE, LOCAL), BF16),
            pltpu.VMEM((2, 8 * ONE, LOCAL), BF16),
            pltpu.VMEM((2, 16 * TWO, LOCAL), BF16),
            pltpu.VMEM((2, 16 * TWO, LOCAL), BF16),
            pltpu.VMEM((3, WIDTH, WIDTH), BF16),
            pltpu.VMEM((WIDTH, WIDTH), BF16),
            pltpu.VMEM((MP, WIDTH, WIDTH), BF16),
            pltpu.VMEM((MP, WIDTH, WIDTH), BF16),
            pltpu.VMEM((MP, WIDTH, WIDTH), BF16),
            pltpu.VMEM((2, 3, WIDTH, LOCAL), BF16),
            pltpu.VMEM((MP, 2 * LOCAL, WIDTH), BF16),
            dma((2, MP, BALLS)),
            dma((2, MP, BALLS)),
            dma((2, 4, MP)),
            dma((2, 3)),
            dma((2, MP, 2)),
            dma((2, MP, BALLS)),
            dma((2, MP, 1)),
            dma((2, MP, 2)),
            dma((2, WIDE // 2, 2)),
            dma((2, WIDE // 2, 2)),
            dma((4, BALLS)),
            dma((7,)),
        ],
        compiler_params=params(collective),
    )(slots, codes, got, mask, keep, *weights)


def on_device(points, mask, perm, w_qkv, w_out, w_gate_up, w_down, w_coarse, w_coarse_out):
    slot, source, codes = index(perm, mask)
    own_gate_up = w_gate_up.reshape(2 * WIDTH, WIDTH)
    own_lift = w_coarse_out.reshape(2 * LOCAL, WIDTH)
    got, got_code, landed, owned_mask, keep, full_qkv, full_out, full_down, full_gate = (
        send_rows(
            source.reshape(SLOTS),
            points,
            codes,
            [
                w_qkv.reshape(3 * WIDTH, LOCAL),
                w_out,
                w_down,
                own_gate_up,
            ],
            1,
        )
    )
    full_qkv = full_qkv.reshape(3, WIDTH, WIDTH)
    full_out = full_out.reshape(WIDTH, WIDTH)
    returned = middle(
        landed.reshape(ROWS), got_code.reshape(SLOTS), got.reshape(SLOTS, LOCAL), owned_mask, keep,
        [full_qkv, full_out, own_gate_up, full_gate, full_down, w_coarse, own_lift], 2,
    )
    return pl.pallas_call(
        finish_kernel,
        out_shape=shape((ROWS, LOCAL), F32),
        in_specs=[SMEM, ANY],
        out_specs=ANY,
        scratch_shapes=[
            pltpu.VMEM((SLOTS, LOCAL), BF16),
            pltpu.VMEM((SLOTS, LOCAL), F32),
            pltpu.VMEM((ROWS, LOCAL), F32),
            pltpu.SemaphoreType.DMA((SLOTS // 1024,)),
            pltpu.SemaphoreType.DMA((ROWS // 512,)),
        ],
        compiler_params=params(),
    )(slot.reshape(ROWS), returned.reshape(SLOTS, LOCAL))


def solution(mesh):
    placed = (
        P("wide", "mp"),
        P("wide"),
        P("wide"),
        P(None, None, "mp"),
        P("mp", None),
        P(None, None, "mp"),
        P("mp", None),
        P(None, None, None, "mp"),
        P(None, "mp", None),
    )
    return jax.shard_map(
        on_device, mesh=mesh, in_specs=placed, out_specs=P("wide", "mp"), check_vma=False
    )
```

```python
import functools

import jax
import jax.numpy as jnp
from jax import lax
from jax.experimental import pallas as pl
from jax.experimental.pallas import tpu as pltpu
from jax.sharding import PartitionSpec as P

BALL = 256
WIDE = 32
MP = 4
ROWS = 4096
CAP = 256
SLOTS = WIDE * CAP
QUARTER = ROWS // MP
WIDTH = 512
LOCAL = WIDTH // MP
HIDDEN = 2048
ONE = QUARTER // 4
TWO = QUARTER // 8
COARSE = ONE + TWO
F32 = jnp.float32
BF16 = jnp.bfloat16
I32 = jnp.int32
MESH = pl.DeviceIdType.MESH
ANY = pl.BlockSpec(memory_space=pl.ANY)
VMEM = pl.BlockSpec(memory_space=pltpu.VMEM)
SMEM = pl.BlockSpec(memory_space=pltpu.SMEM)
LIMIT = 56 * 1024 * 1024


def shape(dims, kind):
    return jax.ShapeDtypeStruct(dims, kind)


def params(collective=None):
    if collective is None:
        return pltpu.CompilerParams(vmem_limit_bytes=LIMIT)
    return pltpu.CompilerParams(
        vmem_limit_bytes=LIMIT, collective_id=collective, has_side_effects=True
    )


def dot(a, b):
    return jnp.dot(a, b, preferred_element_type=F32)


def dot_t(a, b):
    return lax.dot_general(a, b, (((1,), (1,)), ((), ())), preferred_element_type=F32)


def norm(values):
    return values * lax.rsqrt(jnp.mean(values * values, -1, keepdims=True) + 1e-06)


UNROLL = 32
NONE = 2 * ROWS


def index_kernel(perm_ref, mask_ref, slot_ref, source_ref, codes_ref):
    perm = perm_ref[...]
    target = perm >> 12
    code = (perm & (ROWS - 1)) * 2 + mask_ref[...]
    rows = lax.broadcasted_iota(I32, (CAP, 128), 0)
    upper = jnp.where(
        lax.broadcasted_iota(I32, (128, 128), 0) < lax.broadcasted_iota(I32, (128, 128), 1), 1.0, 0.0
    ).astype(BF16)
    which = lax.broadcasted_iota(I32, (WIDE, 128), 0)
    lane = lax.broadcasted_iota(I32, (1, 128), 1).astype(F32)
    carry = jnp.zeros((WIDE, 1), F32)
    found = jnp.zeros((5 * WIDE, CAP), F32)
    for c in range(ROWS // 128):
        row = slice(c, c + 1)
        hot = jnp.where(which == target[row, :], 1.0, 0.0)
        before = dot(hot.astype(BF16), upper) + carry
        rank = jnp.sum(hot * before, 0, keepdims=True).astype(I32)
        slot_ref[row, :] = target[row, :] * CAP + rank
        carry = carry + jnp.sum(hot, 1, keepdims=True)
        placed = jnp.where(rows == rank, 1.0, 0.0).astype(BF16)
        high = (code[row, :] >> 6).astype(F32)
        low = (code[row, :] & 63).astype(F32)
        values = jnp.concatenate([hot * lane, hot * float(c), hot * high, hot * low, hot], 0)
        found = found + dot_t(values.astype(BF16), placed)
    source = (found[:WIDE] + found[WIDE : 2 * WIDE] * 128.0).astype(I32)
    codes = (found[2 * WIDE : 3 * WIDE] * 64.0 + found[3 * WIDE : 4 * WIDE]).astype(I32)
    codes = jnp.where(found[4 * WIDE :] > 0.5, codes, NONE)
    for h in range(2):
        at = slice(h * 128, (h + 1) * 128)
        source_ref[:, h, :] = source[:, at]
        codes_ref[:, h, :] = codes[:, at]


def index(perm, mask):
    return pl.pallas_call(
        index_kernel,
        out_shape=[shape((32, 128), I32), shape((WIDE, 2, 128), I32), shape((WIDE, 2, 128), I32)],
        in_specs=[VMEM] * 2,
        out_specs=[VMEM] * 3,
        compiler_params=params(),
    )(perm.reshape(32, 128), mask.reshape(32, 128))


def invert(codes_ref, slot_ref, mask_ref, keep_ref):
    balls = ROWS // BALL
    rows = lax.broadcasted_iota(I32, (256, 128), 0)
    which = lax.broadcasted_iota(I32, (balls, 128), 0)
    lane = lax.broadcasted_iota(I32, (1, 128), 1).astype(F32)
    found = jnp.zeros((3 * balls, 256), F32)
    for c in range(WIDE):
        for h in range(2):
            code = codes_ref[c, h : h + 1, :]
            landing = code >> 1
            hot = jnp.where(which == (landing >> 8), 1.0, 0.0)
            placed = jnp.where(rows == (landing & 255), 1.0, 0.0).astype(BF16)
            real = (code & 1).astype(F32)
            values = jnp.concatenate([hot * lane, hot * float(2 * c + h), hot * real], 0)
            found = found + dot_t(values.astype(BF16), placed)
    slots = (found[:balls] + found[balls : 2 * balls] * 128.0).astype(I32)
    for h in range(2):
        slot_ref[:, h, :] = slots[:, h * 128 : (h + 1) * 128]
    mask = found[2 * balls :]
    mask_ref[...] = mask.astype(I32)
    mask = mask.astype(BF16)
    for f, first in ((4, 0), (8, 8)):
        side = f // 2
        count = balls // side
        total = jnp.zeros((count, 128), F32)
        for j in range(side):
            r = lax.broadcasted_iota(I32, (count, balls), 0)
            c = lax.broadcasted_iota(I32, (count, balls), 1)
            pick = jnp.where(c == r * side + j, 1.0, 0.0).astype(BF16)
            r = lax.broadcasted_iota(I32, (256, 128), 0)
            c = lax.broadcasted_iota(I32, (256, 128), 1)
            runs = jnp.where(c == r // f + j * (128 // side), 1.0, 0.0).astype(BF16)
            total = total + dot(dot(pick, mask).astype(BF16), runs)
        keep_ref[first : first + count, :] = jnp.where(total > 0.5, 1, 0)


def run_matrix(r, c):
    hot = jnp.logical_or(
        jnp.logical_and(c < 64, r // 4 == c), jnp.logical_and(c >= 64, r // 8 == c - 64)
    )
    return jnp.where(hot, 1.0, 0.0).astype(BF16)


def widen(src, dst, rows):
    @pl.loop(0, rows // 256)
    def _(i):
        at = pl.ds(pl.multiple_of(i * 256, 256), 256)
        dst[at, :] = src[at, :].astype(dst.dtype)


def finish_kernel(slot_ref, got_ref, out_ref, narrow, wide, done, in_sem, out_sem):
    def chunk(ref, i, size):
        return ref.at[pl.ds(pl.multiple_of(i * size, size), size), :]

    def load(i):
        return pltpu.make_async_copy(chunk(got_ref, i, 1024), chunk(narrow, i, 1024), in_sem.at[i])

    def store(i):
        return pltpu.make_async_copy(chunk(done, i, 512), chunk(out_ref, i, 512), out_sem.at[i])

    for i in range(SLOTS // 1024):
        load(i).start()
    for i in range(SLOTS // 1024):
        load(i).wait()
        widen(chunk(narrow, i, 1024), chunk(wide, i, 1024), 1024)

    @pl.loop(0, ROWS // 512)
    def _(i):
        @pl.loop(0, 512 // UNROLL)
        def _(j):
            base = i * 512 + j * UNROLL
            lines = [wide[pl.ds(slot_ref[base + u], 1), :] for u in range(UNROLL)]
            for u in range(UNROLL):
                done[pl.ds(base + u, 1), :] = lines[u]

        store(i).start()

    @pl.loop(0, ROWS // 512)
    def _(i):
        store(i).wait()


def remote(src, dst, send, recv, device):
    return pltpu.make_async_remote_copy(
        src_ref=src, dst_ref=dst, send_sem=send, recv_sem=recv, device_id=device, device_id_type=MESH
    )


def turn_of(me, k):
    return lax.rem(me + lax.rem(k * 7, WIDE), WIDE)


def gather_bucket(line, lookup, wide, staged, packed, peer):
    @pl.loop(0, CAP // UNROLL)
    def _(i):
        begin = i * UNROLL
        lines = [wide[pl.ds(lookup(peer * CAP + begin + u), 1), :] for u in range(UNROLL)]
        for u in range(UNROLL):
            staged[line, pl.ds(begin + u, 1), :] = lines[u]

    packed[peer] = staged[line].astype(BF16)


def send_kernel(
    source_ref, points_ref, codes_ref, qkv_ref, out_ref, down_ref, gate_ref,
    got_ref, got_codes_out, slot_ref, mask_ref, keep_ref, all_qkv, all_out, all_down, all_gate,
    got_codes_ref, wide, staged, packed, send, recv, own, w_send, w_recv, w_own,
):
    me = lax.axis_index("wide")
    mp = lax.axis_index("mp")
    core = lax.rem(me, 2)
    partner = me + 1 - 2 * core
    after, ahead = lax.rem(mp + 1, MP), lax.rem(mp + 2, MP)
    behind = lax.rem(mp + 3, MP)
    barrier = pltpu.get_barrier_semaphore()

    @pl.loop(1, WIDE)
    def _(k):
        pl.semaphore_signal(
            barrier, inc=1, device_id={"wide": lax.rem(me + k, WIDE)}, device_id_type=MESH
        )

    for other in (after, behind):
        pl.semaphore_signal(barrier, inc=1, device_id={"mp": other}, device_id_type=MESH)
    widen(points_ref, wide, ROWS)

    def part(first, count):
        def rows(ref, quarter):
            return pl.ds(pl.multiple_of(first * quarter, 16), count * quarter)

        def cut(j, ref, shard):
            if j == 0:
                return ref.at[rows(ref, 384), pl.ds(pl.multiple_of(shard * 128, 128), 128)]
            quarter = (0, 32, 128, 128)[j]
            return ref.at[shard, rows(ref, quarter), :]

        def own_cut(j, ref):
            quarter = (384, 32, 128, 128)[j]
            return ref.at[rows(ref, quarter), :]

        return cut, own_cut

    half, own_half = part(2 * core, 2)
    first, _ = part(2 * core, 1)
    second, _ = part(2 * core + 1, 1)
    every, own_every = part(0, 4)
    shards = [qkv_ref, out_ref, down_ref, gate_ref]
    full = [all_qkv, all_out, all_down, all_gate]
    count = len(shards)

    def weight(j, kind, cut, src, shard, device):
        return remote(
            src, cut(j, full[j], shard), w_send.at[j, kind], w_recv.at[j, kind], device
        )

    def weight_copies(j):
        ref = full[j]
        mine = own_half(j, shards[j])
        return [
            weight(j, 0, half, mine, mp, {"mp": after}),
            weight(j, 1, half, mine, mp, {"mp": behind}),
            weight(j, 2, first, first(j, ref, behind), behind, {"mp": after}),
            weight(j, 3, second, second(j, ref, after), after, {"mp": behind}),
            weight(j, 4, half, half(j, ref, behind), behind, {"wide": partner}),
            weight(j, 5, half, half(j, ref, after), after, {"wide": partner}),
            weight(j, 6, first, first(j, ref, ahead), ahead, {"wide": partner}),
            weight(j, 7, second, second(j, ref, ahead), ahead, {"wide": partner}),
        ]

    weights = [weight_copies(j) for j in range(count)]

    def rows_copy(k):
        peer = turn_of(me, k)
        return remote(
            packed.at[peer], got_ref.at[me], send.at[k, 0], recv.at[k, 0], {"wide": peer}
        )

    def codes_copy(k):
        peer = turn_of(me, k)
        return remote(
            codes_ref.at[peer], got_codes_ref.at[me], send.at[k, 1], recv.at[k, 1], {"wide": peer}
        )

    pl.semaphore_wait(barrier, WIDE + 1)
    for j in range(count):
        weights[j][0].start()
        weights[j][1].start()

    @pl.loop(1, WIDE)
    def _(k):
        codes_copy(k).start()

    @pl.loop(1, WIDE)
    def _(k):
        gather_bucket(0, lambda s: source_ref[s], wide, staged, packed, turn_of(me, k))
        rows_copy(k).start()

    gather_bucket(0, lambda s: source_ref[s], wide, staged, packed, me)
    mine = [
        pltpu.make_async_copy(packed.at[me], got_ref.at[me], own.at[0]),
        pltpu.make_async_copy(codes_ref.at[me], got_codes_ref.at[me], own.at[1]),
    ]
    for j in range(count):
        mine.append(
            pltpu.make_async_copy(own_every(j, shards[j]), every(j, full[j], mp), w_own.at[j])
        )
    for copy in mine:
        copy.start()

    def forward(j):
        weights[j][0].wait_recv()
        weights[j][2].start()
        weights[j][4].start()
        weights[j][1].wait_recv()
        weights[j][3].start()
        weights[j][5].start()

    def forward_last(j):
        weights[j][2].wait_recv()
        weights[j][6].start()
        weights[j][3].wait_recv()
        weights[j][7].start()

    for j in range(count):
        forward(j)
    for copy in mine:
        copy.wait()

    @pl.loop(1, WIDE)
    def _(k):
        codes_copy(k).wait()

    invert(got_codes_ref, slot_ref, mask_ref, keep_ref)
    got_codes_out[...] = got_codes_ref[...]
    for j in range(count):
        forward_last(j)

    @pl.loop(1, WIDE)
    def _(k):
        rows_copy(k).wait()

    for j in range(count):
        for kind in range(4):
            weights[j][kind].wait_send()
        for kind in range(4, 8):
            weights[j][kind].wait()


def send_rows(source, points, codes, weights, collective):
    return pl.pallas_call(
        send_kernel,
        out_shape=[
            shape((WIDE, CAP, LOCAL), BF16),
            shape((WIDE, 2, 128), I32),
            shape((16, 2, 128), I32),
            shape((16, 256), I32),
            shape((12, 128), I32),
            shape((3 * WIDTH, WIDTH), BF16),
            shape((MP, LOCAL, WIDTH), BF16),
            shape((MP, WIDTH, WIDTH), BF16),
            shape((MP, WIDTH, WIDTH), BF16),
        ],
        in_specs=[SMEM, VMEM, ANY] + [VMEM] * 4,
        out_specs=[ANY] + [VMEM] * 4 + [ANY] * 4,
        scratch_shapes=[
            pltpu.VMEM((WIDE, 2, 128), I32),
            pltpu.VMEM((ROWS, LOCAL), F32),
            pltpu.VMEM((1, CAP, LOCAL), F32),
            pltpu.VMEM((WIDE, CAP, LOCAL), BF16),
            pltpu.SemaphoreType.DMA((WIDE, 2)),
            pltpu.SemaphoreType.DMA((WIDE, 2)),
            pltpu.SemaphoreType.DMA((2,)),
            pltpu.SemaphoreType.DMA((4, 8)),
            pltpu.SemaphoreType.DMA((4, 8)),
            pltpu.SemaphoreType.DMA((4,)),
        ],
        compiler_params=params(collective),
    )(source, points, codes, *weights)


SCALE = 0.125 * 1.4426950408889634


def lanes(count):
    return lax.broadcasted_iota(I32, (count, 128), 1)


def columns_of(flags):
    eye = lax.broadcasted_iota(I32, (128, 128), 0) == lax.broadcasted_iota(I32, (128, 128), 1)
    row = jnp.broadcast_to(jnp.where(flags, 1.0, 0.0), (128, 128)).astype(BF16)
    return dot_t(jnp.where(eye, 1.0, 0.0).astype(BF16), row)


def augment(keys, values, columns):
    lane = lanes(keys.shape[0])
    low = lane < 64
    bias = jnp.where(columns > 0.5, 0.0, -1e30)
    keys = keys.astype(F32)
    values = values.astype(F32)
    return (
        (
            jnp.where(low, keys, jnp.where(lane == 64, bias, 0.0)).astype(BF16),
            jnp.where(low, jnp.where(lane == 0, bias, 0.0), keys).astype(BF16),
        ),
        (jnp.where(low, values, 1.0).astype(BF16), jnp.where(low, 1.0, values).astype(BF16)),
    )


def attend_pair(queries, own_keys, own_values, masked, keys, values):
    count = queries.shape[0]
    lane = lanes(count)
    low = lane < 64
    queries = queries.astype(F32)
    own_keys = own_keys.astype(F32)
    own_values = own_values.astype(F32)
    out = []
    for head in range(2):
        mine = low if head == 0 else jnp.logical_not(low)
        spare = jnp.where(lane == (64 if head == 0 else 0), 1.0, 0.0)
        q = jnp.where(mine, queries, spare).astype(BF16)
        scores = dot_t(q, keys(head))
        alone = jnp.sum(jnp.where(mine, queries * own_keys, 0.0), -1, keepdims=True)
        top = jnp.maximum(jnp.max(scores, -1, keepdims=True), alone)
        weights = jnp.exp2(scores - top).astype(BF16)
        own = jnp.where(masked, jnp.exp2(alone - top), 0.0)
        total = dot(weights, values(head))
        out.append(total + own * jnp.where(mine, own_values, 1.0))
    sums = pltpu.roll(jnp.where(low, out[1], out[0]), 64, 1)
    return (jnp.where(low, out[0], out[1]) / sums).astype(BF16)


def attend_ball(queries, keys, values, allowed):
    low = lanes(BALL) < 64
    out = []
    for head in range(2):
        mine = low if head == 0 else jnp.logical_not(low)
        q = jnp.where(mine, queries, jnp.zeros_like(queries))
        scores = jnp.where(allowed, dot_t(q, keys), -1e30)
        weights = jnp.exp2(scores - jnp.max(scores, -1, keepdims=True))
        total = jnp.sum(weights, -1, keepdims=True)
        out.append(dot(weights.astype(BF16), values) / total)
    return jnp.where(low, out[0], out[1]).astype(BF16)


def fine_ball(x, real, qkv_ref, out_ref):
    x = x.astype(F32)
    normed = norm(x).astype(BF16)
    q = (dot(normed, qkv_ref[0]) * SCALE).astype(BF16)
    k = dot(normed, qkv_ref[1]).astype(BF16)
    v = dot(normed, qkv_ref[2]).astype(BF16)
    rows = lax.broadcasted_iota(I32, (BALL, BALL), 0)
    cols = lax.broadcasted_iota(I32, (BALL, BALL), 1)
    allowed = jnp.logical_or(real, rows == cols)
    mixed = []
    for g in range(MP):
        at = slice(g * 128, (g + 1) * 128)
        mixed.append(attend_ball(q[:, at], k[:, at], v[:, at], allowed))
    state = x + dot(jnp.concatenate(mixed, 1), out_ref[...])
    high = state.astype(BF16)
    rest = (state - high.astype(F32)).astype(BF16)
    runs, counted = pooling(real, 4)
    pooled = (dot(runs, high) + dot(runs, rest)) / jnp.maximum(counted, 1.0)
    return state, pooled.astype(BF16)


def pooling(real, factor):
    count_rows = BALL // factor
    r = lax.broadcasted_iota(I32, (count_rows, BALL), 0)
    c = lax.broadcasted_iota(I32, (count_rows, BALL), 1)
    hot = jnp.where(jnp.logical_and(r == c // factor, real), 1.0, 0.0)
    return hot.astype(BF16), jnp.sum(hot, 1, keepdims=True)


BALLS = QUARTER // BALL


def forward_tile(state, mp, gate_ref, up_ref, down_ref):
    normed = norm(state).astype(BF16)
    total = state
    for c in range(MP):
        shard = lax.rem(mp + c, MP)
        half = dot(normed, gate_ref[shard]) * 0.5
        up = dot(normed, up_ref[c])
        activated = ((half + half * jnp.tanh(half)) * up).astype(BF16)
        total = total + dot(activated, down_ref[shard])
    return total


def relatives(me):
    low = lax.rem(me, 2)
    high = lax.rem(me // 2, 2)
    first = me + 1 - 2 * low
    second = me + 2 - 4 * high
    third = first + 2 - 4 * high
    return (first, second, third)


def middle_kernel(
    slot_ref, code_ref, got_ref, mask_ref, keep_ref, qkv_hbm, out_hbm, gate_up_hbm, gate_hbm, down_hbm, coarse_hbm,
    lift_hbm, back_ref,
    turned_ref, lifted_ref, outgoing, r_sem,
    wide, staged, packed, x, state, pooled, tiles, one, two, mate_one, mate_two, mate_keep,
    mixed, all_mixed, lifted, keys_one, values_one, keys_two, values_two, qkv_ref, out_ref, gate_ref, up_ref, down_ref, w_ref, lift_ref,
    x_sem, p_sem, e_sem, k_sem, m_sem, t_sem, l_sem, g_sem, b_sem, f_sem, own, loads,
):
    me = lax.axis_index("wide")
    mp = lax.axis_index("mp")
    others = relatives(me)
    barrier = pltpu.get_barrier_semaphore()
    for k in range(1, MP):
        pl.semaphore_signal(
            barrier, inc=1, device_id={"mp": lax.rem(mp + k, MP)}, device_id_type=MESH
        )

    @pl.loop(1, WIDE)
    def _(k):
        pl.semaphore_signal(
            barrier, inc=1, device_id={"wide": lax.rem(me + k, WIDE)}, device_id_type=MESH
        )

    def chip(i):
        return 2 * lax.rem(i * 7, WIDE // 2)

    load = [
        pltpu.make_async_copy(src, dst, loads.at[j])
        for j, (src, dst) in enumerate([
            (qkv_hbm, qkv_ref),
            (out_hbm, out_ref),
            (gate_up_hbm.at[pl.ds(WIDTH, WIDTH), :], up_ref.at[0]),
            (down_hbm, down_ref),
            (coarse_hbm, w_ref),
            (lift_hbm, lift_ref.at[0]),
            (gate_hbm, gate_ref),
        ])
    ]
    for copy in load:
        copy.start()
    widen(got_ref, wide, SLOTS)
    pl.semaphore_wait(barrier, MP - 1 + WIDE - 1)

    def rows(t, size):
        return pl.ds(pl.multiple_of(t * size, size), size)

    def cols(g):
        return pl.ds(pl.multiple_of(g * LOCAL, LOCAL), LOCAL)

    def peer(k):
        return lax.rem(mp + k, MP)

    def to_mp(src, dst, sem, k, t):
        return remote(src, dst, sem.at[0, k, t], sem.at[1, k, t], {"mp": peer(k)})

    def piece(shards, owner):
        return up_ref.at[shards, pl.ds(pl.multiple_of(owner * 16, 16), 16), :]

    def lift_rows(owner):
        return pl.ds(pl.multiple_of(owner // 2 * 16, 16), 16)

    def lift_cols(owner):
        return pl.ds(pl.multiple_of(lax.rem(owner, 2) * 256, 256), 256)

    def lift_piece(shards, owner):
        return lift_ref.at[shards, lift_rows(owner), lift_cols(owner)]

    def fetch(k):
        src = gate_up_hbm.at[pl.ds(pl.multiple_of(WIDTH + me * 16, 16), 16), :]
        return to_mp(src, piece(MP - k, me), g_sem, k, 0)

    def fetch_lift(k):
        src = lift_hbm.at[lift_rows(me), lift_cols(me)]
        return to_mp(src, lift_piece(MP - k, me), g_sem, k, 1)

    def spread_to(part, i, t):
        to = {"wide": lax.rem(me + chip(i), WIDE)}
        return remote(part, part, b_sem.at[0, i, t], b_sem.at[1, i, t], to)

    def broadcast(i):
        return spread_to(piece(pl.ds(1, 3), me), i, 0)

    def broadcast_lift(i):
        return spread_to(lift_piece(pl.ds(1, 3), me), i, 1)

    def hand_over(part, i, t):
        return remote(part, part, f_sem.at[0, i, t], f_sem.at[1, i, t], {"wide": others[0]})

    def pass_on(i):
        return hand_over(piece(pl.ds(1, 3), lax.rem(me + WIDE - chip(i), WIDE)), i, 0)

    def pass_on_lift(i):
        return hand_over(lift_piece(pl.ds(1, 3), lax.rem(me + WIDE - chip(i), WIDE)), i, 1)

    for k in (2, 1, 3):
        fetch(k).start()
        fetch_lift(k).start()

    def turn(k, t):
        return to_mp(packed.at[peer(k) * BALLS + t], x.at[rows(t, BALL), cols(mp)], x_sem, k, t)

    def keep_turn(t):
        return pltpu.make_async_copy(
            packed.at[mp * BALLS + t], x.at[rows(t, BALL), cols(mp)], own.at[0, t]
        )

    def send_ball(t):
        for k in (2, 1, 3):
            gather_bucket(0, lambda s: slot_ref[s], wide, staged, packed, peer(k) * BALLS + t)
            turn(k, t).start()
        gather_bucket(0, lambda s: slot_ref[s], wide, staged, packed, mp * BALLS + t)
        keep_turn(t).start()

    send_ball(0)
    for k in (1, 3, 2):
        fetch(k).wait_recv()
        fetch_lift(k).wait_recv()

    @pl.loop(1, WIDE // 2)
    def _(i):
        broadcast(i).start()

    pass_on(0).start()

    @pl.loop(1, BALLS)
    def _(t):
        send_ball(t)

    @pl.loop(1, WIDE // 2)
    def _(i):
        broadcast_lift(i).start()

    pass_on_lift(0).start()

    def flags(j):
        return remote(
            keep_ref, mate_keep.at[j], k_sem.at[0, j], k_sem.at[1, j], {"wide": others[j]}
        )

    for j in range(3):
        flags(j).start()
    load[0].wait()
    load[1].wait()

    def share(k, t):
        return to_mp(pooled.at[mp, t], pooled.at[mp, t], p_sem, k, t)

    @pl.loop(0, BALLS)
    def _(t):
        for k in (1, 3, 2):
            turn(k, t).wait_recv()
        keep_turn(t).wait()
        real = mask_ref[pl.ds(mp * BALLS + t, 1), :] > 0
        out, means = fine_ball(x[rows(t, BALL), :], real, qkv_ref, out_ref)
        state[rows(t, BALL), :] = out
        pooled[mp, t] = means
        for k in (2, 1, 3):
            share(k, t).start()

    load[2].wait()
    load[3].wait()
    load[6].wait()

    def give(k, t):
        return to_mp(
            tiles.at[rows(t, BALL), cols(peer(k))],
            turned_ref.at[rows(mp * BALLS + t, BALL), :],
            t_sem,
            k,
            t,
        )

    def keep_give(t):
        return pltpu.make_async_copy(
            tiles.at[rows(t, BALL), cols(mp)],
            turned_ref.at[rows(mp * BALLS + t, BALL), :],
            own.at[1, t],
        )

    def feed(t, count):
        at = pl.ds(t * BALL, count * BALL)
        tiles[at, :] = forward_tile(state[at, :], mp, gate_ref, up_ref, down_ref).astype(BF16)
        for u in range(t, t + count):
            for k in (2, 1, 3):
                give(k, u).start()
            keep_give(u).start()

    @pl.loop(1, WIDE // 2)
    def _(i):
        broadcast(i).wait_recv()
        pass_on(i).start()

    @pl.loop(0, WIDE // 2)
    def _(i):
        pass_on(i).wait_recv()

    feed(0, 2)

    def pass_one(q):
        return remote(
            one.at[pl.ds(1, 2), rows(q, ONE), :],
            mate_one.at[:, rows(q, ONE), :],
            e_sem.at[0, 3, q],
            e_sem.at[1, 3, q],
            {"wide": others[0]},
        )

    def pass_two(j, q):
        return remote(
            two.at[pl.ds(1, 2), rows(q, TWO), :],
            mate_two.at[j, :, rows(q, TWO), :],
            e_sem.at[0, j, q],
            e_sem.at[1, j, q],
            {"wide": others[j]},
        )

    pair = lax.broadcasted_iota(I32, (32, 64), 0) == lax.broadcasted_iota(I32, (32, 64), 1) // 2
    pair = jnp.where(pair, 1.0, 0.0).astype(BF16)
    load[4].wait()

    def project(q):
        firsts, seconds = [], []
        for ball in range(BALLS):
            real = mask_ref[pl.ds(q * BALLS + ball, 1), :] > 0
            means = pooled[q, ball].astype(F32)
            firsts.append(norm(means).astype(BF16))
            sums = means * pooling(real, 4)[1]
            high = sums.astype(BF16)
            rest = (sums - high.astype(F32)).astype(BF16)
            counted = jnp.maximum(pooling(real, 8)[1], 1.0)
            seconds.append(norm((dot(pair, high) + dot(pair, rest)) / counted).astype(BF16))
        firsts = jnp.concatenate(firsts, 0)
        seconds = jnp.concatenate(seconds, 0)
        for t in (1, 2):
            two[t, rows(q, TWO), :] = dot(seconds, w_ref[1, t]).astype(BF16)
            one[t, rows(q, ONE), :] = dot(firsts, w_ref[0, t]).astype(BF16)
        for j in (1, 2, 0):
            pass_two(j, q).start()
        pass_one(q).start()
        two[0, rows(q, TWO), :] = (dot(seconds, w_ref[1, 0]) * SCALE).astype(BF16)
        one[0, rows(q, ONE), :] = (dot(firsts, w_ref[0, 0]) * SCALE).astype(BF16)

    project(mp)
    for k in (1, 3, 2):

        @pl.loop(0, BALLS)
        def _(t):
            share(MP - k, t).wait_recv()

        project(peer(k))

    feed(2, 1)

    @pl.loop(1, WIDE // 2)
    def _(i):
        broadcast_lift(i).wait_recv()
        pass_on_lift(i).start()


    def hand_to(q, k, level):
        at = pl.ds(0, ONE) if level == 0 else pl.ds(ONE, TWO)
        return to_mp(mixed.at[q, at, :], all_mixed.at[at, cols(mp)], m_sem, k, level)

    def hand(k, level):
        return hand_to(peer(k), k, level)

    def keep_hand(level):
        at = pl.ds(0, ONE) if level == 0 else pl.ds(ONE, TWO)
        return pltpu.make_async_copy(
            mixed.at[mp, at, :], all_mixed.at[at, cols(mp)], own.at[2, level]
        )

    for j in range(3):
        flags(j).wait()

    def fill(keys_ref, values_ref, begin, src, first, flag):
        for c in range(src.shape[1] // 128):
            at = slice(c * 128, (c + 1) * 128)
            here = flag[first + c : first + c + 1, :] > 0
            keys, values = augment(src[0, at, :], src[1, at, :], columns_of(here))
            to = slice(begin + c * 128, begin + (c + 1) * 128)
            for head in range(2):
                keys_ref[head, to, :] = keys[head]
                values_ref[head, to, :] = values[head]

    def masked_of(keys_ref, at):
        spare = keys_ref[0, at, :].astype(F32)
        return jnp.min(jnp.where(lanes(256) == 64, spare, 0.0), -1, keepdims=True) < 0.0

    mine = keep_ref[...]
    fill(keys_one, values_one, 0, one.at[1:], 0, mine)

    @pl.loop(0, MP)
    def _(q):
        pass_one(q).wait()

    fill(keys_one, values_one, 4 * ONE, mate_one, 0, mate_keep[0])

    @pl.loop(1, MP + 1)
    def _(k):
        q = peer(k)
        at = rows(q, ONE)
        mixed[q, 0:ONE, :] = attend_pair(
            one[0, at, :], one[1, at, :], one[2, at, :], masked_of(keys_one, at),
            lambda head: keys_one[head], lambda head: values_one[head],
        )

        @pl.when(k < MP)
        def _():
            hand(k, 0).start()

    keep_hand(0).start()

    fill(keys_two, values_two, 0, two.at[1:], 8, mine)

    @pl.loop(0, MP)
    def _(q):
        for j in range(3):
            pass_two(j, q).wait()

    for j in range(3):
        fill(keys_two, values_two, (j + 1) * 4 * TWO, mate_two.at[j], 8, mate_keep[j])

    @pl.loop(0, 2)
    def _(p):
        at = rows(p, 256)
        both = attend_pair(
            two[0, at, :], two[1, at, :], two[2, at, :], masked_of(keys_two, at),
            lambda head: keys_two[head], lambda head: values_two[head],
        )
        for h in range(2):
            q = p * 2 + h
            k = lax.rem(q + MP - mp, MP)
            mixed[q, ONE:COARSE, :] = both[h * TWO : (h + 1) * TWO]

            @pl.when(k > 0)
            def _():
                hand_to(q, k, 1).start()

    keep_hand(1).start()

    feed(3, 1)

    load[5].wait()

    @pl.loop(0, WIDE // 2)
    def _(i):
        pass_on_lift(i).wait_recv()

    for level in range(2):
        keep_hand(level).wait()
        for k in (1, 3, 2):
            hand(k, level).wait()
    for level, begin, size in ((0, 0, 64), (1, ONE, 32)):
        span = slice(begin, begin + size * BALLS)
        total = jnp.zeros((size * BALLS, WIDTH), F32)
        for g in range(MP):
            total = total + dot(
                all_mixed[span, cols(peer(g))],
                lift_ref[g, level * LOCAL : (level + 1) * LOCAL, :],
            )
        total = total.astype(BF16)
        for ball in range(BALLS):
            at = slice(0, 64) if level == 0 else slice(64, 96)
            lifted[ball, at, :] = total[ball * size : (ball + 1) * size]

    def rise(k):
        return to_mp(lifted.at[:, :, cols(peer(k))], lifted_ref.at[pl.ds(mp * BALLS, BALLS)], l_sem, k, 0)

    for k in (2, 1, 3):
        rise(k).start()
    keep_rise = pltpu.make_async_copy(
        lifted.at[:, :, cols(mp)], lifted_ref.at[pl.ds(mp * BALLS, BALLS)], own.at[3, 0]
    )
    keep_rise.start()

    @pl.loop(0, BALLS)
    def _(t):
        keep_give(t).wait()
        for k in (1, 3, 2):
            give(k, t).wait_recv()

    runs = run_matrix(
        lax.broadcasted_iota(I32, (BALL, 96), 0), lax.broadcasted_iota(I32, (BALL, 96), 1)
    )

    def update(q):
        @pl.loop(0, BALLS)
        def _(t):
            i = q * BALLS + t
            at = rows(i, BALL)
            wide[at, :] = turned_ref[at, :].astype(F32) + dot(runs, lifted_ref[i])

    keep_rise.wait()
    update(mp)
    for k in (1, 3, 2):
        rise(k).wait_recv()
        update(peer(MP - k))
    wide[ROWS : ROWS + 8, :] = jnp.zeros((8, LOCAL), F32)

    def rows_copy(k):
        to = turn_of(me, k)
        return remote(
            outgoing.at[to], back_ref.at[me], r_sem.at[0, k], r_sem.at[1, k], {"wide": to}
        )

    @pl.loop(1, WIDE)
    def _(k):
        gather_bucket(0, lambda s: code_ref[s] >> 1, wide, staged, outgoing, turn_of(me, k))
        rows_copy(k).start()

    gather_bucket(0, lambda s: code_ref[s] >> 1, wide, staged, outgoing, me)
    last = pltpu.make_async_copy(outgoing.at[me], back_ref.at[me], own.at[3, 1])
    last.start()

    @pl.loop(0, BALLS)
    def _(t):
        for k in (1, 3, 2):
            turn(k, t).wait_send()
            share(k, t).wait_send()
            give(k, t).wait_send()

    @pl.loop(1, WIDE // 2)
    def _(i):
        broadcast(i).wait_send()
        broadcast_lift(i).wait_send()

    @pl.loop(0, WIDE // 2)
    def _(i):
        pass_on(i).wait_send()
        pass_on_lift(i).wait_send()

    for k in (1, 3, 2):
        fetch(k).wait_send()
        fetch_lift(k).wait_send()
        rise(k).wait_send()
    last.wait()

    @pl.loop(1, WIDE)
    def _(k):
        rows_copy(k).wait()


def middle(slots, codes, got, mask, keep, weights, collective):
    dma = pltpu.SemaphoreType.DMA
    return pl.pallas_call(
        middle_kernel,
        out_shape=shape((WIDE, CAP, LOCAL), BF16),
        in_specs=[SMEM, SMEM, VMEM, VMEM, VMEM] + [ANY] * 7,
        out_specs=ANY,
        scratch_shapes=[
            pltpu.VMEM((ROWS, LOCAL), BF16),
            pltpu.VMEM((MP * BALLS, 96, LOCAL), BF16),
            pltpu.VMEM((WIDE, CAP, LOCAL), BF16),
            dma((2, WIDE)),
            pltpu.VMEM((SLOTS, LOCAL), F32),
            pltpu.VMEM((1, CAP, LOCAL), F32),
            pltpu.VMEM((MP * BALLS, BALL, LOCAL), BF16),
            pltpu.VMEM((QUARTER, WIDTH), BF16),
            pltpu.VMEM((QUARTER, WIDTH), F32),
            pltpu.VMEM((MP, BALLS, 64, WIDTH), BF16),
            pltpu.VMEM((QUARTER, WIDTH), BF16),
            pltpu.VMEM((3, 4 * ONE, LOCAL), BF16),
            pltpu.VMEM((3, 4 * TWO, LOCAL), BF16),
            pltpu.VMEM((2, 4 * ONE, LOCAL), BF16),
            pltpu.VMEM((3, 2, 4 * TWO, LOCAL), BF16),
            pltpu.VMEM((3, 12, 128), I32),
            pltpu.VMEM((MP, COARSE, LOCAL), BF16),
            pltpu.VMEM((COARSE, WIDTH), BF16),
            pltpu.VMEM((BALLS, 96, WIDTH), BF16),
            pltpu.VMEM((2, 8 * ONE, LOCAL), BF16),
            pltpu.VMEM((2, 8 * ONE, LOCAL), BF16),
            pltpu.VMEM((2, 16 * TWO, LOCAL), BF16),
            pltpu.VMEM((2, 16 * TWO, LOCAL), BF16),
            pltpu.VMEM((3, WIDTH, WIDTH), BF16),
            pltpu.VMEM((WIDTH, WIDTH), BF16),
            pltpu.VMEM((MP, WIDTH, WIDTH), BF16),
            pltpu.VMEM((MP, WIDTH, WIDTH), BF16),
            pltpu.VMEM((MP, WIDTH, WIDTH), BF16),
            pltpu.VMEM((2, 3, WIDTH, LOCAL), BF16),
            pltpu.VMEM((MP, 2 * LOCAL, WIDTH), BF16),
            dma((2, MP, BALLS)),
            dma((2, MP, BALLS)),
            dma((2, 4, MP)),
            dma((2, 3)),
            dma((2, MP, 2)),
            dma((2, MP, BALLS)),
            dma((2, MP, 1)),
            dma((2, MP, 2)),
            dma((2, WIDE // 2, 2)),
            dma((2, WIDE // 2, 2)),
            dma((4, BALLS)),
            dma((7,)),
        ],
        compiler_params=params(collective),
    )(slots, codes, got, mask, keep, *weights)


def on_device(points, mask, perm, w_qkv, w_out, w_gate_up, w_down, w_coarse, w_coarse_out):
    slot, source, codes = index(perm, mask)
    own_gate_up = w_gate_up.reshape(2 * WIDTH, WIDTH)
    own_lift = w_coarse_out.reshape(2 * LOCAL, WIDTH)
    got, got_code, landed, owned_mask, keep, full_qkv, full_out, full_down, full_gate = (
        send_rows(
            source.reshape(SLOTS),
            points,
            codes,
            [
                w_qkv.reshape(3 * WIDTH, LOCAL),
                w_out,
                w_down,
                own_gate_up,
            ],
            1,
        )
    )
    full_qkv = full_qkv.reshape(3, WIDTH, WIDTH)
    full_out = full_out.reshape(WIDTH, WIDTH)
    returned = middle(
        landed.reshape(ROWS), got_code.reshape(SLOTS), got.reshape(SLOTS, LOCAL), owned_mask, keep,
        [full_qkv, full_out, own_gate_up, full_gate, full_down, w_coarse, own_lift], 2,
    )
    return pl.pallas_call(
        finish_kernel,
        out_shape=shape((ROWS, LOCAL), F32),
        in_specs=[SMEM, ANY],
        out_specs=ANY,
        scratch_shapes=[
            pltpu.VMEM((SLOTS, LOCAL), BF16),
            pltpu.VMEM((SLOTS, LOCAL), F32),
            pltpu.VMEM((ROWS, LOCAL), F32),
            pltpu.SemaphoreType.DMA((SLOTS // 1024,)),
            pltpu.SemaphoreType.DMA((ROWS // 512,)),
        ],
        compiler_params=params(),
    )(slot.reshape(ROWS), returned.reshape(SLOTS, LOCAL))


def solution(mesh):
    placed = (
        P("wide", "mp"),
        P("wide"),
        P("wide"),
        P(None, None, "mp"),
        P("mp", None),
        P(None, None, "mp"),
        P("mp", None),
        P(None, None, None, "mp"),
        P(None, "mp", None),
    )
    return jax.shard_map(
        on_device, mesh=mesh, in_specs=placed, out_specs=P("wide", "mp"), check_vma=False
    )
```

```python
import functools

import jax
import jax.numpy as jnp
from jax import lax
from jax.experimental import pallas as pl
from jax.experimental.pallas import tpu as pltpu
from jax.sharding import PartitionSpec as P

BALL = 256
WIDE = 32
MP = 4
ROWS = 4096
CAP = 256
SLOTS = WIDE * CAP
QUARTER = ROWS // MP
WIDTH = 512
LOCAL = WIDTH // MP
HIDDEN = 2048
ONE = QUARTER // 4
TWO = QUARTER // 8
COARSE = ONE + TWO
F32 = jnp.float32
BF16 = jnp.bfloat16
I32 = jnp.int32
MESH = pl.DeviceIdType.MESH
ANY = pl.BlockSpec(memory_space=pl.ANY)
VMEM = pl.BlockSpec(memory_space=pltpu.VMEM)
SMEM = pl.BlockSpec(memory_space=pltpu.SMEM)
LIMIT = 56 * 1024 * 1024


def shape(dims, kind):
    return jax.ShapeDtypeStruct(dims, kind)


def params(collective=None):
    if collective is None:
        return pltpu.CompilerParams(vmem_limit_bytes=LIMIT)
    return pltpu.CompilerParams(
        vmem_limit_bytes=LIMIT, collective_id=collective, has_side_effects=True
    )


def dot(a, b):
    return jnp.dot(a, b, preferred_element_type=F32)


def dot_t(a, b):
    return lax.dot_general(a, b, (((1,), (1,)), ((), ())), preferred_element_type=F32)


def norm(values):
    return values * lax.rsqrt(jnp.mean(values * values, -1, keepdims=True) + 1e-06)


UNROLL = 32
NONE = 2 * ROWS


def index_kernel(perm_ref, mask_ref, slot_ref, source_ref, codes_ref):
    perm = perm_ref[...]
    target = perm >> 12
    code = (perm & (ROWS - 1)) * 2 + mask_ref[...]
    rows = lax.broadcasted_iota(I32, (CAP, 256), 0)
    upper = jnp.where(rows < lax.broadcasted_iota(I32, (256, 256), 1), 1.0, 0.0).astype(BF16)
    which = lax.broadcasted_iota(I32, (WIDE, 256), 0)
    lane = lax.broadcasted_iota(I32, (1, 256), 1).astype(F32)
    carry = jnp.zeros((WIDE, 1), F32)
    found = jnp.zeros((5 * WIDE, CAP), F32)
    for c in range(ROWS // 256):
        first, second = slice(2 * c, 2 * c + 1), slice(2 * c + 1, 2 * c + 2)
        goal = jnp.concatenate([target[first, :], target[second, :]], 1)
        both = jnp.concatenate([code[first, :], code[second, :]], 1)
        hot = jnp.where(which == goal, 1.0, 0.0)
        before = dot(hot.astype(BF16), upper) + carry
        rank = jnp.sum(hot * before, 0, keepdims=True).astype(I32)
        slot = goal * CAP + rank
        slot_ref[first, :] = slot[:, :128]
        slot_ref[second, :] = slot[:, 128:]
        carry = carry + jnp.sum(hot, 1, keepdims=True)
        placed = jnp.where(rows == rank, 1.0, 0.0).astype(BF16)
        high = (both >> 6).astype(F32)
        low = (both & 63).astype(F32)
        values = jnp.concatenate([hot * lane, hot * float(c), hot * high, hot * low, hot], 0)
        found = found + dot_t(values.astype(BF16), placed)
    source = (found[:WIDE] + found[WIDE : 2 * WIDE] * 256.0).astype(I32)
    codes = (found[2 * WIDE : 3 * WIDE] * 64.0 + found[3 * WIDE : 4 * WIDE]).astype(I32)
    codes = jnp.where(found[4 * WIDE :] > 0.5, codes, NONE)
    for h in range(2):
        at = slice(h * 128, (h + 1) * 128)
        source_ref[:, h, :] = source[:, at]
        codes_ref[:, h, :] = codes[:, at]


def index(perm, mask):
    return pl.pallas_call(
        index_kernel,
        out_shape=[shape((32, 128), I32), shape((WIDE, 2, 128), I32), shape((WIDE, 2, 128), I32)],
        in_specs=[VMEM] * 2,
        out_specs=[VMEM] * 3,
        compiler_params=params(),
    )(perm.reshape(32, 128), mask.reshape(32, 128))


def invert(codes_ref, slot_ref, mask_ref, keep_ref):
    balls = ROWS // BALL
    rows = lax.broadcasted_iota(I32, (256, 128), 0)
    which = lax.broadcasted_iota(I32, (balls, 128), 0)
    lane = lax.broadcasted_iota(I32, (1, 128), 1).astype(F32)
    found = jnp.zeros((3 * balls, 256), F32)
    for c in range(WIDE):
        for h in range(2):
            code = codes_ref[c, h : h + 1, :]
            landing = code >> 1
            hot = jnp.where(which == (landing >> 8), 1.0, 0.0)
            placed = jnp.where(rows == (landing & 255), 1.0, 0.0).astype(BF16)
            real = (code & 1).astype(F32)
            values = jnp.concatenate([hot * lane, hot * float(2 * c + h), hot * real], 0)
            found = found + dot_t(values.astype(BF16), placed)
    slots = (found[:balls] + found[balls : 2 * balls] * 128.0).astype(I32)
    for h in range(2):
        slot_ref[:, h, :] = slots[:, h * 128 : (h + 1) * 128]
    mask = found[2 * balls :]
    mask_ref[...] = mask.astype(I32)
    mask = mask.astype(BF16)
    for f, first in ((4, 0), (8, 8)):
        side = f // 2
        count = balls // side
        total = jnp.zeros((count, 128), F32)
        for j in range(side):
            r = lax.broadcasted_iota(I32, (count, balls), 0)
            c = lax.broadcasted_iota(I32, (count, balls), 1)
            pick = jnp.where(c == r * side + j, 1.0, 0.0).astype(BF16)
            r = lax.broadcasted_iota(I32, (256, 128), 0)
            c = lax.broadcasted_iota(I32, (256, 128), 1)
            runs = jnp.where(c == r // f + j * (128 // side), 1.0, 0.0).astype(BF16)
            total = total + dot(dot(pick, mask).astype(BF16), runs)
        keep_ref[first : first + count, :] = jnp.where(total > 0.5, 1, 0)


def run_matrix(r, c):
    hot = jnp.logical_or(
        jnp.logical_and(c < 64, r // 4 == c), jnp.logical_and(c >= 64, r // 8 == c - 64)
    )
    return jnp.where(hot, 1.0, 0.0).astype(BF16)


def widen(src, dst, rows):
    @pl.loop(0, rows // 256)
    def _(i):
        at = pl.ds(pl.multiple_of(i * 256, 256), 256)
        dst[at, :] = src[at, :].astype(dst.dtype)


def finish_kernel(slot_ref, got_ref, out_ref, narrow, wide, done, in_sem, out_sem):
    def chunk(ref, i, size):
        return ref.at[pl.ds(pl.multiple_of(i * size, size), size), :]

    def load(i):
        return pltpu.make_async_copy(chunk(got_ref, i, 1024), chunk(narrow, i, 1024), in_sem.at[i])

    def store(i):
        return pltpu.make_async_copy(chunk(done, i, 512), chunk(out_ref, i, 512), out_sem.at[i])

    for i in range(SLOTS // 1024):
        load(i).start()
    for i in range(SLOTS // 1024):
        load(i).wait()
        widen(chunk(narrow, i, 1024), chunk(wide, i, 1024), 1024)

    @pl.loop(0, ROWS // 512)
    def _(i):
        @pl.loop(0, 512 // UNROLL)
        def _(j):
            base = i * 512 + j * UNROLL
            lines = [wide[pl.ds(slot_ref[base + u], 1), :] for u in range(UNROLL)]
            for u in range(UNROLL):
                done[pl.ds(base + u, 1), :] = lines[u]

        store(i).start()

    @pl.loop(0, ROWS // 512)
    def _(i):
        store(i).wait()


def remote(src, dst, send, recv, device):
    return pltpu.make_async_remote_copy(
        src_ref=src, dst_ref=dst, send_sem=send, recv_sem=recv, device_id=device, device_id_type=MESH
    )


def turn_of(me, k):
    return lax.rem(me + lax.rem(k * 7, WIDE), WIDE)


def gather_bucket(line, lookup, wide, staged, packed, peer):
    @pl.loop(0, CAP // UNROLL)
    def _(i):
        begin = i * UNROLL
        lines = [wide[pl.ds(lookup(peer * CAP + begin + u), 1), :] for u in range(UNROLL)]
        for u in range(UNROLL):
            staged[line, pl.ds(begin + u, 1), :] = lines[u]

    packed[peer] = staged[line].astype(BF16)


def send_kernel(
    source_ref, points_ref, codes_ref, qkv_ref, out_ref, down_ref, gate_ref,
    got_ref, got_codes_out, slot_ref, mask_ref, keep_ref, all_qkv, all_out, all_down, all_gate,
    got_codes_ref, wide, staged, packed, send, recv, own, w_send, w_recv, w_own,
):
    me = lax.axis_index("wide")
    mp = lax.axis_index("mp")
    core = lax.rem(me, 2)
    partner = me + 1 - 2 * core
    after, ahead = lax.rem(mp + 1, MP), lax.rem(mp + 2, MP)
    behind = lax.rem(mp + 3, MP)
    barrier = pltpu.get_barrier_semaphore()

    @pl.loop(1, WIDE)
    def _(k):
        pl.semaphore_signal(
            barrier, inc=1, device_id={"wide": lax.rem(me + k, WIDE)}, device_id_type=MESH
        )

    for other in (after, behind):
        pl.semaphore_signal(barrier, inc=1, device_id={"mp": other}, device_id_type=MESH)
    widen(points_ref, wide, ROWS)

    def part(first, count):
        def rows(ref, quarter):
            return pl.ds(pl.multiple_of(first * quarter, 16), count * quarter)

        def cut(j, ref, shard):
            if j == 0:
                return ref.at[rows(ref, 384), pl.ds(pl.multiple_of(shard * 128, 128), 128)]
            quarter = (0, 32, 128, 128)[j]
            return ref.at[shard, rows(ref, quarter), :]

        def own_cut(j, ref):
            quarter = (384, 32, 128, 128)[j]
            return ref.at[rows(ref, quarter), :]

        return cut, own_cut

    half, own_half = part(2 * core, 2)
    first, _ = part(2 * core, 1)
    second, _ = part(2 * core + 1, 1)
    every, own_every = part(0, 4)
    shards = [qkv_ref, out_ref, down_ref, gate_ref]
    full = [all_qkv, all_out, all_down, all_gate]
    count = len(shards)

    def weight(j, kind, cut, src, shard, device):
        return remote(
            src, cut(j, full[j], shard), w_send.at[j, kind], w_recv.at[j, kind], device
        )

    def weight_copies(j):
        ref = full[j]
        mine = own_half(j, shards[j])
        return [
            weight(j, 0, half, mine, mp, {"mp": after}),
            weight(j, 1, half, mine, mp, {"mp": behind}),
            weight(j, 2, first, first(j, ref, behind), behind, {"mp": after}),
            weight(j, 3, second, second(j, ref, after), after, {"mp": behind}),
            weight(j, 4, half, half(j, ref, behind), behind, {"wide": partner}),
            weight(j, 5, half, half(j, ref, after), after, {"wide": partner}),
            weight(j, 6, first, first(j, ref, ahead), ahead, {"wide": partner}),
            weight(j, 7, second, second(j, ref, ahead), ahead, {"wide": partner}),
        ]

    weights = [weight_copies(j) for j in range(count)]

    def rows_copy(k):
        peer = turn_of(me, k)
        return remote(
            packed.at[peer], got_ref.at[me], send.at[k, 0], recv.at[k, 0], {"wide": peer}
        )

    def codes_copy(k):
        peer = turn_of(me, k)
        return remote(
            codes_ref.at[peer], got_codes_ref.at[me], send.at[k, 1], recv.at[k, 1], {"wide": peer}
        )

    pl.semaphore_wait(barrier, WIDE + 1)
    for j in range(count):
        weights[j][0].start()
        weights[j][1].start()

    @pl.loop(1, WIDE)
    def _(k):
        codes_copy(k).start()

    @pl.loop(1, WIDE)
    def _(k):
        gather_bucket(0, lambda s: source_ref[s], wide, staged, packed, turn_of(me, k))
        rows_copy(k).start()

    gather_bucket(0, lambda s: source_ref[s], wide, staged, packed, me)
    mine = [
        pltpu.make_async_copy(packed.at[me], got_ref.at[me], own.at[0]),
        pltpu.make_async_copy(codes_ref.at[me], got_codes_ref.at[me], own.at[1]),
    ]
    for j in range(count):
        mine.append(
            pltpu.make_async_copy(own_every(j, shards[j]), every(j, full[j], mp), w_own.at[j])
        )
    for copy in mine:
        copy.start()

    def forward(j):
        weights[j][0].wait_recv()
        weights[j][2].start()
        weights[j][4].start()
        weights[j][1].wait_recv()
        weights[j][3].start()
        weights[j][5].start()

    def forward_last(j):
        weights[j][2].wait_recv()
        weights[j][6].start()
        weights[j][3].wait_recv()
        weights[j][7].start()

    for j in range(count):
        forward(j)
    for copy in mine:
        copy.wait()

    @pl.loop(1, WIDE)
    def _(k):
        codes_copy(k).wait()

    invert(got_codes_ref, slot_ref, mask_ref, keep_ref)
    got_codes_out[...] = got_codes_ref[...]
    for j in range(count):
        forward_last(j)

    @pl.loop(1, WIDE)
    def _(k):
        rows_copy(k).wait()

    for j in range(count):
        for kind in range(4):
            weights[j][kind].wait_send()
        for kind in range(4, 8):
            weights[j][kind].wait()


def send_rows(source, points, codes, weights, collective):
    return pl.pallas_call(
        send_kernel,
        out_shape=[
            shape((WIDE, CAP, LOCAL), BF16),
            shape((WIDE, 2, 128), I32),
            shape((16, 2, 128), I32),
            shape((16, 256), I32),
            shape((12, 128), I32),
            shape((3 * WIDTH, WIDTH), BF16),
            shape((MP, LOCAL, WIDTH), BF16),
            shape((MP, WIDTH, WIDTH), BF16),
            shape((MP, WIDTH, WIDTH), BF16),
        ],
        in_specs=[SMEM, VMEM, ANY] + [VMEM] * 4,
        out_specs=[ANY] + [VMEM] * 4 + [ANY] * 4,
        scratch_shapes=[
            pltpu.VMEM((WIDE, 2, 128), I32),
            pltpu.VMEM((ROWS, LOCAL), F32),
            pltpu.VMEM((1, CAP, LOCAL), F32),
            pltpu.VMEM((WIDE, CAP, LOCAL), BF16),
            pltpu.SemaphoreType.DMA((WIDE, 2)),
            pltpu.SemaphoreType.DMA((WIDE, 2)),
            pltpu.SemaphoreType.DMA((2,)),
            pltpu.SemaphoreType.DMA((4, 8)),
            pltpu.SemaphoreType.DMA((4, 8)),
            pltpu.SemaphoreType.DMA((4,)),
        ],
        compiler_params=params(collective),
    )(source, points, codes, *weights)


SCALE = 0.125 * 1.4426950408889634


def lanes(count):
    return lax.broadcasted_iota(I32, (count, 128), 1)


def columns_of(flags):
    eye = lax.broadcasted_iota(I32, (128, 128), 0) == lax.broadcasted_iota(I32, (128, 128), 1)
    row = jnp.broadcast_to(jnp.where(flags, 1.0, 0.0), (128, 128)).astype(BF16)
    return dot_t(jnp.where(eye, 1.0, 0.0).astype(BF16), row)


def augment(keys, values, columns):
    lane = lanes(keys.shape[0])
    low = lane < 64
    bias = jnp.where(columns > 0.5, 0.0, -1e30)
    keys = keys.astype(F32)
    values = values.astype(F32)
    return (
        (
            jnp.where(low, keys, jnp.where(lane == 64, bias, 0.0)).astype(BF16),
            jnp.where(low, jnp.where(lane == 0, bias, 0.0), keys).astype(BF16),
        ),
        (jnp.where(low, values, 1.0).astype(BF16), jnp.where(low, 1.0, values).astype(BF16)),
    )


def attend_pair(queries, own_keys, own_values, masked, keys, values):
    count = queries.shape[0]
    lane = lanes(count)
    low = lane < 64
    queries = queries.astype(F32)
    own_keys = own_keys.astype(F32)
    own_values = own_values.astype(F32)
    out = []
    for head in range(2):
        mine = low if head == 0 else jnp.logical_not(low)
        spare = jnp.where(lane == (64 if head == 0 else 0), 1.0, 0.0)
        q = jnp.where(mine, queries, spare).astype(BF16)
        scores = dot_t(q, keys(head))
        alone = jnp.sum(jnp.where(mine, queries * own_keys, 0.0), -1, keepdims=True)
        top = jnp.maximum(jnp.max(scores, -1, keepdims=True), alone)
        weights = jnp.exp2(scores - top).astype(BF16)
        own = jnp.where(masked, jnp.exp2(alone - top), 0.0)
        total = dot(weights, values(head))
        out.append(total + own * jnp.where(mine, own_values, 1.0))
    sums = pltpu.roll(jnp.where(low, out[1], out[0]), 64, 1)
    return (jnp.where(low, out[0], out[1]) / sums).astype(BF16)


def attend_ball(queries, keys, values, allowed):
    low = lanes(BALL) < 64
    out = []
    for head in range(2):
        mine = low if head == 0 else jnp.logical_not(low)
        q = jnp.where(mine, queries, jnp.zeros_like(queries))
        scores = jnp.where(allowed, dot_t(q, keys), -1e30)
        weights = jnp.exp2(scores - jnp.max(scores, -1, keepdims=True))
        total = jnp.sum(weights, -1, keepdims=True)
        out.append(dot(weights.astype(BF16), values) / total)
    return jnp.where(low, out[0], out[1]).astype(BF16)


def fine_ball(x, real, qkv_ref, out_ref):
    x = x.astype(F32)
    normed = norm(x).astype(BF16)
    q = (dot(normed, qkv_ref[0]) * SCALE).astype(BF16)
    k = dot(normed, qkv_ref[1]).astype(BF16)
    v = dot(normed, qkv_ref[2]).astype(BF16)
    rows = lax.broadcasted_iota(I32, (BALL, BALL), 0)
    cols = lax.broadcasted_iota(I32, (BALL, BALL), 1)
    allowed = jnp.logical_or(real, rows == cols)
    mixed = []
    for g in range(MP):
        at = slice(g * 128, (g + 1) * 128)
        mixed.append(attend_ball(q[:, at], k[:, at], v[:, at], allowed))
    state = x + dot(jnp.concatenate(mixed, 1), out_ref[...])
    high = state.astype(BF16)
    rest = (state - high.astype(F32)).astype(BF16)
    runs, counted = pooling(real, 4)
    pooled = (dot(runs, high) + dot(runs, rest)) / jnp.maximum(counted, 1.0)
    return state, pooled.astype(BF16)


def pooling(real, factor):
    count_rows = BALL // factor
    r = lax.broadcasted_iota(I32, (count_rows, BALL), 0)
    c = lax.broadcasted_iota(I32, (count_rows, BALL), 1)
    hot = jnp.where(jnp.logical_and(r == c // factor, real), 1.0, 0.0)
    return hot.astype(BF16), jnp.sum(hot, 1, keepdims=True)


BALLS = QUARTER // BALL


def forward_tile(state, mp, gate_ref, up_ref, down_ref):
    normed = norm(state).astype(BF16)
    total = state
    for c in range(MP):
        shard = lax.rem(mp + c, MP)
        half = dot(normed, gate_ref[shard]) * 0.5
        up = dot(normed, up_ref[c])
        activated = ((half + half * jnp.tanh(half)) * up).astype(BF16)
        total = total + dot(activated, down_ref[shard])
    return total


def relatives(me):
    low = lax.rem(me, 2)
    high = lax.rem(me // 2, 2)
    first = me + 1 - 2 * low
    second = me + 2 - 4 * high
    third = first + 2 - 4 * high
    return (first, second, third)


def middle_kernel(
    slot_ref, code_ref, got_ref, mask_ref, keep_ref, qkv_hbm, out_hbm, gate_up_hbm, gate_hbm, down_hbm, coarse_hbm,
    lift_hbm, back_ref,
    turned_ref, lifted_ref, outgoing, r_sem,
    wide, staged, packed, x, state, pooled, tiles, one, two, mate_one, mate_two, mate_keep,
    mixed, all_mixed, lifted, keys_one, values_one, keys_two, values_two, qkv_ref, out_ref, gate_ref, up_ref, down_ref, w_ref, lift_ref,
    x_sem, p_sem, e_sem, k_sem, m_sem, t_sem, l_sem, g_sem, b_sem, f_sem, own, loads,
):
    me = lax.axis_index("wide")
    mp = lax.axis_index("mp")
    others = relatives(me)
    barrier = pltpu.get_barrier_semaphore()
    for k in range(1, MP):
        pl.semaphore_signal(
            barrier, inc=1, device_id={"mp": lax.rem(mp + k, MP)}, device_id_type=MESH
        )

    @pl.loop(1, WIDE)
    def _(k):
        pl.semaphore_signal(
            barrier, inc=1, device_id={"wide": lax.rem(me + k, WIDE)}, device_id_type=MESH
        )

    def chip(i):
        return 2 * lax.rem(i * 7, WIDE // 2)

    load = [
        pltpu.make_async_copy(src, dst, loads.at[j])
        for j, (src, dst) in enumerate([
            (qkv_hbm, qkv_ref),
            (out_hbm, out_ref),
            (gate_up_hbm.at[pl.ds(WIDTH, WIDTH), :], up_ref.at[0]),
            (down_hbm, down_ref),
            (coarse_hbm, w_ref),
            (lift_hbm, lift_ref.at[0]),
            (gate_hbm, gate_ref),
        ])
    ]
    for copy in load:
        copy.start()
    widen(got_ref, wide, SLOTS)
    pl.semaphore_wait(barrier, MP - 1 + WIDE - 1)

    def rows(t, size):
        return pl.ds(pl.multiple_of(t * size, size), size)

    def cols(g):
        return pl.ds(pl.multiple_of(g * LOCAL, LOCAL), LOCAL)

    def peer(k):
        return lax.rem(mp + k, MP)

    def to_mp(src, dst, sem, k, t):
        return remote(src, dst, sem.at[0, k, t], sem.at[1, k, t], {"mp": peer(k)})

    def piece(shards, owner):
        return up_ref.at[shards, pl.ds(pl.multiple_of(owner * 16, 16), 16), :]

    def lift_rows(owner):
        return pl.ds(pl.multiple_of(owner // 2 * 16, 16), 16)

    def lift_cols(owner):
        return pl.ds(pl.multiple_of(lax.rem(owner, 2) * 256, 256), 256)

    def lift_piece(shards, owner):
        return lift_ref.at[shards, lift_rows(owner), lift_cols(owner)]

    def fetch(k):
        src = gate_up_hbm.at[pl.ds(pl.multiple_of(WIDTH + me * 16, 16), 16), :]
        return to_mp(src, piece(MP - k, me), g_sem, k, 0)

    def fetch_lift(k):
        src = lift_hbm.at[lift_rows(me), lift_cols(me)]
        return to_mp(src, lift_piece(MP - k, me), g_sem, k, 1)

    def spread_to(part, i, t):
        to = {"wide": lax.rem(me + chip(i), WIDE)}
        return remote(part, part, b_sem.at[0, i, t], b_sem.at[1, i, t], to)

    def broadcast(i):
        return spread_to(piece(pl.ds(1, 3), me), i, 0)

    def broadcast_lift(i):
        return spread_to(lift_piece(pl.ds(1, 3), me), i, 1)

    def hand_over(part, i, t):
        return remote(part, part, f_sem.at[0, i, t], f_sem.at[1, i, t], {"wide": others[0]})

    def pass_on(i):
        return hand_over(piece(pl.ds(1, 3), lax.rem(me + WIDE - chip(i), WIDE)), i, 0)

    def pass_on_lift(i):
        return hand_over(lift_piece(pl.ds(1, 3), lax.rem(me + WIDE - chip(i), WIDE)), i, 1)

    for k in (2, 1, 3):
        fetch(k).start()
        fetch_lift(k).start()

    def turn(k, t):
        return to_mp(packed.at[peer(k) * BALLS + t], x.at[rows(t, BALL), cols(mp)], x_sem, k, t)

    def keep_turn(t):
        return pltpu.make_async_copy(
            packed.at[mp * BALLS + t], x.at[rows(t, BALL), cols(mp)], own.at[0, t]
        )

    def send_ball(t):
        for k in (2, 1, 3):
            gather_bucket(0, lambda s: slot_ref[s], wide, staged, packed, peer(k) * BALLS + t)
            turn(k, t).start()
        gather_bucket(0, lambda s: slot_ref[s], wide, staged, packed, mp * BALLS + t)
        keep_turn(t).start()

    send_ball(0)
    for k in (1, 3, 2):
        fetch(k).wait_recv()
        fetch_lift(k).wait_recv()

    @pl.loop(1, WIDE // 2)
    def _(i):
        broadcast(i).start()

    pass_on(0).start()

    @pl.loop(1, BALLS)
    def _(t):
        send_ball(t)

    @pl.loop(1, WIDE // 2)
    def _(i):
        broadcast_lift(i).start()

    pass_on_lift(0).start()

    def flags(j):
        return remote(
            keep_ref, mate_keep.at[j], k_sem.at[0, j], k_sem.at[1, j], {"wide": others[j]}
        )

    for j in range(3):
        flags(j).start()
    load[0].wait()
    load[1].wait()

    def share(k, t):
        return to_mp(pooled.at[mp, t], pooled.at[mp, t], p_sem, k, t)

    @pl.loop(0, BALLS)
    def _(t):
        for k in (1, 3, 2):
            turn(k, t).wait_recv()
        keep_turn(t).wait()
        real = mask_ref[pl.ds(mp * BALLS + t, 1), :] > 0
        out, means = fine_ball(x[rows(t, BALL), :], real, qkv_ref, out_ref)
        state[rows(t, BALL), :] = out
        pooled[mp, t] = means
        for k in (2, 1, 3):
            share(k, t).start()

    load[2].wait()
    load[3].wait()
    load[6].wait()

    def give(k, t):
        return to_mp(
            tiles.at[rows(t, BALL), cols(peer(k))],
            turned_ref.at[rows(mp * BALLS + t, BALL), :],
            t_sem,
            k,
            t,
        )

    def keep_give(t):
        return pltpu.make_async_copy(
            tiles.at[rows(t, BALL), cols(mp)],
            turned_ref.at[rows(mp * BALLS + t, BALL), :],
            own.at[1, t],
        )

    def feed(t, count):
        at = pl.ds(t * BALL, count * BALL)
        tiles[at, :] = forward_tile(state[at, :], mp, gate_ref, up_ref, down_ref).astype(BF16)
        for u in range(t, t + count):
            for k in (2, 1, 3):
                give(k, u).start()
            keep_give(u).start()

    @pl.loop(1, WIDE // 2)
    def _(i):
        broadcast(i).wait_recv()
        pass_on(i).start()

    @pl.loop(0, WIDE // 2)
    def _(i):
        pass_on(i).wait_recv()

    feed(0, 2)

    def pass_one(q):
        return remote(
            one.at[pl.ds(1, 2), rows(q, ONE), :],
            mate_one.at[:, rows(q, ONE), :],
            e_sem.at[0, 3, q],
            e_sem.at[1, 3, q],
            {"wide": others[0]},
        )

    def pass_two(j, q):
        return remote(
            two.at[pl.ds(1, 2), rows(q, TWO), :],
            mate_two.at[j, :, rows(q, TWO), :],
            e_sem.at[0, j, q],
            e_sem.at[1, j, q],
            {"wide": others[j]},
        )

    pair = lax.broadcasted_iota(I32, (32, 64), 0) == lax.broadcasted_iota(I32, (32, 64), 1) // 2
    pair = jnp.where(pair, 1.0, 0.0).astype(BF16)
    load[4].wait()

    def project(q):
        firsts, seconds = [], []
        for ball in range(BALLS):
            real = mask_ref[pl.ds(q * BALLS + ball, 1), :] > 0
            means = pooled[q, ball].astype(F32)
            firsts.append(norm(means).astype(BF16))
            sums = means * pooling(real, 4)[1]
            high = sums.astype(BF16)
            rest = (sums - high.astype(F32)).astype(BF16)
            counted = jnp.maximum(pooling(real, 8)[1], 1.0)
            seconds.append(norm((dot(pair, high) + dot(pair, rest)) / counted).astype(BF16))
        firsts = jnp.concatenate(firsts, 0)
        seconds = jnp.concatenate(seconds, 0)
        for t in (1, 2):
            two[t, rows(q, TWO), :] = dot(seconds, w_ref[1, t]).astype(BF16)
            one[t, rows(q, ONE), :] = dot(firsts, w_ref[0, t]).astype(BF16)
        for j in (1, 2, 0):
            pass_two(j, q).start()
        pass_one(q).start()
        two[0, rows(q, TWO), :] = (dot(seconds, w_ref[1, 0]) * SCALE).astype(BF16)
        one[0, rows(q, ONE), :] = (dot(firsts, w_ref[0, 0]) * SCALE).astype(BF16)

    project(mp)
    for k in (1, 3, 2):

        @pl.loop(0, BALLS)
        def _(t):
            share(MP - k, t).wait_recv()

        project(peer(k))

    feed(2, 1)

    @pl.loop(1, WIDE // 2)
    def _(i):
        broadcast_lift(i).wait_recv()
        pass_on_lift(i).start()


    def hand_to(q, k, level):
        at = pl.ds(0, ONE) if level == 0 else pl.ds(ONE, TWO)
        return to_mp(mixed.at[q, at, :], all_mixed.at[at, cols(mp)], m_sem, k, level)

    def hand(k, level):
        return hand_to(peer(k), k, level)

    def keep_hand(level):
        at = pl.ds(0, ONE) if level == 0 else pl.ds(ONE, TWO)
        return pltpu.make_async_copy(
            mixed.at[mp, at, :], all_mixed.at[at, cols(mp)], own.at[2, level]
        )

    for j in range(3):
        flags(j).wait()

    def fill(keys_ref, values_ref, begin, src, first, flag):
        for c in range(src.shape[1] // 128):
            at = slice(c * 128, (c + 1) * 128)
            here = flag[first + c : first + c + 1, :] > 0
            keys, values = augment(src[0, at, :], src[1, at, :], columns_of(here))
            to = slice(begin + c * 128, begin + (c + 1) * 128)
            for head in range(2):
                keys_ref[head, to, :] = keys[head]
                values_ref[head, to, :] = values[head]

    def masked_of(keys_ref, at):
        spare = keys_ref[0, at, :].astype(F32)
        return jnp.min(jnp.where(lanes(256) == 64, spare, 0.0), -1, keepdims=True) < 0.0

    mine = keep_ref[...]
    fill(keys_one, values_one, 0, one.at[1:], 0, mine)

    @pl.loop(0, MP)
    def _(q):
        pass_one(q).wait()

    fill(keys_one, values_one, 4 * ONE, mate_one, 0, mate_keep[0])

    @pl.loop(1, MP + 1)
    def _(k):
        q = peer(k)
        at = rows(q, ONE)
        mixed[q, 0:ONE, :] = attend_pair(
            one[0, at, :], one[1, at, :], one[2, at, :], masked_of(keys_one, at),
            lambda head: keys_one[head], lambda head: values_one[head],
        )

        @pl.when(k < MP)
        def _():
            hand(k, 0).start()

    keep_hand(0).start()

    fill(keys_two, values_two, 0, two.at[1:], 8, mine)

    @pl.loop(0, MP)
    def _(q):
        for j in range(3):
            pass_two(j, q).wait()

    for j in range(3):
        fill(keys_two, values_two, (j + 1) * 4 * TWO, mate_two.at[j], 8, mate_keep[j])

    @pl.loop(0, 2)
    def _(p):
        at = rows(p, 256)
        both = attend_pair(
            two[0, at, :], two[1, at, :], two[2, at, :], masked_of(keys_two, at),
            lambda head: keys_two[head], lambda head: values_two[head],
        )
        for h in range(2):
            q = p * 2 + h
            k = lax.rem(q + MP - mp, MP)
            mixed[q, ONE:COARSE, :] = both[h * TWO : (h + 1) * TWO]

            @pl.when(k > 0)
            def _():
                hand_to(q, k, 1).start()

    keep_hand(1).start()

    feed(3, 1)

    load[5].wait()

    @pl.loop(0, WIDE // 2)
    def _(i):
        pass_on_lift(i).wait_recv()

    for level in range(2):
        keep_hand(level).wait()
        for k in (1, 3, 2):
            hand(k, level).wait()
    for level, begin, size in ((0, 0, 64), (1, ONE, 32)):
        span = slice(begin, begin + size * BALLS)
        total = jnp.zeros((size * BALLS, WIDTH), F32)
        for g in range(MP):
            total = total + dot(
                all_mixed[span, cols(peer(g))],
                lift_ref[g, level * LOCAL : (level + 1) * LOCAL, :],
            )
        total = total.astype(BF16)
        for ball in range(BALLS):
            at = slice(0, 64) if level == 0 else slice(64, 96)
            lifted[ball, at, :] = total[ball * size : (ball + 1) * size]

    def rise(k):
        return to_mp(lifted.at[:, :, cols(peer(k))], lifted_ref.at[pl.ds(mp * BALLS, BALLS)], l_sem, k, 0)

    for k in (2, 1, 3):
        rise(k).start()
    keep_rise = pltpu.make_async_copy(
        lifted.at[:, :, cols(mp)], lifted_ref.at[pl.ds(mp * BALLS, BALLS)], own.at[3, 0]
    )
    keep_rise.start()

    @pl.loop(0, BALLS)
    def _(t):
        keep_give(t).wait()
        for k in (1, 3, 2):
            give(k, t).wait_recv()

    runs = run_matrix(
        lax.broadcasted_iota(I32, (BALL, 96), 0), lax.broadcasted_iota(I32, (BALL, 96), 1)
    )

    def update(q):
        @pl.loop(0, BALLS)
        def _(t):
            i = q * BALLS + t
            at = rows(i, BALL)
            wide[at, :] = turned_ref[at, :].astype(F32) + dot(runs, lifted_ref[i])

    keep_rise.wait()
    update(mp)
    for k in (1, 3, 2):
        rise(k).wait_recv()
        update(peer(MP - k))
    wide[ROWS : ROWS + 8, :] = jnp.zeros((8, LOCAL), F32)

    def rows_copy(k):
        to = turn_of(me, k)
        return remote(
            outgoing.at[to], back_ref.at[me], r_sem.at[0, k], r_sem.at[1, k], {"wide": to}
        )

    @pl.loop(1, WIDE)
    def _(k):
        gather_bucket(0, lambda s: code_ref[s] >> 1, wide, staged, outgoing, turn_of(me, k))
        rows_copy(k).start()

    gather_bucket(0, lambda s: code_ref[s] >> 1, wide, staged, outgoing, me)
    last = pltpu.make_async_copy(outgoing.at[me], back_ref.at[me], own.at[3, 1])
    last.start()

    @pl.loop(0, BALLS)
    def _(t):
        for k in (1, 3, 2):
            turn(k, t).wait_send()
            share(k, t).wait_send()
            give(k, t).wait_send()

    @pl.loop(1, WIDE // 2)
    def _(i):
        broadcast(i).wait_send()
        broadcast_lift(i).wait_send()

    @pl.loop(0, WIDE // 2)
    def _(i):
        pass_on(i).wait_send()
        pass_on_lift(i).wait_send()

    for k in (1, 3, 2):
        fetch(k).wait_send()
        fetch_lift(k).wait_send()
        rise(k).wait_send()
    last.wait()

    @pl.loop(1, WIDE)
    def _(k):
        rows_copy(k).wait()


def middle(slots, codes, got, mask, keep, weights, collective):
    dma = pltpu.SemaphoreType.DMA
    return pl.pallas_call(
        middle_kernel,
        out_shape=shape((WIDE, CAP, LOCAL), BF16),
        in_specs=[SMEM, SMEM, VMEM, VMEM, VMEM] + [ANY] * 7,
        out_specs=ANY,
        scratch_shapes=[
            pltpu.VMEM((ROWS, LOCAL), BF16),
            pltpu.VMEM((MP * BALLS, 96, LOCAL), BF16),
            pltpu.VMEM((WIDE, CAP, LOCAL), BF16),
            dma((2, WIDE)),
            pltpu.VMEM((SLOTS, LOCAL), F32),
            pltpu.VMEM((1, CAP, LOCAL), F32),
            pltpu.VMEM((MP * BALLS, BALL, LOCAL), BF16),
            pltpu.VMEM((QUARTER, WIDTH), BF16),
            pltpu.VMEM((QUARTER, WIDTH), F32),
            pltpu.VMEM((MP, BALLS, 64, WIDTH), BF16),
            pltpu.VMEM((QUARTER, WIDTH), BF16),
            pltpu.VMEM((3, 4 * ONE, LOCAL), BF16),
            pltpu.VMEM((3, 4 * TWO, LOCAL), BF16),
            pltpu.VMEM((2, 4 * ONE, LOCAL), BF16),
            pltpu.VMEM((3, 2, 4 * TWO, LOCAL), BF16),
            pltpu.VMEM((3, 12, 128), I32),
            pltpu.VMEM((MP, COARSE, LOCAL), BF16),
            pltpu.VMEM((COARSE, WIDTH), BF16),
            pltpu.VMEM((BALLS, 96, WIDTH), BF16),
            pltpu.VMEM((2, 8 * ONE, LOCAL), BF16),
            pltpu.VMEM((2, 8 * ONE, LOCAL), BF16),
            pltpu.VMEM((2, 16 * TWO, LOCAL), BF16),
            pltpu.VMEM((2, 16 * TWO, LOCAL), BF16),
            pltpu.VMEM((3, WIDTH, WIDTH), BF16),
            pltpu.VMEM((WIDTH, WIDTH), BF16),
            pltpu.VMEM((MP, WIDTH, WIDTH), BF16),
            pltpu.VMEM((MP, WIDTH, WIDTH), BF16),
            pltpu.VMEM((MP, WIDTH, WIDTH), BF16),
            pltpu.VMEM((2, 3, WIDTH, LOCAL), BF16),
            pltpu.VMEM((MP, 2 * LOCAL, WIDTH), BF16),
            dma((2, MP, BALLS)),
            dma((2, MP, BALLS)),
            dma((2, 4, MP)),
            dma((2, 3)),
            dma((2, MP, 2)),
            dma((2, MP, BALLS)),
            dma((2, MP, 1)),
            dma((2, MP, 2)),
            dma((2, WIDE // 2, 2)),
            dma((2, WIDE // 2, 2)),
            dma((4, BALLS)),
            dma((7,)),
        ],
        compiler_params=params(collective),
    )(slots, codes, got, mask, keep, *weights)


def on_device(points, mask, perm, w_qkv, w_out, w_gate_up, w_down, w_coarse, w_coarse_out):
    slot, source, codes = index(perm, mask)
    own_gate_up = w_gate_up.reshape(2 * WIDTH, WIDTH)
    own_lift = w_coarse_out.reshape(2 * LOCAL, WIDTH)
    got, got_code, landed, owned_mask, keep, full_qkv, full_out, full_down, full_gate = (
        send_rows(
            source.reshape(SLOTS),
            points,
            codes,
            [
                w_qkv.reshape(3 * WIDTH, LOCAL),
                w_out,
                w_down,
                own_gate_up,
            ],
            1,
        )
    )
    full_qkv = full_qkv.reshape(3, WIDTH, WIDTH)
    full_out = full_out.reshape(WIDTH, WIDTH)
    returned = middle(
        landed.reshape(ROWS), got_code.reshape(SLOTS), got.reshape(SLOTS, LOCAL), owned_mask, keep,
        [full_qkv, full_out, own_gate_up, full_gate, full_down, w_coarse, own_lift], 2,
    )
    return pl.pallas_call(
        finish_kernel,
        out_shape=shape((ROWS, LOCAL), F32),
        in_specs=[SMEM, ANY],
        out_specs=ANY,
        scratch_shapes=[
            pltpu.VMEM((SLOTS, LOCAL), BF16),
            pltpu.VMEM((SLOTS, LOCAL), F32),
            pltpu.VMEM((ROWS, LOCAL), F32),
            pltpu.SemaphoreType.DMA((SLOTS // 1024,)),
            pltpu.SemaphoreType.DMA((ROWS // 512,)),
        ],
        compiler_params=params(),
    )(slot.reshape(ROWS), returned.reshape(SLOTS, LOCAL))


def solution(mesh):
    placed = (
        P("wide", "mp"),
        P("wide"),
        P("wide"),
        P(None, None, "mp"),
        P("mp", None),
        P(None, None, "mp"),
        P("mp", None),
        P(None, None, None, "mp"),
        P(None, "mp", None),
    )
    return jax.shard_map(
        on_device, mesh=mesh, in_specs=placed, out_specs=P("wide", "mp"), check_vma=False
    )
```
